32 devices in a mesh: section: 4 (over y, x), tp: 4 (over z), seq: 2 (over core).
Axes of the slice: x: 2, y: 2, z: 4, core: 2. Of those that a mesh axis runs over, the one named last changes fastest.
Arguments:
- residual_entering: float32 [4, 2, 512, 1024], P(None, 'seq', None, 'tp'), may hold values from -6 to 6
- upstream_sensitivity: float32 [4, 2, 512, 1024], P(None, 'seq', None, 'tp'), may hold values from -6 to 6
- piece_lead_lines: float32 [4, 4, 2, 1024], P(None, None, 'seq', 'tp'), may hold values from -6 to 6
- dividend_start: float32 [2, 4, 2, 1024], P(None, None, 'seq', 'tp'), may hold values from -6 to 6
- divisor_start: float32 [2, 4, 2, 1024], P(None, None, 'seq', 'tp'), may hold values from 0.5 to 4
- power_offset_start: float32 [2, 4, 2, 1024], P(None, None, 'seq', 'tp'), may hold values from -2 to 2
- attend_standard_scale: float32 [2, 1024], P(None, 'tp'), may hold values from 0.5 to 1.5
- attend_standard_offset: float32 [2, 1024], P(None, 'tp'), may hold values from -1.5 to 1.5
- attend_lag_fractions: float32 [2, 3, 1024], P(None, None, 'tp'), may hold values from 0.05 to 0.95
- fading_log_rate: float32 [2, 1024], P(None, 'tp'), may hold values from -6 to -1
- reward_first_word: float32 [2, 1024], P(None, 'tp'), may hold values from -1 to 1
- attend_entry_matrix: bfloat16 [2, 3, 1024, 1024], P(None, None, None, 'tp'), may hold values from -0.1875 to 0.1875
- attend_exit_matrix: bfloat16 [2, 1024, 1024], P(None, 'tp'), may hold values from -0.75 to 0.75
- feed_standard_scale: float32 [2, 1024], P(None, 'tp'), may hold values from 0.5 to 1.5
- feed_standard_offset: float32 [2, 1024], P(None, 'tp'), may hold values from -1.5 to 1.5
- feed_lag_fractions: float32 [2, 2, 1024], P(None, None, 'tp'), may hold values from 0.05 to 0.95
- feed_lookup_matrix: bfloat16 [2, 1024, 4096], P(None, None, 'tp'), may hold values from -0.1875 to 0.1875
- feed_content_matrix: bfloat16 [2, 4096, 1024], P(None, 'tp'), may hold values from -0.09375 to 0.09375
- feed_gate_matrix: bfloat16 [2, 1024, 1024], P(None, None, 'tp'), may hold values from -0.1875 to 0.1875
Outputs:
- outputs: float32 [4, 2, 512, 1024], P(None, 'seq', 'section', 'tp')
- inputs_grad: float32 [4, 2, 512, 1024], P(None, 'seq', 'section', 'tp')
- prev_grad: float32 [4, 4, 2, 1024], P(None, None, 'seq', 'tp')
- num_grad: float32 [2, 4, 2, 1024], P(None, None, 'seq', 'tp')
- den_grad: float32 [2, 4, 2, 1024], P(None, None, 'seq', 'tp')
- max_grad: float32 [2, 4, 2, 1024], P(None, None, 'seq', 'tp')
- tm_gain_grad: float32 [2, 1024], P(None, 'tp')
- tm_bias_grad: float32 [2, 1024], P(None, 'tp')
- tm_mix_grad: float32 [2, 3, 1024], P(None, None, 'tp')
- decay_grad: float32 [2, 1024], P(None, 'tp')
- bonus_grad: float32 [2, 1024], P(None, 'tp')
- tm_in_grad: float32 [2, 3, 1024, 1024], P(None, None, None, 'tp')
- tm_out_grad: float32 [2, 1024, 1024], P(None, 'tp')
- cm_gain_grad: float32 [2, 1024], P(None, 'tp')
- cm_bias_grad: float32 [2, 1024], P(None, 'tp')
- cm_mix_grad: float32 [2, 2, 1024], P(None, None, 'tp')
- cm_key_grad: float32 [2, 1024, 4096], P(None, None, 'tp')
- cm_value_grad: float32 [2, 4096, 1024], P(None, 'tp')
- cm_recept_grad: float32 [2, 1024, 1024], P(None, None, 'tp')
The draws below stay inside these ranges and needn't reach their ends.
All inputs are finite; a program needn't handle non-finite values.
Results may differ from the reference program's by a relative error of at most 0.013.
Values may be sent and summed in bfloat16 or wider, within the bound.
A program may use at most 448 MiB of HBM per device.

```python
import math
from functools import partial
import jax
import jax.numpy as jnp
from jax import lax

EMBED_SIZE = 1024
FF = 4096
DEPTH_TOTAL = 2
MB = 4
SEG_LEN = 512
NSEG = 2


def shard_levels(stream_key, shape, shards, smallest, top_value):
    gain, own = 1.0, jax.random.fold_in(stream_key, 6)
    for axis_at, blocks in shards:
        steps = jnp.exp(jax.random.uniform(jax.random.fold_in(own, axis_at), (blocks,), jnp.float32, smallest / len(shards), top_value / len(shards)))
        gain = gain * jnp.repeat(steps, shape[axis_at] // blocks).reshape([-1 if axis == axis_at else 1 for axis in range(len(shape))])
    return gain


def centred(key, shape, spread, limit, shards=(), held_as=jnp.bfloat16):
    entries = jax.random.normal(key, shape, jnp.float32) * spread
    if len(shards) > 0:
        entries = shard_levels(key, shape, shards, -0.22, 0.18) * entries
    return jnp.clip(entries, min=-limit, max=limit).astype(held_as)


def setup_inputs(seed: int = 0) -> dict:
    seeds = jax.random.split(jax.random.key(seed), 20)
    return {
        "residual_entering": centred(seeds[0], (MB, NSEG, SEG_LEN, EMBED_SIZE), 1.0, 6.0, ((1, 2), (3, 4)), jnp.float32),
        "upstream_sensitivity": centred(seeds[1], (MB, NSEG, SEG_LEN, EMBED_SIZE), 1.0, 6.0, ((1, 2), (3, 4)), jnp.float32),
        "piece_lead_lines": centred(seeds[2], (2 * DEPTH_TOTAL, MB, NSEG, EMBED_SIZE), 1.0, 6.0, ((2, 2), (3, 4)), jnp.float32),
        "dividend_start": centred(seeds[3], (DEPTH_TOTAL, MB, NSEG, EMBED_SIZE), 1.0, 6.0, ((2, 2), (3, 4)), jnp.float32),
        "divisor_start": jnp.clip(jnp.exp(math.log(4.0) - 2.0794415 * jax.random.uniform(seeds[4], (DEPTH_TOTAL, MB, NSEG, EMBED_SIZE), jnp.float32) ** shard_levels(seeds[4], (DEPTH_TOTAL, MB, NSEG, EMBED_SIZE), ((2, 2), (3, 4)), -0.2, 0.2)), 0.5, 4.0),
        "power_offset_start": jnp.clip(jax.random.uniform(seeds[5], (DEPTH_TOTAL, MB, NSEG, EMBED_SIZE), jnp.float32, -2.0, 2.0) * shard_levels(seeds[5], (DEPTH_TOTAL, MB, NSEG, EMBED_SIZE), ((2, 2), (3, 4)), -0.4, 0.0), -2.0, 2.0),
        "attend_standard_scale": jnp.clip(1.0 + 0.1 * jax.random.normal(seeds[6], (DEPTH_TOTAL, EMBED_SIZE), jnp.float32), 0.5, 1.5),
        "attend_standard_offset": centred(seeds[7], (DEPTH_TOTAL, EMBED_SIZE), 0.3, 1.5, ((1, 4),), jnp.float32),
        "attend_lag_fractions": jnp.clip(0.05 + 0.9 * jax.random.uniform(seeds[8], (DEPTH_TOTAL, 3, EMBED_SIZE), jnp.float32) ** shard_levels(seeds[8], (DEPTH_TOTAL, 3, EMBED_SIZE), ((2, 4),), -0.2, 0.2), 0.05, 0.95),
        "fading_log_rate": jnp.clip(-6.0 + 5.0 * jax.random.uniform(seeds[9], (DEPTH_TOTAL, EMBED_SIZE), jnp.float32) ** shard_levels(seeds[9], (DEPTH_TOTAL, EMBED_SIZE), ((1, 4),), -0.2, 0.2), -6.0, -1.0),
        "reward_first_word": jnp.clip(jax.random.uniform(seeds[10], (DEPTH_TOTAL, EMBED_SIZE), jnp.float32, -1.0, 1.0) * shard_levels(seeds[10], (DEPTH_TOTAL, EMBED_SIZE), ((1, 4),), -0.4, 0.0), -1.0, 1.0),
        "attend_entry_matrix": centred(seeds[11], (DEPTH_TOTAL, 3, EMBED_SIZE, EMBED_SIZE), EMBED_SIZE ** -0.5, 0.1875, ((3, 4),)),
        "attend_exit_matrix": centred(seeds[12], (DEPTH_TOTAL, EMBED_SIZE, EMBED_SIZE), (EMBED_SIZE // 16) ** -0.5, 0.75, ((1, 4),)),
        "feed_standard_scale": jnp.clip(1.0 + 0.1 * jax.random.normal(seeds[13], (DEPTH_TOTAL, EMBED_SIZE), jnp.float32), 0.5, 1.5),
        "feed_standard_offset": centred(seeds[14], (DEPTH_TOTAL, EMBED_SIZE), 0.3, 1.5, ((1, 4),), jnp.float32),
        "feed_lag_fractions": jnp.clip(0.05 + 0.9 * jax.random.uniform(seeds[15], (DEPTH_TOTAL, 2, EMBED_SIZE), jnp.float32) ** shard_levels(seeds[15], (DEPTH_TOTAL, 2, EMBED_SIZE), ((2, 4),), -0.2, 0.2), 0.05, 0.95),
        "feed_lookup_matrix": centred(seeds[16], (DEPTH_TOTAL, EMBED_SIZE, FF), EMBED_SIZE ** -0.5, 0.1875, ((2, 4),)),
        "feed_content_matrix": centred(seeds[17], (DEPTH_TOTAL, FF, EMBED_SIZE), FF ** -0.5, 0.09375, ((1, 4),)),
        "feed_gate_matrix": centred(seeds[18], (DEPTH_TOTAL, EMBED_SIZE, EMBED_SIZE), EMBED_SIZE ** -0.5, 0.1875, ((2, 4),)),
    }


@jax.custom_vjp
def low(v):
    return lax.optimization_barrier(v.astype(jnp.bfloat16)).astype(jnp.float32)

@jax.custom_vjp
def low_back(v):
    return v

def low_keep(v):
    return (low(v), None)

def low_pass(kept, grad):
    return (grad,)

def back_keep(v):
    return (v, None)

def back_low(kept, grad):
    return (low(grad),)
low.defvjp(low_keep, low_pass)
low_back.defvjp(back_keep, back_low)
epsilon = 1e-05

def matmul(left_side, right_side):
    return jnp.dot(left_side, right_side, precision=lax.Precision.HIGHEST)

def normalize(incoming_lines, scale_entries, offset_entries):
    center = incoming_lines - lax.optimization_barrier(jnp.mean(incoming_lines, axis=-1, keepdims=True))
    inv_scale = lax.rsqrt(lax.optimization_barrier(jnp.mean(center * center, axis=-1, keepdims=True)) + epsilon)
    return center * inv_scale * scale_entries + offset_entries

def mixtures(incoming_lines, earlier_line, scale_entries, offset_entries, blend_lines):
    normed = normalize(incoming_lines, scale_entries, offset_entries)
    shifted = jnp.concatenate([earlier_line[None, :], normed[:-1]], axis=0)
    return [low(normed * blend_lines[position] + shifted * (1.0 - blend_lines[position])) for position in range(blend_lines.shape[0])]

def averaged_content_words(incoming_lookups, incoming_contents, fading_entries, reward_entries, dividend_entries, divisor_entries, peak_line):
    decay_rate = jnp.exp(fading_entries)

    def advance(state_in, block_in):
        numer_in, denom_in, topmost = state_in
        lookup_now, value_now = block_in
        leading_power = reward_entries + lookup_now
        peak_exp = jnp.maximum(topmost, leading_power)
        older = jnp.exp(topmost - peak_exp)
        newer = jnp.exp(leading_power - peak_exp)
        result = (older * numer_in + newer * value_now) / (older * denom_in + newer)
        decayed = topmost - decay_rate
        peak_exp = jnp.maximum(decayed, lookup_now)
        older = jnp.exp(decayed - peak_exp)
        newer = jnp.exp(lookup_now - peak_exp)
        return ((older * numer_in + newer * value_now, older * denom_in + newer, peak_exp), result)
    unused, results = lax.scan(advance, (dividend_entries, divisor_entries, peak_line), (incoming_lookups, incoming_contents))
    return results

def attend_blend(incoming_lines, earlier_line, carry_collection, scale_entries, offset_entries, blend_lines, fading_entries, reward_entries, entry_matrix, exit_matrix):
    mixed_rows = mixtures(incoming_lines, earlier_line, scale_entries, offset_entries, blend_lines)
    lookups_here = low_back(matmul(mixed_rows[0], entry_matrix[0]))
    contents_here = low_back(matmul(mixed_rows[1], entry_matrix[1]))
    recept = low_back(matmul(mixed_rows[2], entry_matrix[2]))
    averaged_content_lines = averaged_content_words(lookups_here, contents_here, fading_entries, reward_entries, carry_collection[0], carry_collection[1], carry_collection[2])
    output = low(jax.nn.sigmoid(recept) * averaged_content_lines)
    return incoming_lines + low_back(matmul(output, exit_matrix))

def channel_mix(incoming_lines, earlier_line, scale_entries, offset_entries, blend_lines, w_key, w_value, w_recept):
    mixed_rows = mixtures(incoming_lines, earlier_line, scale_entries, offset_entries, blend_lines)
    hidden_pre = low_back(matmul(mixed_rows[0], w_key))
    hidden = low(jnp.square(jax.nn.softplus(hidden_pre)))
    kv_rows = low_back(matmul(hidden, w_value))
    gate_pre = low_back(matmul(mixed_rows[1], w_recept))
    return incoming_lines + jax.nn.sigmoid(gate_pre) * kv_rows

def segment(incoming_lines, earlier_lines, carry_collection, learned_settings):
    attend_standard_scale, attend_standard_offset, attend_lag_fractions, fading_log_rate, reward_first_word, attend_entry_matrix, attend_exit_matrix, feed_standard_scale, feed_standard_offset, feed_lag_fractions, feed_lookup_matrix, feed_content_matrix, feed_gate_matrix = learned_settings
    incoming_signal = incoming_lines
    for level_index in range(DEPTH_TOTAL):
        incoming_signal = attend_blend(incoming_signal, earlier_lines[2 * level_index], carry_collection[:, level_index], attend_standard_scale[level_index], attend_standard_offset[level_index], attend_lag_fractions[level_index], fading_log_rate[level_index], reward_first_word[level_index], attend_entry_matrix[level_index], attend_exit_matrix[level_index])
        incoming_signal = channel_mix(incoming_signal, earlier_lines[2 * level_index + 1], feed_standard_scale[level_index], feed_standard_offset[level_index], feed_lag_fractions[level_index], feed_lookup_matrix[level_index], feed_content_matrix[level_index], feed_gate_matrix[level_index])
    return incoming_signal

def forward(rows_all, piece_lead_lines, dividend_start, divisor_start, power_offset_start, *learned_settings):
    segments = MB * NSEG
    flat_rows = rows_all.reshape(segments, SEG_LEN, EMBED_SIZE)
    prev_flat = jnp.moveaxis(piece_lead_lines.reshape(2 * DEPTH_TOTAL, segments, EMBED_SIZE), 1, 0)
    state_flat = jnp.moveaxis(jnp.stack([dividend_start, divisor_start, power_offset_start]).reshape(3, DEPTH_TOTAL, segments, EMBED_SIZE), 2, 0)
    outputs = jax.vmap(partial(segment, learned_settings=learned_settings))(flat_rows, prev_flat, state_flat)
    return outputs.reshape(MB, NSEG, SEG_LEN, EMBED_SIZE)

def reference(residual_entering, upstream_sensitivity, piece_lead_lines, dividend_start, divisor_start, power_offset_start, attend_standard_scale, attend_standard_offset, attend_lag_fractions, fading_log_rate, reward_first_word, attend_entry_matrix, attend_exit_matrix, feed_standard_scale, feed_standard_offset, feed_lag_fractions, feed_lookup_matrix, feed_content_matrix, feed_gate_matrix):
    real_numbers = [tensor_entry.astype(jnp.float32) for tensor_entry in (residual_entering, piece_lead_lines, dividend_start, divisor_start, power_offset_start, attend_standard_scale, attend_standard_offset, attend_lag_fractions, fading_log_rate, reward_first_word, attend_entry_matrix, attend_exit_matrix, feed_standard_scale, feed_standard_offset, feed_lag_fractions, feed_lookup_matrix, feed_content_matrix, feed_gate_matrix)]
    outputs, pullback = jax.vjp(forward, *real_numbers)
    gradients = pullback(upstream_sensitivity.astype(jnp.float32))
    return (outputs, gradients[0], gradients[1], gradients[2], gradients[3], gradients[4], gradients[5], gradients[6], gradients[7], gradients[8], gradients[9], gradients[10], gradients[11], gradients[12], gradients[13], gradients[14], gradients[15], gradients[16], gradients[17])
```

```python
from functools import partial

import jax
import jax.numpy as jnp
from jax import lax
from jax.experimental import pallas as pl
from jax.experimental.pallas import tpu as pltpu
from jax.sharding import PartitionSpec as P

BLOCK = 128


epsilon = 1e-05


def product(left_side, right_side):
    return jnp.dot(left_side, right_side, preferred_element_type=jnp.float32)


def inner_rows(left_side, right_side):
    return lax.dot_general(
        left_side, right_side, (((0,), (0,)), ((), ())), preferred_element_type=jnp.float32
    )


def against(left_side, right_side):
    return lax.dot_general(
        left_side, right_side, (((1,), (1,)), ((), ())), preferred_element_type=jnp.float32
    )


def weighted_value_blocks(
    block_length,
    incoming_lookups,
    incoming_contents,
    fading_entries,
    reward_entries,
    dividend_entries,
    divisor_entries,
    peak_line,
):
    decay_rate = jnp.exp(fading_entries)
    total_rows, channels = incoming_lookups.shape
    places = jnp.arange(block_length, dtype=jnp.float32)
    earlier = places[:, None] > places[None, :]
    spacing = places[:, None] - 1.0 - places[None, :]
    remain = block_length - 1.0 - places

    def advance(state_in, block_in):
        numer_in, denom_in, topmost = state_in
        lookup_piece_tile, value_block = block_in
        spread_exp = lookup_piece_tile[None, :, :] - spacing[:, :, None] * decay_rate
        spread_exp = jnp.where(earlier[:, :, None], spread_exp, -1e30)
        leading_power = reward_entries + lookup_piece_tile
        start_exp = topmost[None, :] - places[:, None] * decay_rate
        peak_exp = jnp.maximum(jnp.maximum(jnp.max(spread_exp, axis=1), leading_power), start_exp)
        weights = jnp.exp(spread_exp - peak_exp[:, None, :])
        from_state = jnp.exp(start_exp - peak_exp)
        own_term = jnp.exp(leading_power - peak_exp)
        numer_out = (
            from_state * numer_in
            + jnp.sum(weights * value_block[None, :, :], axis=1)
            + own_term * value_block
        )
        denom_out = from_state * denom_in + jnp.sum(weights, axis=1) + own_term
        ending = lookup_piece_tile - remain[:, None] * decay_rate
        stopping = topmost - block_length * decay_rate
        new_top = jnp.maximum(jnp.max(ending, axis=0), stopping)
        scaled = jnp.exp(ending - new_top[None, :])
        carried = jnp.exp(stopping - new_top)
        new_numer = carried * numer_in + jnp.sum(scaled * value_block, axis=0)
        new_denom = carried * denom_in + jnp.sum(scaled, axis=0)
        return ((new_numer, new_denom, new_top), numer_out / denom_out)

    blocks = total_rows // block_length
    unused, results = lax.scan(
        jax.checkpoint(advance),
        (dividend_entries, divisor_entries, peak_line),
        (
            incoming_lookups.reshape(blocks, block_length, channels),
            incoming_contents.reshape(blocks, block_length, channels),
        ),
    )
    return results.reshape(total_rows, channels)


def spread_plain(rows_in):
    features = rows_in.shape[1] * lax.axis_size("tp")
    mean_row = lax.psum(jnp.sum(rows_in, axis=1), "tp") / features
    center = rows_in - mean_row[:, None]
    inv_std = lax.rsqrt(lax.psum(jnp.sum(center * center, axis=1), "tp") / features + epsilon)
    normal_share = center * inv_std[:, None]
    normal_full = lax.all_gather(normal_share.astype(jnp.bfloat16), "tp", axis=1, tiled=True)
    return normal_share, inv_std, normal_full


def mix_plain(normal_full, small_full, mix_count):
    normed = normal_full.astype(jnp.float32) * small_full[0] + small_full[1]
    shifted = jnp.concatenate([small_full[2:3], normed[:-1]], axis=0)
    gap = normed - shifted
    mixed = [(shifted + gap * small_full[3 + i]).astype(jnp.bfloat16) for i in range(mix_count)]
    return mixed, gap


def scatter_plain(branch):
    return lax.psum_scatter(
        branch.astype(jnp.bfloat16), "tp", scatter_dimension=1, tiled=True
    ).astype(jnp.float32)


def time_forward_plain(rows_in, small_full, small_own, wkv_rows, entry_matrix, exit_matrix):
    normal_share, inv_std, normal_full = spread_plain(rows_in)
    mixed, gap = mix_plain(normal_full, small_full, 3)
    lookups, contents, recept = [product(mixed[i], entry_matrix[i]) for i in range(3)]
    averaged, pullback = jax.vjp(
        partial(weighted_value_blocks, BLOCK), lookups, contents, *[wkv_rows[i] for i in range(5)]
    )
    gate = jax.nn.sigmoid(recept)
    output = (gate * averaged).astype(jnp.bfloat16)
    rows_out = rows_in + scatter_plain(product(output, exit_matrix))
    kept = (normal_share, inv_std, normal_full, mixed, gap, averaged, pullback, gate, output)
    return rows_out, kept


def channel_forward_plain(rows_in, small_full, small_own, w_key, w_value, w_gate):
    normal_share, inv_std, normal_full = spread_plain(rows_in)
    mixed, gap = mix_plain(normal_full, small_full, 2)
    hidden_pre = product(mixed[0], w_key)
    soft = jax.nn.softplus(hidden_pre)
    hidden = jnp.square(soft).astype(jnp.bfloat16)
    gate = jax.nn.sigmoid(product(mixed[1], w_gate))
    kv_share = scatter_plain(product(hidden, w_value))
    kept = (normal_share, inv_std, normal_full, mixed, gap, hidden_pre, soft, hidden, gate, kv_share)
    return rows_in + gate * kv_share, kept


def norm_back_plain(rows_grad, mix_grads, gap, normal_full, normal_share, inv_std, small_full, small_own):
    share = normal_share.shape[1]
    features = small_full.shape[1]
    to_normed = sum(grad * small_full[3 + i] for i, grad in enumerate(mix_grads))
    to_shifted = sum(grad * (1.0 - small_full[3 + i]) for i, grad in enumerate(mix_grads))
    ratio_grads = [jnp.sum(grad * gap, axis=0) for grad in mix_grads]
    ratio_grads += [jnp.zeros_like(ratio_grads[0])] * (3 - len(mix_grads))
    to_normed = to_normed + jnp.concatenate([to_shifted[1:], jnp.zeros_like(to_shifted[:1])], axis=0)
    normed_grad = scatter_plain(to_normed)
    edge = lax.psum_scatter(
        jnp.stack([to_shifted[0]] + ratio_grads), "tp", scatter_dimension=1, tiled=True
    )
    scaled = normed_grad * small_own[0]
    first, second = lax.psum((jnp.sum(scaled, axis=1), jnp.sum(scaled * normal_share, axis=1)), "tp")
    rows_back = rows_grad + inv_std[:, None] * (
        scaled - first[:, None] / features - normal_share * (second[:, None] / features)
    )
    gain_grad = jnp.sum(normed_grad * normal_share, axis=0)
    bias_grad = jnp.sum(normed_grad, axis=0)
    zero = jnp.zeros((2, share), jnp.float32)
    return rows_back, jnp.concatenate([gain_grad[None], bias_grad[None], edge, zero], axis=0)


def time_backward_plain(rows_grad, kept, small_full, small_own, wkv_rows, entry_matrix, exit_matrix):
    normal_share, inv_std, normal_full, mixed, gap, averaged, pullback, gate, output = kept
    branch_grad = lax.all_gather(rows_grad.astype(jnp.bfloat16), "tp", axis=1, tiled=True)
    exit_grad = inner_rows(output, branch_grad)
    output_grad = against(branch_grad, exit_matrix)
    state_grads = pullback(output_grad * gate)
    pre_grads = [
        state_grads[0].astype(jnp.bfloat16),
        state_grads[1].astype(jnp.bfloat16),
        (output_grad * averaged * gate * (1.0 - gate)).astype(jnp.bfloat16),
    ]
    entry_grad = jnp.stack([inner_rows(mixed[i], pre_grads[i]) for i in range(3)])
    mix_grads = [against(pre_grads[i], entry_matrix[i]) for i in range(3)]
    rows_back, small_grad = norm_back_plain(
        rows_grad, mix_grads, gap, normal_full, normal_share, inv_std, small_full, small_own
    )
    wkv_grad = jnp.concatenate([jnp.stack(state_grads[2:]), jnp.zeros((3, gate.shape[1]))], axis=0)
    return rows_back, small_grad, wkv_grad, (entry_grad.astype(jnp.bfloat16), exit_grad.astype(jnp.bfloat16))


def channel_backward_plain(rows_grad, kept, small_full, small_own, w_key, w_value, w_gate):
    normal_share, inv_std, normal_full, mixed, gap, hidden_pre, soft, hidden, gate, kv_share = kept
    branch_grad = lax.all_gather((rows_grad * gate).astype(jnp.bfloat16), "tp", axis=1, tiled=True)
    value_grad = inner_rows(hidden, branch_grad)
    hidden_grad = (
        against(branch_grad, w_value) * 2.0 * soft * jax.nn.sigmoid(hidden_pre)
    ).astype(jnp.bfloat16)
    gate_grad = (rows_grad * kv_share * gate * (1.0 - gate)).astype(jnp.bfloat16)
    key_grad = inner_rows(mixed[0], hidden_grad)
    recept_grad = inner_rows(mixed[1], gate_grad)
    mix_grads = [against(hidden_grad, w_key), against(gate_grad, w_gate)]
    rows_back, small_grad = norm_back_plain(
        rows_grad, mix_grads, gap, normal_full, normal_share, inv_std, small_full, small_own
    )
    grads = tuple(grad.astype(jnp.bfloat16) for grad in (key_grad, value_grad, recept_grad))
    return rows_back, small_grad, grads


CHUNK = 128
LANES = 128
SUB = 8
MESH = pl.DeviceIdType.MESH
NO_POWER = -1e30


def to_row_tile(*columns):
    lane = lax.broadcasted_iota(jnp.int32, (CHUNK, LANES), 1)
    wide = jnp.zeros((CHUNK, LANES), jnp.float32)
    for place, column in enumerate(columns):
        wide = jnp.where(lane == place, column, wide)
    return jnp.transpose(wide)[:SUB]


def to_columns(tiles):
    count = len(tiles)
    filler = [jnp.zeros((LANES - SUB * count, CHUNK), jnp.float32)]
    return jnp.transpose(jnp.concatenate(list(tiles) + filler, axis=0))


STEP = CHUNK // SUB


def shift_rows(value, first_row):
    ends = pltpu.roll(value[CHUNK - SUB :], 1, 0)
    at = lax.broadcasted_iota(jnp.int32, ends.shape, 0)
    return jnp.concatenate([jnp.where(at == 0, first_row, ends), value[: CHUNK - SUB]], axis=0)


def unshift_rows(value, last_row):
    starts = pltpu.roll(value[:SUB], SUB - 1, 0)
    at = lax.broadcasted_iota(jnp.int32, starts.shape, 0)
    return jnp.concatenate([value[SUB:], jnp.where(at == SUB - 1, last_row, starts)], axis=0)


def to_stretches(tokens_ref, rows_ref):
    def step(c, unused):
        base = pl.multiple_of(c * CHUNK, CHUNK)
        for s in range(STEP):
            for g in range(tokens_ref.shape[0]):
                rows_ref[pl.ds(base + s * SUB, SUB), g * LANES : (g + 1) * LANES] = tokens_ref[
                    g, pl.ds(base + s, SUB, stride=STEP), :
                ]
        return unused

    lax.fori_loop(0, rows_ref.shape[0] // CHUNK, step, 0)


def to_tokens(rows_ref, tokens_ref, c):
    base = pl.multiple_of(c * CHUNK, CHUNK)
    for s in range(STEP):
        for g in range(tokens_ref.shape[0]):
            tokens_ref[g, pl.ds(base + s, SUB, stride=STEP), :] = rows_ref[
                pl.ds(base + s * SUB, SUB), g * LANES : (g + 1) * LANES
            ]


class Peers:
    def __init__(self, count, width):
        self.count, self.width = count, width
        self.me = lax.axis_index("tp")

    def to(self, k):
        return lax.rem(self.me + k, self.count)

    def source(self, k):
        return lax.rem(self.me + self.count - k, self.count)

    def columns(self, owner):
        if isinstance(owner, int):
            return slice(owner * self.width, (owner + 1) * self.width)
        return pl.ds(pl.multiple_of(owner * self.width, LANES), self.width)

    def greet(self, others):
        barrier = pltpu.get_barrier_semaphore()
        places = [{"tp": self.to(k)} for k in range(1, self.count)] + others
        for place in places:
            pl.semaphore_signal(barrier, inc=1, device_id=place, device_id_type=MESH)
        pl.semaphore_wait(barrier, len(places))

    def copy(self, device, source_ref, target_ref, send, receive):
        return pltpu.make_async_remote_copy(
            src_ref=source_ref, dst_ref=target_ref, send_sem=send, recv_sem=receive,
            device_id={"tp": device}, device_id_type=MESH,
        )


def rows_of(c):
    return pl.ds(pl.multiple_of(c * CHUNK, CHUNK), CHUNK)


class Tiles:
    def __init__(self, peers, stat, sems):
        self.peers, self.stat, self.sems = peers, stat, sems

    def copy(self, k, c, owner):
        tile = self.stat.at[owner, c]
        return self.peers.copy(
            self.peers.to(k), tile, tile, self.sems[0].at[k - 1, c], self.sems[1].at[k - 1, c]
        )

    def start(self, c):
        for k in range(1, self.peers.count):
            self.copy(k, c, self.peers.me).start()

    def arrived(self, c):
        for k in range(1, self.peers.count):
            self.copy(k, c, self.peers.source(k)).wait_recv()

    def sent(self, c):
        for k in range(1, self.peers.count):
            self.copy(k, c, self.peers.me).wait_send()


class Gather:
    def __init__(self, peers, pay, sems):
        self.peers, self.pay, self.sems = peers, pay, sems

    def copy(self, way, hop, c, owner, which):
        slot = lax.rem(which, self.pay.shape[0])
        block = self.pay.at[slot, rows_of(c), self.peers.columns(owner)]
        device = jnp.clip(self.peers.me + (1 - 2 * way), 0, self.peers.count - 1)
        return self.peers.copy(
            device, block, block, self.sems[0].at[slot, way, hop - 1, c], self.sems[1].at[slot, way, hop - 1, c]
        )

    def onward(self, way):
        return self.peers.me < self.peers.count - 1 if way == 0 else self.peers.me > 0

    def owner(self, way, hop):
        return self.peers.me - hop if way == 0 else self.peers.me + hop

    def comes(self, way, hop):
        owner = self.owner(way, hop)
        return owner >= 0 if way == 0 else owner < self.peers.count

    def start(self, c, which):
        for way in (0, 1):
            @pl.when(self.onward(way))
            def _():
                self.copy(way, 1, c, self.peers.me, which).start()

    def relay(self, hop, c, which):
        for way in (0, 1):
            @pl.when(self.comes(way, hop))
            def _():
                self.copy(way, hop, c, self.owner(way, hop), which).wait_recv()
                if hop < self.peers.count - 1:
                    @pl.when(self.onward(way))
                    def _():
                        self.copy(way, hop + 1, c, self.owner(way, hop), which).start()

    def sent(self, c, which):
        for way in (0, 1):
            for hop in range(1, self.peers.count):
                @pl.when(self.comes(way, hop - 1) & self.onward(way))
                def _():
                    self.copy(way, hop, c, self.owner(way, hop - 1), which).wait_send()


class Scatter:
    def __init__(self, peers, part, stage, land, sems):
        self.peers, self.part, self.stage, self.land, self.sems = peers, part, stage, land, sems

    def landing(self, way, target, owner):
        if way == 0:
            return self.peers.columns(target)
        return self.peers.columns(jnp.where(target == owner, self.peers.count, target))

    def copy(self, way, c, target, which):
        slot, device = lax.rem(which, 2), jnp.clip(self.peers.me + (1 - 2 * way), 0, self.peers.count - 1)
        return self.peers.copy(
            device, self.stage.at[rows_of(c), self.peers.columns(target)],
            self.land.at[slot, rows_of(c), self.landing(way, target, device)],
            self.sems[0].at[slot, way, target, c], self.sems[1].at[slot, way, target, c],
        )

    def come(self, way, c, target, which):
        slot, columns = lax.rem(which, 2), self.landing(way, target, self.peers.me)
        block = self.land.at[slot, rows_of(c), columns]
        self.peers.copy(
            self.peers.me, block, block, self.sems[0].at[slot, way, target, c], self.sems[1].at[slot, way, target, c]
        ).wait_recv()
        return self.land[slot, rows_of(c), columns].astype(jnp.float32)

    def inward(self, way):
        return self.peers.me > 0 if way == 0 else self.peers.me < self.peers.count - 1

    def passes(self, way, target):
        return self.peers.me < target if way == 0 else self.peers.me > target

    def lag(self, way):
        return self.peers.me if way == 0 else self.peers.count - 1 - self.peers.me

    def push(self, way, c, which):
        rows = rows_of(c)
        targets = range(self.peers.count - 1, 0, -1) if way == 0 else range(self.peers.count - 1)
        for target in targets:
            columns = self.peers.columns(target)

            @pl.when(self.passes(way, target))
            def _():
                @pl.when(which > 0)
                def _():
                    self.copy(way, c, target, which - 1).wait_send()

                @pl.when(self.inward(way))
                def _():
                    self.stage[rows, columns] = (
                        self.part[rows, columns] + self.come(way, c, target, which)
                    ).astype(jnp.bfloat16)

                @pl.when(jnp.logical_not(self.inward(way)))
                def _():
                    self.stage[rows, columns] = self.part[rows, columns].astype(jnp.bfloat16)

                self.copy(way, c, target, which).start()

    def total(self, c, which):
        rows, mine = rows_of(c), self.peers.columns(self.peers.me)
        for way in (0, 1):
            @pl.when(self.inward(way))
            def _():
                self.part[rows, mine] += self.come(way, c, self.peers.me, which)
        return self.part[rows, mine]

    def sent(self, c, which):
        for target in range(self.peers.count):
            for way in (0, 1):
                @pl.when(self.passes(way, target))
                def _():
                    self.copy(way, c, target, which).wait_send()


def ticks_of(peers, chunks, passes, before, backward, begin, gather, compute, scatter):
    count = peers.count
    period = max(2 * count - 2, chunks + 1)

    def split(at):
        which, i = lax.div(at, period), lax.rem(at, period)
        chunk = chunks - 1 - i if backward else i
        return which, jnp.clip(chunk, 0, chunks - 1), (at >= 0) & (i < chunks) & (which < passes)

    def tick(t):
        which, c, there = split(t)
        last = (which == passes) & (lax.rem(t, period) < chunks)

        @pl.when(there | last)
        def _():
            begin(which, c)

        def relay(hop):
            moved, c_hop, there = split(t - hop)

            @pl.when(there)
            def _():
                gather.relay(hop, c_hop, moved + before)

        def push(middle):
            for way in (0, 1):
                lag = scatter.lag(way)
                moved, c_way, there = split(t - (count - 1) - lag)

                @pl.when(there & ((lag == 1) == middle))
                def _():
                    scatter.push(way, c_way, moved + before)

        relay(count - 1)
        which, c, there = split(t - (count - 1))

        @pl.when(there)
        def _():
            compute(which, c)

        push(False)
        for hop in range(1, count - 1):
            relay(hop)
        push(True)
    return tick


def mix_chunk(peers, c, pay, tiles, full_ref, mixed_ref, normal_ref, edge_ref, std_ref, last_ref):
    count, width = peers.count, peers.width
    tiles.arrived(c)
    columns = to_columns([tiles.stat[source, c] for source in range(count)])
    middles = [columns[:, SUB * source : SUB * source + 1] for source in range(count)]
    center = sum(middles) / count
    square = sum(columns[:, SUB * source + 1 : SUB * source + 2] for source in range(count))
    square = square + width * sum((middle - center) * (middle - center) for middle in middles)
    inv_std = lax.rsqrt(square / (count * width) + epsilon)
    std_ref[rows_of(c), :] = jnp.broadcast_to(inv_std, (CHUNK, LANES))
    for source in range(count):
        part = slice(source * width, (source + 1) * width)
        normal = (
            pay[rows_of(c), part].astype(jnp.float32) + (middles[source] - center)
        ) * inv_std
        normal_ref[rows_of(c), part] = normal.astype(jnp.bfloat16)
        normed = normal * full_ref[0:1, part] + full_ref[1:2, part]
        before = last_ref[0:1, part]
        edge_ref[pl.ds(c, 1), part] = before
        shifted = shift_rows(normed, before)
        last_ref[0:1, part] = normed[CHUNK - 1 : CHUNK]
        gap = normed - shifted
        for i in range(mixed_ref.shape[0]):
            mixed_ref[i, :, part] = (shifted + gap * full_ref[3 + i : 4 + i, part]).astype(
                jnp.bfloat16
            )


def wkv_join(left, right, fall):
    fallen = left[2] - fall
    peak = jnp.maximum(fallen, right[2])
    old, new = jnp.exp(fallen - peak), jnp.exp(right[2] - peak)
    return old * left[0] + new * right[0], old * left[1] + new * right[1], peak


def choose(mask, first, second):
    return tuple(jnp.where(mask, a, b) for a, b in zip(first, second))


def wkv_forward(base, key_ref, value_ref, decay, bonus, carry_ref, out_ref, state_ref):
    steps = STEP

    def at(s):
        return pl.ds(base + s * SUB, SUB)

    state = (value_ref[at(0), :], jnp.ones_like(decay), key_ref[at(0), :])
    for s in range(1, steps):
        key = key_ref[at(s), :]
        state = wkv_join(state, (value_ref[at(s), :], 1.0, key), decay)
    place = lax.broadcasted_iota(jnp.int32, decay.shape, 0)
    carry = tuple(carry_ref[i] for i in range(3))
    state = choose(place == 0, wkv_join(carry, state, steps * decay), state)
    for reach in (1, 2, 4):
        left = tuple(pltpu.roll(part, reach, 0) for part in state)
        state = choose(place >= reach, wkv_join(left, state, reach * steps * decay), state)
    after = tuple(pltpu.roll(part, 1, 0) for part in state)
    for i in range(3):
        carry_ref[i] = after[i]
    numer, denom, power = choose(place == 0, carry, after)
    for s in range(steps):
        key, value = key_ref[at(s), :], value_ref[at(s), :]
        lead = bonus + key
        peak = jnp.maximum(power, lead)
        old, new = jnp.exp(power - peak), jnp.exp(lead - peak)
        out_ref[at(s), :] = (old * numer + new * value) / (old * denom + new)
        state_ref[0, at(s), :] = numer
        state_ref[1, at(s), :] = denom
        state_ref[2, at(s), :] = power
        numer, denom, power = wkv_join((numer, denom, power), (value, 1.0, key), decay)


def wkv_backward(
    base, key_ref, value_ref, decay, bonus, out_ref, state_ref, up_ref, carry_ref, sum_ref, work_ref, grad_ref
):
    steps = STEP

    def at(s):
        return pl.ds(base + s * SUB, SUB)

    state = None
    for s in reversed(range(steps)):
        lead = bonus + key_ref[at(s), :]
        power = state_ref[2, at(s), :]
        peak = jnp.maximum(power, lead)
        new = jnp.exp(lead - peak)
        share = up_ref[s * SUB : (s + 1) * SUB, :] / (
            jnp.exp(power - peak) * state_ref[1, at(s), :] + new
        )
        work_ref[0, s], work_ref[1, s], work_ref[2, s] = share, peak, new * share
        here = (share, -share * out_ref[at(s), :], -peak)
        state = here if state is None else wkv_join(state, here, decay)
    place = lax.broadcasted_iota(jnp.int32, decay.shape, 0)
    carry = tuple(carry_ref[i] for i in range(3))
    state = choose(place == SUB - 1, wkv_join(carry, state, steps * decay), state)
    for reach in (1, 2, 4):
        later = tuple(pltpu.roll(part, SUB - reach, 0) for part in state)
        state = choose(place < SUB - reach, wkv_join(later, state, reach * steps * decay), state)
    after = tuple(pltpu.roll(part, SUB - 1, 0) for part in state)
    for i in range(3):
        carry_ref[i] = after[i]
    numer, denom, power = choose(place == SUB - 1, carry, after)
    for s in reversed(range(steps)):
        key, value, out = key_ref[at(s), :], value_ref[at(s), :], out_ref[at(s), :]
        share, peak, own = work_ref[0, s], work_ref[1, s], work_ref[2, s]
        reach = jnp.exp(key + power)
        direct = own * (value - out)
        grad_ref[0, s * SUB : (s + 1) * SUB, :] = direct + reach * (value * numer + denom)
        grad_ref[1, s * SUB : (s + 1) * SUB, :] = own + reach * numer
        sum_ref[1] += direct
        sum_ref[0] += jnp.exp(state_ref[2, at(s), :] + power - decay) * (
            state_ref[0, at(s), :] * numer + state_ref[1, at(s), :] * denom
        )
        numer, denom, power = wkv_join(
            (numer, denom, power), (share, -share * out, -peak), decay
        )


def load(pairs, sems, start):
    copies = [
        pltpu.make_async_copy(source, target, sems.at[start + i]) for i, (source, target) in enumerate(pairs)
    ]
    for copy in copies:
        copy.start()
    return copies


def soft_plus(value):
    small = jnp.exp(-jnp.abs(value))
    share = 1.0 / (1.0 + small)
    rest = jnp.where(small < 1e-3, small - 0.5 * small * small, jnp.log(1.0 + small))
    return jnp.maximum(value, 0.0) + rest, jnp.where(value >= 0.0, share, small * share)


def from_tokens(tokens_hbm, micro, tokens_ref, sems):
    return [
        pltpu.make_async_copy(tokens_hbm.at[micro, 0, :, pl.ds(g * LANES, LANES)], tokens_ref.at[g], sems.at[g])
        for g in range(tokens_ref.shape[0])
    ]


def to_sections(sections, rows_ref, tokens_ref, out_hbm, sems):
    send, receive = sems
    micro = lax.axis_index("section")
    groups = range(tokens_ref.shape[0])

    def ends(c, source, g):
        return tokens_ref.at[g, rows_of(c)], out_hbm.at[source, 0, :, pl.ds(g * LANES, LANES)]

    def copy(c, source, g):
        held, target = ends(c, source, g)
        return pltpu.make_async_remote_copy(
            src_ref=held, dst_ref=target, send_sem=send.at[c, g], recv_sem=receive.at[source, g],
            device_id={"section": c}, device_id_type=MESH,
        )

    def own(g):
        return pltpu.make_async_copy(*ends(micro, micro, g), send.at[micro, g])

    def start(c):
        to_tokens(rows_ref, tokens_ref, c)

        @pl.when(c == micro)
        def _():
            for g in groups:
                own(g).start()

        @pl.when(c != micro)
        def _():
            for g in groups:
                copy(c, micro, g).start()

    def wait():
        for g in groups:
            for k in range(1, sections):
                other = lax.rem(micro + k, sections)
                copy(other, micro, g).wait_send()
                copy(other, other, g).wait_recv()
            own(g).wait()

    return start, wait


def mix_chunk_back(
    peers, c, ratios, full_ref, normal_ref, edge_ref, mixed_ref, mix_grad, later_ref, edges_ref, part_ref, tiles
):
    count = peers.count
    rows = rows_of(c)
    first = second = 0.0
    for source in range(count):
        part = peers.columns(source)
        normal = normal_ref[rows, part].astype(jnp.float32)
        gain = full_ref[0:1, part]
        normed = normal * gain + full_ref[1:2, part]
        before = shift_rows(normed, edge_ref[pl.ds(c, 1), part])
        gap = normed - before
        direct = shifted = 0.0
        for i in range(ratios):
            grad = mix_grad(i, part)
            ratio = full_ref[3 + i : 4 + i, part]
            mixed_ref[i, rows, part] = (before + gap * ratio).astype(jnp.bfloat16)
            taken = grad * ratio
            direct = direct + taken
            shifted = shifted + (grad - taken)
            edges_ref[3 + i : 4 + i, part] += jnp.sum(grad * gap, axis=0, keepdims=True)
        value = direct + unshift_rows(shifted, later_ref[0:1, part])
        later_ref[0:1, part] = shifted[0:1]
        part_ref[rows, part] = value
        scaled = value * gain
        first = first + jnp.sum(scaled, axis=1, keepdims=True)
        second = second + jnp.sum(scaled * normal, axis=1, keepdims=True)
    tiles.stat[peers.me, c] = to_row_tile(first, second)
    tiles.start(c)


STEPS = 7
COPIES = 21


class Summed:
    def __init__(self, grad, core_land, cross_land, own_land, result, sems):
        self.grad, self.core_land, self.cross_land, self.own_land = grad, core_land, cross_land, own_land
        self.result, self.sems = result, sems
        self.rows = grad.shape[-2]
        self.half, self.piece, self.sub = self.rows // 2, self.rows // 8, self.rows // 16
        self.q, self.s = lax.axis_index("seq"), lax.axis_index("section")
        self.y, self.x = lax.div(self.s, 2), lax.rem(self.s, 2)
        self.sibling = {"seq": 1 - self.q}
        self.over_x = {"section": self.s + 1 - 2 * self.x}
        self.over_y = {"section": self.s + 2 - 4 * self.y}

    def at(self, ref, start, size):
        return ref.at[pl.ds(pl.multiple_of(start, 16), size), :]

    def spot(self, q, y, x, part):
        return q * self.half + (2 * y + x) * self.piece + part * self.sub

    def send(self, which, source, target, place):
        return pltpu.make_async_remote_copy(
            src_ref=source, dst_ref=target, send_sem=self.sems[0].at[which], recv_sem=self.sems[1].at[which],
            device_id=place, device_id_type=MESH,
        )

    def add(self, start, land, land_start, size):
        columns = self.grad.shape[-1]
        block = min(size, max(16, 32768 // columns))

        def step(i, unused):
            mine = self.at(self.grad, start + i * block, block)
            come = self.at(land, land_start + i * block, block)
            mine[...] = (mine[...].astype(jnp.float32) + come[...].astype(jnp.float32)).astype(jnp.bfloat16)
            return unused

        lax.fori_loop(0, size // block, step, 0)

    def to_core(self):
        other = self.at(self.grad, (1 - self.q) * self.half, self.half)
        return [self.send(0, other, self.core_land, self.sibling)]

    def cross(self, y, x):
        out = []
        for k in (0, 1):
            for part, place, (py, px) in (
                (0, self.over_x, (k, 1 - x)), (1, self.over_y, (1 - y, k)),
            ):
                spot = self.spot(0, py, px, part)
                out.append(
                    self.send(
                        1 + 2 * k + part, self.at(self.grad, self.q * self.half + spot, self.sub),
                        self.at(self.cross_land, spot, self.sub), place,
                    )
                )
        return out

    def own(self):
        out = []
        for part, place, (py, px) in (
            (0, self.over_y, (1 - self.y, self.x)), (1, self.over_x, (self.y, 1 - self.x)),
        ):
            source = self.at(self.grad, self.spot(self.q, py, px, part), self.sub)
            out.append(self.send(5 + part, source, self.at(self.own_land, part * self.sub, self.sub), place))
        return out

    def share(self, which, q, y, x, part, size, place, held):
        spot = self.spot(q, y, x, part)
        return self.send(which, self.at(held, spot, size), self.at(self.result, spot, size), place)

    def back_own(self, q, y, x):
        return [
            self.share(7, q, y, x, 0, self.sub, self.over_y, self.grad),
            self.share(8, q, y, x, 1, self.sub, self.over_x, self.grad),
            self.share(9, q, y, x, 0, self.piece, self.sibling, self.grad),
        ]

    def back_cross(self):
        q, y, x = self.q, self.y, self.x
        return [
            self.share(10, q, y, x, 0, self.sub, self.over_x, self.result),
            self.share(11, q, 1 - y, x, 0, self.sub, self.over_x, self.result),
            self.share(12, q, y, x, 1, self.sub, self.over_y, self.result),
            self.share(13, q, y, 1 - x, 1, self.sub, self.over_y, self.result),
            self.share(14, q, 1 - y, x, 0, self.sub, self.sibling, self.result),
            self.share(15, q, y, 1 - x, 1, self.sub, self.sibling, self.result),
        ]

    def back_core(self):
        q, y, x = self.q, self.y, self.x
        return [
            self.share(16, q, y, 1 - x, 0, self.sub, self.sibling, self.result),
            self.share(17, q, 1 - y, 1 - x, 0, self.sub, self.sibling, self.result),
            self.share(18, q, 1 - y, x, 1, self.sub, self.sibling, self.result),
            self.share(19, q, 1 - y, 1 - x, 1, self.sub, self.sibling, self.result),
        ]

    def keep(self):
        spot = self.spot(self.q, self.y, self.x, 0)
        return pltpu.make_async_copy(
            self.at(self.grad, spot, self.piece), self.at(self.result, spot, self.piece), self.sems[0].at[20]
        )

    def arrive(self, which, ref, start, size):
        view = self.at(ref, start, size)
        self.send(which, view, view, self.sibling).wait_recv()

    def step(self, number):
        q, y, x = self.q, self.y, self.x
        if number == 0:
            started = self.to_core()
        elif number == 1:
            self.arrive(0, self.core_land, 0, self.half)
            self.add(q * self.half, self.core_land, 0, self.half)
            started = self.cross(y, x)
        elif number == 2:
            for k in (0, 1):
                for part, (py, px) in ((0, (k, x)), (1, (y, k))):
                    spot = self.spot(0, py, px, part)
                    self.arrive(1 + 2 * k + part, self.cross_land, spot, self.sub)
                    self.add(q * self.half + spot, self.cross_land, spot, self.sub)
            started = self.own()
        elif number == 3:
            for part in (0, 1):
                self.arrive(5 + part, self.own_land, part * self.sub, self.sub)
                self.add(self.spot(q, y, x, part), self.own_land, part * self.sub, self.sub)
            started = self.back_own(q, y, x) + [self.keep()]
        elif number == 4:
            self.arrive(7, self.result, self.spot(q, 1 - y, x, 0), self.sub)
            self.arrive(8, self.result, self.spot(q, y, 1 - x, 1), self.sub)
            self.keep().wait()
            started = self.back_cross()
        elif number == 5:
            self.arrive(9, self.result, self.spot(1 - q, y, x, 0), self.piece)
            self.arrive(10, self.result, self.spot(q, y, 1 - x, 0), self.sub)
            self.arrive(11, self.result, self.spot(q, 1 - y, 1 - x, 0), self.sub)
            self.arrive(12, self.result, self.spot(q, 1 - y, x, 1), self.sub)
            self.arrive(13, self.result, self.spot(q, 1 - y, 1 - x, 1), self.sub)
            started = self.back_core()
        else:
            o = 1 - q
            self.arrive(14, self.result, self.spot(o, 1 - y, x, 0), self.sub)
            self.arrive(15, self.result, self.spot(o, y, 1 - x, 1), self.sub)
            self.arrive(16, self.result, self.spot(o, y, 1 - x, 0), self.sub)
            self.arrive(17, self.result, self.spot(o, 1 - y, 1 - x, 0), self.sub)
            self.arrive(18, self.result, self.spot(o, 1 - y, x, 1), self.sub)
            self.arrive(19, self.result, self.spot(o, 1 - y, 1 - x, 1), self.sub)
            started = []
        for copy in started:
            copy.start()

    def sent_grad(self):
        copies = self.to_core() + self.cross(self.y, self.x) + self.own() + self.back_own(self.q, self.y, self.x)
        for copy in copies:
            copy.wait_send()

    def sent_rest(self):
        for copy in self.back_cross() + self.back_core():
            copy.wait_send()


GROUPS = (
    (0, (1,), (1, 2, 4, 5, 6, 11)),
    (0, (0, 2), (0, 1, 3, 4, 5, 11)),
    (1, (3, 4, 5, 6), (1, 2, 4, 5, 6, 12)),
)


def both_kernel(
    count, sections, cores, depth,
    rows_hbm, up_hbm, lead_ref, numer_ref, denom_ref, power_ref, attend_gain, attend_bias, attend_mix, fading_ref, bonus_ref,
    feed_gain, feed_bias, feed_mix, entry_hbm, exit_hbm, key_hbm, content_hbm, gate_hbm,
    out_hbm, back_hbm, table_ref, entry_sum, exit_sum, key_sum, content_sum, gate_sum,
    normal_ref, std_ref, key_ref, value_ref, averaged_ref, state_ref, open_ref, hidden_ref, slope_ref, gate_ref, kv_ref,
    full_ref, edge_ref, rows_ref, tokens_ref, grad_ref, back_ref,
    entry_ref, exit_ref, w_key, w_content, w_gate,
    entry_grad, exit_grad, key_grad, content_grad, gate_grad,
    entry_core, exit_core, key_core, content_core, gate_core,
    entry_cross, exit_cross, key_cross, content_cross, gate_cross,
    entry_own, exit_own, key_own, content_own, gate_own,
    pay, stat, part, stage, land, mixed_ref, pre_grads, up_ref, work_ref, pair_ref, carry_ref, sum_ref,
    output_ref, hidden_grad, last_ref, later_ref, edges_ref, edge_land, small_ref,
    load_sems, token_sems, back_sems, fs, fr, os, orr, bs, br, gs, gr, ts, tr, ss, sr, es, er, ws, wr,
    table_send, table_recv,
):
    length, width = rows_ref.shape
    hidden_width = hidden_ref.shape[2]
    chunks = length // CHUNK
    passes = 2 * depth
    period = max(2 * count - 2, chunks + 1)
    peers = Peers(count, width)
    mine = peers.columns(peers.me)
    micro, core = lax.axis_index("section"), lax.axis_index("seq")
    first = from_tokens(rows_hbm, micro, tokens_ref, token_sems)
    second = from_tokens(up_hbm, micro, back_ref, back_sems)
    for copy in first + second:
        copy.start()
    weights = load(
        (
            (entry_hbm, entry_ref), (exit_hbm, exit_ref), (key_hbm, w_key), (content_hbm, w_content),
            (gate_hbm, w_gate),
        ),
        load_sems,
        0,
    )
    full_ref[...] = jnp.zeros_like(full_ref)
    for j in range(2 * depth):
        level = j // 2
        gain, bias, mix = (attend_gain, attend_bias, attend_mix) if j % 2 == 0 else (feed_gain, feed_bias, feed_mix)
        full_ref[j, 0:1, mine] = gain[level : level + 1, :]
        full_ref[j, 1:2, mine] = bias[level : level + 1, :]
        full_ref[j, 2:3, mine] = lead_ref[j, micro]
        full_ref[j, 3 : 3 + mix.shape[1], mine] = mix[level]
    gather = Gather(peers, pay, (gs, gr))
    tiles = Tiles(peers, stat, (ts, tr))
    scatter = Scatter(peers, part, stage, land, (ss, sr))
    start_out, wait_out = to_sections(sections, rows_ref, tokens_ref, out_hbm, (os, orr))
    start_back, wait_back = to_sections(sections, grad_ref, back_ref, back_hbm, (bs, br))

    def full_copy(k, owner):
        block = full_ref.at[:, :, peers.columns(owner)]
        return peers.copy(peers.to(k), block, block, fs.at[k - 1], fr.at[k - 1])

    def sums(group, level):
        parts = (
            (key_grad, key_core, key_cross, key_own, key_sum),
            (content_grad, content_core, content_cross, content_own, content_sum),
            (gate_grad, gate_core, gate_cross, gate_own, gate_sum),
        )
        entry = (entry_grad, entry_core, entry_cross, entry_own, entry_sum)
        parts += tuple(
            (*(ref.at[i] for ref in entry[:4]), entry_sum.at[:, i]) for i in range(3)
        )
        parts += ((exit_grad, exit_core, exit_cross, exit_own, exit_sum),)
        out = []
        for place in GROUPS[group][1]:
            grad, core_land, cross_land, own_land, result = parts[place]
            out.append(
                Summed(
                    grad, core_land, cross_land, own_land, result.at[level],
                    (ws.at[level, place], wr.at[level, place]),
                )
            )
        return out

    def sum_step(group, level, number):
        for matrix in sums(group, level):
            matrix.step(number)

    def table_place(k):
        return lax.rem(micro * cores + core + k, sections * cores)

    def table_copy(k, owner):
        other = table_place(k)
        return pltpu.make_async_remote_copy(
            src_ref=small_ref, dst_ref=table_ref.at[owner], send_sem=table_send.at[k - 1], recv_sem=table_recv.at[k - 1],
            device_id={"section": lax.div(other, cores), "seq": lax.rem(other, cores)}, device_id_type=MESH,
        )

    others = [table_place(k) for k in range(1, sections * cores)]
    peers.greet([{"section": lax.div(other, cores), "seq": lax.rem(other, cores)} for other in others])
    for k in range(1, count):
        full_copy(k, peers.me).start()
    for copy in first:
        copy.wait()
    to_stretches(tokens_ref, rows_ref)

    def begin_forward(j, c):
        rows = rows_of(c)

        @pl.when(j > 0)
        def _():
            value = scatter.total(c, j - 1)
            tiles.sent(c)

            @pl.when(lax.rem(j, 2) == 1)
            def _():
                rows_ref[rows, :] += value

            @pl.when(lax.rem(j, 2) == 0)
            def _():
                level = lax.div(j, 2) - 1
                kv_ref[level, rows, :] = value
                rows_ref[rows, :] += gate_ref[level, rows, :] * value

        @pl.when(j < 2 * depth)
        def _():
            lines = rows_ref[rows, :]
            middle = jnp.mean(lines, axis=1, keepdims=True)
            center = lines - middle
            square = jnp.sum(center * center, axis=1, keepdims=True)
            pay[lax.rem(j, 2), rows, mine] = center.astype(jnp.bfloat16)
            tiles.stat[peers.me, c] = to_row_tile(middle, square)
            tiles.start(c)
            gather.start(c, j)

        @pl.when(j == 2 * depth)
        def _():
            start_out(c)

    def attend_forward(level, c):
        rows = rows_of(c)

        @pl.when(c == 0)
        def _():
            for i, start_ref in enumerate((numer_ref, denom_ref, power_ref)):
                carry_ref[i] = jnp.broadcast_to(start_ref[level, micro], (SUB, width))

        decay = jnp.broadcast_to(jnp.exp(fading_ref[pl.ds(level, 1), :]), (SUB, width))
        bonus = jnp.broadcast_to(bonus_ref[pl.ds(level, 1), :], (SUB, width))
        key_ref[level, rows, :] = product(mixed_ref[0, 0:CHUNK], entry_ref[level, 0])
        value_ref[level, rows, :] = product(mixed_ref[1, 0:CHUNK], entry_ref[level, 1])
        gate = jax.nn.sigmoid(product(mixed_ref[2, 0:CHUNK], entry_ref[level, 2]))
        open_ref[level, rows, :] = gate
        wkv_forward(
            pl.multiple_of(c * CHUNK, CHUNK), key_ref.at[level], value_ref.at[level], decay, bonus, carry_ref,
            averaged_ref.at[level], state_ref.at[level],
        )
        output = (gate * averaged_ref[level, rows, :]).astype(jnp.bfloat16)
        for target in range(count):
            block = peers.columns(target)
            part[rows, block] = product(output, exit_ref[level, :, block])

    def feed_forward(level, c):
        rows = rows_of(c)
        for start in range(0, hidden_ref.shape[2], width):
            block = slice(start, start + width)
            soft, slope = soft_plus(product(mixed_ref[0, 0:CHUNK], w_key[level, :, block]))
            hidden_ref[level, rows, block] = (soft * soft).astype(jnp.bfloat16)
            slope_ref[level, rows, block] = (2.0 * soft * slope).astype(jnp.bfloat16)
        for target in range(count):
            block = peers.columns(target)
            part[rows, block] = product(hidden_ref[level, rows, :], w_content[level, :, block])
        gate_ref[level, rows, :] = jax.nn.sigmoid(product(mixed_ref[1, 0:CHUNK], w_gate[level]))

    def forward(j, c):
        @pl.when((j == 0) & (c == 0))
        def _():
            for k in range(1, count):
                full_copy(k, peers.source(k)).wait_recv()
            for copy in weights:
                copy.wait()

        @pl.when(c == 0)
        def _():
            last_ref[0:1, :] = full_ref[j, 2:3, :]

        mix_chunk(
            peers, c, pay.at[lax.rem(j, 2)], tiles, full_ref.at[j], mixed_ref.at[:, pl.ds(0, CHUNK)], normal_ref.at[j], edge_ref.at[j], std_ref.at[j],
            last_ref,
        )
        level = lax.div(j, 2)

        @pl.when(lax.rem(j, 2) == 0)
        def _():
            attend_forward(level, c)

        @pl.when(lax.rem(j, 2) == 1)
        def _():
            feed_forward(level, c)

        gather.sent(c, j)

    def edge_copies(j, source_of):
        return [
            peers.copy(
                peers.to(k), edges_ref.at[j, :, peers.columns(peers.to(k))], edge_land.at[j, source_of(k)],
                es.at[j, k - 1], er.at[j, k - 1],
            )
            for k in range(1, count)
        ]

    def end_pass(j, c):
        rows = rows_of(c)
        normed_grad = scatter.total(c, 2 * passes - 1 - j)
        tiles.arrived(c)
        totals = tiles.stat[0, c]
        for source in range(1, count):
            totals = totals + tiles.stat[source, c]
        columns = to_columns([totals])
        normal = normal_ref[j, rows, mine].astype(jnp.float32)
        scale = 1.0 / (count * width)
        grad_ref[rows, :] += std_ref[j, rows, 0:1] * (
            normed_grad * full_ref[j, 0:1, mine] - columns[:, 0:1] * scale - normal * (columns[:, 1:2] * scale)
        )
        small_ref[j, 0:1, :] += jnp.sum(normed_grad * normal, axis=0, keepdims=True)
        small_ref[j, 1:2, :] += jnp.sum(normed_grad, axis=0, keepdims=True)

        @pl.when(c == 0)
        def _():
            for copy in edge_copies(j, peers.source):
                copy.wait_recv()
            edges = edges_ref[j, :, mine]
            for k in range(1, count):
                edges = edges + edge_land[j, peers.source(k)]
            small_ref[j, 2:6, :] = edges[2:6]

    def begin_backward(which, c):
        rows = rows_of(c)
        j = passes - 1 - which

        @pl.when(which > 0)
        def _():
            end_pass(j + 1, c)
            gather.sent(c, passes + which - 1)
            tiles.sent(c)

        @pl.when((which < passes) & (lax.rem(which, 2) == 0))
        def _():
            pay[lax.rem(which, 2), rows, mine] = (grad_ref[rows, :] * gate_ref[lax.div(j, 2), rows, :]).astype(jnp.bfloat16)

        @pl.when((which < passes) & (lax.rem(which, 2) == 1))
        def _():
            pay[lax.rem(which, 2), rows, mine] = grad_ref[rows, :].astype(jnp.bfloat16)

        @pl.when(which < passes)
        def _():
            gather.start(c, passes + which)

        @pl.when(which == passes)
        def _():
            start_back(c)

    def attend_backward(j, c):
        level = lax.div(j, 2)
        rows = rows_of(c)
        decay = jnp.broadcast_to(jnp.exp(fading_ref[pl.ds(level, 1), :]), (SUB, width))
        bonus = jnp.broadcast_to(bonus_ref[pl.ds(level, 1), :], (SUB, width))

        @pl.when(c == chunks - 1)
        def _():
            sum_ref[...] = jnp.zeros_like(sum_ref)
            carry_ref[0] = jnp.zeros((SUB, width), jnp.float32)
            carry_ref[1] = jnp.zeros((SUB, width), jnp.float32)
            carry_ref[2] = jnp.full((SUB, width), NO_POWER, jnp.float32)

        output_grad = against(pay[1, rows, :], exit_ref[level])
        gate = open_ref[level, rows, :]
        up = output_grad * gate
        up_ref[...] = up
        averaged = averaged_ref[level, rows, :]
        pre_grads[2, rows, :] = (up * averaged * (1.0 - gate)).astype(jnp.bfloat16)
        output_ref[rows, :] = (gate * averaged).astype(jnp.bfloat16)
        wkv_backward(
            pl.multiple_of(c * CHUNK, CHUNK), key_ref.at[level], value_ref.at[level], decay, bonus,
            averaged_ref.at[level], state_ref.at[level],
            up_ref, carry_ref, sum_ref, work_ref, pair_ref,
        )
        pre_grads[0, rows, :] = pair_ref[0].astype(jnp.bfloat16)
        pre_grads[1, rows, :] = pair_ref[1].astype(jnp.bfloat16)
        mix_chunk_back(
            peers, c, 3, full_ref.at[j], normal_ref.at[j], edge_ref.at[j], mixed_ref,
            lambda i, columns: against(pre_grads[i, rows, :], entry_ref[level, i, columns, :]),
            later_ref, edges_ref.at[j], part, tiles,
        )

        @pl.when(c == 0)
        def _():
            numer, denom = carry_ref[0, SUB - 1 :, :], carry_ref[1, SUB - 1 :, :]
            lift = jnp.exp(power_ref[level, micro] + carry_ref[2, SUB - 1 :, :])
            out = passes + level
            small_ref[out, 0:1, :] = -decay[0:1] * jnp.sum(sum_ref[0], axis=0, keepdims=True)
            small_ref[out, 1:2, :] = jnp.sum(sum_ref[1], axis=0, keepdims=True)
            small_ref[out, 2:3, :] = lift * numer
            small_ref[out, 3:4, :] = lift * denom
            small_ref[out, 4:5, :] = lift * (numer_ref[level, micro] * numer + denom_ref[level, micro] * denom)

    def feed_backward(j, c):
        rows = rows_of(c)
        level = lax.div(j, 2)
        gate = gate_ref[level, rows, :]
        pre_grads[0, rows, :] = (grad_ref[rows, :] * gate * kv_ref[level, rows, :] * (1.0 - gate)).astype(jnp.bfloat16)
        for start in range(0, hidden_width, width):
            block = slice(start, start + width)
            into = against(pay[0, rows, :], w_content[level, block, :])
            hidden_grad[rows, block] = (into * slope_ref[level, rows, block].astype(jnp.float32)).astype(jnp.bfloat16)

        def mix_grad(i, columns):
            if i == 0:
                return against(hidden_grad[rows, :], w_key[level, columns, :])
            return against(pre_grads[0, rows, :], w_gate[level, columns, :])

        mix_chunk_back(
            peers, c, 2, full_ref.at[j], normal_ref.at[j], edge_ref.at[j], mixed_ref, mix_grad,
            later_ref, edges_ref.at[j], part, tiles,
        )

    def backward(which, c):
        j = passes - 1 - which

        @pl.when(c == chunks - 1)
        def _():
            later_ref[...] = jnp.zeros_like(later_ref)

        @pl.when(lax.rem(which, 2) == 0)
        def _():
            feed_backward(j, c)

        @pl.when(lax.rem(which, 2) == 1)
        def _():
            attend_backward(j, c)

        @pl.when(c == 0)
        def _():
            edges_ref[j, 2:3, :] = later_ref[0:1, :]
            for copy in edge_copies(j, lambda k: peers.me):
                copy.start()

    def weigh(place, level):
        for source in range(count):
            block = peers.columns(source)
            if place == 0:
                key_grad[block, :] = inner_rows(mixed_ref[0, :, block], hidden_grad[...]).astype(jnp.bfloat16)
            elif place == 2:
                gate_grad[block, :] = inner_rows(mixed_ref[1, :, block], pre_grads[0]).astype(jnp.bfloat16)
            elif 3 <= place < 6:
                i = place - 3
                entry_grad[i, block, :] = inner_rows(mixed_ref[i, :, block], pre_grads[i]).astype(jnp.bfloat16)
            elif place == 6:
                exit_grad[:, block] = inner_rows(output_ref[...], pay[1, :, block]).astype(jnp.bfloat16)
        if place == 1:
            for start in range(0, hidden_width, width):
                block = slice(start, start + width)
                content_grad[block, :] = inner_rows(hidden_ref[level, :, block], pay[0]).astype(jnp.bfloat16)

    base, final = chunks + count - 1, passes * period + chunks - 1

    def when_taken(group, number, t):
        kind, places, later = GROUPS[group]
        since = t - (base + period * kind + later[number])
        taken = (since >= 0) & (lax.rem(since, 2 * period) == 0) & (since < 2 * period * depth)
        return taken, depth - 1 - lax.div(since, 2 * period)

    def extra(t):
        for group in range(len(GROUPS)):
            for number in reversed(range(STEPS - 1)):
                taken, level = when_taken(group, number, t)

                @pl.when(taken)
                def _():
                    if number == 0:
                        @pl.when(level < depth - 1)
                        def _():
                            for matrix in sums(group, jnp.minimum(level + 1, depth - 1)):
                                matrix.sent_grad()

                        for place in GROUPS[group][1]:
                            weigh(place, jnp.clip(level, 0, depth - 1))
                    sum_step(group, jnp.clip(level, 0, depth - 1), number)

    forward_tick = ticks_of(peers, chunks, passes, 0, False, begin_forward, gather, forward, scatter)
    backward_tick = ticks_of(peers, chunks, passes, passes, True, begin_backward, gather, backward, scatter)
    turn = (passes - 1) * period + chunks + count - 1

    def tick(t, unused):
        @pl.when(t < passes * period + chunks)
        def _():
            forward_tick(t)

        @pl.when(t == turn - 1)
        def _():
            for copy in second:
                copy.wait()
            to_stretches(back_ref, grad_ref)
            small_ref[...] = jnp.zeros_like(small_ref)
            edges_ref[...] = jnp.zeros_like(edges_ref)

        @pl.when(t >= turn)
        def _():
            backward_tick(t - turn)
            extra(t - turn)

        return unused

    lax.fori_loop(0, turn + final + 1, tick, 0)

    for k in range(1, sections * cores):
        table_copy(k, micro * cores + core).start()
    table_ref[micro * cores + core] = small_ref[...]
    left = []
    for group, (kind, places, later) in enumerate(GROUPS):
        for level in reversed(range(depth)):
            start = base + period * (kind + 2 * (depth - 1 - level))
            for number in range(STEPS):
                at = start + (later[number] if number < STEPS - 1 else later[-1] + 5)
                if at > final or number == STEPS - 1:
                    left.append((at, group, level, number))
    for at, group, level, number in sorted(left):
        sum_step(group, level, number)
    for c in range(chunks):
        scatter.sent(c, 2 * passes - 1)
    for j in range(passes):
        for copy in edge_copies(j, lambda k: peers.me):
            copy.wait_send()
    for group in range(len(GROUPS)):
        for level in range(depth):
            for matrix in sums(group, level):
                matrix.sent_rest()
                if level == 0:
                    matrix.sent_grad()
    for k in range(1, sections * cores):
        table_copy(k, micro * cores + core).wait_send()
        other = lax.rem(micro * cores + core + sections * cores - k, sections * cores)
        table_copy(k, other).wait_recv()
    for k in range(1, count):
        full_copy(k, peers.me).wait_send()
    wait_out()
    wait_back()


BF16, F32 = jnp.bfloat16, jnp.float32


def struct(*shape, dtype=F32):
    return jax.ShapeDtypeStruct(shape, dtype)


def run_kernel(body, collective, outs, scratch, operands, flops):
    def spec(inside):
        return pl.BlockSpec(memory_space=pltpu.VMEM if inside else pl.ANY)

    return pl.pallas_call(
        body,
        out_shape=[out for out, inside in outs],
        in_specs=[spec(inside) for operand, inside in operands],
        out_specs=[spec(inside) for out, inside in outs],
        scratch_shapes=scratch,
        compiler_params=pltpu.CompilerParams(
            collective_id=collective, has_side_effects=True, vmem_limit_bytes=63 * 1024 * 1024
        ),
        cost_estimate=pl.CostEstimate(flops=flops, bytes_accessed=2**25, transcendentals=2**23),
    )(*[operand for operand, inside in operands])


def pair_of(shape):
    return [pltpu.SemaphoreType.DMA(shape)] * 2


def run_fast(
    residual_entering, upstream_sensitivity, piece_lead_lines, dividend_start, divisor_start, power_offset_start,
    attend_standard_scale, attend_standard_offset, attend_lag_fractions, fading_log_rate, reward_first_word,
    attend_entry_matrix, attend_exit_matrix, feed_standard_scale, feed_standard_offset, feed_lag_fractions,
    feed_lookup_matrix, feed_content_matrix, feed_gate_matrix,
):
    count, sections, cores = (lax.axis_size(axis) for axis in ("tp", "section", "seq"))
    length, width = residual_entering.shape[2:]
    depth, features, hidden = feed_lookup_matrix.shape[0], count * width, feed_lookup_matrix.shape[2]
    chunks, subs = length // CHUNK, 2 * depth
    flops = 2 * depth * length * features * (4 * width + 2 * hidden + width)
    groups = width // LANES
    starts = (dividend_start, divisor_start, power_offset_start)
    weights = (attend_entry_matrix, attend_exit_matrix, feed_lookup_matrix, feed_content_matrix, feed_gate_matrix)
    shares = struct(sections, 1, CHUNK, width)
    lines = (depth, length, width)
    shapes = [weight.shape[1:] for weight in weights]

    def held(*shape, dtype=F32):
        return pltpu.VMEM(shape, dtype)

    def rows_cut(by):
        return [held(*shape[:-2], shape[-2] // by, shape[-1], dtype=BF16) for shape in shapes]

    outs = [(shares, False), (shares, False), (struct(sections * cores, subs + depth, SUB, width), True)]
    outs += [(struct(*weight.shape, dtype=BF16), False) for weight in weights]
    scratch = [held(subs, length, features, dtype=BF16), held(subs, length, LANES), held(*lines), held(*lines)]
    scratch += [held(*lines), held(depth, 3, *lines[1:]), held(*lines)]
    scratch += [held(depth, length, hidden, dtype=BF16)] * 2 + [held(*lines)] * 2
    scratch += [held(subs, SUB, features)] * 2 + [held(length, width), held(groups, length, LANES)] * 2
    scratch += [held(*weight.shape, dtype=BF16) for weight in weights] + rows_cut(1) + rows_cut(2) + rows_cut(2) + rows_cut(8)
    scratch += [
        held(2, length, features, dtype=BF16), held(count, chunks, SUB, LANES), held(length, features),
        held(length, features, dtype=BF16), held(2, length, features + width, dtype=BF16),
    ]
    scratch += [
        held(3, length, features, dtype=BF16), held(3, length, width, dtype=BF16), held(CHUNK, width),
        held(3, STEP, SUB, width), held(2, CHUNK, width), held(3, SUB, width), held(2, SUB, width),
        held(length, width, dtype=BF16), held(length, hidden, dtype=BF16), held(SUB, features), held(SUB, features),
        held(subs, SUB, features), held(subs, count, SUB, width), held(subs + depth, SUB, width),
    ]
    scratch += [pltpu.SemaphoreType.DMA((n,)) for n in (len(weights), groups, groups)] + pair_of((count - 1,))
    scratch += pair_of((sections, groups)) + pair_of((sections, groups))
    scratch += pair_of((2, 2, count - 1, chunks)) + pair_of((count - 1, chunks)) + pair_of((2, 2, count, chunks))
    scratch += pair_of((subs, count - 1)) + pair_of((depth, len(weights) + 2, COPIES))
    scratch += pair_of((sections * cores - 1,))
    operands = [(residual_entering, False), (upstream_sensitivity, False)]
    operands += [
        (value, True)
        for value in (
            piece_lead_lines, *starts, attend_standard_scale, attend_standard_offset, attend_lag_fractions,
            fading_log_rate, reward_first_word, feed_standard_scale, feed_standard_offset, feed_lag_fractions,
        )
    ]
    operands += [(value, False) for value in weights]
    out_share, back_share, table, *sums = run_kernel(
        partial(both_kernel, count, sections, cores, depth), 0, outs, scratch, operands, 3 * flops
    )
    return finish(cores, depth, out_share, back_share, table, sums)


def finish_kernel(cores, depth, table_ref, *refs):
    wide, narrow = refs[:7], refs[7:14]
    prev, numer, denom, power = refs[14:18]
    attend_gain, attend_bias, attend_mix, decay, bonus, feed_gain, feed_bias, feed_mix = refs[18:]
    for source, target in zip(wide, narrow):
        target[...] = source[...].astype(jnp.float32)

    @pl.when(pl.program_id(0) == 0)
    def _():
        core = lax.axis_index("seq")
        places, subs = table_ref.shape[0], 2 * depth
        for m in range(places // cores):
            for j in range(subs):
                prev[j, m] = table_ref[m * cores + core, j, 2:3, :]
            for level in range(depth):
                for i, state in enumerate((numer, denom, power)):
                    state[level, m] = table_ref[m * cores + core, subs + level, 2 + i : 3 + i, :]
        for level in range(depth):
            for j, gain, bias, mix in (
                (2 * level, attend_gain, attend_bias, attend_mix), (2 * level + 1, feed_gain, feed_bias, feed_mix),
            ):
                total = sum(table_ref[place, j] for place in range(places))
                gain[level : level + 1, :] = total[0:1]
                bias[level : level + 1, :] = total[1:2]
                mix[level] = total[3 : 3 + mix.shape[1]]
            total = sum(table_ref[place, subs + level] for place in range(places))
            decay[level : level + 1, :] = total[0:1]
            bonus[level : level + 1, :] = total[1:2]


def finish(cores, depth, out_share, back_share, table, sums):
    steps = 8
    wide = [value.reshape(-1, value.shape[-1]) for value in (out_share, back_share, *sums)]
    blocks = [
        pl.BlockSpec((value.shape[0] // steps, value.shape[1]), lambda i: (i, 0)) for value in wide
    ]
    width = table.shape[-1]
    micros = table.shape[0] // cores
    small = [(2 * depth, micros, 1, width)] + [(depth, micros, 1, width)] * 3
    small += [(depth, width), (depth, width), (depth, 3, width), (depth, width), (depth, width)]
    small += [(depth, width), (depth, width), (depth, 2, width)]

    def whole(shape):
        return pl.BlockSpec(shape, lambda i: (0,) * len(shape))

    got = pl.pallas_call(
        partial(finish_kernel, cores, depth),
        grid=(steps,),
        out_shape=[struct(*value.shape) for value in wide] + [struct(*shape) for shape in small],
        in_specs=[whole(table.shape)] + blocks,
        out_specs=blocks + [whole(shape) for shape in small],
        compiler_params=pltpu.CompilerParams(vmem_limit_bytes=60 * 1024 * 1024),
    )(table, *wide)
    shares = [value.reshape(whole.shape) for value, whole in zip(got, (out_share, back_share))]
    entry, leave, key, content, gate = [
        value.reshape(whole.shape) for value, whole in zip(got[2:7], sums)
    ]
    small = got[7:]
    return (*shares, *small[:9], entry, leave, *small[9:], key, content, gate)


def run_plain(
    residual_entering,
    upstream_sensitivity,
    piece_lead_lines,
    dividend_start,
    divisor_start,
    power_offset_start,
    attend_standard_scale,
    attend_standard_offset,
    attend_lag_fractions,
    fading_log_rate,
    reward_first_word,
    attend_entry_matrix,
    attend_exit_matrix,
    feed_standard_scale,
    feed_standard_offset,
    feed_lag_fractions,
    feed_lookup_matrix,
    feed_content_matrix,
    feed_gate_matrix,
):
    sections = lax.axis_size("section")
    micro = lax.axis_index("section")
    length, share = residual_entering.shape[2:]
    depth = attend_entry_matrix.shape[0]

    def own(array):
        return lax.dynamic_index_in_dim(array, micro, 0, keepdims=False)

    blank = jnp.zeros((1, share), jnp.float32)
    lead = lax.dynamic_index_in_dim(piece_lead_lines[:, :, 0], micro, 1, keepdims=False)
    starts = [
        lax.dynamic_index_in_dim(start[:, :, 0], micro, 1, keepdims=False)
        for start in (dividend_start, divisor_start, power_offset_start)
    ]
    small_rows, wkv_rows = [], []
    for level in range(depth):
        for gain, bias, mix, j in (
            (attend_standard_scale, attend_standard_offset, attend_lag_fractions, 2 * level),
            (feed_standard_scale, feed_standard_offset, feed_lag_fractions, 2 * level + 1),
        ):
            rows = [gain[level][None], bias[level][None], lead[j][None], mix[level]]
            rows += [blank] * (5 - mix.shape[1])
            small_rows.append(jnp.concatenate(rows, axis=0))
        wkv_rows.append(
            jnp.stack(
                [fading_log_rate[level], reward_first_word[level]]
                + [start[level] for start in starts]
                + [blank[0]] * 3
            )
        )
    small_own = jnp.stack(small_rows)
    small_full = lax.all_gather(small_own, "tp", axis=2, tiled=True)

    rows = own(residual_entering)[0]
    kept = []
    for level in range(depth):
        for j in (2 * level, 2 * level + 1):
            if j % 2 == 0:
                rows, saved = time_forward_plain(
                    rows, small_full[j], small_own[j], wkv_rows[level],
                    attend_entry_matrix[level], attend_exit_matrix[level],
                )
            else:
                rows, saved = channel_forward_plain(
                    rows, small_full[j], small_own[j],
                    feed_lookup_matrix[level], feed_content_matrix[level], feed_gate_matrix[level],
                )
            kept.append(saved)

    def to_tokens(value):
        pieces = value.reshape(sections, length // sections, share)
        return lax.all_to_all(pieces, "section", 0, 0)[:, None]

    out_share = to_tokens(rows)
    grad = own(upstream_sensitivity)[0]
    small_grads, wkv_grads = [None] * (2 * depth), [None] * depth
    weight_grads = [None] * (2 * depth)
    summed = None
    for level in reversed(range(depth)):
        for j in (2 * level + 1, 2 * level):
            if j % 2 == 0:
                grad, small_grads[j], wkv_grads[level], weights = time_backward_plain(
                    grad, kept[j], small_full[j], small_own[j], wkv_rows[level],
                    attend_entry_matrix[level], attend_exit_matrix[level],
                )
            else:
                grad, small_grads[j], weights = channel_backward_plain(
                    grad, kept[j], small_full[j], small_own[j],
                    feed_lookup_matrix[level], feed_content_matrix[level], feed_gate_matrix[level],
                )
            weight_grads[j] = weights
        both = weight_grads[2 * level + 1], weight_grads[2 * level]
        if summed is not None:
            both, summed = lax.optimization_barrier((both, summed))
            weight_grads[2 * level + 3], weight_grads[2 * level + 2] = summed
        summed = lax.psum(both, ("section", "seq"))
    weight_grads[1], weight_grads[0] = summed
    back_share = to_tokens(grad)

    table = jnp.stack(small_grads + wkv_grads)
    tables = lax.all_gather(table, ("section", "seq"), axis=0)
    sums = [
        jnp.stack([weight_grads[2 * level + kind][place] for level in range(depth)])
        for kind, place in ((0, 0), (0, 1), (1, 0), (1, 1), (1, 2))
    ]
    return out_share, back_share, tables, sums


def per_device(*arrays):
    residual_entering, lookup = arrays[0], arrays[16]
    sections, cores = lax.axis_size("section"), lax.axis_size("seq")
    micros, unused, length, share = residual_entering.shape
    depth, features, hidden = lookup.shape
    fits = sections == 4 and cores == 2 and micros == sections and length == sections * CHUNK
    fits = fits and share % 256 == 0 and features % 256 == 0 and hidden % 256 == 0 and hidden % share == 0
    fits = fits and 2 < lax.axis_size("tp") <= LANES // SUB
    if fits:
        return run_fast(*arrays)
    out_share, back_share, table, sums = run_plain(*arrays)
    tables = table.reshape(sections, cores, *table.shape[1:])
    mine = lax.dynamic_index_in_dim(tables, lax.axis_index("seq"), 1, keepdims=False)
    total = jnp.sum(tables, axis=(0, 1))
    prev_grad = jnp.moveaxis(mine[:, : 2 * depth, 2], 0, 1)[:, :, None]
    state_grads = [jnp.moveaxis(mine[:, 2 * depth :, 2 + i], 0, 1)[:, :, None] for i in range(3)]

    weights = [grad.astype(jnp.float32) for grad in sums]
    return (
        out_share,
        back_share,
        prev_grad,
        *state_grads,
        total[0 : 2 * depth : 2, 0],
        total[0 : 2 * depth : 2, 1],
        total[0 : 2 * depth : 2, 3:6],
        total[2 * depth :, 0],
        total[2 * depth :, 1],
        weights[0],
        weights[1],
        total[1 : 2 * depth : 2, 0],
        total[1 : 2 * depth : 2, 1],
        total[1 : 2 * depth : 2, 3:5],
        weights[2],
        weights[3],
        weights[4],
    )


def solution(mesh):
    rows = P(None, "seq", None, "tp")
    line, mix = P(None, "tp"), P(None, None, "tp")
    columns, depths = P(None, None, "tp"), P(None, "tp", None)
    entry = P(None, None, None, "tp")
    state = P(None, None, "seq", "tp")
    tokens = P(None, "seq", "section", "tp")
    return jax.shard_map(
        per_device,
        mesh=mesh,
        in_specs=(
            rows, rows, state, state, state, state,
            line, line, mix, line, line, entry, depths,
            line, line, mix, columns, depths, columns,
        ),
        out_specs=(
            tokens, tokens, state, state, state, state,
            line, line, mix, line, line, entry, depths,
            line, line, mix, columns, depths, columns,
        ),
        check_vma=False,
    )
```

```python
from functools import partial

import jax
import jax.numpy as jnp
from jax import lax
from jax.experimental import pallas as pl
from jax.experimental.pallas import tpu as pltpu
from jax.sharding import PartitionSpec as P

BLOCK = 128


epsilon = 1e-05


def product(left_side, right_side):
    return jnp.dot(left_side, right_side, preferred_element_type=jnp.float32)


def inner_rows(left_side, right_side):
    return lax.dot_general(
        left_side, right_side, (((0,), (0,)), ((), ())), preferred_element_type=jnp.float32
    )


def against(left_side, right_side):
    return lax.dot_general(
        left_side, right_side, (((1,), (1,)), ((), ())), preferred_element_type=jnp.float32
    )


def weighted_value_blocks(
    block_length,
    incoming_lookups,
    incoming_contents,
    fading_entries,
    reward_entries,
    dividend_entries,
    divisor_entries,
    peak_line,
):
    decay_rate = jnp.exp(fading_entries)
    total_rows, channels = incoming_lookups.shape
    places = jnp.arange(block_length, dtype=jnp.float32)
    earlier = places[:, None] > places[None, :]
    spacing = places[:, None] - 1.0 - places[None, :]
    remain = block_length - 1.0 - places

    def advance(state_in, block_in):
        numer_in, denom_in, topmost = state_in
        lookup_piece_tile, value_block = block_in
        spread_exp = lookup_piece_tile[None, :, :] - spacing[:, :, None] * decay_rate
        spread_exp = jnp.where(earlier[:, :, None], spread_exp, -1e30)
        leading_power = reward_entries + lookup_piece_tile
        start_exp = topmost[None, :] - places[:, None] * decay_rate
        peak_exp = jnp.maximum(jnp.maximum(jnp.max(spread_exp, axis=1), leading_power), start_exp)
        weights = jnp.exp(spread_exp - peak_exp[:, None, :])
        from_state = jnp.exp(start_exp - peak_exp)
        own_term = jnp.exp(leading_power - peak_exp)
        numer_out = (
            from_state * numer_in
            + jnp.sum(weights * value_block[None, :, :], axis=1)
            + own_term * value_block
        )
        denom_out = from_state * denom_in + jnp.sum(weights, axis=1) + own_term
        ending = lookup_piece_tile - remain[:, None] * decay_rate
        stopping = topmost - block_length * decay_rate
        new_top = jnp.maximum(jnp.max(ending, axis=0), stopping)
        scaled = jnp.exp(ending - new_top[None, :])
        carried = jnp.exp(stopping - new_top)
        new_numer = carried * numer_in + jnp.sum(scaled * value_block, axis=0)
        new_denom = carried * denom_in + jnp.sum(scaled, axis=0)
        return ((new_numer, new_denom, new_top), numer_out / denom_out)

    blocks = total_rows // block_length
    unused, results = lax.scan(
        jax.checkpoint(advance),
        (dividend_entries, divisor_entries, peak_line),
        (
            incoming_lookups.reshape(blocks, block_length, channels),
            incoming_contents.reshape(blocks, block_length, channels),
        ),
    )
    return results.reshape(total_rows, channels)


def spread_plain(rows_in):
    features = rows_in.shape[1] * lax.axis_size("tp")
    mean_row = lax.psum(jnp.sum(rows_in, axis=1), "tp") / features
    center = rows_in - mean_row[:, None]
    inv_std = lax.rsqrt(lax.psum(jnp.sum(center * center, axis=1), "tp") / features + epsilon)
    normal_share = center * inv_std[:, None]
    normal_full = lax.all_gather(normal_share.astype(jnp.bfloat16), "tp", axis=1, tiled=True)
    return normal_share, inv_std, normal_full


def mix_plain(normal_full, small_full, mix_count):
    normed = normal_full.astype(jnp.float32) * small_full[0] + small_full[1]
    shifted = jnp.concatenate([small_full[2:3], normed[:-1]], axis=0)
    gap = normed - shifted
    mixed = [(shifted + gap * small_full[3 + i]).astype(jnp.bfloat16) for i in range(mix_count)]
    return mixed, gap


def scatter_plain(branch):
    return lax.psum_scatter(
        branch.astype(jnp.bfloat16), "tp", scatter_dimension=1, tiled=True
    ).astype(jnp.float32)


def time_forward_plain(rows_in, small_full, small_own, wkv_rows, entry_matrix, exit_matrix):
    normal_share, inv_std, normal_full = spread_plain(rows_in)
    mixed, gap = mix_plain(normal_full, small_full, 3)
    lookups, contents, recept = [product(mixed[i], entry_matrix[i]) for i in range(3)]
    averaged, pullback = jax.vjp(
        partial(weighted_value_blocks, BLOCK), lookups, contents, *[wkv_rows[i] for i in range(5)]
    )
    gate = jax.nn.sigmoid(recept)
    output = (gate * averaged).astype(jnp.bfloat16)
    rows_out = rows_in + scatter_plain(product(output, exit_matrix))
    kept = (normal_share, inv_std, normal_full, mixed, gap, averaged, pullback, gate, output)
    return rows_out, kept


def channel_forward_plain(rows_in, small_full, small_own, w_key, w_value, w_gate):
    normal_share, inv_std, normal_full = spread_plain(rows_in)
    mixed, gap = mix_plain(normal_full, small_full, 2)
    hidden_pre = product(mixed[0], w_key)
    soft = jax.nn.softplus(hidden_pre)
    hidden = jnp.square(soft).astype(jnp.bfloat16)
    gate = jax.nn.sigmoid(product(mixed[1], w_gate))
    kv_share = scatter_plain(product(hidden, w_value))
    kept = (normal_share, inv_std, normal_full, mixed, gap, hidden_pre, soft, hidden, gate, kv_share)
    return rows_in + gate * kv_share, kept


def norm_back_plain(rows_grad, mix_grads, gap, normal_full, normal_share, inv_std, small_full, small_own):
    share = normal_share.shape[1]
    features = small_full.shape[1]
    to_normed = sum(grad * small_full[3 + i] for i, grad in enumerate(mix_grads))
    to_shifted = sum(grad * (1.0 - small_full[3 + i]) for i, grad in enumerate(mix_grads))
    ratio_grads = [jnp.sum(grad * gap, axis=0) for grad in mix_grads]
    ratio_grads += [jnp.zeros_like(ratio_grads[0])] * (3 - len(mix_grads))
    to_normed = to_normed + jnp.concatenate([to_shifted[1:], jnp.zeros_like(to_shifted[:1])], axis=0)
    normed_grad = scatter_plain(to_normed)
    edge = lax.psum_scatter(
        jnp.stack([to_shifted[0]] + ratio_grads), "tp", scatter_dimension=1, tiled=True
    )
    scaled = normed_grad * small_own[0]
    first, second = lax.psum((jnp.sum(scaled, axis=1), jnp.sum(scaled * normal_share, axis=1)), "tp")
    rows_back = rows_grad + inv_std[:, None] * (
        scaled - first[:, None] / features - normal_share * (second[:, None] / features)
    )
    gain_grad = jnp.sum(normed_grad * normal_share, axis=0)
    bias_grad = jnp.sum(normed_grad, axis=0)
    zero = jnp.zeros((2, share), jnp.float32)
    return rows_back, jnp.concatenate([gain_grad[None], bias_grad[None], edge, zero], axis=0)


def time_backward_plain(rows_grad, kept, small_full, small_own, wkv_rows, entry_matrix, exit_matrix):
    normal_share, inv_std, normal_full, mixed, gap, averaged, pullback, gate, output = kept
    branch_grad = lax.all_gather(rows_grad.astype(jnp.bfloat16), "tp", axis=1, tiled=True)
    exit_grad = inner_rows(output, branch_grad)
    output_grad = against(branch_grad, exit_matrix)
    state_grads = pullback(output_grad * gate)
    pre_grads = [
        state_grads[0].astype(jnp.bfloat16),
        state_grads[1].astype(jnp.bfloat16),
        (output_grad * averaged * gate * (1.0 - gate)).astype(jnp.bfloat16),
    ]
    entry_grad = jnp.stack([inner_rows(mixed[i], pre_grads[i]) for i in range(3)])
    mix_grads = [against(pre_grads[i], entry_matrix[i]) for i in range(3)]
    rows_back, small_grad = norm_back_plain(
        rows_grad, mix_grads, gap, normal_full, normal_share, inv_std, small_full, small_own
    )
    wkv_grad = jnp.concatenate([jnp.stack(state_grads[2:]), jnp.zeros((3, gate.shape[1]))], axis=0)
    return rows_back, small_grad, wkv_grad, (entry_grad.astype(jnp.bfloat16), exit_grad.astype(jnp.bfloat16))


def channel_backward_plain(rows_grad, kept, small_full, small_own, w_key, w_value, w_gate):
    normal_share, inv_std, normal_full, mixed, gap, hidden_pre, soft, hidden, gate, kv_share = kept
    branch_grad = lax.all_gather((rows_grad * gate).astype(jnp.bfloat16), "tp", axis=1, tiled=True)
    value_grad = inner_rows(hidden, branch_grad)
    hidden_grad = (
        against(branch_grad, w_value) * 2.0 * soft * jax.nn.sigmoid(hidden_pre)
    ).astype(jnp.bfloat16)
    gate_grad = (rows_grad * kv_share * gate * (1.0 - gate)).astype(jnp.bfloat16)
    key_grad = inner_rows(mixed[0], hidden_grad)
    recept_grad = inner_rows(mixed[1], gate_grad)
    mix_grads = [against(hidden_grad, w_key), against(gate_grad, w_gate)]
    rows_back, small_grad = norm_back_plain(
        rows_grad, mix_grads, gap, normal_full, normal_share, inv_std, small_full, small_own
    )
    grads = tuple(grad.astype(jnp.bfloat16) for grad in (key_grad, value_grad, recept_grad))
    return rows_back, small_grad, grads


CHUNK = 128
LANES = 128
SUB = 8
PAIR = 2
MESH = pl.DeviceIdType.MESH
NO_POWER = -1e30


def to_row_tile(*columns):
    lane = lax.broadcasted_iota(jnp.int32, (CHUNK, LANES), 1)
    wide = jnp.zeros((CHUNK, LANES), jnp.float32)
    for place, column in enumerate(columns):
        wide = jnp.where(lane == place, column, wide)
    return jnp.transpose(wide)[:PAIR]


def to_columns(tiles):
    count = len(tiles)
    filler = [jnp.zeros((LANES - PAIR * count, CHUNK), jnp.float32)]
    return jnp.transpose(jnp.concatenate(list(tiles) + filler, axis=0))


STEP = CHUNK // SUB


def shift_rows(value, first_row):
    ends = pltpu.roll(value[CHUNK - SUB :], 1, 0)
    at = lax.broadcasted_iota(jnp.int32, ends.shape, 0)
    return jnp.concatenate([jnp.where(at == 0, first_row, ends), value[: CHUNK - SUB]], axis=0)


def unshift_rows(value, last_row):
    starts = pltpu.roll(value[:SUB], SUB - 1, 0)
    at = lax.broadcasted_iota(jnp.int32, starts.shape, 0)
    return jnp.concatenate([value[SUB:], jnp.where(at == SUB - 1, last_row, starts)], axis=0)


def to_stretches(tokens_ref, rows_ref):
    def step(c, unused):
        base = pl.multiple_of(c * CHUNK, CHUNK)
        for s in range(STEP):
            for g in range(tokens_ref.shape[0]):
                rows_ref[pl.ds(base + s * SUB, SUB), g * LANES : (g + 1) * LANES] = tokens_ref[
                    g, pl.ds(base + s, SUB, stride=STEP), :
                ]
        return unused

    lax.fori_loop(0, rows_ref.shape[0] // CHUNK, step, 0)


def to_tokens(rows_ref, tokens_ref, c):
    base = pl.multiple_of(c * CHUNK, CHUNK)
    for s in range(STEP):
        for g in range(tokens_ref.shape[0]):
            tokens_ref[g, pl.ds(base + s, SUB, stride=STEP), :] = rows_ref[
                pl.ds(base + s * SUB, SUB), g * LANES : (g + 1) * LANES
            ]


class Peers:
    def __init__(self, count, width):
        self.count, self.width = count, width
        self.me = lax.axis_index("tp")

    def to(self, k):
        return lax.rem(self.me + k, self.count)

    def source(self, k):
        return lax.rem(self.me + self.count - k, self.count)

    def columns(self, owner):
        if isinstance(owner, int):
            return slice(owner * self.width, (owner + 1) * self.width)
        return pl.ds(pl.multiple_of(owner * self.width, LANES), self.width)

    def greet(self, others):
        barrier = pltpu.get_barrier_semaphore()
        places = [{"tp": self.to(k)} for k in range(1, self.count)] + others
        for place in places:
            pl.semaphore_signal(barrier, inc=1, device_id=place, device_id_type=MESH)
        pl.semaphore_wait(barrier, len(places))

    def copy(self, device, source_ref, target_ref, send, receive):
        return pltpu.make_async_remote_copy(
            src_ref=source_ref, dst_ref=target_ref, send_sem=send, recv_sem=receive,
            device_id={"tp": device}, device_id_type=MESH,
        )


def rows_of(c):
    return pl.ds(pl.multiple_of(c * CHUNK, CHUNK), CHUNK)


class Tiles:
    def __init__(self, peers, stat, sems):
        self.peers, self.stat, self.sems = peers, stat, sems

    def copy(self, k, c, owner):
        tile = self.stat.at[owner, c]
        return self.peers.copy(
            self.peers.to(k), tile, tile, self.sems[0].at[k - 1, c], self.sems[1].at[k - 1, c]
        )

    def start(self, c):
        for k in range(1, self.peers.count):
            self.copy(k, c, self.peers.me).start()

    def arrived(self, c):
        for k in range(1, self.peers.count):
            self.copy(k, c, self.peers.source(k)).wait_recv()

    def sent(self, c):
        for k in range(1, self.peers.count):
            self.copy(k, c, self.peers.me).wait_send()


class Gather:
    def __init__(self, peers, pay, sems):
        self.peers, self.pay, self.sems = peers, pay, sems

    def copy(self, way, hop, c, owner, which):
        slot = lax.rem(which, self.pay.shape[0])
        block = self.pay.at[slot, rows_of(c), self.peers.columns(owner)]
        device = jnp.clip(self.peers.me + (1 - 2 * way), 0, self.peers.count - 1)
        return self.peers.copy(
            device, block, block, self.sems[0].at[slot, way, hop - 1, c], self.sems[1].at[slot, way, hop - 1, c]
        )

    def onward(self, way):
        return self.peers.me < self.peers.count - 1 if way == 0 else self.peers.me > 0

    def owner(self, way, hop):
        return self.peers.me - hop if way == 0 else self.peers.me + hop

    def comes(self, way, hop):
        owner = self.owner(way, hop)
        return owner >= 0 if way == 0 else owner < self.peers.count

    def start(self, c, which):
        for way in (0, 1):
            @pl.when(self.onward(way))
            def _():
                self.copy(way, 1, c, self.peers.me, which).start()

    def relay(self, hop, c, which):
        for way in (0, 1):
            @pl.when(self.comes(way, hop))
            def _():
                self.copy(way, hop, c, self.owner(way, hop), which).wait_recv()
                if hop < self.peers.count - 1:
                    @pl.when(self.onward(way))
                    def _():
                        self.copy(way, hop + 1, c, self.owner(way, hop), which).start()

    def sent(self, c, which):
        for way in (0, 1):
            for hop in range(1, self.peers.count):
                @pl.when(self.comes(way, hop - 1) & self.onward(way))
                def _():
                    self.copy(way, hop, c, self.owner(way, hop - 1), which).wait_send()


class Scatter:
    def __init__(self, peers, part, stage, land, sems):
        self.peers, self.part, self.stage, self.land, self.sems = peers, part, stage, land, sems

    def landing(self, way, target, owner):
        if way == 0:
            return self.peers.columns(target)
        return self.peers.columns(jnp.where(target == owner, self.peers.count, target))

    def copy(self, way, c, target, which):
        slot, device = lax.rem(which, 2), jnp.clip(self.peers.me + (1 - 2 * way), 0, self.peers.count - 1)
        return self.peers.copy(
            device, self.stage.at[rows_of(c), self.peers.columns(target)],
            self.land.at[slot, rows_of(c), self.landing(way, target, device)],
            self.sems[0].at[slot, way, target, c], self.sems[1].at[slot, way, target, c],
        )

    def come(self, way, c, target, which):
        slot, columns = lax.rem(which, 2), self.landing(way, target, self.peers.me)
        block = self.land.at[slot, rows_of(c), columns]
        self.peers.copy(
            self.peers.me, block, block, self.sems[0].at[slot, way, target, c], self.sems[1].at[slot, way, target, c]
        ).wait_recv()
        return self.land[slot, rows_of(c), columns].astype(jnp.float32)

    def inward(self, way):
        return self.peers.me > 0 if way == 0 else self.peers.me < self.peers.count - 1

    def passes(self, way, target):
        return self.peers.me < target if way == 0 else self.peers.me > target

    def lag(self, way):
        return self.peers.me if way == 0 else self.peers.count - 1 - self.peers.me

    def push(self, way, c, which):
        rows = rows_of(c)
        targets = range(self.peers.count - 1, 0, -1) if way == 0 else range(self.peers.count - 1)
        for target in targets:
            columns = self.peers.columns(target)

            @pl.when(self.passes(way, target))
            def _():
                @pl.when(which > 0)
                def _():
                    self.copy(way, c, target, which - 1).wait_send()

                @pl.when(self.inward(way))
                def _():
                    self.stage[rows, columns] = (
                        self.part[rows, columns] + self.come(way, c, target, which)
                    ).astype(jnp.bfloat16)

                @pl.when(jnp.logical_not(self.inward(way)))
                def _():
                    self.stage[rows, columns] = self.part[rows, columns].astype(jnp.bfloat16)

                self.copy(way, c, target, which).start()

    def total(self, c, which):
        rows, mine = rows_of(c), self.peers.columns(self.peers.me)
        for way in (0, 1):
            @pl.when(self.inward(way))
            def _():
                self.part[rows, mine] += self.come(way, c, self.peers.me, which)
        return self.part[rows, mine]

    def sent(self, c, which):
        for target in range(self.peers.count):
            for way in (0, 1):
                @pl.when(self.passes(way, target))
                def _():
                    self.copy(way, c, target, which).wait_send()


def ticks_of(peers, chunks, passes, before, backward, begin, gather, compute, scatter):
    count = peers.count
    period = max(2 * count - 2, chunks + 1)

    def split(at):
        which, i = lax.div(at, period), lax.rem(at, period)
        chunk = chunks - 1 - i if backward else i
        return which, jnp.clip(chunk, 0, chunks - 1), (at >= 0) & (i < chunks) & (which < passes)

    def tick(t):
        which, c, there = split(t)
        last = (which == passes) & (lax.rem(t, period) < chunks)

        @pl.when(there | last)
        def _():
            begin(which, c)

        def relay(hop):
            moved, c_hop, there = split(t - hop)

            @pl.when(there)
            def _():
                gather.relay(hop, c_hop, moved + before)

        def push(middle):
            for way in (0, 1):
                lag = scatter.lag(way)
                moved, c_way, there = split(t - (count - 1) - lag)

                @pl.when(there & ((lag == 1) == middle))
                def _():
                    scatter.push(way, c_way, moved + before)

        relay(count - 1)
        which, c, there = split(t - (count - 1))

        @pl.when(there)
        def _():
            compute(which, c)

        push(False)
        for hop in range(1, count - 1):
            relay(hop)
        push(True)
    return tick


def mix_chunk(peers, c, pay, tiles, full_ref, mixed_ref, normal_ref, edge_ref, std_ref, last_ref):
    count, width = peers.count, peers.width
    tiles.arrived(c)
    columns = to_columns([tiles.stat[source, c] for source in range(count)])
    middles = [columns[:, PAIR * source : PAIR * source + 1] for source in range(count)]
    center = sum(middles) / count
    square = sum(columns[:, PAIR * source + 1 : PAIR * source + 2] for source in range(count))
    square = square + width * sum((middle - center) * (middle - center) for middle in middles)
    inv_std = lax.rsqrt(square / (count * width) + epsilon)
    std_ref[rows_of(c), :] = jnp.broadcast_to(inv_std, (CHUNK, LANES))
    for source in range(count):
        part = slice(source * width, (source + 1) * width)
        normal = (
            pay[rows_of(c), part].astype(jnp.float32) + (middles[source] - center)
        ) * inv_std
        normal_ref[rows_of(c), part] = normal.astype(jnp.bfloat16)
        normed = normal * full_ref[0:1, part] + full_ref[1:2, part]
        before = last_ref[0:1, part]
        edge_ref[pl.ds(c, 1), part] = before
        shifted = shift_rows(normed, before)
        last_ref[0:1, part] = normed[CHUNK - 1 : CHUNK]
        gap = normed - shifted
        for i in range(mixed_ref.shape[0]):
            mixed_ref[i, :, part] = (shifted + gap * full_ref[3 + i : 4 + i, part]).astype(
                jnp.bfloat16
            )


def wkv_join(left, right, fall):
    fallen = left[2] - fall
    peak = jnp.maximum(fallen, right[2])
    old, new = jnp.exp(fallen - peak), jnp.exp(right[2] - peak)
    return old * left[0] + new * right[0], old * left[1] + new * right[1], peak


def choose(mask, first, second):
    return tuple(jnp.where(mask, a, b) for a, b in zip(first, second))


def wkv_forward(base, key_ref, value_ref, decay, bonus, carry_ref, out_ref, state_ref):
    steps = STEP

    def at(s):
        return pl.ds(base + s * SUB, SUB)

    state = (value_ref[at(0), :], jnp.ones_like(decay), key_ref[at(0), :])
    for s in range(1, steps):
        key = key_ref[at(s), :]
        state = wkv_join(state, (value_ref[at(s), :], 1.0, key), decay)
    place = lax.broadcasted_iota(jnp.int32, decay.shape, 0)
    carry = tuple(carry_ref[i] for i in range(3))
    state = choose(place == 0, wkv_join(carry, state, steps * decay), state)
    for reach in (1, 2, 4):
        left = tuple(pltpu.roll(part, reach, 0) for part in state)
        state = choose(place >= reach, wkv_join(left, state, reach * steps * decay), state)
    after = tuple(pltpu.roll(part, 1, 0) for part in state)
    for i in range(3):
        carry_ref[i] = after[i]
    numer, denom, power = choose(place == 0, carry, after)
    for s in range(steps):
        key, value = key_ref[at(s), :], value_ref[at(s), :]
        lead = bonus + key
        peak = jnp.maximum(power, lead)
        old, new = jnp.exp(power - peak), jnp.exp(lead - peak)
        out_ref[at(s), :] = (old * numer + new * value) / (old * denom + new)
        state_ref[0, at(s), :] = numer
        state_ref[1, at(s), :] = denom
        state_ref[2, at(s), :] = power
        numer, denom, power = wkv_join((numer, denom, power), (value, 1.0, key), decay)


def wkv_backward(
    base, key_ref, value_ref, decay, bonus, out_ref, state_ref, up_ref, carry_ref, sum_ref, work_ref, grad_ref
):
    steps = STEP

    def at(s):
        return pl.ds(base + s * SUB, SUB)

    state = None
    for s in reversed(range(steps)):
        lead = bonus + key_ref[at(s), :]
        power = state_ref[2, at(s), :]
        peak = jnp.maximum(power, lead)
        new = jnp.exp(lead - peak)
        share = up_ref[s * SUB : (s + 1) * SUB, :] / (
            jnp.exp(power - peak) * state_ref[1, at(s), :] + new
        )
        work_ref[0, s], work_ref[1, s], work_ref[2, s] = share, peak, new * share
        here = (share, -share * out_ref[at(s), :], -peak)
        state = here if state is None else wkv_join(state, here, decay)
    place = lax.broadcasted_iota(jnp.int32, decay.shape, 0)
    carry = tuple(carry_ref[i] for i in range(3))
    state = choose(place == SUB - 1, wkv_join(carry, state, steps * decay), state)
    for reach in (1, 2, 4):
        later = tuple(pltpu.roll(part, SUB - reach, 0) for part in state)
        state = choose(place < SUB - reach, wkv_join(later, state, reach * steps * decay), state)
    after = tuple(pltpu.roll(part, SUB - 1, 0) for part in state)
    for i in range(3):
        carry_ref[i] = after[i]
    numer, denom, power = choose(place == SUB - 1, carry, after)
    for s in reversed(range(steps)):
        key, value, out = key_ref[at(s), :], value_ref[at(s), :], out_ref[at(s), :]
        share, peak, own = work_ref[0, s], work_ref[1, s], work_ref[2, s]
        reach = jnp.exp(key + power)
        direct = own * (value - out)
        grad_ref[0, s * SUB : (s + 1) * SUB, :] = direct + reach * (value * numer + denom)
        grad_ref[1, s * SUB : (s + 1) * SUB, :] = own + reach * numer
        sum_ref[1] += direct
        sum_ref[0] += jnp.exp(state_ref[2, at(s), :] + power - decay) * (
            state_ref[0, at(s), :] * numer + state_ref[1, at(s), :] * denom
        )
        numer, denom, power = wkv_join(
            (numer, denom, power), (share, -share * out, -peak), decay
        )


def load(pairs, sems, start):
    copies = [
        pltpu.make_async_copy(source, target, sems.at[start + i]) for i, (source, target) in enumerate(pairs)
    ]
    for copy in copies:
        copy.start()
    return copies


def soft_plus(value):
    small = jnp.exp(-jnp.abs(value))
    share = 1.0 / (1.0 + small)
    rest = jnp.where(small < 1e-3, small - 0.5 * small * small, jnp.log(1.0 + small))
    return jnp.maximum(value, 0.0) + rest, jnp.where(value >= 0.0, share, small * share)


def from_tokens(tokens_hbm, micro, tokens_ref, sems):
    return [
        pltpu.make_async_copy(tokens_hbm.at[micro, 0, :, pl.ds(g * LANES, LANES)], tokens_ref.at[g], sems.at[g])
        for g in range(tokens_ref.shape[0])
    ]


def to_sections(sections, rows_ref, tokens_ref, out_hbm, sems):
    send, receive = sems
    micro = lax.axis_index("section")
    groups = range(tokens_ref.shape[0])

    def ends(c, source, g):
        return tokens_ref.at[g, rows_of(c)], out_hbm.at[source, 0, :, pl.ds(g * LANES, LANES)]

    def copy(c, source, g):
        held, target = ends(c, source, g)
        return pltpu.make_async_remote_copy(
            src_ref=held, dst_ref=target, send_sem=send.at[c, g], recv_sem=receive.at[source, g],
            device_id={"section": c}, device_id_type=MESH,
        )

    def own(g):
        return pltpu.make_async_copy(*ends(micro, micro, g), send.at[micro, g])

    def start(c):
        to_tokens(rows_ref, tokens_ref, c)

        @pl.when(c == micro)
        def _():
            for g in groups:
                own(g).start()

        @pl.when(c != micro)
        def _():
            for g in groups:
                copy(c, micro, g).start()

    def wait():
        for g in groups:
            for k in range(1, sections):
                other = lax.rem(micro + k, sections)
                copy(other, micro, g).wait_send()
                copy(other, other, g).wait_recv()
            own(g).wait()

    return start, wait


def mix_chunk_back(
    peers, c, ratios, full_ref, normal_ref, edge_ref, mixed_ref, mix_grad, later_ref, edges_ref, part_ref, tiles
):
    count = peers.count
    rows = rows_of(c)
    first = second = 0.0
    for source in range(count):
        part = peers.columns(source)
        normal = normal_ref[rows, part].astype(jnp.float32)
        gain = full_ref[0:1, part]
        normed = normal * gain + full_ref[1:2, part]
        before = shift_rows(normed, edge_ref[pl.ds(c, 1), part])
        gap = normed - before
        direct = shifted = 0.0
        for i in range(ratios):
            grad = mix_grad(i, part)
            ratio = full_ref[3 + i : 4 + i, part]
            mixed_ref[i, rows, part] = (before + gap * ratio).astype(jnp.bfloat16)
            taken = grad * ratio
            direct = direct + taken
            shifted = shifted + (grad - taken)
            edges_ref[3 + i : 4 + i, part] += jnp.sum(grad * gap, axis=0, keepdims=True)
        value = direct + unshift_rows(shifted, later_ref[0:1, part])
        later_ref[0:1, part] = shifted[0:1]
        part_ref[rows, part] = value
        scaled = value * gain
        first = first + jnp.sum(scaled, axis=1, keepdims=True)
        second = second + jnp.sum(scaled * normal, axis=1, keepdims=True)
    tiles.stat[peers.me, c] = to_row_tile(first, second)
    tiles.start(c)


STEPS = 7
COPIES = 15
EVERY = slice(None)


class Summed:
    def __init__(self, grad, core_land, cross_land, own_land, result, sems):
        self.grad, self.core_land, self.cross_land, self.own_land = grad, core_land, cross_land, own_land
        self.result, self.sems = result, sems
        self.lead = (EVERY,) * (len(grad.shape) - 6)
        self.q, section = lax.axis_index("seq"), lax.axis_index("section")
        self.y, self.x = lax.div(section, 2), lax.rem(section, 2)
        self.sibling = {"seq": 1 - self.q}
        self.over_x = {"section": section + 1 - 2 * self.x}
        self.over_y = {"section": section + 2 - 4 * self.y}

    def at(self, ref, *place):
        return ref.at[(*self.lead, *place)]

    def send(self, which, source, target, place):
        return pltpu.make_async_remote_copy(
            src_ref=source, dst_ref=target, send_sem=self.sems[0].at[which], recv_sem=self.sems[1].at[which],
            device_id=place, device_id_type=MESH,
        )

    def share(self, which, held, device, *place):
        return self.send(which, self.at(held, *place), self.at(self.result, *place), device)

    def arrive(self, which, ref, *place):
        view = self.at(ref, *place)
        self.send(which, view, view, self.sibling).wait_recv()

    def add(self, place, land, land_place):
        mine, come = self.at(self.grad, *place), self.at(land, *land_place)
        rows = mine.shape[-2]
        block = min(rows, 32)
        for k in range(3 if self.lead else 1):
            for start in range(0, rows, block):
                view = (*((k,) if self.lead else ()), slice(start, start + block), EVERY)
                mine[view] = (mine[view].astype(jnp.float32) + come[view].astype(jnp.float32)).astype(jnp.bfloat16)

    def add_half(self):
        def step(i, unused):
            place = lax.div(i, 4), lax.rem(lax.div(i, 2), 2), lax.rem(i, 2)
            self.add((self.q, *place), self.core_land, place)
            return unused

        lax.fori_loop(0, 8, step, 0)

    def to_core(self):
        return [self.send(0, self.at(self.grad, 1 - self.q), self.core_land, self.sibling)]

    def cross(self):
        first, second = (EVERY, 1 - self.x, 0), (1 - self.y, EVERY, 1)
        return [
            self.send(1, self.at(self.grad, self.q, *first), self.at(self.cross_land, *first), self.over_x),
            self.send(2, self.at(self.grad, self.q, *second), self.at(self.cross_land, *second), self.over_y),
        ]

    def own(self):
        q, y, x = self.q, self.y, self.x
        return [
            self.send(3, self.at(self.grad, q, 1 - y, x, 0), self.at(self.own_land, 0), self.over_y),
            self.send(4, self.at(self.grad, q, y, 1 - x, 1), self.at(self.own_land, 1), self.over_x),
        ]

    def back_own(self):
        q, y, x = self.q, self.y, self.x
        return [
            self.share(5, self.grad, self.over_y, q, y, x, 0), self.share(6, self.grad, self.over_x, q, y, x, 1),
            self.share(7, self.grad, self.sibling, q, y, x),
        ]

    def back_cross(self):
        q, y, x = self.q, self.y, self.x
        return [
            self.share(8, self.result, self.over_x, q, EVERY, x, 0), self.share(9, self.result, self.over_y, q, y, EVERY, 1),
            self.share(10, self.result, self.sibling, q, 1 - y, x, 0),
            self.share(11, self.result, self.sibling, q, y, 1 - x, 1),
        ]

    def back_core(self):
        q, y, x = self.q, self.y, self.x
        return [
            self.share(12, self.result, self.sibling, q, EVERY, 1 - x, 0),
            self.share(13, self.result, self.sibling, q, 1 - y, EVERY, 1),
        ]

    def keep(self):
        place = self.q, self.y, self.x
        return pltpu.make_async_copy(self.at(self.grad, *place), self.at(self.result, *place), self.sems[0].at[14])

    def step(self, number):
        q, y, x = self.q, self.y, self.x
        started = []
        if number == 0:
            started = self.to_core()
        elif number == 1:
            self.arrive(0, self.core_land)
            self.add_half()
            started = self.cross()
        elif number == 2:
            self.arrive(1, self.cross_land, EVERY, x, 0)
            self.arrive(2, self.cross_land, y, EVERY, 1)
            for k in (0, 1):
                self.add((q, k, x, 0), self.cross_land, (k, x, 0))
                self.add((q, y, k, 1), self.cross_land, (y, k, 1))
            started = self.own()
        elif number == 3:
            for part in (0, 1):
                self.arrive(3 + part, self.own_land, part)
                self.add((q, y, x, part), self.own_land, (part,))
            started = self.back_own() + [self.keep()]
        elif number == 4:
            self.arrive(5, self.result, q, 1 - y, x, 0)
            self.arrive(6, self.result, q, y, 1 - x, 1)
            self.keep().wait()
            started = self.back_cross()
        elif number == 5:
            self.arrive(7, self.result, 1 - q, y, x)
            self.arrive(8, self.result, q, EVERY, 1 - x, 0)
            self.arrive(9, self.result, q, 1 - y, EVERY, 1)
            started = self.back_core()
        else:
            self.arrive(10, self.result, 1 - q, 1 - y, x, 0)
            self.arrive(11, self.result, 1 - q, y, 1 - x, 1)
            self.arrive(12, self.result, 1 - q, EVERY, 1 - x, 0)
            self.arrive(13, self.result, 1 - q, 1 - y, EVERY, 1)
        for copy in started:
            copy.start()

    def sent_grad(self):
        for copy in self.to_core() + self.cross() + self.own() + self.back_own():
            copy.wait_send()

    def sent_rest(self):
        for copy in self.back_cross() + self.back_core():
            copy.wait_send()


GROUPS = (
    (0, (1,), (1, 2, 4, 5, 6, 11)),
    (0, (0, 2), (0, 1, 3, 4, 5, 11)),
    (1, (3, 4), (1, 2, 4, 5, 6, 12)),
)


def both_kernel(
    count, sections, cores, depth,
    rows_hbm, up_hbm, lead_ref, numer_ref, denom_ref, power_ref, attend_gain, attend_bias, attend_mix, fading_ref, bonus_ref,
    feed_gain, feed_bias, feed_mix, entry_hbm, exit_hbm, key_hbm, content_hbm, gate_hbm,
    out_hbm, back_hbm, table_ref, entry_sum, exit_sum, key_sum, content_sum, gate_sum,
    normal_ref, std_ref, key_ref, value_ref, averaged_ref, state_ref, open_ref, hidden_ref, slope_ref, gate_ref, kv_ref,
    full_ref, edge_ref, rows_ref, tokens_ref, grad_ref, back_ref,
    entry_ref, exit_ref, w_key, w_content, w_gate,
    entry_grad, exit_grad, key_grad, content_grad, gate_grad,
    entry_core, exit_core, key_core, content_core, gate_core,
    entry_cross, exit_cross, key_cross, content_cross, gate_cross,
    entry_own, exit_own, key_own, content_own, gate_own,
    pay, stat, part, stage, land, mixed_ref, pre_grads, up_ref, work_ref, pair_ref, carry_ref, sum_ref,
    output_ref, hidden_grad, last_ref, later_ref, edges_ref, edge_land, small_ref,
    load_sems, token_sems, back_sems, fs, fr, os, orr, bs, br, gs, gr, ts, tr, ss, sr, es, er, ws, wr,
    table_send, table_recv,
):
    length, width = rows_ref.shape
    hidden_width = hidden_ref.shape[2]
    chunks = length // CHUNK
    passes = 2 * depth
    period = max(2 * count - 2, chunks + 1)
    peers = Peers(count, width)
    mine = peers.columns(peers.me)
    micro, core = lax.axis_index("section"), lax.axis_index("seq")
    first = from_tokens(rows_hbm, micro, tokens_ref, token_sems)
    second = from_tokens(up_hbm, micro, back_ref, back_sems)
    for copy in first + second:
        copy.start()
    weights = load(
        (
            (entry_hbm, entry_ref), (exit_hbm, exit_ref), (key_hbm, w_key), (content_hbm, w_content),
            (gate_hbm, w_gate),
        ),
        load_sems,
        0,
    )
    full_ref[...] = jnp.zeros_like(full_ref)
    for j in range(2 * depth):
        level = j // 2
        gain, bias, mix = (attend_gain, attend_bias, attend_mix) if j % 2 == 0 else (feed_gain, feed_bias, feed_mix)
        full_ref[j, 0:1, mine] = gain[level : level + 1, :]
        full_ref[j, 1:2, mine] = bias[level : level + 1, :]
        full_ref[j, 2:3, mine] = lead_ref[j, micro]
        for i in range(mix.shape[0] if j % 2 == 0 else mix.shape[1]):
            full_ref[j, 3 + i : 4 + i, mine] = mix[i, level : level + 1] if j % 2 == 0 else mix[level, i : i + 1]
    gather = Gather(peers, pay, (gs, gr))
    tiles = Tiles(peers, stat, (ts, tr))
    scatter = Scatter(peers, part, stage, land, (ss, sr))
    start_out, wait_out = to_sections(sections, rows_ref, tokens_ref, out_hbm, (os, orr))
    start_back, wait_back = to_sections(sections, grad_ref, back_ref, back_hbm, (bs, br))

    def full_copy(k, owner):
        block = full_ref.at[:, :, peers.columns(owner)]
        return peers.copy(peers.to(k), block, block, fs.at[k - 1], fr.at[k - 1])

    def sums(group, level):
        parts = (
            (key_grad, key_core, key_cross, key_own, key_sum),
            (content_grad, content_core, content_cross, content_own, content_sum),
            (gate_grad, gate_core, gate_cross, gate_own, gate_sum),
        )
        entry = (entry_grad, entry_core, entry_cross, entry_own, entry_sum)
        parts += (entry, (exit_grad, exit_core, exit_cross, exit_own, exit_sum))
        out = []
        for place in GROUPS[group][1]:
            grad, core_land, cross_land, own_land, result = parts[place]
            out.append(
                Summed(
                    grad, core_land, cross_land, own_land, result.at[level],
                    (ws.at[level, place], wr.at[level, place]),
                )
            )
        return out

    def sum_step(group, level, number):
        for matrix in sums(group, level):
            matrix.step(number)

    def table_place(k):
        return lax.rem(micro * cores + core + k, sections * cores)

    def table_copy(k, owner):
        other = table_place(k)
        return pltpu.make_async_remote_copy(
            src_ref=small_ref, dst_ref=table_ref.at[owner], send_sem=table_send.at[k - 1], recv_sem=table_recv.at[k - 1],
            device_id={"section": lax.div(other, cores), "seq": lax.rem(other, cores)}, device_id_type=MESH,
        )

    others = [table_place(k) for k in range(1, sections * cores)]
    peers.greet([{"section": lax.div(other, cores), "seq": lax.rem(other, cores)} for other in others])
    for k in range(1, count):
        full_copy(k, peers.me).start()
    for copy in first:
        copy.wait()
    to_stretches(tokens_ref, rows_ref)

    def begin_forward(j, c):
        rows = rows_of(c)

        @pl.when(j > 0)
        def _():
            value = scatter.total(c, j - 1)
            tiles.sent(c)

            @pl.when(lax.rem(j, 2) == 1)
            def _():
                rows_ref[rows, :] += value

            @pl.when(lax.rem(j, 2) == 0)
            def _():
                level = lax.div(j, 2) - 1
                kv_ref[level, rows, :] = value
                rows_ref[rows, :] += gate_ref[level, rows, :] * value

        @pl.when(j < 2 * depth)
        def _():
            lines = rows_ref[rows, :]
            middle = jnp.mean(lines, axis=1, keepdims=True)
            center = lines - middle
            square = jnp.sum(center * center, axis=1, keepdims=True)
            pay[lax.rem(j, 2), rows, mine] = center.astype(jnp.bfloat16)
            tiles.stat[peers.me, c] = to_row_tile(middle, square)
            tiles.start(c)
            gather.start(c, j)

        @pl.when(j == 2 * depth)
        def _():
            start_out(c)

    def attend_forward(level, c):
        rows = rows_of(c)

        @pl.when(c == 0)
        def _():
            for i, start_ref in enumerate((numer_ref, denom_ref, power_ref)):
                carry_ref[i] = jnp.broadcast_to(start_ref[level, micro], (SUB, width))

        decay = jnp.broadcast_to(jnp.exp(fading_ref[pl.ds(level, 1), :]), (SUB, width))
        bonus = jnp.broadcast_to(bonus_ref[pl.ds(level, 1), :], (SUB, width))
        key_ref[level, rows, :] = product(mixed_ref[0, 0:CHUNK], entry_ref[level, 0])
        value_ref[level, rows, :] = product(mixed_ref[1, 0:CHUNK], entry_ref[level, 1])
        gate = jax.nn.sigmoid(product(mixed_ref[2, 0:CHUNK], entry_ref[level, 2]))
        open_ref[level, rows, :] = gate
        wkv_forward(
            pl.multiple_of(c * CHUNK, CHUNK), key_ref.at[level], value_ref.at[level], decay, bonus, carry_ref,
            averaged_ref.at[level], state_ref.at[level],
        )
        output = (gate * averaged_ref[level, rows, :]).astype(jnp.bfloat16)
        for target in range(count):
            block = peers.columns(target)
            part[rows, block] = product(output, exit_ref[level, :, block])

    def feed_forward(level, c):
        rows = rows_of(c)
        for start in range(0, hidden_ref.shape[2], width):
            block = slice(start, start + width)
            soft, slope = soft_plus(product(mixed_ref[0, 0:CHUNK], w_key[level, :, block]))
            hidden_ref[level, rows, block] = (soft * soft).astype(jnp.bfloat16)
            slope_ref[level, rows, block] = (2.0 * soft * slope).astype(jnp.bfloat16)
        for target in range(count):
            block = peers.columns(target)
            part[rows, block] = product(hidden_ref[level, rows, :], w_content[level, :, block])
        gate_ref[level, rows, :] = jax.nn.sigmoid(product(mixed_ref[1, 0:CHUNK], w_gate[level]))

    def forward(j, c):
        @pl.when((j == 0) & (c == 0))
        def _():
            for k in range(1, count):
                full_copy(k, peers.source(k)).wait_recv()
            for copy in weights:
                copy.wait()

        @pl.when(c == 0)
        def _():
            last_ref[0:1, :] = full_ref[j, 2:3, :]

        def mix(count_mixed):
            mix_chunk(
                peers, c, pay.at[lax.rem(j, 2)], tiles, full_ref.at[j], mixed_ref.at[pl.ds(0, count_mixed), pl.ds(0, CHUNK)],
                normal_ref.at[j], edge_ref.at[j], std_ref.at[j], last_ref,
            )

        level = lax.div(j, 2)

        @pl.when(lax.rem(j, 2) == 0)
        def _():
            mix(3)
            attend_forward(level, c)

        @pl.when(lax.rem(j, 2) == 1)
        def _():
            mix(2)
            feed_forward(level, c)

        gather.sent(c, j)

    def edge_copies(j, source_of):
        return [
            peers.copy(
                peers.to(k), edges_ref.at[j, :, peers.columns(peers.to(k))], edge_land.at[j, source_of(k)],
                es.at[j, k - 1], er.at[j, k - 1],
            )
            for k in range(1, count)
        ]

    def end_pass(j, c):
        rows = rows_of(c)
        normed_grad = scatter.total(c, 2 * passes - 1 - j)
        tiles.arrived(c)
        totals = tiles.stat[0, c]
        for source in range(1, count):
            totals = totals + tiles.stat[source, c]
        columns = to_columns([totals])
        normal = normal_ref[j, rows, mine].astype(jnp.float32)
        scale = 1.0 / (count * width)
        grad_ref[rows, :] += std_ref[j, rows, 0:1] * (
            normed_grad * full_ref[j, 0:1, mine] - columns[:, 0:1] * scale - normal * (columns[:, 1:2] * scale)
        )
        small_ref[j, 0:1, :] += jnp.sum(normed_grad * normal, axis=0, keepdims=True)
        small_ref[j, 1:2, :] += jnp.sum(normed_grad, axis=0, keepdims=True)

        @pl.when(c == 0)
        def _():
            for copy in edge_copies(j, peers.source):
                copy.wait_recv()
            edges = edges_ref[j, :, mine]
            for k in range(1, count):
                edges = edges + edge_land[j, peers.source(k)]
            small_ref[j, 2:6, :] = edges[2:6]

    def begin_backward(which, c):
        rows = rows_of(c)
        j = passes - 1 - which

        @pl.when(which > 0)
        def _():
            end_pass(j + 1, c)
            gather.sent(c, passes + which - 1)
            tiles.sent(c)

        @pl.when((which < passes) & (lax.rem(which, 2) == 0))
        def _():
            pay[lax.rem(which, 2), rows, mine] = (grad_ref[rows, :] * gate_ref[lax.div(j, 2), rows, :]).astype(jnp.bfloat16)

        @pl.when((which < passes) & (lax.rem(which, 2) == 1))
        def _():
            pay[lax.rem(which, 2), rows, mine] = grad_ref[rows, :].astype(jnp.bfloat16)

        @pl.when(which < passes)
        def _():
            gather.start(c, passes + which)

        @pl.when(which == passes)
        def _():
            start_back(c)

    def attend_backward(j, c):
        level = lax.div(j, 2)
        rows = rows_of(c)
        decay = jnp.broadcast_to(jnp.exp(fading_ref[pl.ds(level, 1), :]), (SUB, width))
        bonus = jnp.broadcast_to(bonus_ref[pl.ds(level, 1), :], (SUB, width))

        @pl.when(c == chunks - 1)
        def _():
            sum_ref[...] = jnp.zeros_like(sum_ref)
            carry_ref[0] = jnp.zeros((SUB, width), jnp.float32)
            carry_ref[1] = jnp.zeros((SUB, width), jnp.float32)
            carry_ref[2] = jnp.full((SUB, width), NO_POWER, jnp.float32)

        output_grad = against(pay[1, rows, :], exit_ref[level])
        gate = open_ref[level, rows, :]
        up = output_grad * gate
        up_ref[...] = up
        averaged = averaged_ref[level, rows, :]
        pre_grads[2, rows, :] = (up * averaged * (1.0 - gate)).astype(jnp.bfloat16)
        output_ref[rows, :] = (gate * averaged).astype(jnp.bfloat16)
        wkv_backward(
            pl.multiple_of(c * CHUNK, CHUNK), key_ref.at[level], value_ref.at[level], decay, bonus,
            averaged_ref.at[level], state_ref.at[level],
            up_ref, carry_ref, sum_ref, work_ref, pair_ref,
        )
        pre_grads[0, rows, :] = pair_ref[0].astype(jnp.bfloat16)
        pre_grads[1, rows, :] = pair_ref[1].astype(jnp.bfloat16)
        mix_chunk_back(
            peers, c, 3, full_ref.at[j], normal_ref.at[j], edge_ref.at[j], mixed_ref,
            lambda i, columns: against(pre_grads[i, rows, :], entry_ref[level, i, columns, :]),
            later_ref, edges_ref.at[j], part, tiles,
        )

        @pl.when(c == 0)
        def _():
            numer, denom = carry_ref[0, SUB - 1 :, :], carry_ref[1, SUB - 1 :, :]
            lift = jnp.exp(power_ref[level, micro] + carry_ref[2, SUB - 1 :, :])
            out = passes + level
            small_ref[out, 0:1, :] = -decay[0:1] * jnp.sum(sum_ref[0], axis=0, keepdims=True)
            small_ref[out, 1:2, :] = jnp.sum(sum_ref[1], axis=0, keepdims=True)
            small_ref[out, 2:3, :] = lift * numer
            small_ref[out, 3:4, :] = lift * denom
            small_ref[out, 4:5, :] = lift * (numer_ref[level, micro] * numer + denom_ref[level, micro] * denom)

    def feed_backward(j, c):
        rows = rows_of(c)
        level = lax.div(j, 2)
        gate = gate_ref[level, rows, :]
        pre_grads[0, rows, :] = (grad_ref[rows, :] * gate * kv_ref[level, rows, :] * (1.0 - gate)).astype(jnp.bfloat16)
        for start in range(0, hidden_width, width):
            block = slice(start, start + width)
            into = against(pay[0, rows, :], w_content[level, block, :])
            hidden_grad[rows, block] = (into * slope_ref[level, rows, block].astype(jnp.float32)).astype(jnp.bfloat16)

        def mix_grad(i, columns):
            if i == 0:
                return against(hidden_grad[rows, :], w_key[level, columns, :])
            return against(pre_grads[0, rows, :], w_gate[level, columns, :])

        mix_chunk_back(
            peers, c, 2, full_ref.at[j], normal_ref.at[j], edge_ref.at[j], mixed_ref, mix_grad,
            later_ref, edges_ref.at[j], part, tiles,
        )

    def backward(which, c):
        j = passes - 1 - which

        @pl.when(c == chunks - 1)
        def _():
            later_ref[...] = jnp.zeros_like(later_ref)

        @pl.when(lax.rem(which, 2) == 0)
        def _():
            feed_backward(j, c)

        @pl.when(lax.rem(which, 2) == 1)
        def _():
            attend_backward(j, c)

        @pl.when(c == 0)
        def _():
            edges_ref[j, 2:3, :] = later_ref[0:1, :]
            for copy in edge_copies(j, lambda k: peers.me):
                copy.start()

    def weigh(place, level):
        if place == 4:
            for source in range(count):
                block = peers.columns(source)
                grad = inner_rows(output_ref[...], pay[1, :, block]).astype(jnp.bfloat16)
                exit_grad[..., block] = grad.reshape(*exit_grad.shape[:-1], width)
            return
        for i in range(4):
            at = i // 2, i % 2
            if place == 1:
                rows = hidden_width // 4
                grad = inner_rows(hidden_ref[level, :, i * rows : (i + 1) * rows], pay[0]).astype(jnp.bfloat16)
                content_grad[at] = grad.reshape(content_grad.shape[2:])
                continue
            rows = slice(i * (pay.shape[2] // 4), (i + 1) * (pay.shape[2] // 4))
            if place == 0:
                grad = inner_rows(mixed_ref[0, :, rows], hidden_grad[...]).astype(jnp.bfloat16)
                key_grad[at] = grad.reshape(key_grad.shape[2:])
            elif place == 2:
                grad = inner_rows(mixed_ref[1, :, rows], pre_grads[0]).astype(jnp.bfloat16)
                gate_grad[at] = grad.reshape(gate_grad.shape[2:])
            else:
                for k in range(3):
                    grad = inner_rows(mixed_ref[k, :, rows], pre_grads[k]).astype(jnp.bfloat16)
                    entry_grad[(k, *at)] = grad.reshape(entry_grad.shape[3:])

    base, final = chunks + count - 1, passes * period + chunks - 1

    def when_taken(group, number, t):
        kind, places, later = GROUPS[group]
        since = t - (base + period * kind + later[number])
        taken = (since >= 0) & (lax.rem(since, 2 * period) == 0) & (since < 2 * period * depth)
        return taken, depth - 1 - lax.div(since, 2 * period)

    def extra(t):
        for group in range(len(GROUPS)):
            for number in reversed(range(STEPS - 1)):
                taken, level = when_taken(group, number, t)

                @pl.when(taken)
                def _():
                    if number == 0:
                        @pl.when(level < depth - 1)
                        def _():
                            for matrix in sums(group, jnp.minimum(level + 1, depth - 1)):
                                matrix.sent_grad()

                        for place in GROUPS[group][1]:
                            weigh(place, jnp.clip(level, 0, depth - 1))
                    sum_step(group, jnp.clip(level, 0, depth - 1), number)

    forward_tick = ticks_of(peers, chunks, passes, 0, False, begin_forward, gather, forward, scatter)
    backward_tick = ticks_of(peers, chunks, passes, passes, True, begin_backward, gather, backward, scatter)
    turn = (passes - 1) * period + chunks + count - 1

    def tick(t, unused):
        @pl.when(t < passes * period + chunks)
        def _():
            forward_tick(t)

        @pl.when(t == turn - 1)
        def _():
            for copy in second:
                copy.wait()
            to_stretches(back_ref, grad_ref)
            small_ref[...] = jnp.zeros_like(small_ref)
            edges_ref[...] = jnp.zeros_like(edges_ref)

        @pl.when(t >= turn)
        def _():
            backward_tick(t - turn)
            extra(t - turn)

        return unused

    lax.fori_loop(0, turn + final + 1, tick, 0)

    for k in range(1, sections * cores):
        table_copy(k, micro * cores + core).start()
    table_ref[micro * cores + core] = small_ref[...]
    left = []
    for group, (kind, places, later) in enumerate(GROUPS):
        for level in reversed(range(depth)):
            start = base + period * (kind + 2 * (depth - 1 - level))
            for number in range(STEPS):
                at = start + (later[number] if number < STEPS - 1 else later[-1] + 5)
                if at > final or number == STEPS - 1:
                    left.append((at, group, level, number))
    for at, group, level, number in sorted(left):
        sum_step(group, level, number)
    for c in range(chunks):
        scatter.sent(c, 2 * passes - 1)
    for j in range(passes):
        for copy in edge_copies(j, lambda k: peers.me):
            copy.wait_send()
    for group in range(len(GROUPS)):
        for level in range(depth):
            for matrix in sums(group, level):
                matrix.sent_rest()
                if level == 0:
                    matrix.sent_grad()
    for k in range(1, sections * cores):
        table_copy(k, micro * cores + core).wait_send()
        other = lax.rem(micro * cores + core + sections * cores - k, sections * cores)
        table_copy(k, other).wait_recv()
    for k in range(1, count):
        full_copy(k, peers.me).wait_send()
    wait_out()
    wait_back()


BF16, F32 = jnp.bfloat16, jnp.float32


def struct(*shape, dtype=F32):
    return jax.ShapeDtypeStruct(shape, dtype)


def run_kernel(body, collective, outs, scratch, operands, flops):
    def spec(inside):
        return pl.BlockSpec(memory_space=pltpu.VMEM if inside else pl.ANY)

    return pl.pallas_call(
        body,
        out_shape=[out for out, inside in outs],
        in_specs=[spec(inside) for operand, inside in operands],
        out_specs=[spec(inside) for out, inside in outs],
        scratch_shapes=scratch,
        compiler_params=pltpu.CompilerParams(
            collective_id=collective, has_side_effects=True, vmem_limit_bytes=63 * 1024 * 1024
        ),
        cost_estimate=pl.CostEstimate(flops=flops, bytes_accessed=2**25, transcendentals=2**23),
    )(*[operand for operand, inside in operands])


def pair_of(shape):
    return [pltpu.SemaphoreType.DMA(shape)] * 2


def run_fast(
    residual_entering, upstream_sensitivity, piece_lead_lines, dividend_start, divisor_start, power_offset_start,
    attend_standard_scale, attend_standard_offset, attend_lag_fractions, fading_log_rate, reward_first_word,
    attend_entry_matrix, attend_exit_matrix, feed_standard_scale, feed_standard_offset, feed_lag_fractions,
    feed_lookup_matrix, feed_content_matrix, feed_gate_matrix,
):
    count, sections, cores = (lax.axis_size(axis) for axis in ("tp", "section", "seq"))
    length, width = residual_entering.shape[2:]
    depth, features, hidden = feed_lookup_matrix.shape[0], count * width, feed_lookup_matrix.shape[2]
    chunks, subs = length // CHUNK, 2 * depth
    flops = 2 * depth * length * features * (4 * width + 2 * hidden + width)
    groups = width // LANES
    starts = (dividend_start, divisor_start, power_offset_start)
    weights = (attend_entry_matrix, attend_exit_matrix, feed_lookup_matrix, feed_content_matrix, feed_gate_matrix)
    shares = struct(sections, 1, CHUNK, width)
    lines = (depth, length, width)
    shapes = [weight.shape[1:] for weight in weights]

    def held(*shape, dtype=F32):
        return pltpu.VMEM(shape, dtype)

    def cut(*parts):
        return [(*shape[:-2], *parts, shape[-2] // 16, shape[-1]) for shape in shapes]

    outs = [(shares, False), (shares, False), (struct(sections * cores, subs + depth, SUB, width), True)]
    outs += [(struct(depth, *shape, dtype=BF16), False) for shape in cut(2, 2, 2, 2)]
    scratch = [held(subs, length, features, dtype=BF16), held(subs, length, LANES), held(*lines), held(*lines)]
    scratch += [held(*lines), held(depth, 3, *lines[1:]), held(*lines)]
    scratch += [held(depth, length, hidden, dtype=BF16)] * 2 + [held(*lines)] * 2
    scratch += [held(subs, SUB, features)] * 2 + [held(length, width), held(groups, length, LANES)] * 2
    scratch += [held(*weight.shape, dtype=BF16) for weight in weights]
    scratch += [
        held(*shape, dtype=BF16)
        for shape in cut(2, 2, 2, 2) + cut(2, 2, 2) + cut(2, 2, 2) + cut(2)
    ]
    scratch += [
        held(2, length, features, dtype=BF16), held(count, chunks, PAIR, LANES), held(length, features),
        held(length, features, dtype=BF16), held(2, length, features + width, dtype=BF16),
    ]
    scratch += [
        held(3, length, features, dtype=BF16), held(3, length, width, dtype=BF16), held(CHUNK, width),
        held(3, STEP, SUB, width), held(2, CHUNK, width), held(3, SUB, width), held(2, SUB, width),
        held(length, width, dtype=BF16), held(length, hidden, dtype=BF16), held(SUB, features), held(SUB, features),
        held(subs, SUB, features), held(subs, count, SUB, width), held(subs + depth, SUB, width),
    ]
    scratch += [pltpu.SemaphoreType.DMA((n,)) for n in (len(weights), groups, groups)] + pair_of((count - 1,))
    scratch += pair_of((sections, groups)) + pair_of((sections, groups))
    scratch += pair_of((2, 2, count - 1, chunks)) + pair_of((count - 1, chunks)) + pair_of((2, 2, count, chunks))
    scratch += pair_of((subs, count - 1)) + pair_of((depth, len(weights), COPIES))
    scratch += pair_of((sections * cores - 1,))
    operands = [(residual_entering, False), (upstream_sensitivity, False)]
    operands += [
        (value, True)
        for value in (
            piece_lead_lines, *starts, attend_standard_scale, attend_standard_offset,
            jnp.swapaxes(attend_lag_fractions, 0, 1),
            fading_log_rate, reward_first_word, feed_standard_scale, feed_standard_offset, feed_lag_fractions,
        )
    ]
    operands += [(value, False) for value in weights]
    out_share, back_share, table, *sums = run_kernel(
        partial(both_kernel, count, sections, cores, depth), 0, outs, scratch, operands, 3 * flops
    )
    return finish(cores, depth, out_share, back_share, table, sums, [weight.shape for weight in weights])


def finish_kernel(cores, depth, table_ref, *refs):
    wide, narrow = refs[:7], refs[7:14]
    prev, numer, denom, power = refs[14:18]
    attend_gain, attend_bias, attend_mix, decay, bonus, feed_gain, feed_bias, feed_mix = refs[18:]
    for source, target in zip(wide, narrow):
        target[...] = source[...].astype(jnp.float32)

    @pl.when(pl.program_id(0) == 0)
    def _():
        core = lax.axis_index("seq")
        places, subs = table_ref.shape[0], 2 * depth
        for m in range(places // cores):
            for j in range(subs):
                prev[j, m] = table_ref[m * cores + core, j, 2:3, :]
            for level in range(depth):
                for i, state in enumerate((numer, denom, power)):
                    state[level, m] = table_ref[m * cores + core, subs + level, 2 + i : 3 + i, :]
        for level in range(depth):
            for j, gain, bias, mix in (
                (2 * level, attend_gain, attend_bias, attend_mix), (2 * level + 1, feed_gain, feed_bias, feed_mix),
            ):
                total = sum(table_ref[place, j] for place in range(places))
                gain[level : level + 1, :] = total[0:1]
                bias[level : level + 1, :] = total[1:2]
                for i in range(mix.shape[0] if mix is attend_mix else mix.shape[1]):
                    place = (i, slice(level, level + 1)) if mix is attend_mix else (level, slice(i, i + 1))
                    mix[place] = total[3 + i : 4 + i]
            total = sum(table_ref[place, subs + level] for place in range(places))
            decay[level : level + 1, :] = total[0:1]
            bonus[level : level + 1, :] = total[1:2]


def finish(cores, depth, out_share, back_share, table, sums, shapes):
    steps = 4
    wide = [value.reshape(-1, value.shape[-1]) for value in (out_share, back_share, *sums)]
    blocks = [
        pl.BlockSpec((value.shape[0] // steps, value.shape[1]), lambda i: (i, 0)) for value in wide
    ]
    width = table.shape[-1]
    micros = table.shape[0] // cores
    small = [(2 * depth, micros, 1, width)] + [(depth, micros, 1, width)] * 3
    small += [(depth, width), (depth, width), (3, depth, width), (depth, width), (depth, width)]
    small += [(depth, width), (depth, width), (depth, 2, width)]

    def whole(shape):
        return pl.BlockSpec(shape, lambda i: (0,) * len(shape))

    got = pl.pallas_call(
        partial(finish_kernel, cores, depth),
        grid=(steps,),
        out_shape=[struct(*value.shape) for value in wide] + [struct(*shape) for shape in small],
        in_specs=[whole(table.shape)] + blocks,
        out_specs=blocks + [whole(shape) for shape in small],
        compiler_params=pltpu.CompilerParams(vmem_limit_bytes=60 * 1024 * 1024),
    )(table, *wide)
    shares = [value.reshape(whole.shape) for value, whole in zip(got, (out_share, back_share))]
    entry, leave, key, content, gate = [
        value.reshape(shape) for value, shape in zip(got[2:7], shapes)
    ]
    small = list(got[7:])
    small[6] = jnp.swapaxes(small[6], 0, 1)
    return (*shares, *small[:9], entry, leave, *small[9:], key, content, gate)


def run_plain(
    residual_entering,
    upstream_sensitivity,
    piece_lead_lines,
    dividend_start,
    divisor_start,
    power_offset_start,
    attend_standard_scale,
    attend_standard_offset,
    attend_lag_fractions,
    fading_log_rate,
    reward_first_word,
    attend_entry_matrix,
    attend_exit_matrix,
    feed_standard_scale,
    feed_standard_offset,
    feed_lag_fractions,
    feed_lookup_matrix,
    feed_content_matrix,
    feed_gate_matrix,
):
    sections = lax.axis_size("section")
    micro = lax.axis_index("section")
    length, share = residual_entering.shape[2:]
    depth = attend_entry_matrix.shape[0]

    def own(array):
        return lax.dynamic_index_in_dim(array, micro, 0, keepdims=False)

    blank = jnp.zeros((1, share), jnp.float32)
    lead = lax.dynamic_index_in_dim(piece_lead_lines[:, :, 0], micro, 1, keepdims=False)
    starts = [
        lax.dynamic_index_in_dim(start[:, :, 0], micro, 1, keepdims=False)
        for start in (dividend_start, divisor_start, power_offset_start)
    ]
    small_rows, wkv_rows = [], []
    for level in range(depth):
        for gain, bias, mix, j in (
            (attend_standard_scale, attend_standard_offset, attend_lag_fractions, 2 * level),
            (feed_standard_scale, feed_standard_offset, feed_lag_fractions, 2 * level + 1),
        ):
            rows = [gain[level][None], bias[level][None], lead[j][None], mix[level]]
            rows += [blank] * (5 - mix.shape[1])
            small_rows.append(jnp.concatenate(rows, axis=0))
        wkv_rows.append(
            jnp.stack(
                [fading_log_rate[level], reward_first_word[level]]
                + [start[level] for start in starts]
                + [blank[0]] * 3
            )
        )
    small_own = jnp.stack(small_rows)
    small_full = lax.all_gather(small_own, "tp", axis=2, tiled=True)

    rows = own(residual_entering)[0]
    kept = []
    for level in range(depth):
        for j in (2 * level, 2 * level + 1):
            if j % 2 == 0:
                rows, saved = time_forward_plain(
                    rows, small_full[j], small_own[j], wkv_rows[level],
                    attend_entry_matrix[level], attend_exit_matrix[level],
                )
            else:
                rows, saved = channel_forward_plain(
                    rows, small_full[j], small_own[j],
                    feed_lookup_matrix[level], feed_content_matrix[level], feed_gate_matrix[level],
                )
            kept.append(saved)

    def to_tokens(value):
        pieces = value.reshape(sections, length // sections, share)
        return lax.all_to_all(pieces, "section", 0, 0)[:, None]

    out_share = to_tokens(rows)
    grad = own(upstream_sensitivity)[0]
    small_grads, wkv_grads = [None] * (2 * depth), [None] * depth
    weight_grads = [None] * (2 * depth)
    summed = None
    for level in reversed(range(depth)):
        for j in (2 * level + 1, 2 * level):
            if j % 2 == 0:
                grad, small_grads[j], wkv_grads[level], weights = time_backward_plain(
                    grad, kept[j], small_full[j], small_own[j], wkv_rows[level],
                    attend_entry_matrix[level], attend_exit_matrix[level],
                )
            else:
                grad, small_grads[j], weights = channel_backward_plain(
                    grad, kept[j], small_full[j], small_own[j],
                    feed_lookup_matrix[level], feed_content_matrix[level], feed_gate_matrix[level],
                )
            weight_grads[j] = weights
        both = weight_grads[2 * level + 1], weight_grads[2 * level]
        if summed is not None:
            both, summed = lax.optimization_barrier((both, summed))
            weight_grads[2 * level + 3], weight_grads[2 * level + 2] = summed
        summed = lax.psum(both, ("section", "seq"))
    weight_grads[1], weight_grads[0] = summed
    back_share = to_tokens(grad)

    table = jnp.stack(small_grads + wkv_grads)
    tables = lax.all_gather(table, ("section", "seq"), axis=0)
    sums = [
        jnp.stack([weight_grads[2 * level + kind][place] for level in range(depth)])
        for kind, place in ((0, 0), (0, 1), (1, 0), (1, 1), (1, 2))
    ]
    return out_share, back_share, tables, sums


def per_device(*arrays):
    residual_entering, lookup = arrays[0], arrays[16]
    sections, cores = lax.axis_size("section"), lax.axis_size("seq")
    micros, unused, length, share = residual_entering.shape
    depth, features, hidden = lookup.shape
    fits = sections == 4 and cores == 2 and micros == sections and length == sections * CHUNK
    fits = fits and share % 256 == 0 and features % 256 == 0 and hidden % 256 == 0 and hidden % share == 0
    fits = fits and 2 < lax.axis_size("tp") <= LANES // SUB
    if fits:
        return run_fast(*arrays)
    out_share, back_share, table, sums = run_plain(*arrays)
    tables = table.reshape(sections, cores, *table.shape[1:])
    mine = lax.dynamic_index_in_dim(tables, lax.axis_index("seq"), 1, keepdims=False)
    total = jnp.sum(tables, axis=(0, 1))
    prev_grad = jnp.moveaxis(mine[:, : 2 * depth, 2], 0, 1)[:, :, None]
    state_grads = [jnp.moveaxis(mine[:, 2 * depth :, 2 + i], 0, 1)[:, :, None] for i in range(3)]

    weights = [grad.astype(jnp.float32) for grad in sums]
    return (
        out_share,
        back_share,
        prev_grad,
        *state_grads,
        total[0 : 2 * depth : 2, 0],
        total[0 : 2 * depth : 2, 1],
        total[0 : 2 * depth : 2, 3:6],
        total[2 * depth :, 0],
        total[2 * depth :, 1],
        weights[0],
        weights[1],
        total[1 : 2 * depth : 2, 0],
        total[1 : 2 * depth : 2, 1],
        total[1 : 2 * depth : 2, 3:5],
        weights[2],
        weights[3],
        weights[4],
    )


def solution(mesh):
    rows = P(None, "seq", None, "tp")
    line, mix = P(None, "tp"), P(None, None, "tp")
    columns, depths = P(None, None, "tp"), P(None, "tp", None)
    entry = P(None, None, None, "tp")
    state = P(None, None, "seq", "tp")
    tokens = P(None, "seq", "section", "tp")
    return jax.shard_map(
        per_device,
        mesh=mesh,
        in_specs=(
            rows, rows, state, state, state, state,
            line, line, mix, line, line, entry, depths,
            line, line, mix, columns, depths, columns,
        ),
        out_specs=(
            tokens, tokens, state, state, state, state,
            line, line, mix, line, line, entry, depths,
            line, line, mix, columns, depths, columns,
        ),
        check_vma=False,
    )
```

```python
from functools import partial

import jax
import jax.numpy as jnp
from jax import lax
from jax.experimental import pallas as pl
from jax.experimental.pallas import tpu as pltpu
from jax.sharding import PartitionSpec as P

BLOCK = 128


epsilon = 1e-05


def product(left_side, right_side):
    return jnp.dot(left_side, right_side, preferred_element_type=jnp.float32)


def inner_rows(left_side, right_side):
    return lax.dot_general(
        left_side, right_side, (((0,), (0,)), ((), ())), preferred_element_type=jnp.float32
    )


def against(left_side, right_side):
    return lax.dot_general(
        left_side, right_side, (((1,), (1,)), ((), ())), preferred_element_type=jnp.float32
    )


def weighted_value_blocks(
    block_length,
    incoming_lookups,
    incoming_contents,
    fading_entries,
    reward_entries,
    dividend_entries,
    divisor_entries,
    peak_line,
):
    decay_rate = jnp.exp(fading_entries)
    total_rows, channels = incoming_lookups.shape
    places = jnp.arange(block_length, dtype=jnp.float32)
    earlier = places[:, None] > places[None, :]
    spacing = places[:, None] - 1.0 - places[None, :]
    remain = block_length - 1.0 - places

    def advance(state_in, block_in):
        numer_in, denom_in, topmost = state_in
        lookup_piece_tile, value_block = block_in
        spread_exp = lookup_piece_tile[None, :, :] - spacing[:, :, None] * decay_rate
        spread_exp = jnp.where(earlier[:, :, None], spread_exp, -1e30)
        leading_power = reward_entries + lookup_piece_tile
        start_exp = topmost[None, :] - places[:, None] * decay_rate
        peak_exp = jnp.maximum(jnp.maximum(jnp.max(spread_exp, axis=1), leading_power), start_exp)
        weights = jnp.exp(spread_exp - peak_exp[:, None, :])
        from_state = jnp.exp(start_exp - peak_exp)
        own_term = jnp.exp(leading_power - peak_exp)
        numer_out = (
            from_state * numer_in
            + jnp.sum(weights * value_block[None, :, :], axis=1)
            + own_term * value_block
        )
        denom_out = from_state * denom_in + jnp.sum(weights, axis=1) + own_term
        ending = lookup_piece_tile - remain[:, None] * decay_rate
        stopping = topmost - block_length * decay_rate
        new_top = jnp.maximum(jnp.max(ending, axis=0), stopping)
        scaled = jnp.exp(ending - new_top[None, :])
        carried = jnp.exp(stopping - new_top)
        new_numer = carried * numer_in + jnp.sum(scaled * value_block, axis=0)
        new_denom = carried * denom_in + jnp.sum(scaled, axis=0)
        return ((new_numer, new_denom, new_top), numer_out / denom_out)

    blocks = total_rows // block_length
    unused, results = lax.scan(
        jax.checkpoint(advance),
        (dividend_entries, divisor_entries, peak_line),
        (
            incoming_lookups.reshape(blocks, block_length, channels),
            incoming_contents.reshape(blocks, block_length, channels),
        ),
    )
    return results.reshape(total_rows, channels)


def spread_plain(rows_in):
    features = rows_in.shape[1] * lax.axis_size("tp")
    mean_row = lax.psum(jnp.sum(rows_in, axis=1), "tp") / features
    center = rows_in - mean_row[:, None]
    inv_std = lax.rsqrt(lax.psum(jnp.sum(center * center, axis=1), "tp") / features + epsilon)
    normal_share = center * inv_std[:, None]
    normal_full = lax.all_gather(normal_share.astype(jnp.bfloat16), "tp", axis=1, tiled=True)
    return normal_share, inv_std, normal_full


def mix_plain(normal_full, small_full, mix_count):
    normed = normal_full.astype(jnp.float32) * small_full[0] + small_full[1]
    shifted = jnp.concatenate([small_full[2:3], normed[:-1]], axis=0)
    gap = normed - shifted
    mixed = [(shifted + gap * small_full[3 + i]).astype(jnp.bfloat16) for i in range(mix_count)]
    return mixed, gap


def scatter_plain(branch):
    return lax.psum_scatter(
        branch.astype(jnp.bfloat16), "tp", scatter_dimension=1, tiled=True
    ).astype(jnp.float32)


def time_forward_plain(rows_in, small_full, small_own, wkv_rows, entry_matrix, exit_matrix):
    normal_share, inv_std, normal_full = spread_plain(rows_in)
    mixed, gap = mix_plain(normal_full, small_full, 3)
    lookups, contents, recept = [product(mixed[i], entry_matrix[i]) for i in range(3)]
    averaged, pullback = jax.vjp(
        partial(weighted_value_blocks, BLOCK), lookups, contents, *[wkv_rows[i] for i in range(5)]
    )
    gate = jax.nn.sigmoid(recept)
    output = (gate * averaged).astype(jnp.bfloat16)
    rows_out = rows_in + scatter_plain(product(output, exit_matrix))
    kept = (normal_share, inv_std, normal_full, mixed, gap, averaged, pullback, gate, output)
    return rows_out, kept


def channel_forward_plain(rows_in, small_full, small_own, w_key, w_value, w_gate):
    normal_share, inv_std, normal_full = spread_plain(rows_in)
    mixed, gap = mix_plain(normal_full, small_full, 2)
    hidden_pre = product(mixed[0], w_key)
    soft = jax.nn.softplus(hidden_pre)
    hidden = jnp.square(soft).astype(jnp.bfloat16)
    gate = jax.nn.sigmoid(product(mixed[1], w_gate))
    kv_share = scatter_plain(product(hidden, w_value))
    kept = (normal_share, inv_std, normal_full, mixed, gap, hidden_pre, soft, hidden, gate, kv_share)
    return rows_in + gate * kv_share, kept


def norm_back_plain(rows_grad, mix_grads, gap, normal_full, normal_share, inv_std, small_full, small_own):
    share = normal_share.shape[1]
    features = small_full.shape[1]
    to_normed = sum(grad * small_full[3 + i] for i, grad in enumerate(mix_grads))
    to_shifted = sum(grad * (1.0 - small_full[3 + i]) for i, grad in enumerate(mix_grads))
    ratio_grads = [jnp.sum(grad * gap, axis=0) for grad in mix_grads]
    ratio_grads += [jnp.zeros_like(ratio_grads[0])] * (3 - len(mix_grads))
    to_normed = to_normed + jnp.concatenate([to_shifted[1:], jnp.zeros_like(to_shifted[:1])], axis=0)
    normed_grad = scatter_plain(to_normed)
    edge = lax.psum_scatter(
        jnp.stack([to_shifted[0]] + ratio_grads), "tp", scatter_dimension=1, tiled=True
    )
    scaled = normed_grad * small_own[0]
    first, second = lax.psum((jnp.sum(scaled, axis=1), jnp.sum(scaled * normal_share, axis=1)), "tp")
    rows_back = rows_grad + inv_std[:, None] * (
        scaled - first[:, None] / features - normal_share * (second[:, None] / features)
    )
    gain_grad = jnp.sum(normed_grad * normal_share, axis=0)
    bias_grad = jnp.sum(normed_grad, axis=0)
    zero = jnp.zeros((2, share), jnp.float32)
    return rows_back, jnp.concatenate([gain_grad[None], bias_grad[None], edge, zero], axis=0)


def time_backward_plain(rows_grad, kept, small_full, small_own, wkv_rows, entry_matrix, exit_matrix):
    normal_share, inv_std, normal_full, mixed, gap, averaged, pullback, gate, output = kept
    branch_grad = lax.all_gather(rows_grad.astype(jnp.bfloat16), "tp", axis=1, tiled=True)
    exit_grad = inner_rows(output, branch_grad)
    output_grad = against(branch_grad, exit_matrix)
    state_grads = pullback(output_grad * gate)
    pre_grads = [
        state_grads[0].astype(jnp.bfloat16),
        state_grads[1].astype(jnp.bfloat16),
        (output_grad * averaged * gate * (1.0 - gate)).astype(jnp.bfloat16),
    ]
    entry_grad = jnp.stack([inner_rows(mixed[i], pre_grads[i]) for i in range(3)])
    mix_grads = [against(pre_grads[i], entry_matrix[i]) for i in range(3)]
    rows_back, small_grad = norm_back_plain(
        rows_grad, mix_grads, gap, normal_full, normal_share, inv_std, small_full, small_own
    )
    wkv_grad = jnp.concatenate([jnp.stack(state_grads[2:]), jnp.zeros((3, gate.shape[1]))], axis=0)
    return rows_back, small_grad, wkv_grad, (entry_grad.astype(jnp.bfloat16), exit_grad.astype(jnp.bfloat16))


def channel_backward_plain(rows_grad, kept, small_full, small_own, w_key, w_value, w_gate):
    normal_share, inv_std, normal_full, mixed, gap, hidden_pre, soft, hidden, gate, kv_share = kept
    branch_grad = lax.all_gather((rows_grad * gate).astype(jnp.bfloat16), "tp", axis=1, tiled=True)
    value_grad = inner_rows(hidden, branch_grad)
    hidden_grad = (
        against(branch_grad, w_value) * 2.0 * soft * jax.nn.sigmoid(hidden_pre)
    ).astype(jnp.bfloat16)
    gate_grad = (rows_grad * kv_share * gate * (1.0 - gate)).astype(jnp.bfloat16)
    key_grad = inner_rows(mixed[0], hidden_grad)
    recept_grad = inner_rows(mixed[1], gate_grad)
    mix_grads = [against(hidden_grad, w_key), against(gate_grad, w_gate)]
    rows_back, small_grad = norm_back_plain(
        rows_grad, mix_grads, gap, normal_full, normal_share, inv_std, small_full, small_own
    )
    grads = tuple(grad.astype(jnp.bfloat16) for grad in (key_grad, value_grad, recept_grad))
    return rows_back, small_grad, grads


CHUNK = 128
LANES = 128
SUB = 8
PAIR = 2
MESH = pl.DeviceIdType.MESH
NO_POWER = -1e30


def to_row_tile(*columns):
    lane = lax.broadcasted_iota(jnp.int32, (CHUNK, LANES), 1)
    wide = jnp.zeros((CHUNK, LANES), jnp.float32)
    for place, column in enumerate(columns):
        wide = jnp.where(lane == place, column, wide)
    return jnp.transpose(wide)[:PAIR]


def to_columns(tiles):
    count = len(tiles)
    filler = [jnp.zeros((LANES - PAIR * count, CHUNK), jnp.float32)]
    return jnp.transpose(jnp.concatenate(list(tiles) + filler, axis=0))


STEP = CHUNK // SUB


def shift_rows(value, first_row):
    ends = pltpu.roll(value[CHUNK - SUB :], 1, 0)
    at = lax.broadcasted_iota(jnp.int32, ends.shape, 0)
    return jnp.concatenate([jnp.where(at == 0, first_row, ends), value[: CHUNK - SUB]], axis=0)


def unshift_rows(value, last_row):
    starts = pltpu.roll(value[:SUB], SUB - 1, 0)
    at = lax.broadcasted_iota(jnp.int32, starts.shape, 0)
    return jnp.concatenate([value[SUB:], jnp.where(at == SUB - 1, last_row, starts)], axis=0)


def to_stretches(tokens_ref, rows_ref):
    def step(c, unused):
        base = pl.multiple_of(c * CHUNK, CHUNK)
        for s in range(STEP):
            for g in range(tokens_ref.shape[0]):
                rows_ref[pl.ds(base + s * SUB, SUB), g * LANES : (g + 1) * LANES] = tokens_ref[
                    g, pl.ds(base + s, SUB, stride=STEP), :
                ]
        return unused

    lax.fori_loop(0, rows_ref.shape[0] // CHUNK, step, 0)


def to_tokens(rows_ref, tokens_ref, c):
    base = pl.multiple_of(c * CHUNK, CHUNK)
    for s in range(STEP):
        for g in range(tokens_ref.shape[0]):
            tokens_ref[g, pl.ds(base + s, SUB, stride=STEP), :] = rows_ref[
                pl.ds(base + s * SUB, SUB), g * LANES : (g + 1) * LANES
            ]


def halves(value, most):
    if isinstance(value, int):
        return value // 2
    return sum(jnp.where(value >= 2 * k, 1, 0) for k in range(1, most // 2 + 1))


def odd(value, most):
    return value - 2 * halves(value, most)


class Here:
    def __init__(self, names):
        self.names, self.at = names, {name: lax.axis_index(name) for name in names}

    def device(self, **other):
        return tuple(other.get(name, self.at[name]) for name in self.names)


class Peers:
    def __init__(self, here, count, width, passes):
        self.here, self.count, self.width, self.passes = here, count, width, passes
        self.me = here.at["tp"]
        self.others = [lax.rem(self.me + k, count) for k in range(count)]
        self.sources = [lax.rem(self.me + count - k, count) for k in range(count)]
        self.beside = jnp.minimum(self.me + 1, count - 1), jnp.maximum(self.me - 1, 0)

    def to(self, k):
        return self.others[k]

    def source(self, k):
        return self.sources[k]

    def slot(self, which):
        return odd(which, self.passes)

    def columns(self, owner):
        if isinstance(owner, int):
            return slice(owner * self.width, (owner + 1) * self.width)
        return pl.ds(pl.multiple_of(owner * self.width, LANES), self.width)

    def greet(self, others):
        barrier = pltpu.get_barrier_semaphore()
        places = [self.here.device(tp=self.to(k)) for k in range(1, self.count)] + others
        for place in places:
            pl.semaphore_signal(barrier, inc=1, device_id=place, device_id_type=MESH)
        pl.semaphore_wait(barrier, len(places))

    def copy(self, device, source_ref, target_ref, send, receive):
        return pltpu.make_async_remote_copy(
            src_ref=source_ref, dst_ref=target_ref, send_sem=send, recv_sem=receive,
            device_id=self.here.device(tp=device), device_id_type=MESH,
        )


def rows_of(c):
    return pl.ds(pl.multiple_of(c * CHUNK, CHUNK), CHUNK)


class Tiles:
    def __init__(self, peers, stat, sems):
        self.peers, self.stat, self.sems = peers, stat, sems

    def copy(self, k, c, owner):
        tile = self.stat.at[owner, c]
        return self.peers.copy(
            self.peers.to(k), tile, tile, self.sems[0].at[k - 1, c], self.sems[1].at[k - 1, c]
        )

    def start(self, c):
        for k in range(1, self.peers.count):
            self.copy(k, c, self.peers.me).start()

    def arrived(self, c):
        for k in range(1, self.peers.count):
            self.copy(k, c, self.peers.source(k)).wait_recv()

    def sent(self, c):
        for k in range(1, self.peers.count):
            self.copy(k, c, self.peers.me).wait_send()


class Gather:
    def __init__(self, peers, pay, sems):
        self.peers, self.pay, self.sems = peers, pay, sems

    def copy(self, way, hop, c, owner, which):
        slot = self.peers.slot(which)
        block = self.pay.at[slot, rows_of(c), self.peers.columns(owner)]
        device = self.peers.beside[way]
        return self.peers.copy(
            device, block, block, self.sems[0].at[slot, way, hop - 1, c], self.sems[1].at[slot, way, hop - 1, c]
        )

    def onward(self, way):
        return self.peers.me < self.peers.count - 1 if way == 0 else self.peers.me > 0

    def owner(self, way, hop):
        return self.peers.me - hop if way == 0 else self.peers.me + hop

    def comes(self, way, hop):
        owner = self.owner(way, hop)
        return owner >= 0 if way == 0 else owner < self.peers.count

    def start(self, c, which):
        for way in (0, 1):
            @pl.when(self.onward(way))
            def _():
                self.copy(way, 1, c, self.peers.me, which).start()

    def relay(self, hop, c, which):
        for way in (0, 1):
            @pl.when(self.comes(way, hop))
            def _():
                self.copy(way, hop, c, self.owner(way, hop), which).wait_recv()
                if hop < self.peers.count - 1:
                    @pl.when(self.onward(way))
                    def _():
                        self.copy(way, hop + 1, c, self.owner(way, hop), which).start()

    def sent(self, c, which):
        for way in (0, 1):
            for hop in range(1, self.peers.count):
                @pl.when(self.comes(way, hop - 1) & self.onward(way))
                def _():
                    self.copy(way, hop, c, self.owner(way, hop - 1), which).wait_send()


class Scatter:
    def __init__(self, peers, part, stage, land, sems):
        self.peers, self.part, self.stage, self.land, self.sems = peers, part, stage, land, sems

    def landing(self, way, target, owner):
        if way == 0:
            return self.peers.columns(target)
        return self.peers.columns(jnp.where(target == owner, self.peers.count, target))

    def copy(self, way, c, target, which):
        slot, device = self.peers.slot(which), self.peers.beside[way]
        return self.peers.copy(
            device, self.stage.at[rows_of(c), self.peers.columns(target)],
            self.land.at[slot, rows_of(c), self.landing(way, target, device)],
            self.sems[0].at[slot, way, target, c], self.sems[1].at[slot, way, target, c],
        )

    def come(self, way, c, target, which):
        slot, columns = self.peers.slot(which), self.landing(way, target, self.peers.me)
        block = self.land.at[slot, rows_of(c), columns]
        self.peers.copy(
            self.peers.me, block, block, self.sems[0].at[slot, way, target, c], self.sems[1].at[slot, way, target, c]
        ).wait_recv()
        return self.land[slot, rows_of(c), columns].astype(jnp.float32)

    def inward(self, way):
        return self.peers.me > 0 if way == 0 else self.peers.me < self.peers.count - 1

    def passes(self, way, target):
        return self.peers.me < target if way == 0 else self.peers.me > target

    def lag(self, way):
        return self.peers.me if way == 0 else self.peers.count - 1 - self.peers.me

    def push(self, way, c, which):
        rows = rows_of(c)
        targets = range(self.peers.count - 1, 0, -1) if way == 0 else range(self.peers.count - 1)
        for target in targets:
            columns = self.peers.columns(target)

            @pl.when(self.passes(way, target))
            def _():
                @pl.when(which > 0)
                def _():
                    self.copy(way, c, target, which - 1).wait_send()

                @pl.when(self.inward(way))
                def _():
                    self.stage[rows, columns] = (
                        self.part[rows, columns] + self.come(way, c, target, which)
                    ).astype(jnp.bfloat16)

                @pl.when(jnp.logical_not(self.inward(way)))
                def _():
                    self.stage[rows, columns] = self.part[rows, columns].astype(jnp.bfloat16)

                self.copy(way, c, target, which).start()

    def total(self, c, which):
        rows, mine = rows_of(c), self.peers.columns(self.peers.me)
        for way in (0, 1):
            @pl.when(self.inward(way))
            def _():
                self.part[rows, mine] += self.come(way, c, self.peers.me, which)
        return self.part[rows, mine]

    def sent(self, c, which):
        for target in range(self.peers.count):
            for way in (0, 1):
                @pl.when(self.passes(way, target))
                def _():
                    self.copy(way, c, target, which).wait_send()


def ticks_of(peers, chunks, passes, before, backward, begin, gather, compute, scatter):
    count = peers.count
    period = max(2 * count - 2, chunks + 1)

    def split(w, i, behind):
        early = i >= behind
        which, at = jnp.where(early, w, w - 1), jnp.where(early, i - behind, i - behind + period)
        chunk = chunks - 1 - at if backward else at
        return which, jnp.clip(chunk, 0, chunks - 1), (which >= 0) & (which < passes) & (at < chunks)

    def tick(w, i):
        which, c, there = split(w, i, 0)
        last = (w == passes) & (i < chunks)

        @pl.when(there | last)
        def _():
            begin(which, c)

        def relay(hop):
            moved, c_hop, there = split(w, i, hop)

            @pl.when(there)
            def _():
                gather.relay(hop, c_hop, moved + before)

        def push(middle):
            for way in (0, 1):
                lag = scatter.lag(way)
                moved, c_way, there = split(w, i, count - 1 + lag)

                @pl.when(there & ((lag == 1) == middle))
                def _():
                    scatter.push(way, c_way, moved + before)

        relay(count - 1)
        which, c, there = split(w, i, count - 1)

        @pl.when(there)
        def _():
            compute(which, c)

        push(False)
        for hop in range(1, count - 1):
            relay(hop)
        push(True)
    return tick


def mix_chunk(peers, c, pay, tiles, full_ref, mixed_ref, normal_ref, edge_ref, std_ref, last_ref):
    count, width = peers.count, peers.width
    tiles.arrived(c)
    columns = to_columns([tiles.stat[source, c] for source in range(count)])
    middles = [columns[:, PAIR * source : PAIR * source + 1] for source in range(count)]
    center = sum(middles) / count
    square = sum(columns[:, PAIR * source + 1 : PAIR * source + 2] for source in range(count))
    square = square + width * sum((middle - center) * (middle - center) for middle in middles)
    inv_std = lax.rsqrt(square / (count * width) + epsilon)
    std_ref[rows_of(c), :] = jnp.broadcast_to(inv_std, (CHUNK, LANES))
    for source in range(count):
        part = slice(source * width, (source + 1) * width)
        normal = (
            pay[rows_of(c), part].astype(jnp.float32) + (middles[source] - center)
        ) * inv_std
        normal_ref[rows_of(c), part] = normal.astype(jnp.bfloat16)
        normed = normal * full_ref[0:1, part] + full_ref[1:2, part]
        before = last_ref[0:1, part]
        edge_ref[pl.ds(c, 1), part] = before
        shifted = shift_rows(normed, before)
        last_ref[0:1, part] = normed[CHUNK - 1 : CHUNK]
        gap = normed - shifted
        for i in range(mixed_ref.shape[0]):
            mixed_ref[i, :, part] = (shifted + gap * full_ref[3 + i : 4 + i, part]).astype(
                jnp.bfloat16
            )


def wkv_join(left, right, fall):
    fallen = left[2] - fall
    peak = jnp.maximum(fallen, right[2])
    old, new = jnp.exp(fallen - peak), jnp.exp(right[2] - peak)
    return old * left[0] + new * right[0], old * left[1] + new * right[1], peak


def choose(mask, first, second):
    return tuple(jnp.where(mask, a, b) for a, b in zip(first, second))


def wkv_forward(base, key_ref, value_ref, decay, bonus, carry_ref, out_ref, state_ref):
    steps = STEP

    def at(s):
        return pl.ds(base + s * SUB, SUB)

    state = (value_ref[at(0), :], jnp.ones_like(decay), key_ref[at(0), :])
    for s in range(1, steps):
        key = key_ref[at(s), :]
        state = wkv_join(state, (value_ref[at(s), :], 1.0, key), decay)
    place = lax.broadcasted_iota(jnp.int32, decay.shape, 0)
    carry = tuple(carry_ref[i] for i in range(3))
    state = choose(place == 0, wkv_join(carry, state, steps * decay), state)
    for reach in (1, 2, 4):
        left = tuple(pltpu.roll(part, reach, 0) for part in state)
        state = choose(place >= reach, wkv_join(left, state, reach * steps * decay), state)
    after = tuple(pltpu.roll(part, 1, 0) for part in state)
    for i in range(3):
        carry_ref[i] = after[i]
    numer, denom, power = choose(place == 0, carry, after)
    for s in range(steps):
        key, value = key_ref[at(s), :], value_ref[at(s), :]
        lead = bonus + key
        peak = jnp.maximum(power, lead)
        old, new = jnp.exp(power - peak), jnp.exp(lead - peak)
        out_ref[at(s), :] = (old * numer + new * value) / (old * denom + new)
        state_ref[0, at(s), :] = numer
        state_ref[1, at(s), :] = denom
        state_ref[2, at(s), :] = power
        numer, denom, power = wkv_join((numer, denom, power), (value, 1.0, key), decay)


def wkv_backward(
    base, key_ref, value_ref, decay, bonus, out_ref, state_ref, up_ref, carry_ref, sum_ref, work_ref, grad_ref
):
    steps = STEP

    def at(s):
        return pl.ds(base + s * SUB, SUB)

    state = None
    for s in reversed(range(steps)):
        lead = bonus + key_ref[at(s), :]
        power = state_ref[2, at(s), :]
        peak = jnp.maximum(power, lead)
        new = jnp.exp(lead - peak)
        share = up_ref[s * SUB : (s + 1) * SUB, :] / (
            jnp.exp(power - peak) * state_ref[1, at(s), :] + new
        )
        work_ref[0, s], work_ref[1, s], work_ref[2, s] = share, peak, new * share
        here = (share, -share * out_ref[at(s), :], -peak)
        state = here if state is None else wkv_join(state, here, decay)
    place = lax.broadcasted_iota(jnp.int32, decay.shape, 0)
    carry = tuple(carry_ref[i] for i in range(3))
    state = choose(place == SUB - 1, wkv_join(carry, state, steps * decay), state)
    for reach in (1, 2, 4):
        later = tuple(pltpu.roll(part, SUB - reach, 0) for part in state)
        state = choose(place < SUB - reach, wkv_join(later, state, reach * steps * decay), state)
    after = tuple(pltpu.roll(part, SUB - 1, 0) for part in state)
    for i in range(3):
        carry_ref[i] = after[i]
    numer, denom, power = choose(place == SUB - 1, carry, after)
    for s in reversed(range(steps)):
        key, value, out = key_ref[at(s), :], value_ref[at(s), :], out_ref[at(s), :]
        share, peak, own = work_ref[0, s], work_ref[1, s], work_ref[2, s]
        reach = jnp.exp(key + power)
        direct = own * (value - out)
        grad_ref[0, s * SUB : (s + 1) * SUB, :] = direct + reach * (value * numer + denom)
        grad_ref[1, s * SUB : (s + 1) * SUB, :] = own + reach * numer
        sum_ref[1] += direct
        sum_ref[0] += jnp.exp(state_ref[2, at(s), :] + power - decay) * (
            state_ref[0, at(s), :] * numer + state_ref[1, at(s), :] * denom
        )
        numer, denom, power = wkv_join(
            (numer, denom, power), (share, -share * out, -peak), decay
        )


def load(pairs, sems, start):
    copies = [
        pltpu.make_async_copy(source, target, sems.at[start + i]) for i, (source, target) in enumerate(pairs)
    ]
    for copy in copies:
        copy.start()
    return copies


def soft_plus(value):
    small = jnp.exp(-jnp.abs(value))
    share = 1.0 / (1.0 + small)
    rest = jnp.where(small < 1e-3, small - 0.5 * small * small, jnp.log(1.0 + small))
    return jnp.maximum(value, 0.0) + rest, jnp.where(value >= 0.0, share, small * share)


def from_tokens(tokens_hbm, micro, tokens_ref, sems):
    return [
        pltpu.make_async_copy(tokens_hbm.at[micro, 0, :, pl.ds(g * LANES, LANES)], tokens_ref.at[g], sems.at[g])
        for g in range(tokens_ref.shape[0])
    ]


def to_sections(here, sections, rows_ref, tokens_ref, out_hbm, sems):
    send, receive = sems
    micro = here.at["section"]
    groups = range(tokens_ref.shape[0])

    def ends(c, source, g):
        return tokens_ref.at[g, rows_of(c)], out_hbm.at[source, 0, :, pl.ds(g * LANES, LANES)]

    def copy(c, source, g):
        held, target = ends(c, source, g)
        return pltpu.make_async_remote_copy(
            src_ref=held, dst_ref=target, send_sem=send.at[c, g], recv_sem=receive.at[source, g],
            device_id=here.device(section=c), device_id_type=MESH,
        )

    def own(g):
        return pltpu.make_async_copy(*ends(micro, micro, g), send.at[micro, g])

    def start(c):
        to_tokens(rows_ref, tokens_ref, c)

        @pl.when(c == micro)
        def _():
            for g in groups:
                own(g).start()

        @pl.when(c != micro)
        def _():
            for g in groups:
                copy(c, micro, g).start()

    def wait():
        for g in groups:
            for k in range(1, sections):
                other = lax.rem(micro + k, sections)
                copy(other, micro, g).wait_send()
                copy(other, other, g).wait_recv()
            own(g).wait()

    return start, wait


def mix_chunk_back(
    peers, c, ratios, full_ref, normal_ref, edge_ref, mixed_ref, mix_grad, later_ref, edges_ref, part_ref, tiles
):
    count = peers.count
    rows = rows_of(c)
    first = second = 0.0
    for source in range(count):
        part = peers.columns(source)
        normal = normal_ref[rows, part].astype(jnp.float32)
        gain = full_ref[0:1, part]
        normed = normal * gain + full_ref[1:2, part]
        before = shift_rows(normed, edge_ref[pl.ds(c, 1), part])
        gap = normed - before
        direct = shifted = 0.0
        for i in range(ratios):
            grad = mix_grad(i, part)
            ratio = full_ref[3 + i : 4 + i, part]
            mixed_ref[i, rows, part] = (before + gap * ratio).astype(jnp.bfloat16)
            taken = grad * ratio
            direct = direct + taken
            shifted = shifted + (grad - taken)
            edges_ref[3 + i : 4 + i, part] += jnp.sum(grad * gap, axis=0, keepdims=True)
        value = direct + unshift_rows(shifted, later_ref[0:1, part])
        later_ref[0:1, part] = shifted[0:1]
        part_ref[rows, part] = value
        scaled = value * gain
        first = first + jnp.sum(scaled, axis=1, keepdims=True)
        second = second + jnp.sum(scaled * normal, axis=1, keepdims=True)
    tiles.stat[peers.me, c] = to_row_tile(first, second)
    tiles.start(c)


STEPS = 7
COPIES = 15
EVERY = slice(None)


class Summed:
    def __init__(self, around, grad, core_land, cross_land, own_land, result, sems):
        self.grad, self.core_land, self.cross_land, self.own_land = grad, core_land, cross_land, own_land
        self.result, self.sems = result, sems
        self.lead = (EVERY,) * (len(grad.shape) - 6)
        (self.q, self.y, self.x), (self.sibling, self.over_x, self.over_y) = around

    def at(self, ref, *place):
        return ref.at[(*self.lead, *place)]

    def send(self, which, source, target, place):
        return pltpu.make_async_remote_copy(
            src_ref=source, dst_ref=target, send_sem=self.sems[0].at[which], recv_sem=self.sems[1].at[which],
            device_id=place, device_id_type=MESH,
        )

    def share(self, which, held, device, *place):
        return self.send(which, self.at(held, *place), self.at(self.result, *place), device)

    def arrive(self, which, ref, *place):
        view = self.at(ref, *place)
        self.send(which, view, view, self.sibling).wait_recv()

    def add(self, place, land, land_place):
        mine, come = self.at(self.grad, *place), self.at(land, *land_place)
        rows = mine.shape[-2]
        block = min(rows, 32)
        for k in range(3 if self.lead else 1):
            for start in range(0, rows, block):
                view = (*((k,) if self.lead else ()), slice(start, start + block), EVERY)
                mine[view] = (mine[view].astype(jnp.float32) + come[view].astype(jnp.float32)).astype(jnp.bfloat16)

    def add_half(self):
        def step(i, unused):
            y, rest = halves(halves(i, 7), 3), i - 4 * halves(halves(i, 7), 3)
            place = y, halves(rest, 3), odd(rest, 3)
            self.add((self.q, *place), self.core_land, place)
            return unused

        lax.fori_loop(0, 8, step, 0)

    def to_core(self):
        return [self.send(0, self.at(self.grad, 1 - self.q), self.core_land, self.sibling)]

    def cross(self):
        first, second = (EVERY, 1 - self.x, 0), (1 - self.y, EVERY, 1)
        return [
            self.send(1, self.at(self.grad, self.q, *first), self.at(self.cross_land, *first), self.over_x),
            self.send(2, self.at(self.grad, self.q, *second), self.at(self.cross_land, *second), self.over_y),
        ]

    def own(self):
        q, y, x = self.q, self.y, self.x
        return [
            self.send(3, self.at(self.grad, q, 1 - y, x, 0), self.at(self.own_land, 0), self.over_y),
            self.send(4, self.at(self.grad, q, y, 1 - x, 1), self.at(self.own_land, 1), self.over_x),
        ]

    def back_own(self):
        q, y, x = self.q, self.y, self.x
        return [
            self.share(5, self.grad, self.over_y, q, y, x, 0), self.share(6, self.grad, self.over_x, q, y, x, 1),
            self.share(7, self.grad, self.sibling, q, y, x),
        ]

    def back_cross(self):
        q, y, x = self.q, self.y, self.x
        return [
            self.share(8, self.result, self.over_x, q, EVERY, x, 0), self.share(9, self.result, self.over_y, q, y, EVERY, 1),
            self.share(10, self.result, self.sibling, q, 1 - y, x, 0),
            self.share(11, self.result, self.sibling, q, y, 1 - x, 1),
        ]

    def back_core(self):
        q, y, x = self.q, self.y, self.x
        return [
            self.share(12, self.result, self.sibling, q, EVERY, 1 - x, 0),
            self.share(13, self.result, self.sibling, q, 1 - y, EVERY, 1),
        ]

    def keep(self):
        place = self.q, self.y, self.x
        return pltpu.make_async_copy(self.at(self.grad, *place), self.at(self.result, *place), self.sems[0].at[14])

    def step(self, number):
        q, y, x = self.q, self.y, self.x
        started = []
        if number == 0:
            started = self.to_core()
        elif number == 1:
            self.arrive(0, self.core_land)
            self.add_half()
            started = self.cross()
        elif number == 2:
            self.arrive(1, self.cross_land, EVERY, x, 0)
            self.arrive(2, self.cross_land, y, EVERY, 1)
            for k in (0, 1):
                self.add((q, k, x, 0), self.cross_land, (k, x, 0))
                self.add((q, y, k, 1), self.cross_land, (y, k, 1))
            started = self.own()
        elif number == 3:
            for part in (0, 1):
                self.arrive(3 + part, self.own_land, part)
                self.add((q, y, x, part), self.own_land, (part,))
            started = self.back_own() + [self.keep()]
        elif number == 4:
            self.arrive(5, self.result, q, 1 - y, x, 0)
            self.arrive(6, self.result, q, y, 1 - x, 1)
            self.keep().wait()
            started = self.back_cross()
        elif number == 5:
            self.arrive(7, self.result, 1 - q, y, x)
            self.arrive(8, self.result, q, EVERY, 1 - x, 0)
            self.arrive(9, self.result, q, 1 - y, EVERY, 1)
            started = self.back_core()
        else:
            self.arrive(10, self.result, 1 - q, 1 - y, x, 0)
            self.arrive(11, self.result, 1 - q, y, 1 - x, 1)
            self.arrive(12, self.result, 1 - q, EVERY, 1 - x, 0)
            self.arrive(13, self.result, 1 - q, 1 - y, EVERY, 1)
        for copy in started:
            copy.start()

    def sent_grad(self):
        for copy in self.to_core() + self.cross() + self.own() + self.back_own():
            copy.wait_send()

    def sent_rest(self):
        for copy in self.back_cross() + self.back_core():
            copy.wait_send()


GROUPS = (
    (0, (1,), (1, 2, 4, 5, 6, 11)),
    (0, (0, 2), (0, 1, 3, 4, 5, 11)),
    (1, (3, 4), (1, 2, 4, 5, 6, 12)),
)


def both_kernel(
    names, count, sections, cores, depth,
    rows_hbm, up_hbm, lead_ref, numer_ref, denom_ref, power_ref, attend_gain, attend_bias, attend_mix, fading_ref, bonus_ref,
    feed_gain, feed_bias, feed_mix, entry_hbm, exit_hbm, key_hbm, content_hbm, gate_hbm,
    out_hbm, back_hbm, table_ref, entry_sum, exit_sum, key_sum, content_sum, gate_sum,
    normal_ref, std_ref, key_ref, value_ref, averaged_ref, state_ref, open_ref, hidden_ref, slope_ref, gate_ref, kv_ref,
    full_ref, edge_ref, rows_ref, tokens_ref, grad_ref, back_ref,
    entry_ref, exit_ref, w_key, w_content, w_gate,
    entry_grad, exit_grad, key_grad, content_grad, gate_grad,
    entry_core, exit_core, key_core, content_core, gate_core,
    entry_cross, exit_cross, key_cross, content_cross, gate_cross,
    entry_own, exit_own, key_own, content_own, gate_own,
    pay, stat, part, stage, land, mixed_ref, pre_grads, up_ref, work_ref, pair_ref, carry_ref, sum_ref,
    output_ref, hidden_grad, last_ref, later_ref, edges_ref, edge_land, small_ref,
    load_sems, token_sems, back_sems, fs, fr, os, orr, bs, br, gs, gr, ts, tr, ss, sr, es, er, ws, wr,
    table_send, table_recv,
):
    length, width = rows_ref.shape
    hidden_width = hidden_ref.shape[2]
    chunks = length // CHUNK
    passes = 2 * depth
    period = max(2 * count - 2, chunks + 1)
    here = Here(names)
    peers = Peers(here, count, width, 2 * passes)
    mine = peers.columns(peers.me)
    micro, core = here.at["section"], here.at["seq"]
    y, x = lax.div(micro, 2), lax.rem(micro, 2)
    neighbours = (
        here.device(seq=1 - core), here.device(section=micro + 1 - 2 * x), here.device(section=micro + 2 - 4 * y)
    )
    around = (core, y, x), neighbours
    first = from_tokens(rows_hbm, micro, tokens_ref, token_sems)
    second = from_tokens(up_hbm, micro, back_ref, back_sems)
    for copy in first + second:
        copy.start()
    weights = load(
        (
            (entry_hbm, entry_ref), (exit_hbm, exit_ref), (key_hbm, w_key), (content_hbm, w_content),
            (gate_hbm, w_gate),
        ),
        load_sems,
        0,
    )
    full_ref[...] = jnp.zeros_like(full_ref)
    for j in range(2 * depth):
        level = j // 2
        gain, bias, mix = (attend_gain, attend_bias, attend_mix) if j % 2 == 0 else (feed_gain, feed_bias, feed_mix)
        full_ref[j, 0:1, mine] = gain[level : level + 1, :]
        full_ref[j, 1:2, mine] = bias[level : level + 1, :]
        full_ref[j, 2:3, mine] = lead_ref[j, micro]
        for i in range(mix.shape[0] if j % 2 == 0 else mix.shape[1]):
            full_ref[j, 3 + i : 4 + i, mine] = mix[i, level : level + 1] if j % 2 == 0 else mix[level, i : i + 1]
    gather = Gather(peers, pay, (gs, gr))
    tiles = Tiles(peers, stat, (ts, tr))
    scatter = Scatter(peers, part, stage, land, (ss, sr))
    start_out, wait_out = to_sections(here, sections, rows_ref, tokens_ref, out_hbm, (os, orr))
    start_back, wait_back = to_sections(here, sections, grad_ref, back_ref, back_hbm, (bs, br))

    def full_copy(k, owner):
        block = full_ref.at[:, :, peers.columns(owner)]
        return peers.copy(peers.to(k), block, block, fs.at[k - 1], fr.at[k - 1])

    def sums(group, level):
        parts = (
            (key_grad, key_core, key_cross, key_own, key_sum),
            (content_grad, content_core, content_cross, content_own, content_sum),
            (gate_grad, gate_core, gate_cross, gate_own, gate_sum),
        )
        entry = (entry_grad, entry_core, entry_cross, entry_own, entry_sum)
        parts += (entry, (exit_grad, exit_core, exit_cross, exit_own, exit_sum))
        out = []
        for place in GROUPS[group][1]:
            grad, core_land, cross_land, own_land, result = parts[place]
            out.append(
                Summed(
                    around, grad, core_land, cross_land, own_land, result.at[level],
                    (ws.at[level, place], wr.at[level, place]),
                )
            )
        return out

    def sum_step(group, level, number):
        for matrix in sums(group, level):
            matrix.step(number)

    def table_place(k):
        return lax.rem(micro * cores + core + k, sections * cores)

    def table_copy(k, owner):
        other = table_place(k)
        return pltpu.make_async_remote_copy(
            src_ref=small_ref, dst_ref=table_ref.at[owner], send_sem=table_send.at[k - 1], recv_sem=table_recv.at[k - 1],
            device_id=here.device(section=lax.div(other, cores), seq=lax.rem(other, cores)), device_id_type=MESH,
        )

    others = [table_place(k) for k in range(1, sections * cores)]
    peers.greet([here.device(section=lax.div(other, cores), seq=lax.rem(other, cores)) for other in others])
    for k in range(1, count):
        full_copy(k, peers.me).start()
    for copy in first:
        copy.wait()
    to_stretches(tokens_ref, rows_ref)

    def begin_forward(j, c):
        rows = rows_of(c)

        @pl.when(j > 0)
        def _():
            value = scatter.total(c, j - 1)
            tiles.sent(c)

            @pl.when(odd(j, passes) == 1)
            def _():
                rows_ref[rows, :] += value

            @pl.when(odd(j, passes) == 0)
            def _():
                level = halves(j, passes) - 1
                kv_ref[level, rows, :] = value
                rows_ref[rows, :] += gate_ref[level, rows, :] * value

        @pl.when(j < 2 * depth)
        def _():
            lines = rows_ref[rows, :]
            middle = jnp.mean(lines, axis=1, keepdims=True)
            center = lines - middle
            square = jnp.sum(center * center, axis=1, keepdims=True)
            pay[odd(j, passes), rows, mine] = center.astype(jnp.bfloat16)
            tiles.stat[peers.me, c] = to_row_tile(middle, square)
            tiles.start(c)
            gather.start(c, j)

        @pl.when(j == 2 * depth)
        def _():
            start_out(c)

    def attend_forward(level, c):
        rows = rows_of(c)

        @pl.when(c == 0)
        def _():
            for i, start_ref in enumerate((numer_ref, denom_ref, power_ref)):
                carry_ref[i] = jnp.broadcast_to(start_ref[level, micro], (SUB, width))

        decay = jnp.broadcast_to(jnp.exp(fading_ref[pl.ds(level, 1), :]), (SUB, width))
        bonus = jnp.broadcast_to(bonus_ref[pl.ds(level, 1), :], (SUB, width))
        key_ref[level, rows, :] = product(mixed_ref[0, 0:CHUNK], entry_ref[level, 0])
        value_ref[level, rows, :] = product(mixed_ref[1, 0:CHUNK], entry_ref[level, 1])
        gate = jax.nn.sigmoid(product(mixed_ref[2, 0:CHUNK], entry_ref[level, 2]))
        open_ref[level, rows, :] = gate
        wkv_forward(
            pl.multiple_of(c * CHUNK, CHUNK), key_ref.at[level], value_ref.at[level], decay, bonus, carry_ref,
            averaged_ref.at[level], state_ref.at[level],
        )
        output = (gate * averaged_ref[level, rows, :]).astype(jnp.bfloat16)
        for target in range(count):
            block = peers.columns(target)
            part[rows, block] = product(output, exit_ref[level, :, block])

    def feed_forward(level, c):
        rows = rows_of(c)
        for start in range(0, hidden_ref.shape[2], width):
            block = slice(start, start + width)
            soft, slope = soft_plus(product(mixed_ref[0, 0:CHUNK], w_key[level, :, block]))
            hidden_ref[level, rows, block] = (soft * soft).astype(jnp.bfloat16)
            slope_ref[level, rows, block] = (2.0 * soft * slope).astype(jnp.bfloat16)
        for target in range(count):
            block = peers.columns(target)
            part[rows, block] = product(hidden_ref[level, rows, :], w_content[level, :, block])
        gate_ref[level, rows, :] = jax.nn.sigmoid(product(mixed_ref[1, 0:CHUNK], w_gate[level]))

    def forward(j, c):
        @pl.when((j == 0) & (c == 0))
        def _():
            for k in range(1, count):
                full_copy(k, peers.source(k)).wait_recv()
            for copy in weights:
                copy.wait()

        @pl.when(c == 0)
        def _():
            last_ref[0:1, :] = full_ref[j, 2:3, :]

        def mix(count_mixed):
            mix_chunk(
                peers, c, pay.at[odd(j, passes)], tiles, full_ref.at[j], mixed_ref.at[pl.ds(0, count_mixed), pl.ds(0, CHUNK)],
                normal_ref.at[j], edge_ref.at[j], std_ref.at[j], last_ref,
            )

        level = halves(j, passes)

        @pl.when(odd(j, passes) == 0)
        def _():
            mix(3)
            attend_forward(level, c)

        @pl.when(odd(j, passes) == 1)
        def _():
            mix(2)
            feed_forward(level, c)

        gather.sent(c, j)

    def edge_copies(j, source_of):
        return [
            peers.copy(
                peers.to(k), edges_ref.at[j, :, peers.columns(peers.to(k))], edge_land.at[j, source_of(k)],
                es.at[j, k - 1], er.at[j, k - 1],
            )
            for k in range(1, count)
        ]

    def end_pass(j, c):
        rows = rows_of(c)
        normed_grad = scatter.total(c, 2 * passes - 1 - j)
        tiles.arrived(c)
        totals = tiles.stat[0, c]
        for source in range(1, count):
            totals = totals + tiles.stat[source, c]
        columns = to_columns([totals])
        normal = normal_ref[j, rows, mine].astype(jnp.float32)
        scale = 1.0 / (count * width)
        grad_ref[rows, :] += std_ref[j, rows, 0:1] * (
            normed_grad * full_ref[j, 0:1, mine] - columns[:, 0:1] * scale - normal * (columns[:, 1:2] * scale)
        )
        small_ref[j, 0:1, :] += jnp.sum(normed_grad * normal, axis=0, keepdims=True)
        small_ref[j, 1:2, :] += jnp.sum(normed_grad, axis=0, keepdims=True)

        @pl.when(c == 0)
        def _():
            for copy in edge_copies(j, peers.source):
                copy.wait_recv()
            edges = edges_ref[j, :, mine]
            for k in range(1, count):
                edges = edges + edge_land[j, peers.source(k)]
            small_ref[j, 2:6, :] = edges[2:6]

    def begin_backward(which, c):
        rows = rows_of(c)
        j = passes - 1 - which

        @pl.when(which > 0)
        def _():
            end_pass(j + 1, c)
            gather.sent(c, passes + which - 1)
            tiles.sent(c)

        @pl.when((which < passes) & (odd(which, passes) == 0))
        def _():
            pay[odd(which, passes), rows, mine] = (grad_ref[rows, :] * gate_ref[halves(j, passes), rows, :]).astype(jnp.bfloat16)

        @pl.when((which < passes) & (odd(which, passes) == 1))
        def _():
            pay[odd(which, passes), rows, mine] = grad_ref[rows, :].astype(jnp.bfloat16)

        @pl.when(which < passes)
        def _():
            gather.start(c, passes + which)

        @pl.when(which == passes)
        def _():
            start_back(c)

    def attend_backward(j, c):
        level = halves(j, passes)
        rows = rows_of(c)
        decay = jnp.broadcast_to(jnp.exp(fading_ref[pl.ds(level, 1), :]), (SUB, width))
        bonus = jnp.broadcast_to(bonus_ref[pl.ds(level, 1), :], (SUB, width))

        @pl.when(c == chunks - 1)
        def _():
            sum_ref[...] = jnp.zeros_like(sum_ref)
            carry_ref[0] = jnp.zeros((SUB, width), jnp.float32)
            carry_ref[1] = jnp.zeros((SUB, width), jnp.float32)
            carry_ref[2] = jnp.full((SUB, width), NO_POWER, jnp.float32)

        output_grad = against(pay[1, rows, :], exit_ref[level])
        gate = open_ref[level, rows, :]
        up = output_grad * gate
        up_ref[...] = up
        averaged = averaged_ref[level, rows, :]
        pre_grads[2, rows, :] = (up * averaged * (1.0 - gate)).astype(jnp.bfloat16)
        output_ref[rows, :] = (gate * averaged).astype(jnp.bfloat16)
        wkv_backward(
            pl.multiple_of(c * CHUNK, CHUNK), key_ref.at[level], value_ref.at[level], decay, bonus,
            averaged_ref.at[level], state_ref.at[level],
            up_ref, carry_ref, sum_ref, work_ref, pair_ref,
        )
        pre_grads[0, rows, :] = pair_ref[0].astype(jnp.bfloat16)
        pre_grads[1, rows, :] = pair_ref[1].astype(jnp.bfloat16)
        mix_chunk_back(
            peers, c, 3, full_ref.at[j], normal_ref.at[j], edge_ref.at[j], mixed_ref,
            lambda i, columns: against(pre_grads[i, rows, :], entry_ref[level, i, columns, :]),
            later_ref, edges_ref.at[j], part, tiles,
        )

        @pl.when(c == 0)
        def _():
            numer, denom = carry_ref[0, SUB - 1 :, :], carry_ref[1, SUB - 1 :, :]
            lift = jnp.exp(power_ref[level, micro] + carry_ref[2, SUB - 1 :, :])
            out = passes + level
            small_ref[out, 0:1, :] = -decay[0:1] * jnp.sum(sum_ref[0], axis=0, keepdims=True)
            small_ref[out, 1:2, :] = jnp.sum(sum_ref[1], axis=0, keepdims=True)
            small_ref[out, 2:3, :] = lift * numer
            small_ref[out, 3:4, :] = lift * denom
            small_ref[out, 4:5, :] = lift * (numer_ref[level, micro] * numer + denom_ref[level, micro] * denom)

    def feed_backward(j, c):
        rows = rows_of(c)
        level = halves(j, passes)
        gate = gate_ref[level, rows, :]
        pre_grads[0, rows, :] = (grad_ref[rows, :] * gate * kv_ref[level, rows, :] * (1.0 - gate)).astype(jnp.bfloat16)
        for start in range(0, hidden_width, width):
            block = slice(start, start + width)
            into = against(pay[0, rows, :], w_content[level, block, :])
            hidden_grad[rows, block] = (into * slope_ref[level, rows, block].astype(jnp.float32)).astype(jnp.bfloat16)

        def mix_grad(i, columns):
            if i == 0:
                return against(hidden_grad[rows, :], w_key[level, columns, :])
            return against(pre_grads[0, rows, :], w_gate[level, columns, :])

        mix_chunk_back(
            peers, c, 2, full_ref.at[j], normal_ref.at[j], edge_ref.at[j], mixed_ref, mix_grad,
            later_ref, edges_ref.at[j], part, tiles,
        )

    def backward(which, c):
        j = passes - 1 - which

        @pl.when(c == chunks - 1)
        def _():
            later_ref[...] = jnp.zeros_like(later_ref)

        @pl.when(odd(which, passes) == 0)
        def _():
            feed_backward(j, c)

        @pl.when(odd(which, passes) == 1)
        def _():
            attend_backward(j, c)

        @pl.when(c == 0)
        def _():
            edges_ref[j, 2:3, :] = later_ref[0:1, :]
            for copy in edge_copies(j, lambda k: peers.me):
                copy.start()

    def weigh(place, level):
        if place == 4:
            for source in range(count):
                block = peers.columns(source)
                grad = inner_rows(output_ref[...], pay[1, :, block]).astype(jnp.bfloat16)
                exit_grad[..., block] = grad.reshape(*exit_grad.shape[:-1], width)
            return
        for i in range(4):
            at = i // 2, i % 2
            if place == 1:
                rows = hidden_width // 4
                grad = inner_rows(hidden_ref[level, :, i * rows : (i + 1) * rows], pay[0]).astype(jnp.bfloat16)
                content_grad[at] = grad.reshape(content_grad.shape[2:])
                continue
            rows = slice(i * (pay.shape[2] // 4), (i + 1) * (pay.shape[2] // 4))
            if place == 0:
                grad = inner_rows(mixed_ref[0, :, rows], hidden_grad[...]).astype(jnp.bfloat16)
                key_grad[at] = grad.reshape(key_grad.shape[2:])
            elif place == 2:
                grad = inner_rows(mixed_ref[1, :, rows], pre_grads[0]).astype(jnp.bfloat16)
                gate_grad[at] = grad.reshape(gate_grad.shape[2:])
            else:
                for k in range(3):
                    grad = inner_rows(mixed_ref[k, :, rows], pre_grads[k]).astype(jnp.bfloat16)
                    entry_grad[(k, *at)] = grad.reshape(entry_grad.shape[3:])

    base, final = chunks + count - 1, passes * period + chunks - 1

    def when_taken(group, number, t):
        kind, places, later = GROUPS[group]
        taken, chosen = False, 0
        for level in range(depth):
            now = t == base + period * kind + later[number] + 2 * period * (depth - 1 - level)
            taken, chosen = taken | now, chosen + jnp.where(now, level, 0)
        return taken, chosen

    def extra(t):
        for group in range(len(GROUPS)):
            for number in reversed(range(STEPS - 1)):
                taken, level = when_taken(group, number, t)

                @pl.when(taken)
                def _():
                    if number == 0:
                        @pl.when(level < depth - 1)
                        def _():
                            for matrix in sums(group, jnp.minimum(level + 1, depth - 1)):
                                matrix.sent_grad()

                        for place in GROUPS[group][1]:
                            weigh(place, jnp.clip(level, 0, depth - 1))
                    sum_step(group, jnp.clip(level, 0, depth - 1), number)

    forward_tick = ticks_of(peers, chunks, passes, 0, False, begin_forward, gather, forward, scatter)
    backward_tick = ticks_of(peers, chunks, passes, passes, True, begin_backward, gather, backward, scatter)
    turn = (passes - 1) * period + chunks + count - 1

    def onward(w, i):
        ends = i == period - 1
        return jnp.where(ends, w + 1, w), jnp.where(ends, 0, i + 1)

    def tick(t, places):
        ahead, behind = places

        @pl.when(t < passes * period + chunks)
        def _():
            forward_tick(*ahead)

        @pl.when(t == turn - 1)
        def _():
            for copy in second:
                copy.wait()
            to_stretches(back_ref, grad_ref)
            small_ref[...] = jnp.zeros_like(small_ref)
            edges_ref[...] = jnp.zeros_like(edges_ref)

        @pl.when(t >= turn)
        def _():
            backward_tick(*behind)
            extra(t - turn)

        moved = onward(*behind)
        return onward(*ahead), tuple(jnp.where(t >= turn, a, b) for a, b in zip(moved, behind))

    start = (jnp.int32(0), jnp.int32(0))
    lax.fori_loop(0, turn + final + 1, tick, (start, start))

    for k in range(1, sections * cores):
        table_copy(k, micro * cores + core).start()
    table_ref[micro * cores + core] = small_ref[...]
    left = []
    for group, (kind, places, later) in enumerate(GROUPS):
        for level in reversed(range(depth)):
            start = base + period * (kind + 2 * (depth - 1 - level))
            for number in range(STEPS):
                at = start + (later[number] if number < STEPS - 1 else later[-1] + 5)
                if at > final or number == STEPS - 1:
                    left.append((at, group, level, number))
    for at, group, level, number in sorted(left):
        sum_step(group, level, number)
    for c in range(chunks):
        scatter.sent(c, 2 * passes - 1)
    for j in range(passes):
        for copy in edge_copies(j, lambda k: peers.me):
            copy.wait_send()
    for group in range(len(GROUPS)):
        for level in range(depth):
            for matrix in sums(group, level):
                matrix.sent_rest()
                if level == 0:
                    matrix.sent_grad()
    for k in range(1, sections * cores):
        table_copy(k, micro * cores + core).wait_send()
        other = lax.rem(micro * cores + core + sections * cores - k, sections * cores)
        table_copy(k, other).wait_recv()
    for k in range(1, count):
        full_copy(k, peers.me).wait_send()
    wait_out()
    wait_back()


BF16, F32 = jnp.bfloat16, jnp.float32


def struct(*shape, dtype=F32):
    return jax.ShapeDtypeStruct(shape, dtype)


def run_kernel(body, collective, outs, scratch, operands, flops):
    def spec(inside):
        return pl.BlockSpec(memory_space=pltpu.VMEM if inside else pl.ANY)

    return pl.pallas_call(
        body,
        out_shape=[out for out, inside in outs],
        in_specs=[spec(inside) for operand, inside in operands],
        out_specs=[spec(inside) for out, inside in outs],
        scratch_shapes=scratch,
        compiler_params=pltpu.CompilerParams(
            collective_id=collective, has_side_effects=True, vmem_limit_bytes=63 * 1024 * 1024
        ),
        cost_estimate=pl.CostEstimate(flops=flops, bytes_accessed=2**25, transcendentals=2**23),
    )(*[operand for operand, inside in operands])


def pair_of(shape):
    return [pltpu.SemaphoreType.DMA(shape)] * 2


def run_fast(
    names, residual_entering, upstream_sensitivity, piece_lead_lines, dividend_start, divisor_start, power_offset_start,
    attend_standard_scale, attend_standard_offset, attend_lag_fractions, fading_log_rate, reward_first_word,
    attend_entry_matrix, attend_exit_matrix, feed_standard_scale, feed_standard_offset, feed_lag_fractions,
    feed_lookup_matrix, feed_content_matrix, feed_gate_matrix,
):
    count, sections, cores = (lax.axis_size(axis) for axis in ("tp", "section", "seq"))
    length, width = residual_entering.shape[2:]
    depth, features, hidden = feed_lookup_matrix.shape[0], count * width, feed_lookup_matrix.shape[2]
    chunks, subs = length // CHUNK, 2 * depth
    flops = 2 * depth * length * features * (4 * width + 2 * hidden + width)
    groups = width // LANES
    starts = (dividend_start, divisor_start, power_offset_start)
    weights = (attend_entry_matrix, attend_exit_matrix, feed_lookup_matrix, feed_content_matrix, feed_gate_matrix)
    shares = struct(sections, 1, CHUNK, width)
    lines = (depth, length, width)
    shapes = [weight.shape[1:] for weight in weights]

    def held(*shape, dtype=F32):
        return pltpu.VMEM(shape, dtype)

    def cut(*parts):
        return [(*shape[:-2], *parts, shape[-2] // 16, shape[-1]) for shape in shapes]

    outs = [(shares, False), (shares, False), (struct(sections * cores, subs + depth, SUB, width), True)]
    outs += [(struct(depth, *shape, dtype=BF16), False) for shape in cut(2, 2, 2, 2)]
    scratch = [held(subs, length, features, dtype=BF16), held(subs, length, LANES), held(*lines), held(*lines)]
    scratch += [held(*lines), held(depth, 3, *lines[1:]), held(*lines)]
    scratch += [held(depth, length, hidden, dtype=BF16)] * 2 + [held(*lines)] * 2
    scratch += [held(subs, SUB, features)] * 2 + [held(length, width), held(groups, length, LANES)] * 2
    scratch += [held(*weight.shape, dtype=BF16) for weight in weights]
    scratch += [
        held(*shape, dtype=BF16)
        for shape in cut(2, 2, 2, 2) + cut(2, 2, 2) + cut(2, 2, 2) + cut(2)
    ]
    scratch += [
        held(2, length, features, dtype=BF16), held(count, chunks, PAIR, LANES), held(length, features),
        held(length, features, dtype=BF16), held(2, length, features + width, dtype=BF16),
    ]
    scratch += [
        held(3, length, features, dtype=BF16), held(3, length, width, dtype=BF16), held(CHUNK, width),
        held(3, STEP, SUB, width), held(2, CHUNK, width), held(3, SUB, width), held(2, SUB, width),
        held(length, width, dtype=BF16), held(length, hidden, dtype=BF16), held(SUB, features), held(SUB, features),
        held(subs, SUB, features), held(subs, count, SUB, width), held(subs + depth, SUB, width),
    ]
    scratch += [pltpu.SemaphoreType.DMA((n,)) for n in (len(weights), groups, groups)] + pair_of((count - 1,))
    scratch += pair_of((sections, groups)) + pair_of((sections, groups))
    scratch += pair_of((2, 2, count - 1, chunks)) + pair_of((count - 1, chunks)) + pair_of((2, 2, count, chunks))
    scratch += pair_of((subs, count - 1)) + pair_of((depth, len(weights), COPIES))
    scratch += pair_of((sections * cores - 1,))
    operands = [(residual_entering, False), (upstream_sensitivity, False)]
    operands += [
        (value, True)
        for value in (
            piece_lead_lines, *starts, attend_standard_scale, attend_standard_offset,
            jnp.swapaxes(attend_lag_fractions, 0, 1),
            fading_log_rate, reward_first_word, feed_standard_scale, feed_standard_offset, feed_lag_fractions,
        )
    ]
    operands += [(value, False) for value in weights]
    out_share, back_share, table, *sums = run_kernel(
        partial(both_kernel, names, count, sections, cores, depth), 0, outs, scratch, operands, 3 * flops
    )
    return finish(cores, depth, out_share, back_share, table, sums, [weight.shape for weight in weights])


def finish_kernel(cores, depth, table_ref, *refs):
    wide, narrow = refs[:7], refs[7:14]
    prev, numer, denom, power = refs[14:18]
    attend_gain, attend_bias, attend_mix, decay, bonus, feed_gain, feed_bias, feed_mix = refs[18:]
    for source, target in zip(wide, narrow):
        target[...] = source[...].astype(jnp.float32)

    @pl.when(pl.program_id(0) == 0)
    def _():
        core = lax.axis_index("seq")
        places, subs = table_ref.shape[0], 2 * depth
        for m in range(places // cores):
            for j in range(subs):
                prev[j, m] = table_ref[m * cores + core, j, 2:3, :]
            for level in range(depth):
                for i, state in enumerate((numer, denom, power)):
                    state[level, m] = table_ref[m * cores + core, subs + level, 2 + i : 3 + i, :]
        for level in range(depth):
            for j, gain, bias, mix in (
                (2 * level, attend_gain, attend_bias, attend_mix), (2 * level + 1, feed_gain, feed_bias, feed_mix),
            ):
                total = sum(table_ref[place, j] for place in range(places))
                gain[level : level + 1, :] = total[0:1]
                bias[level : level + 1, :] = total[1:2]
                for i in range(mix.shape[0] if mix is attend_mix else mix.shape[1]):
                    place = (i, slice(level, level + 1)) if mix is attend_mix else (level, slice(i, i + 1))
                    mix[place] = total[3 + i : 4 + i]
            total = sum(table_ref[place, subs + level] for place in range(places))
            decay[level : level + 1, :] = total[0:1]
            bonus[level : level + 1, :] = total[1:2]


def finish(cores, depth, out_share, back_share, table, sums, shapes):
    steps = 4
    wide = [value.reshape(-1, value.shape[-1]) for value in (out_share, back_share, *sums)]
    blocks = [
        pl.BlockSpec((value.shape[0] // steps, value.shape[1]), lambda i: (i, 0)) for value in wide
    ]
    width = table.shape[-1]
    micros = table.shape[0] // cores
    small = [(2 * depth, micros, 1, width)] + [(depth, micros, 1, width)] * 3
    small += [(depth, width), (depth, width), (3, depth, width), (depth, width), (depth, width)]
    small += [(depth, width), (depth, width), (depth, 2, width)]

    def whole(shape):
        return pl.BlockSpec(shape, lambda i: (0,) * len(shape))

    got = pl.pallas_call(
        partial(finish_kernel, cores, depth),
        grid=(steps,),
        out_shape=[struct(*value.shape) for value in wide] + [struct(*shape) for shape in small],
        in_specs=[whole(table.shape)] + blocks,
        out_specs=blocks + [whole(shape) for shape in small],
        compiler_params=pltpu.CompilerParams(vmem_limit_bytes=60 * 1024 * 1024),
    )(table, *wide)
    shares = [value.reshape(whole.shape) for value, whole in zip(got, (out_share, back_share))]
    entry, leave, key, content, gate = [
        value.reshape(shape) for value, shape in zip(got[2:7], shapes)
    ]
    small = list(got[7:])
    small[6] = jnp.swapaxes(small[6], 0, 1)
    return (*shares, *small[:9], entry, leave, *small[9:], key, content, gate)


def run_plain(
    residual_entering,
    upstream_sensitivity,
    piece_lead_lines,
    dividend_start,
    divisor_start,
    power_offset_start,
    attend_standard_scale,
    attend_standard_offset,
    attend_lag_fractions,
    fading_log_rate,
    reward_first_word,
    attend_entry_matrix,
    attend_exit_matrix,
    feed_standard_scale,
    feed_standard_offset,
    feed_lag_fractions,
    feed_lookup_matrix,
    feed_content_matrix,
    feed_gate_matrix,
):
    sections = lax.axis_size("section")
    micro = lax.axis_index("section")
    length, share = residual_entering.shape[2:]
    depth = attend_entry_matrix.shape[0]

    def own(array):
        return lax.dynamic_index_in_dim(array, micro, 0, keepdims=False)

    blank = jnp.zeros((1, share), jnp.float32)
    lead = lax.dynamic_index_in_dim(piece_lead_lines[:, :, 0], micro, 1, keepdims=False)
    starts = [
        lax.dynamic_index_in_dim(start[:, :, 0], micro, 1, keepdims=False)
        for start in (dividend_start, divisor_start, power_offset_start)
    ]
    small_rows, wkv_rows = [], []
    for level in range(depth):
        for gain, bias, mix, j in (
            (attend_standard_scale, attend_standard_offset, attend_lag_fractions, 2 * level),
            (feed_standard_scale, feed_standard_offset, feed_lag_fractions, 2 * level + 1),
        ):
            rows = [gain[level][None], bias[level][None], lead[j][None], mix[level]]
            rows += [blank] * (5 - mix.shape[1])
            small_rows.append(jnp.concatenate(rows, axis=0))
        wkv_rows.append(
            jnp.stack(
                [fading_log_rate[level], reward_first_word[level]]
                + [start[level] for start in starts]
                + [blank[0]] * 3
            )
        )
    small_own = jnp.stack(small_rows)
    small_full = lax.all_gather(small_own, "tp", axis=2, tiled=True)

    rows = own(residual_entering)[0]
    kept = []
    for level in range(depth):
        for j in (2 * level, 2 * level + 1):
            if j % 2 == 0:
                rows, saved = time_forward_plain(
                    rows, small_full[j], small_own[j], wkv_rows[level],
                    attend_entry_matrix[level], attend_exit_matrix[level],
                )
            else:
                rows, saved = channel_forward_plain(
                    rows, small_full[j], small_own[j],
                    feed_lookup_matrix[level], feed_content_matrix[level], feed_gate_matrix[level],
                )
            kept.append(saved)

    def to_tokens(value):
        pieces = value.reshape(sections, length // sections, share)
        return lax.all_to_all(pieces, "section", 0, 0)[:, None]

    out_share = to_tokens(rows)
    grad = own(upstream_sensitivity)[0]
    small_grads, wkv_grads = [None] * (2 * depth), [None] * depth
    weight_grads = [None] * (2 * depth)
    summed = None
    for level in reversed(range(depth)):
        for j in (2 * level + 1, 2 * level):
            if j % 2 == 0:
                grad, small_grads[j], wkv_grads[level], weights = time_backward_plain(
                    grad, kept[j], small_full[j], small_own[j], wkv_rows[level],
                    attend_entry_matrix[level], attend_exit_matrix[level],
                )
            else:
                grad, small_grads[j], weights = channel_backward_plain(
                    grad, kept[j], small_full[j], small_own[j],
                    feed_lookup_matrix[level], feed_content_matrix[level], feed_gate_matrix[level],
                )
            weight_grads[j] = weights
        both = weight_grads[2 * level + 1], weight_grads[2 * level]
        if summed is not None:
            both, summed = lax.optimization_barrier((both, summed))
            weight_grads[2 * level + 3], weight_grads[2 * level + 2] = summed
        summed = lax.psum(both, ("section", "seq"))
    weight_grads[1], weight_grads[0] = summed
    back_share = to_tokens(grad)

    table = jnp.stack(small_grads + wkv_grads)
    tables = lax.all_gather(table, ("section", "seq"), axis=0)
    sums = [
        jnp.stack([weight_grads[2 * level + kind][place] for level in range(depth)])
        for kind, place in ((0, 0), (0, 1), (1, 0), (1, 1), (1, 2))
    ]
    return out_share, back_share, tables, sums


def per_device(names, *arrays):
    residual_entering, lookup = arrays[0], arrays[16]
    sections, cores = lax.axis_size("section"), lax.axis_size("seq")
    micros, unused, length, share = residual_entering.shape
    depth, features, hidden = lookup.shape
    fits = sections == 4 and cores == 2 and micros == sections and length == sections * CHUNK
    fits = fits and share % 256 == 0 and features % 256 == 0 and hidden % 256 == 0 and hidden % share == 0
    fits = fits and 2 < lax.axis_size("tp") <= LANES // SUB
    if fits:
        return run_fast(names, *arrays)
    out_share, back_share, table, sums = run_plain(*arrays)
    tables = table.reshape(sections, cores, *table.shape[1:])
    mine = lax.dynamic_index_in_dim(tables, lax.axis_index("seq"), 1, keepdims=False)
    total = jnp.sum(tables, axis=(0, 1))
    prev_grad = jnp.moveaxis(mine[:, : 2 * depth, 2], 0, 1)[:, :, None]
    state_grads = [jnp.moveaxis(mine[:, 2 * depth :, 2 + i], 0, 1)[:, :, None] for i in range(3)]

    weights = [grad.astype(jnp.float32) for grad in sums]
    return (
        out_share,
        back_share,
        prev_grad,
        *state_grads,
        total[0 : 2 * depth : 2, 0],
        total[0 : 2 * depth : 2, 1],
        total[0 : 2 * depth : 2, 3:6],
        total[2 * depth :, 0],
        total[2 * depth :, 1],
        weights[0],
        weights[1],
        total[1 : 2 * depth : 2, 0],
        total[1 : 2 * depth : 2, 1],
        total[1 : 2 * depth : 2, 3:5],
        weights[2],
        weights[3],
        weights[4],
    )


def solution(mesh):
    rows = P(None, "seq", None, "tp")
    line, mix = P(None, "tp"), P(None, None, "tp")
    columns, depths = P(None, None, "tp"), P(None, "tp", None)
    entry = P(None, None, None, "tp")
    state = P(None, None, "seq", "tp")
    tokens = P(None, "seq", "section", "tp")
    return jax.shard_map(
        partial(per_device, mesh.axis_names),
        mesh=mesh,
        in_specs=(
            rows, rows, state, state, state, state,
            line, line, mix, line, line, entry, depths,
            line, line, mix, columns, depths, columns,
        ),
        out_specs=(
            tokens, tokens, state, state, state, state,
            line, line, mix, line, line, entry, depths,
            line, line, mix, columns, depths, columns,
        ),
        check_vma=False,
    )
```

```python
from functools import partial

import jax
import jax.numpy as jnp
from jax import lax
from jax.experimental import pallas as pl
from jax.experimental.pallas import tpu as pltpu
from jax.sharding import PartitionSpec as P

BLOCK = 128


epsilon = 1e-05


def product(left_side, right_side):
    return jnp.dot(left_side, right_side, preferred_element_type=jnp.float32)


def inner_rows(left_side, right_side):
    return lax.dot_general(
        left_side, right_side, (((0,), (0,)), ((), ())), preferred_element_type=jnp.float32
    )


def against(left_side, right_side):
    return lax.dot_general(
        left_side, right_side, (((1,), (1,)), ((), ())), preferred_element_type=jnp.float32
    )


def weighted_value_blocks(
    block_length,
    incoming_lookups,
    incoming_contents,
    fading_entries,
    reward_entries,
    dividend_entries,
    divisor_entries,
    peak_line,
):
    decay_rate = jnp.exp(fading_entries)
    total_rows, channels = incoming_lookups.shape
    places = jnp.arange(block_length, dtype=jnp.float32)
    earlier = places[:, None] > places[None, :]
    spacing = places[:, None] - 1.0 - places[None, :]
    remain = block_length - 1.0 - places

    def advance(state_in, block_in):
        numer_in, denom_in, topmost = state_in
        lookup_piece_tile, value_block = block_in
        spread_exp = lookup_piece_tile[None, :, :] - spacing[:, :, None] * decay_rate
        spread_exp = jnp.where(earlier[:, :, None], spread_exp, -1e30)
        leading_power = reward_entries + lookup_piece_tile
        start_exp = topmost[None, :] - places[:, None] * decay_rate
        peak_exp = jnp.maximum(jnp.maximum(jnp.max(spread_exp, axis=1), leading_power), start_exp)
        weights = jnp.exp(spread_exp - peak_exp[:, None, :])
        from_state = jnp.exp(start_exp - peak_exp)
        own_term = jnp.exp(leading_power - peak_exp)
        numer_out = (
            from_state * numer_in
            + jnp.sum(weights * value_block[None, :, :], axis=1)
            + own_term * value_block
        )
        denom_out = from_state * denom_in + jnp.sum(weights, axis=1) + own_term
        ending = lookup_piece_tile - remain[:, None] * decay_rate
        stopping = topmost - block_length * decay_rate
        new_top = jnp.maximum(jnp.max(ending, axis=0), stopping)
        scaled = jnp.exp(ending - new_top[None, :])
        carried = jnp.exp(stopping - new_top)
        new_numer = carried * numer_in + jnp.sum(scaled * value_block, axis=0)
        new_denom = carried * denom_in + jnp.sum(scaled, axis=0)
        return ((new_numer, new_denom, new_top), numer_out / denom_out)

    blocks = total_rows // block_length
    unused, results = lax.scan(
        jax.checkpoint(advance),
        (dividend_entries, divisor_entries, peak_line),
        (
            incoming_lookups.reshape(blocks, block_length, channels),
            incoming_contents.reshape(blocks, block_length, channels),
        ),
    )
    return results.reshape(total_rows, channels)


def spread_plain(rows_in):
    features = rows_in.shape[1] * lax.axis_size("tp")
    mean_row = lax.psum(jnp.sum(rows_in, axis=1), "tp") / features
    center = rows_in - mean_row[:, None]
    inv_std = lax.rsqrt(lax.psum(jnp.sum(center * center, axis=1), "tp") / features + epsilon)
    normal_share = center * inv_std[:, None]
    normal_full = lax.all_gather(normal_share.astype(jnp.bfloat16), "tp", axis=1, tiled=True)
    return normal_share, inv_std, normal_full


def mix_plain(normal_full, small_full, mix_count):
    normed = normal_full.astype(jnp.float32) * small_full[0] + small_full[1]
    shifted = jnp.concatenate([small_full[2:3], normed[:-1]], axis=0)
    gap = normed - shifted
    mixed = [(shifted + gap * small_full[3 + i]).astype(jnp.bfloat16) for i in range(mix_count)]
    return mixed, gap


def scatter_plain(branch):
    return lax.psum_scatter(
        branch.astype(jnp.bfloat16), "tp", scatter_dimension=1, tiled=True
    ).astype(jnp.float32)


def time_forward_plain(rows_in, small_full, small_own, wkv_rows, entry_matrix, exit_matrix):
    normal_share, inv_std, normal_full = spread_plain(rows_in)
    mixed, gap = mix_plain(normal_full, small_full, 3)
    lookups, contents, recept = [product(mixed[i], entry_matrix[i]) for i in range(3)]
    averaged, pullback = jax.vjp(
        partial(weighted_value_blocks, BLOCK), lookups, contents, *[wkv_rows[i] for i in range(5)]
    )
    gate = jax.nn.sigmoid(recept)
    output = (gate * averaged).astype(jnp.bfloat16)
    rows_out = rows_in + scatter_plain(product(output, exit_matrix))
    kept = (normal_share, inv_std, normal_full, mixed, gap, averaged, pullback, gate, output)
    return rows_out, kept


def channel_forward_plain(rows_in, small_full, small_own, w_key, w_value, w_gate):
    normal_share, inv_std, normal_full = spread_plain(rows_in)
    mixed, gap = mix_plain(normal_full, small_full, 2)
    hidden_pre = product(mixed[0], w_key)
    soft = jax.nn.softplus(hidden_pre)
    hidden = jnp.square(soft).astype(jnp.bfloat16)
    gate = jax.nn.sigmoid(product(mixed[1], w_gate))
    kv_share = scatter_plain(product(hidden, w_value))
    kept = (normal_share, inv_std, normal_full, mixed, gap, hidden_pre, soft, hidden, gate, kv_share)
    return rows_in + gate * kv_share, kept


def norm_back_plain(rows_grad, mix_grads, gap, normal_full, normal_share, inv_std, small_full, small_own):
    share = normal_share.shape[1]
    features = small_full.shape[1]
    to_normed = sum(grad * small_full[3 + i] for i, grad in enumerate(mix_grads))
    to_shifted = sum(grad * (1.0 - small_full[3 + i]) for i, grad in enumerate(mix_grads))
    ratio_grads = [jnp.sum(grad * gap, axis=0) for grad in mix_grads]
    ratio_grads += [jnp.zeros_like(ratio_grads[0])] * (3 - len(mix_grads))
    to_normed = to_normed + jnp.concatenate([to_shifted[1:], jnp.zeros_like(to_shifted[:1])], axis=0)
    normed_grad = scatter_plain(to_normed)
    edge = lax.psum_scatter(
        jnp.stack([to_shifted[0]] + ratio_grads), "tp", scatter_dimension=1, tiled=True
    )
    scaled = normed_grad * small_own[0]
    first, second = lax.psum((jnp.sum(scaled, axis=1), jnp.sum(scaled * normal_share, axis=1)), "tp")
    rows_back = rows_grad + inv_std[:, None] * (
        scaled - first[:, None] / features - normal_share * (second[:, None] / features)
    )
    gain_grad = jnp.sum(normed_grad * normal_share, axis=0)
    bias_grad = jnp.sum(normed_grad, axis=0)
    zero = jnp.zeros((2, share), jnp.float32)
    return rows_back, jnp.concatenate([gain_grad[None], bias_grad[None], edge, zero], axis=0)


def time_backward_plain(rows_grad, kept, small_full, small_own, wkv_rows, entry_matrix, exit_matrix):
    normal_share, inv_std, normal_full, mixed, gap, averaged, pullback, gate, output = kept
    branch_grad = lax.all_gather(rows_grad.astype(jnp.bfloat16), "tp", axis=1, tiled=True)
    exit_grad = inner_rows(output, branch_grad)
    output_grad = against(branch_grad, exit_matrix)
    state_grads = pullback(output_grad * gate)
    pre_grads = [
        state_grads[0].astype(jnp.bfloat16),
        state_grads[1].astype(jnp.bfloat16),
        (output_grad * averaged * gate * (1.0 - gate)).astype(jnp.bfloat16),
    ]
    entry_grad = jnp.stack([inner_rows(mixed[i], pre_grads[i]) for i in range(3)])
    mix_grads = [against(pre_grads[i], entry_matrix[i]) for i in range(3)]
    rows_back, small_grad = norm_back_plain(
        rows_grad, mix_grads, gap, normal_full, normal_share, inv_std, small_full, small_own
    )
    wkv_grad = jnp.concatenate([jnp.stack(state_grads[2:]), jnp.zeros((3, gate.shape[1]))], axis=0)
    return rows_back, small_grad, wkv_grad, (entry_grad.astype(jnp.bfloat16), exit_grad.astype(jnp.bfloat16))


def channel_backward_plain(rows_grad, kept, small_full, small_own, w_key, w_value, w_gate):
    normal_share, inv_std, normal_full, mixed, gap, hidden_pre, soft, hidden, gate, kv_share = kept
    branch_grad = lax.all_gather((rows_grad * gate).astype(jnp.bfloat16), "tp", axis=1, tiled=True)
    value_grad = inner_rows(hidden, branch_grad)
    hidden_grad = (
        against(branch_grad, w_value) * 2.0 * soft * jax.nn.sigmoid(hidden_pre)
    ).astype(jnp.bfloat16)
    gate_grad = (rows_grad * kv_share * gate * (1.0 - gate)).astype(jnp.bfloat16)
    key_grad = inner_rows(mixed[0], hidden_grad)
    recept_grad = inner_rows(mixed[1], gate_grad)
    mix_grads = [against(hidden_grad, w_key), against(gate_grad, w_gate)]
    rows_back, small_grad = norm_back_plain(
        rows_grad, mix_grads, gap, normal_full, normal_share, inv_std, small_full, small_own
    )
    grads = tuple(grad.astype(jnp.bfloat16) for grad in (key_grad, value_grad, recept_grad))
    return rows_back, small_grad, grads


CHUNK = 128
LANES = 128
SUB = 8
PAIR = 2
MESH = pl.DeviceIdType.MESH
NO_POWER = -1e30


def to_row_tile(*columns):
    lane = lax.broadcasted_iota(jnp.int32, (CHUNK, LANES), 1)
    wide = jnp.zeros((CHUNK, LANES), jnp.float32)
    for place, column in enumerate(columns):
        wide = jnp.where(lane == place, column, wide)
    return jnp.transpose(wide)[:PAIR]


def to_columns(tiles):
    count = len(tiles)
    filler = [jnp.zeros((LANES - PAIR * count, CHUNK), jnp.float32)]
    return jnp.transpose(jnp.concatenate(list(tiles) + filler, axis=0))


STEP = CHUNK // SUB


def shift_rows(value, first_row):
    ends = pltpu.roll(value[CHUNK - SUB :], 1, 0)
    at = lax.broadcasted_iota(jnp.int32, ends.shape, 0)
    return jnp.concatenate([jnp.where(at == 0, first_row, ends), value[: CHUNK - SUB]], axis=0)


def unshift_rows(value, last_row):
    starts = pltpu.roll(value[:SUB], SUB - 1, 0)
    at = lax.broadcasted_iota(jnp.int32, starts.shape, 0)
    return jnp.concatenate([value[SUB:], jnp.where(at == SUB - 1, last_row, starts)], axis=0)


def to_stretches(tokens_ref, rows_ref):
    def step(c, unused):
        base = pl.multiple_of(c * CHUNK, CHUNK)
        for s in range(STEP):
            for g in range(tokens_ref.shape[0]):
                rows_ref[pl.ds(base + s * SUB, SUB), g * LANES : (g + 1) * LANES] = tokens_ref[
                    g, pl.ds(base + s, SUB, stride=STEP), :
                ]
        return unused

    lax.fori_loop(0, rows_ref.shape[0] // CHUNK, step, 0)


def to_tokens(rows_ref, tokens_ref, c):
    base = pl.multiple_of(c * CHUNK, CHUNK)
    for s in range(STEP):
        for g in range(tokens_ref.shape[0]):
            tokens_ref[g, pl.ds(base + s, SUB, stride=STEP), :] = rows_ref[
                pl.ds(base + s * SUB, SUB), g * LANES : (g + 1) * LANES
            ]


def halves(value, most):
    if isinstance(value, int):
        return value // 2
    return sum(jnp.where(value >= 2 * k, 1, 0) for k in range(1, most // 2 + 1))


def odd(value, most):
    return value - 2 * halves(value, most)


class Here:
    def __init__(self, names):
        self.names, self.at = names, {name: lax.axis_index(name) for name in names}

    def device(self, **other):
        return tuple(other.get(name, self.at[name]) for name in self.names)


class Peers:
    def __init__(self, here, count, width, passes):
        self.here, self.count, self.width, self.passes = here, count, width, passes
        self.me = here.at["tp"]
        self.others = [lax.rem(self.me + k, count) for k in range(count)]
        self.sources = [lax.rem(self.me + count - k, count) for k in range(count)]
        self.beside = jnp.minimum(self.me + 1, count - 1), jnp.maximum(self.me - 1, 0)

    def to(self, k):
        return self.others[k]

    def source(self, k):
        return self.sources[k]

    def slot(self, which):
        return odd(which, self.passes)

    def columns(self, owner):
        if isinstance(owner, int):
            return slice(owner * self.width, (owner + 1) * self.width)
        return pl.ds(pl.multiple_of(owner * self.width, LANES), self.width)

    def greet(self, others):
        barrier = pltpu.get_barrier_semaphore()
        places = [self.here.device(tp=self.to(k)) for k in range(1, self.count)] + others
        for place in places:
            pl.semaphore_signal(barrier, inc=1, device_id=place, device_id_type=MESH)
        pl.semaphore_wait(barrier, len(places))

    def copy(self, device, source_ref, target_ref, send, receive):
        return pltpu.make_async_remote_copy(
            src_ref=source_ref, dst_ref=target_ref, send_sem=send, recv_sem=receive,
            device_id=self.here.device(tp=device), device_id_type=MESH,
        )


def rows_of(c):
    return pl.ds(pl.multiple_of(c * CHUNK, CHUNK), CHUNK)


class Tiles:
    def __init__(self, peers, stat, sems):
        self.peers, self.stat, self.sems = peers, stat, sems

    def copy(self, k, c, owner):
        tile = self.stat.at[owner, c]
        return self.peers.copy(
            self.peers.to(k), tile, tile, self.sems[0].at[k - 1, c], self.sems[1].at[k - 1, c]
        )

    def start(self, c):
        for k in range(1, self.peers.count):
            self.copy(k, c, self.peers.me).start()

    def arrived(self, c):
        for k in range(1, self.peers.count):
            self.copy(k, c, self.peers.source(k)).wait_recv()

    def sent(self, c):
        for k in range(1, self.peers.count):
            self.copy(k, c, self.peers.me).wait_send()


class Gather:
    def __init__(self, peers, pay, sems):
        self.peers, self.pay, self.sems = peers, pay, sems

    def copy(self, way, hop, c, owner, which):
        slot = self.peers.slot(which)
        block = self.pay.at[slot, rows_of(c), self.peers.columns(owner)]
        device = self.peers.beside[way]
        return self.peers.copy(
            device, block, block, self.sems[0].at[slot, way, hop - 1, c], self.sems[1].at[slot, way, hop - 1, c]
        )

    def onward(self, way):
        return self.peers.me < self.peers.count - 1 if way == 0 else self.peers.me > 0

    def owner(self, way, hop):
        return self.peers.me - hop if way == 0 else self.peers.me + hop

    def comes(self, way, hop):
        owner = self.owner(way, hop)
        return owner >= 0 if way == 0 else owner < self.peers.count

    def start(self, c, which):
        for way in (0, 1):
            @pl.when(self.onward(way))
            def _():
                self.copy(way, 1, c, self.peers.me, which).start()

    def relay(self, hop, c, which):
        for way in (0, 1):
            @pl.when(self.comes(way, hop))
            def _():
                self.copy(way, hop, c, self.owner(way, hop), which).wait_recv()
                if hop < self.peers.count - 1:
                    @pl.when(self.onward(way))
                    def _():
                        self.copy(way, hop + 1, c, self.owner(way, hop), which).start()

    def sent(self, c, which):
        for way in (0, 1):
            for hop in range(1, self.peers.count):
                @pl.when(self.comes(way, hop - 1) & self.onward(way))
                def _():
                    self.copy(way, hop, c, self.owner(way, hop - 1), which).wait_send()


class Scatter:
    def __init__(self, peers, part, stage, land, sems):
        self.peers, self.part, self.stage, self.land, self.sems = peers, part, stage, land, sems

    def landing(self, way, target, owner):
        if way == 0:
            return self.peers.columns(target)
        return self.peers.columns(jnp.where(target == owner, self.peers.count, target))

    def copy(self, way, c, target, which):
        slot, device = self.peers.slot(which), self.peers.beside[way]
        return self.peers.copy(
            device, self.stage.at[rows_of(c), self.peers.columns(target)],
            self.land.at[slot, rows_of(c), self.landing(way, target, device)],
            self.sems[0].at[slot, way, target, c], self.sems[1].at[slot, way, target, c],
        )

    def come(self, way, c, target, which):
        slot, columns = self.peers.slot(which), self.landing(way, target, self.peers.me)
        block = self.land.at[slot, rows_of(c), columns]
        self.peers.copy(
            self.peers.me, block, block, self.sems[0].at[slot, way, target, c], self.sems[1].at[slot, way, target, c]
        ).wait_recv()
        return self.land[slot, rows_of(c), columns].astype(jnp.float32)

    def inward(self, way):
        return self.peers.me > 0 if way == 0 else self.peers.me < self.peers.count - 1

    def passes(self, way, target):
        return self.peers.me < target if way == 0 else self.peers.me > target

    def lag(self, way):
        return self.peers.me if way == 0 else self.peers.count - 1 - self.peers.me

    def push(self, way, c, which):
        rows = rows_of(c)
        targets = range(self.peers.count - 1, 0, -1) if way == 0 else range(self.peers.count - 1)
        for target in targets:
            columns = self.peers.columns(target)

            @pl.when(self.passes(way, target))
            def _():
                @pl.when(which > 0)
                def _():
                    self.copy(way, c, target, which - 1).wait_send()

                @pl.when(self.inward(way))
                def _():
                    self.stage[rows, columns] = (
                        self.part[rows, columns] + self.come(way, c, target, which)
                    ).astype(jnp.bfloat16)

                @pl.when(jnp.logical_not(self.inward(way)))
                def _():
                    self.stage[rows, columns] = self.part[rows, columns].astype(jnp.bfloat16)

                self.copy(way, c, target, which).start()

    def total(self, c, which):
        rows, mine = rows_of(c), self.peers.columns(self.peers.me)
        for way in (0, 1):
            @pl.when(self.inward(way))
            def _():
                self.part[rows, mine] += self.come(way, c, self.peers.me, which)
        return self.part[rows, mine]

    def sent(self, c, which):
        for target in range(self.peers.count):
            for way in (0, 1):
                @pl.when(self.passes(way, target))
                def _():
                    self.copy(way, c, target, which).wait_send()


def ticks_of(peers, chunks, passes, before, backward, begin, gather, compute, scatter):
    count = peers.count
    period = max(2 * count - 2, chunks + 1)

    def split(w, i, behind):
        early = i >= behind
        which, at = jnp.where(early, w, w - 1), jnp.where(early, i - behind, i - behind + period)
        chunk = chunks - 1 - at if backward else at
        return which, jnp.clip(chunk, 0, chunks - 1), (which >= 0) & (which < passes) & (at < chunks)

    def tick(w, i):
        which, c, there = split(w, i, 0)
        last = (w == passes) & (i < chunks)

        @pl.when(there | last)
        def _():
            begin(which, c)

        def relay(hop):
            moved, c_hop, there = split(w, i, hop)

            @pl.when(there)
            def _():
                gather.relay(hop, c_hop, moved + before)

        def push(middle):
            for way in (0, 1):
                lag = scatter.lag(way)
                moved, c_way, there = split(w, i, count - 1 + lag)

                @pl.when(there & ((lag == 1) == middle))
                def _():
                    scatter.push(way, c_way, moved + before)

        relay(count - 1)
        which, c, there = split(w, i, count - 1)

        @pl.when(there)
        def _():
            compute(which, c)

        push(False)
        for hop in range(1, count - 1):
            relay(hop)
        push(True)
    return tick


def mix_chunk(peers, c, pay, tiles, full_ref, mixed_ref, normal_ref, edge_ref, std_ref, last_ref):
    count, width = peers.count, peers.width
    tiles.arrived(c)
    columns = to_columns([tiles.stat[source, c] for source in range(count)])
    middles = [columns[:, PAIR * source : PAIR * source + 1] for source in range(count)]
    center = sum(middles) / count
    square = sum(columns[:, PAIR * source + 1 : PAIR * source + 2] for source in range(count))
    square = square + width * sum((middle - center) * (middle - center) for middle in middles)
    inv_std = lax.rsqrt(square / (count * width) + epsilon)
    std_ref[rows_of(c), :] = jnp.broadcast_to(inv_std, (CHUNK, LANES))
    for source in range(count):
        part = slice(source * width, (source + 1) * width)
        normal = (
            pay[rows_of(c), part].astype(jnp.float32) + (middles[source] - center)
        ) * inv_std
        normal_ref[rows_of(c), part] = normal.astype(jnp.bfloat16)
        normed = normal * full_ref[0:1, part] + full_ref[1:2, part]
        before = last_ref[0:1, part]
        edge_ref[pl.ds(c, 1), part] = before
        shifted = shift_rows(normed, before)
        last_ref[0:1, part] = normed[CHUNK - 1 : CHUNK]
        gap = normed - shifted
        for i in range(mixed_ref.shape[0]):
            mixed_ref[i, :, part] = (shifted + gap * full_ref[3 + i : 4 + i, part]).astype(
                jnp.bfloat16
            )


def wkv_join(left, right, fall):
    fallen = left[2] - fall
    peak = jnp.maximum(fallen, right[2])
    old, new = jnp.exp(fallen - peak), jnp.exp(right[2] - peak)
    return old * left[0] + new * right[0], old * left[1] + new * right[1], peak


def choose(mask, first, second):
    return tuple(jnp.where(mask, a, b) for a, b in zip(first, second))


def wkv_forward(base, key_ref, value_ref, decay, bonus, carry_ref, out_ref, state_ref):
    steps = STEP

    def at(s):
        return pl.ds(base + s * SUB, SUB)

    state = (value_ref[at(0), :], jnp.ones_like(decay), key_ref[at(0), :])
    for s in range(1, steps):
        key = key_ref[at(s), :]
        state = wkv_join(state, (value_ref[at(s), :], 1.0, key), decay)
    place = lax.broadcasted_iota(jnp.int32, decay.shape, 0)
    carry = tuple(carry_ref[i] for i in range(3))
    state = choose(place == 0, wkv_join(carry, state, steps * decay), state)
    for reach in (1, 2, 4):
        left = tuple(pltpu.roll(part, reach, 0) for part in state)
        state = choose(place >= reach, wkv_join(left, state, reach * steps * decay), state)
    after = tuple(pltpu.roll(part, 1, 0) for part in state)
    for i in range(3):
        carry_ref[i] = after[i]
    numer, denom, power = choose(place == 0, carry, after)
    for s in range(steps):
        key, value = key_ref[at(s), :], value_ref[at(s), :]
        lead = bonus + key
        peak = jnp.maximum(power, lead)
        old, new = jnp.exp(power - peak), jnp.exp(lead - peak)
        out_ref[at(s), :] = (old * numer + new * value) / (old * denom + new)
        state_ref[0, at(s), :] = numer
        state_ref[1, at(s), :] = denom
        state_ref[2, at(s), :] = power
        numer, denom, power = wkv_join((numer, denom, power), (value, 1.0, key), decay)


def wkv_backward(
    base, key_ref, value_ref, decay, bonus, out_ref, state_ref, up_ref, carry_ref, sum_ref, work_ref, grad_ref
):
    steps = STEP

    def at(s):
        return pl.ds(base + s * SUB, SUB)

    state = None
    for s in reversed(range(steps)):
        lead = bonus + key_ref[at(s), :]
        power = state_ref[2, at(s), :]
        peak = jnp.maximum(power, lead)
        new = jnp.exp(lead - peak)
        share = up_ref[s * SUB : (s + 1) * SUB, :] / (
            jnp.exp(power - peak) * state_ref[1, at(s), :] + new
        )
        work_ref[0, s], work_ref[1, s], work_ref[2, s] = share, peak, new * share
        here = (share, -share * out_ref[at(s), :], -peak)
        state = here if state is None else wkv_join(state, here, decay)
    place = lax.broadcasted_iota(jnp.int32, decay.shape, 0)
    carry = tuple(carry_ref[i] for i in range(3))
    state = choose(place == SUB - 1, wkv_join(carry, state, steps * decay), state)
    for reach in (1, 2, 4):
        later = tuple(pltpu.roll(part, SUB - reach, 0) for part in state)
        state = choose(place < SUB - reach, wkv_join(later, state, reach * steps * decay), state)
    after = tuple(pltpu.roll(part, SUB - 1, 0) for part in state)
    for i in range(3):
        carry_ref[i] = after[i]
    numer, denom, power = choose(place == SUB - 1, carry, after)
    for s in reversed(range(steps)):
        key, value, out = key_ref[at(s), :], value_ref[at(s), :], out_ref[at(s), :]
        share, peak, own = work_ref[0, s], work_ref[1, s], work_ref[2, s]
        reach = jnp.exp(key + power)
        direct = own * (value - out)
        grad_ref[0, s * SUB : (s + 1) * SUB, :] = direct + reach * (value * numer + denom)
        grad_ref[1, s * SUB : (s + 1) * SUB, :] = own + reach * numer
        sum_ref[1] += direct
        sum_ref[0] += jnp.exp(state_ref[2, at(s), :] + power - decay) * (
            state_ref[0, at(s), :] * numer + state_ref[1, at(s), :] * denom
        )
        numer, denom, power = wkv_join(
            (numer, denom, power), (share, -share * out, -peak), decay
        )


def load(pairs, sems, start):
    copies = [
        pltpu.make_async_copy(source, target, sems.at[start + i]) for i, (source, target) in enumerate(pairs)
    ]
    for copy in copies:
        copy.start()
    return copies


def soft_plus(value):
    small = jnp.exp(-jnp.abs(value))
    share = 1.0 / (1.0 + small)
    rest = jnp.where(small < 1e-3, small - 0.5 * small * small, jnp.log(1.0 + small))
    return jnp.maximum(value, 0.0) + rest, jnp.where(value >= 0.0, share, small * share)


def from_tokens(tokens_hbm, micro, tokens_ref, sems):
    return [
        pltpu.make_async_copy(tokens_hbm.at[micro, 0, :, pl.ds(g * LANES, LANES)], tokens_ref.at[g], sems.at[g])
        for g in range(tokens_ref.shape[0])
    ]


def to_sections(here, sections, rows_ref, tokens_ref, out_hbm, sems):
    send, receive = sems
    micro = here.at["section"]
    groups = range(tokens_ref.shape[0])

    def ends(c, source, g):
        return tokens_ref.at[g, rows_of(c)], out_hbm.at[source, 0, :, pl.ds(g * LANES, LANES)]

    def copy(c, source, g):
        held, target = ends(c, source, g)
        return pltpu.make_async_remote_copy(
            src_ref=held, dst_ref=target, send_sem=send.at[c, g], recv_sem=receive.at[source, g],
            device_id=here.device(section=c), device_id_type=MESH,
        )

    def own(g):
        return pltpu.make_async_copy(*ends(micro, micro, g), send.at[micro, g])

    def start(c):
        to_tokens(rows_ref, tokens_ref, c)

        @pl.when(c == micro)
        def _():
            for g in groups:
                own(g).start()

        @pl.when(c != micro)
        def _():
            for g in groups:
                copy(c, micro, g).start()

    def wait():
        for g in groups:
            for k in range(1, sections):
                other = lax.rem(micro + k, sections)
                copy(other, micro, g).wait_send()
                copy(other, other, g).wait_recv()
            own(g).wait()

    return start, wait


def mix_chunk_back(
    peers, c, ratios, full_ref, normal_ref, edge_ref, mixed_ref, mix_grad, later_ref, edges_ref, part_ref, tiles
):
    count = peers.count
    rows = rows_of(c)
    first = second = 0.0
    for source in range(count):
        part = peers.columns(source)
        normal = normal_ref[rows, part].astype(jnp.float32)
        gain = full_ref[0:1, part]
        normed = normal * gain + full_ref[1:2, part]
        before = shift_rows(normed, edge_ref[pl.ds(c, 1), part])
        gap = normed - before
        direct = shifted = 0.0
        for i in range(ratios):
            grad = mix_grad(i, part)
            ratio = full_ref[3 + i : 4 + i, part]
            mixed_ref[i, rows, part] = (before + gap * ratio).astype(jnp.bfloat16)
            taken = grad * ratio
            direct = direct + taken
            shifted = shifted + (grad - taken)
            edges_ref[3 + i : 4 + i, part] += jnp.sum(grad * gap, axis=0, keepdims=True)
        value = direct + unshift_rows(shifted, later_ref[0:1, part])
        later_ref[0:1, part] = shifted[0:1]
        part_ref[rows, part] = value
        scaled = value * gain
        first = first + jnp.sum(scaled, axis=1, keepdims=True)
        second = second + jnp.sum(scaled * normal, axis=1, keepdims=True)
    tiles.stat[peers.me, c] = to_row_tile(first, second)
    tiles.start(c)


STEPS = 7
COPIES = 15
EVERY = slice(None)


class Summed:
    def __init__(self, around, grad, core_land, cross_land, own_land, result, sems):
        self.grad, self.core_land, self.cross_land, self.own_land = grad, core_land, cross_land, own_land
        self.result, self.sems = result, sems
        self.lead = (EVERY,) * (len(grad.shape) - 6)
        (self.q, self.y, self.x), (self.sibling, self.over_x, self.over_y) = around

    def at(self, ref, *place):
        return ref.at[(*self.lead, *place)]

    def send(self, which, source, target, place):
        return pltpu.make_async_remote_copy(
            src_ref=source, dst_ref=target, send_sem=self.sems[0].at[which], recv_sem=self.sems[1].at[which],
            device_id=place, device_id_type=MESH,
        )

    def share(self, which, held, device, *place):
        return self.send(which, self.at(held, *place), self.at(self.result, *place), device)

    def arrive(self, which, ref, *place):
        view = self.at(ref, *place)
        self.send(which, view, view, self.sibling).wait_recv()

    def add(self, place, land, land_place):
        mine, come = self.at(self.grad, *place), self.at(land, *land_place)
        rows = mine.shape[-2]
        block = min(rows, 32)
        for k in range(3 if self.lead else 1):
            for start in range(0, rows, block):
                view = (*((k,) if self.lead else ()), slice(start, start + block), EVERY)
                mine[view] = (mine[view].astype(jnp.float32) + come[view].astype(jnp.float32)).astype(jnp.bfloat16)

    def add_half(self):
        def step(i, unused):
            y, rest = halves(halves(i, 7), 3), i - 4 * halves(halves(i, 7), 3)
            place = y, halves(rest, 3), odd(rest, 3)
            self.add((self.q, *place), self.core_land, place)
            return unused

        lax.fori_loop(0, 8, step, 0)

    def to_core(self):
        return [self.send(0, self.at(self.grad, 1 - self.q), self.core_land, self.sibling)]

    def cross(self):
        first, second = (EVERY, 1 - self.x, 0), (1 - self.y, EVERY, 1)
        return [
            self.send(1, self.at(self.grad, self.q, *first), self.at(self.cross_land, *first), self.over_x),
            self.send(2, self.at(self.grad, self.q, *second), self.at(self.cross_land, *second), self.over_y),
        ]

    def own(self):
        q, y, x = self.q, self.y, self.x
        return [
            self.send(3, self.at(self.grad, q, 1 - y, x, 0), self.at(self.own_land, 0), self.over_y),
            self.send(4, self.at(self.grad, q, y, 1 - x, 1), self.at(self.own_land, 1), self.over_x),
        ]

    def back_own(self):
        q, y, x = self.q, self.y, self.x
        return [
            self.share(5, self.grad, self.over_y, q, y, x, 0), self.share(6, self.grad, self.over_x, q, y, x, 1),
            self.share(7, self.grad, self.sibling, q, y, x),
        ]

    def back_cross(self):
        q, y, x = self.q, self.y, self.x
        return [
            self.share(8, self.result, self.over_x, q, EVERY, x, 0), self.share(9, self.result, self.over_y, q, y, EVERY, 1),
            self.share(10, self.result, self.sibling, q, 1 - y, x, 0),
            self.share(11, self.result, self.sibling, q, y, 1 - x, 1),
        ]

    def back_core(self):
        q, y, x = self.q, self.y, self.x
        return [
            self.share(12, self.result, self.sibling, q, EVERY, 1 - x, 0),
            self.share(13, self.result, self.sibling, q, 1 - y, EVERY, 1),
        ]

    def keep(self):
        place = self.q, self.y, self.x
        return pltpu.make_async_copy(self.at(self.grad, *place), self.at(self.result, *place), self.sems[0].at[14])

    def step(self, number):
        q, y, x = self.q, self.y, self.x
        started = []
        if number == 0:
            started = self.to_core()
        elif number == 1:
            self.arrive(0, self.core_land)
            self.add_half()
            started = self.cross()
        elif number == 2:
            self.arrive(1, self.cross_land, EVERY, x, 0)
            self.arrive(2, self.cross_land, y, EVERY, 1)
            for k in (0, 1):
                self.add((q, k, x, 0), self.cross_land, (k, x, 0))
                self.add((q, y, k, 1), self.cross_land, (y, k, 1))
            started = self.own()
        elif number == 3:
            for part in (0, 1):
                self.arrive(3 + part, self.own_land, part)
                self.add((q, y, x, part), self.own_land, (part,))
            started = self.back_own() + [self.keep()]
        elif number == 4:
            self.arrive(5, self.result, q, 1 - y, x, 0)
            self.arrive(6, self.result, q, y, 1 - x, 1)
            self.keep().wait()
            started = self.back_cross()
        elif number == 5:
            self.arrive(7, self.result, 1 - q, y, x)
            self.arrive(8, self.result, q, EVERY, 1 - x, 0)
            self.arrive(9, self.result, q, 1 - y, EVERY, 1)
            started = self.back_core()
        else:
            self.arrive(10, self.result, 1 - q, 1 - y, x, 0)
            self.arrive(11, self.result, 1 - q, y, 1 - x, 1)
            self.arrive(12, self.result, 1 - q, EVERY, 1 - x, 0)
            self.arrive(13, self.result, 1 - q, 1 - y, EVERY, 1)
        for copy in started:
            copy.start()

    def sent_grad(self):
        for copy in self.to_core() + self.cross() + self.own() + self.back_own():
            copy.wait_send()

    def sent_rest(self):
        for copy in self.back_cross() + self.back_core():
            copy.wait_send()


GROUPS = (
    (0, (1,), (1, 2, 4, 5, 6, 11)),
    (0, (0, 2), (0, 1, 3, 4, 5, 11)),
    (1, (4, 3), (1, 2, 4, 5, 6, 12)),
)


def both_kernel(
    names, count, sections, cores, depth,
    rows_hbm, up_hbm, lead_ref, numer_ref, denom_ref, power_ref, attend_gain, attend_bias, attend_mix, fading_ref, bonus_ref,
    feed_gain, feed_bias, feed_mix, entry_hbm, exit_hbm, key_hbm, content_hbm, gate_hbm,
    out_hbm, back_hbm, table_ref, entry_sum, exit_sum, key_sum, content_sum, gate_sum,
    normal_ref, std_ref, key_ref, value_ref, averaged_ref, state_ref, open_ref, hidden_ref, slope_ref, gate_ref, kv_ref,
    full_ref, edge_ref, rows_ref, tokens_ref, grad_ref, back_ref,
    entry_ref, exit_ref, w_key, w_content, w_gate,
    entry_grad, exit_grad, key_grad, content_grad, gate_grad,
    entry_core, exit_core, key_core, content_core, gate_core,
    entry_cross, exit_cross, key_cross, content_cross, gate_cross,
    entry_own, exit_own, key_own, content_own, gate_own,
    pay, stat, part, stage, land, mixed_ref, pre_grads, up_ref, work_ref, pair_ref, carry_ref, sum_ref,
    output_ref, hidden_grad, last_ref, later_ref, edges_ref, edge_land, small_ref,
    load_sems, token_sems, back_sems, fs, fr, os, orr, bs, br, gs, gr, ts, tr, ss, sr, es, er, ws, wr,
    table_send, table_recv,
):
    length, width = rows_ref.shape
    hidden_width = hidden_ref.shape[2]
    chunks = length // CHUNK
    passes = 2 * depth
    period = max(2 * count - 2, chunks + 1)
    here = Here(names)
    peers = Peers(here, count, width, 2 * passes)
    mine = peers.columns(peers.me)
    micro, core = here.at["section"], here.at["seq"]
    y, x = lax.div(micro, 2), lax.rem(micro, 2)
    neighbours = (
        here.device(seq=1 - core), here.device(section=micro + 1 - 2 * x), here.device(section=micro + 2 - 4 * y)
    )
    around = (core, y, x), neighbours
    first = from_tokens(rows_hbm, micro, tokens_ref, token_sems)
    second = from_tokens(up_hbm, micro, back_ref, back_sems)
    for copy in first + second:
        copy.start()
    weights = load(
        (
            (entry_hbm, entry_ref), (exit_hbm, exit_ref), (key_hbm, w_key), (content_hbm, w_content),
            (gate_hbm, w_gate),
        ),
        load_sems,
        0,
    )
    full_ref[...] = jnp.zeros_like(full_ref)
    for j in range(2 * depth):
        level = j // 2
        gain, bias, mix = (attend_gain, attend_bias, attend_mix) if j % 2 == 0 else (feed_gain, feed_bias, feed_mix)
        full_ref[j, 0:1, mine] = gain[level : level + 1, :]
        full_ref[j, 1:2, mine] = bias[level : level + 1, :]
        full_ref[j, 2:3, mine] = lead_ref[j, micro]
        for i in range(mix.shape[0] if j % 2 == 0 else mix.shape[1]):
            full_ref[j, 3 + i : 4 + i, mine] = mix[i, level : level + 1] if j % 2 == 0 else mix[level, i : i + 1]
    gather = Gather(peers, pay, (gs, gr))
    tiles = Tiles(peers, stat, (ts, tr))
    scatter = Scatter(peers, part, stage, land, (ss, sr))
    start_out, wait_out = to_sections(here, sections, rows_ref, tokens_ref, out_hbm, (os, orr))
    start_back, wait_back = to_sections(here, sections, grad_ref, back_ref, back_hbm, (bs, br))

    def full_copy(k, owner):
        block = full_ref.at[:, :, peers.columns(owner)]
        return peers.copy(peers.to(k), block, block, fs.at[k - 1], fr.at[k - 1])

    def sums(group, level):
        parts = (
            (key_grad, key_core, key_cross, key_own, key_sum),
            (content_grad, content_core, content_cross, content_own, content_sum),
            (gate_grad, gate_core, gate_cross, gate_own, gate_sum),
        )
        entry = (entry_grad, entry_core, entry_cross, entry_own, entry_sum)
        parts += (entry, (exit_grad, exit_core, exit_cross, exit_own, exit_sum))
        out = []
        for place in GROUPS[group][1]:
            grad, core_land, cross_land, own_land, result = parts[place]
            out.append(
                Summed(
                    around, grad, core_land, cross_land, own_land, result.at[level],
                    (ws.at[level, place], wr.at[level, place]),
                )
            )
        return out

    def sum_step(group, level, number):
        for matrix in sums(group, level):
            matrix.step(number)

    def table_place(k):
        return lax.rem(micro * cores + core + k, sections * cores)

    def table_copy(k, owner):
        other = table_place(k)
        return pltpu.make_async_remote_copy(
            src_ref=small_ref, dst_ref=table_ref.at[owner], send_sem=table_send.at[k - 1], recv_sem=table_recv.at[k - 1],
            device_id=here.device(section=lax.div(other, cores), seq=lax.rem(other, cores)), device_id_type=MESH,
        )

    for copy in first:
        copy.wait()
    to_stretches(tokens_ref, rows_ref)
    others = [table_place(k) for k in range(1, sections * cores)]
    peers.greet([here.device(section=lax.div(other, cores), seq=lax.rem(other, cores)) for other in others])
    for k in range(1, count):
        full_copy(k, peers.me).start()
    def begin_forward(j, c):
        rows = rows_of(c)

        @pl.when(j > 0)
        def _():
            value = scatter.total(c, j - 1)
            tiles.sent(c)

            @pl.when(odd(j, passes) == 1)
            def _():
                rows_ref[rows, :] += value

            @pl.when(odd(j, passes) == 0)
            def _():
                level = halves(j, passes) - 1
                kv_ref[level, rows, :] = value
                rows_ref[rows, :] += gate_ref[level, rows, :] * value

        @pl.when(j < 2 * depth)
        def _():
            lines = rows_ref[rows, :]
            middle = jnp.mean(lines, axis=1, keepdims=True)
            center = lines - middle
            square = jnp.sum(center * center, axis=1, keepdims=True)
            pay[odd(j, passes), rows, mine] = center.astype(jnp.bfloat16)
            tiles.stat[peers.me, c] = to_row_tile(middle, square)
            tiles.start(c)
            gather.start(c, j)

        @pl.when(j == 2 * depth)
        def _():
            start_out(c)

    def attend_forward(level, c):
        rows = rows_of(c)

        @pl.when(c == 0)
        def _():
            for i, start_ref in enumerate((numer_ref, denom_ref, power_ref)):
                carry_ref[i] = jnp.broadcast_to(start_ref[level, micro], (SUB, width))

        decay = jnp.broadcast_to(jnp.exp(fading_ref[pl.ds(level, 1), :]), (SUB, width))
        bonus = jnp.broadcast_to(bonus_ref[pl.ds(level, 1), :], (SUB, width))
        key_ref[level, rows, :] = product(mixed_ref[0, 0:CHUNK], entry_ref[level, 0])
        value_ref[level, rows, :] = product(mixed_ref[1, 0:CHUNK], entry_ref[level, 1])
        gate = jax.nn.sigmoid(product(mixed_ref[2, 0:CHUNK], entry_ref[level, 2]))
        open_ref[level, rows, :] = gate
        wkv_forward(
            pl.multiple_of(c * CHUNK, CHUNK), key_ref.at[level], value_ref.at[level], decay, bonus, carry_ref,
            averaged_ref.at[level], state_ref.at[level],
        )
        output = (gate * averaged_ref[level, rows, :]).astype(jnp.bfloat16)
        for target in range(count):
            block = peers.columns(target)
            part[rows, block] = product(output, exit_ref[level, :, block])

    def feed_forward(level, c):
        rows = rows_of(c)
        for start in range(0, hidden_ref.shape[2], width):
            block = slice(start, start + width)
            soft, slope = soft_plus(product(mixed_ref[0, 0:CHUNK], w_key[level, :, block]))
            hidden_ref[level, rows, block] = (soft * soft).astype(jnp.bfloat16)
            slope_ref[level, rows, block] = (2.0 * soft * slope).astype(jnp.bfloat16)
        for target in range(count):
            block = peers.columns(target)
            part[rows, block] = product(hidden_ref[level, rows, :], w_content[level, :, block])
        gate_ref[level, rows, :] = jax.nn.sigmoid(product(mixed_ref[1, 0:CHUNK], w_gate[level]))

    def forward(j, c):
        @pl.when((j == 0) & (c == 0))
        def _():
            for k in range(1, count):
                full_copy(k, peers.source(k)).wait_recv()
            for copy in weights:
                copy.wait()

        @pl.when(c == 0)
        def _():
            last_ref[0:1, :] = full_ref[j, 2:3, :]

        def mix(count_mixed):
            mix_chunk(
                peers, c, pay.at[odd(j, passes)], tiles, full_ref.at[j], mixed_ref.at[pl.ds(0, count_mixed), pl.ds(0, CHUNK)],
                normal_ref.at[j], edge_ref.at[j], std_ref.at[j], last_ref,
            )

        level = halves(j, passes)

        @pl.when(odd(j, passes) == 0)
        def _():
            mix(3)
            attend_forward(level, c)

        @pl.when(odd(j, passes) == 1)
        def _():
            mix(2)
            feed_forward(level, c)

        gather.sent(c, j)

    def edge_copies(j, source_of):
        return [
            peers.copy(
                peers.to(k), edges_ref.at[j, :, peers.columns(peers.to(k))], edge_land.at[j, source_of(k)],
                es.at[j, k - 1], er.at[j, k - 1],
            )
            for k in range(1, count)
        ]

    def end_pass(j, c):
        rows = rows_of(c)
        normed_grad = scatter.total(c, 2 * passes - 1 - j)
        tiles.arrived(c)
        totals = tiles.stat[0, c]
        for source in range(1, count):
            totals = totals + tiles.stat[source, c]
        columns = to_columns([totals])
        normal = normal_ref[j, rows, mine].astype(jnp.float32)
        scale = 1.0 / (count * width)
        grad_ref[rows, :] += std_ref[j, rows, 0:1] * (
            normed_grad * full_ref[j, 0:1, mine] - columns[:, 0:1] * scale - normal * (columns[:, 1:2] * scale)
        )
        small_ref[j, 0:1, :] += jnp.sum(normed_grad * normal, axis=0, keepdims=True)
        small_ref[j, 1:2, :] += jnp.sum(normed_grad, axis=0, keepdims=True)

        @pl.when(c == 0)
        def _():
            for copy in edge_copies(j, peers.source):
                copy.wait_recv()
            edges = edges_ref[j, :, mine]
            for k in range(1, count):
                edges = edges + edge_land[j, peers.source(k)]
            small_ref[j, 2:6, :] = edges[2:6]

    def begin_backward(which, c):
        rows = rows_of(c)
        j = passes - 1 - which

        @pl.when(which > 0)
        def _():
            end_pass(j + 1, c)
            gather.sent(c, passes + which - 1)
            tiles.sent(c)

        @pl.when((which < passes) & (odd(which, passes) == 0))
        def _():
            pay[odd(which, passes), rows, mine] = (grad_ref[rows, :] * gate_ref[halves(j, passes), rows, :]).astype(jnp.bfloat16)

        @pl.when((which < passes) & (odd(which, passes) == 1))
        def _():
            pay[odd(which, passes), rows, mine] = grad_ref[rows, :].astype(jnp.bfloat16)

        @pl.when(which < passes)
        def _():
            gather.start(c, passes + which)

        @pl.when(which == passes)
        def _():
            start_back(c)

    def attend_backward(j, c):
        level = halves(j, passes)
        rows = rows_of(c)
        decay = jnp.broadcast_to(jnp.exp(fading_ref[pl.ds(level, 1), :]), (SUB, width))
        bonus = jnp.broadcast_to(bonus_ref[pl.ds(level, 1), :], (SUB, width))

        @pl.when(c == chunks - 1)
        def _():
            sum_ref[...] = jnp.zeros_like(sum_ref)
            carry_ref[0] = jnp.zeros((SUB, width), jnp.float32)
            carry_ref[1] = jnp.zeros((SUB, width), jnp.float32)
            carry_ref[2] = jnp.full((SUB, width), NO_POWER, jnp.float32)

        output_grad = against(pay[1, rows, :], exit_ref[level])
        gate = open_ref[level, rows, :]
        up = output_grad * gate
        up_ref[...] = up
        averaged = averaged_ref[level, rows, :]
        pre_grads[2, rows, :] = (up * averaged * (1.0 - gate)).astype(jnp.bfloat16)
        output_ref[rows, :] = (gate * averaged).astype(jnp.bfloat16)
        wkv_backward(
            pl.multiple_of(c * CHUNK, CHUNK), key_ref.at[level], value_ref.at[level], decay, bonus,
            averaged_ref.at[level], state_ref.at[level],
            up_ref, carry_ref, sum_ref, work_ref, pair_ref,
        )
        pre_grads[0, rows, :] = pair_ref[0].astype(jnp.bfloat16)
        pre_grads[1, rows, :] = pair_ref[1].astype(jnp.bfloat16)
        mix_chunk_back(
            peers, c, 3, full_ref.at[j], normal_ref.at[j], edge_ref.at[j], mixed_ref,
            lambda i, columns: against(pre_grads[i, rows, :], entry_ref[level, i, columns, :]),
            later_ref, edges_ref.at[j], part, tiles,
        )

        @pl.when(c == 0)
        def _():
            numer, denom = carry_ref[0, SUB - 1 :, :], carry_ref[1, SUB - 1 :, :]
            lift = jnp.exp(power_ref[level, micro] + carry_ref[2, SUB - 1 :, :])
            out = passes + level
            small_ref[out, 0:1, :] = -decay[0:1] * jnp.sum(sum_ref[0], axis=0, keepdims=True)
            small_ref[out, 1:2, :] = jnp.sum(sum_ref[1], axis=0, keepdims=True)
            small_ref[out, 2:3, :] = lift * numer
            small_ref[out, 3:4, :] = lift * denom
            small_ref[out, 4:5, :] = lift * (numer_ref[level, micro] * numer + denom_ref[level, micro] * denom)

    def feed_backward(j, c):
        rows = rows_of(c)
        level = halves(j, passes)
        gate = gate_ref[level, rows, :]
        pre_grads[0, rows, :] = (grad_ref[rows, :] * gate * kv_ref[level, rows, :] * (1.0 - gate)).astype(jnp.bfloat16)
        for start in range(0, hidden_width, width):
            block = slice(start, start + width)
            into = against(pay[0, rows, :], w_content[level, block, :])
            hidden_grad[rows, block] = (into * slope_ref[level, rows, block].astype(jnp.float32)).astype(jnp.bfloat16)

        def mix_grad(i, columns):
            if i == 0:
                return against(hidden_grad[rows, :], w_key[level, columns, :])
            return against(pre_grads[0, rows, :], w_gate[level, columns, :])

        mix_chunk_back(
            peers, c, 2, full_ref.at[j], normal_ref.at[j], edge_ref.at[j], mixed_ref, mix_grad,
            later_ref, edges_ref.at[j], part, tiles,
        )

    def backward(which, c):
        j = passes - 1 - which

        @pl.when(c == chunks - 1)
        def _():
            later_ref[...] = jnp.zeros_like(later_ref)

        @pl.when(odd(which, passes) == 0)
        def _():
            feed_backward(j, c)

        @pl.when(odd(which, passes) == 1)
        def _():
            attend_backward(j, c)

        @pl.when(c == 0)
        def _():
            edges_ref[j, 2:3, :] = later_ref[0:1, :]
            for copy in edge_copies(j, lambda k: peers.me):
                copy.start()

    def weigh(place, level):
        if place == 4:
            for source in range(count):
                block = peers.columns(source)
                grad = inner_rows(output_ref[...], pay[1, :, block]).astype(jnp.bfloat16)
                exit_grad[..., block] = grad.reshape(*exit_grad.shape[:-1], width)
            return
        for i in range(4):
            at = i // 2, i % 2
            if place == 1:
                rows = hidden_width // 4
                grad = inner_rows(hidden_ref[level, :, i * rows : (i + 1) * rows], pay[0]).astype(jnp.bfloat16)
                content_grad[at] = grad.reshape(content_grad.shape[2:])
                continue
            rows = slice(i * (pay.shape[2] // 4), (i + 1) * (pay.shape[2] // 4))
            if place == 0:
                grad = inner_rows(mixed_ref[0, :, rows], hidden_grad[...]).astype(jnp.bfloat16)
                key_grad[at] = grad.reshape(key_grad.shape[2:])
            elif place == 2:
                grad = inner_rows(mixed_ref[1, :, rows], pre_grads[0]).astype(jnp.bfloat16)
                gate_grad[at] = grad.reshape(gate_grad.shape[2:])
            else:
                for k in range(3):
                    grad = inner_rows(mixed_ref[k, :, rows], pre_grads[k]).astype(jnp.bfloat16)
                    entry_grad[(k, *at)] = grad.reshape(entry_grad.shape[3:])

    base, final = chunks + count - 1, passes * period + chunks - 1

    def when_taken(group, number, t):
        kind, places, later = GROUPS[group]
        taken, chosen = False, 0
        for level in range(depth):
            now = t == base + period * kind + later[number] + 2 * period * (depth - 1 - level)
            taken, chosen = taken | now, chosen + jnp.where(now, level, 0)
        return taken, chosen

    def extra(t):
        for group in range(len(GROUPS)):
            for number in reversed(range(STEPS - 1)):
                taken, level = when_taken(group, number, t)

                @pl.when(taken)
                def _():
                    if number == 0:
                        @pl.when(level < depth - 1)
                        def _():
                            for matrix in sums(group, jnp.minimum(level + 1, depth - 1)):
                                matrix.sent_grad()

                        for place in GROUPS[group][1]:
                            weigh(place, jnp.clip(level, 0, depth - 1))
                    sum_step(group, jnp.clip(level, 0, depth - 1), number)

    forward_tick = ticks_of(peers, chunks, passes, 0, False, begin_forward, gather, forward, scatter)
    backward_tick = ticks_of(peers, chunks, passes, passes, True, begin_backward, gather, backward, scatter)
    turn = (passes - 1) * period + chunks + count - 2

    def onward(w, i):
        ends = i == period - 1
        return jnp.where(ends, w + 1, w), jnp.where(ends, 0, i + 1)

    def tick(t, places):
        ahead, behind = places

        @pl.when(t < passes * period + chunks)
        def _():
            forward_tick(*ahead)

        @pl.when(t == turn - 1)
        def _():
            for copy in second:
                copy.wait()
            to_stretches(back_ref, grad_ref)
            small_ref[...] = jnp.zeros_like(small_ref)
            edges_ref[...] = jnp.zeros_like(edges_ref)

        @pl.when(t >= turn)
        def _():
            backward_tick(*behind)
            extra(t - turn)

        moved = onward(*behind)
        return onward(*ahead), tuple(jnp.where(t >= turn, a, b) for a, b in zip(moved, behind))

    start = (jnp.int32(0), jnp.int32(0))
    lax.fori_loop(0, turn + final + 1, tick, (start, start))

    for k in range(1, sections * cores):
        table_copy(k, micro * cores + core).start()
    table_ref[micro * cores + core] = small_ref[...]
    left = []
    for group, (kind, places, later) in enumerate(GROUPS):
        for level in reversed(range(depth)):
            start = base + period * (kind + 2 * (depth - 1 - level))
            for number in range(STEPS):
                at = start + (later[number] if number < STEPS - 1 else later[-1] + 5)
                if at > final or number == STEPS - 1:
                    left.append((at, group, level, number))
    for at, group, level, number in sorted(left):
        sum_step(group, level, number)
    for c in range(chunks):
        scatter.sent(c, 2 * passes - 1)
    for j in range(passes):
        for copy in edge_copies(j, lambda k: peers.me):
            copy.wait_send()
    for group in range(len(GROUPS)):
        for level in range(depth):
            for matrix in sums(group, level):
                matrix.sent_rest()
                if level == 0:
                    matrix.sent_grad()
    for k in range(1, sections * cores):
        table_copy(k, micro * cores + core).wait_send()
        other = lax.rem(micro * cores + core + sections * cores - k, sections * cores)
        table_copy(k, other).wait_recv()
    for k in range(1, count):
        full_copy(k, peers.me).wait_send()
    wait_out()
    wait_back()


BF16, F32 = jnp.bfloat16, jnp.float32


def struct(*shape, dtype=F32):
    return jax.ShapeDtypeStruct(shape, dtype)


def run_kernel(body, collective, outs, scratch, operands, flops):
    def spec(inside):
        return pl.BlockSpec(memory_space=pltpu.VMEM if inside else pl.ANY)

    return pl.pallas_call(
        body,
        out_shape=[out for out, inside in outs],
        in_specs=[spec(inside) for operand, inside in operands],
        out_specs=[spec(inside) for out, inside in outs],
        scratch_shapes=scratch,
        compiler_params=pltpu.CompilerParams(
            collective_id=collective, has_side_effects=True, vmem_limit_bytes=63 * 1024 * 1024
        ),
        cost_estimate=pl.CostEstimate(flops=flops, bytes_accessed=2**25, transcendentals=2**23),
    )(*[operand for operand, inside in operands])


def pair_of(shape):
    return [pltpu.SemaphoreType.DMA(shape)] * 2


def run_fast(
    names, residual_entering, upstream_sensitivity, piece_lead_lines, dividend_start, divisor_start, power_offset_start,
    attend_standard_scale, attend_standard_offset, attend_lag_fractions, fading_log_rate, reward_first_word,
    attend_entry_matrix, attend_exit_matrix, feed_standard_scale, feed_standard_offset, feed_lag_fractions,
    feed_lookup_matrix, feed_content_matrix, feed_gate_matrix,
):
    count, sections, cores = (lax.axis_size(axis) for axis in ("tp", "section", "seq"))
    length, width = residual_entering.shape[2:]
    depth, features, hidden = feed_lookup_matrix.shape[0], count * width, feed_lookup_matrix.shape[2]
    chunks, subs = length // CHUNK, 2 * depth
    flops = 2 * depth * length * features * (4 * width + 2 * hidden + width)
    groups = width // LANES
    starts = (dividend_start, divisor_start, power_offset_start)
    weights = (attend_entry_matrix, attend_exit_matrix, feed_lookup_matrix, feed_content_matrix, feed_gate_matrix)
    shares = struct(sections, 1, CHUNK, width)
    lines = (depth, length, width)
    shapes = [weight.shape[1:] for weight in weights]

    def held(*shape, dtype=F32):
        return pltpu.VMEM(shape, dtype)

    def cut(*parts):
        return [(*shape[:-2], *parts, shape[-2] // 16, shape[-1]) for shape in shapes]

    outs = [(shares, False), (shares, False), (struct(sections * cores, subs + depth, SUB, width), True)]
    outs += [(struct(depth, *shape, dtype=BF16), False) for shape in cut(2, 2, 2, 2)]
    scratch = [held(subs, length, features, dtype=BF16), held(subs, length, LANES), held(*lines), held(*lines)]
    scratch += [held(*lines), held(depth, 3, *lines[1:]), held(*lines)]
    scratch += [held(depth, length, hidden, dtype=BF16)] * 2 + [held(*lines)] * 2
    scratch += [held(subs, SUB, features)] * 2 + [held(length, width), held(groups, length, LANES)] * 2
    scratch += [held(*weight.shape, dtype=BF16) for weight in weights]
    scratch += [
        held(*shape, dtype=BF16)
        for shape in cut(2, 2, 2, 2) + cut(2, 2, 2) + cut(2, 2, 2) + cut(2)
    ]
    scratch += [
        held(2, length, features, dtype=BF16), held(count, chunks, PAIR, LANES), held(length, features),
        held(length, features, dtype=BF16), held(2, length, features + width, dtype=BF16),
    ]
    scratch += [
        held(3, length, features, dtype=BF16), held(3, length, width, dtype=BF16), held(CHUNK, width),
        held(3, STEP, SUB, width), held(2, CHUNK, width), held(3, SUB, width), held(2, SUB, width),
        held(length, width, dtype=BF16), held(length, hidden, dtype=BF16), held(SUB, features), held(SUB, features),
        held(subs, SUB, features), held(subs, count, SUB, width), held(subs + depth, SUB, width),
    ]
    scratch += [pltpu.SemaphoreType.DMA((n,)) for n in (len(weights), groups, groups)] + pair_of((count - 1,))
    scratch += pair_of((sections, groups)) + pair_of((sections, groups))
    scratch += pair_of((2, 2, count - 1, chunks)) + pair_of((count - 1, chunks)) + pair_of((2, 2, count, chunks))
    scratch += pair_of((subs, count - 1)) + pair_of((depth, len(weights), COPIES))
    scratch += pair_of((sections * cores - 1,))
    operands = [(residual_entering, False), (upstream_sensitivity, False)]
    operands += [
        (value, True)
        for value in (
            piece_lead_lines, *starts, attend_standard_scale, attend_standard_offset,
            jnp.swapaxes(attend_lag_fractions, 0, 1),
            fading_log_rate, reward_first_word, feed_standard_scale, feed_standard_offset, feed_lag_fractions,
        )
    ]
    operands += [(value, False) for value in weights]
    out_share, back_share, table, *sums = run_kernel(
        partial(both_kernel, names, count, sections, cores, depth), 0, outs, scratch, operands, 3 * flops
    )
    return finish(cores, depth, out_share, back_share, table, sums, [weight.shape for weight in weights])


def finish_kernel(cores, depth, table_ref, *refs):
    wide, narrow = refs[:7], refs[7:14]
    prev, numer, denom, power = refs[14:18]
    attend_gain, attend_bias, attend_mix, decay, bonus, feed_gain, feed_bias, feed_mix = refs[18:]
    for source, target in zip(wide, narrow):
        target[...] = source[...].astype(jnp.float32)

    @pl.when(pl.program_id(0) == 0)
    def _():
        core = lax.axis_index("seq")
        places, subs = table_ref.shape[0], 2 * depth
        for m in range(places // cores):
            for j in range(subs):
                prev[j, m] = table_ref[m * cores + core, j, 2:3, :]
            for level in range(depth):
                for i, state in enumerate((numer, denom, power)):
                    state[level, m] = table_ref[m * cores + core, subs + level, 2 + i : 3 + i, :]
        for level in range(depth):
            for j, gain, bias, mix in (
                (2 * level, attend_gain, attend_bias, attend_mix), (2 * level + 1, feed_gain, feed_bias, feed_mix),
            ):
                total = sum(table_ref[place, j] for place in range(places))
                gain[level : level + 1, :] = total[0:1]
                bias[level : level + 1, :] = total[1:2]
                for i in range(mix.shape[0] if mix is attend_mix else mix.shape[1]):
                    place = (i, slice(level, level + 1)) if mix is attend_mix else (level, slice(i, i + 1))
                    mix[place] = total[3 + i : 4 + i]
            total = sum(table_ref[place, subs + level] for place in range(places))
            decay[level : level + 1, :] = total[0:1]
            bonus[level : level + 1, :] = total[1:2]


def finish(cores, depth, out_share, back_share, table, sums, shapes):
    steps = 4
    wide = [value.reshape(-1, value.shape[-1]) for value in (out_share, back_share, *sums)]
    blocks = [
        pl.BlockSpec((value.shape[0] // steps, value.shape[1]), lambda i: (i, 0)) for value in wide
    ]
    width = table.shape[-1]
    micros = table.shape[0] // cores
    small = [(2 * depth, micros, 1, width)] + [(depth, micros, 1, width)] * 3
    small += [(depth, width), (depth, width), (3, depth, width), (depth, width), (depth, width)]
    small += [(depth, width), (depth, width), (depth, 2, width)]

    def whole(shape):
        return pl.BlockSpec(shape, lambda i: (0,) * len(shape))

    got = pl.pallas_call(
        partial(finish_kernel, cores, depth),
        grid=(steps,),
        out_shape=[struct(*value.shape) for value in wide] + [struct(*shape) for shape in small],
        in_specs=[whole(table.shape)] + blocks,
        out_specs=blocks + [whole(shape) for shape in small],
        compiler_params=pltpu.CompilerParams(vmem_limit_bytes=60 * 1024 * 1024),
    )(table, *wide)
    shares = [value.reshape(whole.shape) for value, whole in zip(got, (out_share, back_share))]
    entry, leave, key, content, gate = [
        value.reshape(shape) for value, shape in zip(got[2:7], shapes)
    ]
    small = list(got[7:])
    small[6] = jnp.swapaxes(small[6], 0, 1)
    return (*shares, *small[:9], entry, leave, *small[9:], key, content, gate)


def run_plain(
    residual_entering,
    upstream_sensitivity,
    piece_lead_lines,
    dividend_start,
    divisor_start,
    power_offset_start,
    attend_standard_scale,
    attend_standard_offset,
    attend_lag_fractions,
    fading_log_rate,
    reward_first_word,
    attend_entry_matrix,
    attend_exit_matrix,
    feed_standard_scale,
    feed_standard_offset,
    feed_lag_fractions,
    feed_lookup_matrix,
    feed_content_matrix,
    feed_gate_matrix,
):
    sections = lax.axis_size("section")
    micro = lax.axis_index("section")
    length, share = residual_entering.shape[2:]
    depth = attend_entry_matrix.shape[0]

    def own(array):
        return lax.dynamic_index_in_dim(array, micro, 0, keepdims=False)

    blank = jnp.zeros((1, share), jnp.float32)
    lead = lax.dynamic_index_in_dim(piece_lead_lines[:, :, 0], micro, 1, keepdims=False)
    starts = [
        lax.dynamic_index_in_dim(start[:, :, 0], micro, 1, keepdims=False)
        for start in (dividend_start, divisor_start, power_offset_start)
    ]
    small_rows, wkv_rows = [], []
    for level in range(depth):
        for gain, bias, mix, j in (
            (attend_standard_scale, attend_standard_offset, attend_lag_fractions, 2 * level),
            (feed_standard_scale, feed_standard_offset, feed_lag_fractions, 2 * level + 1),
        ):
            rows = [gain[level][None], bias[level][None], lead[j][None], mix[level]]
            rows += [blank] * (5 - mix.shape[1])
            small_rows.append(jnp.concatenate(rows, axis=0))
        wkv_rows.append(
            jnp.stack(
                [fading_log_rate[level], reward_first_word[level]]
                + [start[level] for start in starts]
                + [blank[0]] * 3
            )
        )
    small_own = jnp.stack(small_rows)
    small_full = lax.all_gather(small_own, "tp", axis=2, tiled=True)

    rows = own(residual_entering)[0]
    kept = []
    for level in range(depth):
        for j in (2 * level, 2 * level + 1):
            if j % 2 == 0:
                rows, saved = time_forward_plain(
                    rows, small_full[j], small_own[j], wkv_rows[level],
                    attend_entry_matrix[level], attend_exit_matrix[level],
                )
            else:
                rows, saved = channel_forward_plain(
                    rows, small_full[j], small_own[j],
                    feed_lookup_matrix[level], feed_content_matrix[level], feed_gate_matrix[level],
                )
            kept.append(saved)

    def to_tokens(value):
        pieces = value.reshape(sections, length // sections, share)
        return lax.all_to_all(pieces, "section", 0, 0)[:, None]

    out_share = to_tokens(rows)
    grad = own(upstream_sensitivity)[0]
    small_grads, wkv_grads = [None] * (2 * depth), [None] * depth
    weight_grads = [None] * (2 * depth)
    summed = None
    for level in reversed(range(depth)):
        for j in (2 * level + 1, 2 * level):
            if j % 2 == 0:
                grad, small_grads[j], wkv_grads[level], weights = time_backward_plain(
                    grad, kept[j], small_full[j], small_own[j], wkv_rows[level],
                    attend_entry_matrix[level], attend_exit_matrix[level],
                )
            else:
                grad, small_grads[j], weights = channel_backward_plain(
                    grad, kept[j], small_full[j], small_own[j],
                    feed_lookup_matrix[level], feed_content_matrix[level], feed_gate_matrix[level],
                )
            weight_grads[j] = weights
        both = weight_grads[2 * level + 1], weight_grads[2 * level]
        if summed is not None:
            both, summed = lax.optimization_barrier((both, summed))
            weight_grads[2 * level + 3], weight_grads[2 * level + 2] = summed
        summed = lax.psum(both, ("section", "seq"))
    weight_grads[1], weight_grads[0] = summed
    back_share = to_tokens(grad)

    table = jnp.stack(small_grads + wkv_grads)
    tables = lax.all_gather(table, ("section", "seq"), axis=0)
    sums = [
        jnp.stack([weight_grads[2 * level + kind][place] for level in range(depth)])
        for kind, place in ((0, 0), (0, 1), (1, 0), (1, 1), (1, 2))
    ]
    return out_share, back_share, tables, sums


def per_device(names, *arrays):
    residual_entering, lookup = arrays[0], arrays[16]
    sections, cores = lax.axis_size("section"), lax.axis_size("seq")
    micros, unused, length, share = residual_entering.shape
    depth, features, hidden = lookup.shape
    fits = sections == 4 and cores == 2 and micros == sections and length == sections * CHUNK
    fits = fits and share % 256 == 0 and features % 256 == 0 and hidden % 256 == 0 and hidden % share == 0
    fits = fits and 2 < lax.axis_size("tp") <= LANES // SUB
    if fits:
        return run_fast(names, *arrays)
    out_share, back_share, table, sums = run_plain(*arrays)
    tables = table.reshape(sections, cores, *table.shape[1:])
    mine = lax.dynamic_index_in_dim(tables, lax.axis_index("seq"), 1, keepdims=False)
    total = jnp.sum(tables, axis=(0, 1))
    prev_grad = jnp.moveaxis(mine[:, : 2 * depth, 2], 0, 1)[:, :, None]
    state_grads = [jnp.moveaxis(mine[:, 2 * depth :, 2 + i], 0, 1)[:, :, None] for i in range(3)]

    weights = [grad.astype(jnp.float32) for grad in sums]
    return (
        out_share,
        back_share,
        prev_grad,
        *state_grads,
        total[0 : 2 * depth : 2, 0],
        total[0 : 2 * depth : 2, 1],
        total[0 : 2 * depth : 2, 3:6],
        total[2 * depth :, 0],
        total[2 * depth :, 1],
        weights[0],
        weights[1],
        total[1 : 2 * depth : 2, 0],
        total[1 : 2 * depth : 2, 1],
        total[1 : 2 * depth : 2, 3:5],
        weights[2],
        weights[3],
        weights[4],
    )


def solution(mesh):
    rows = P(None, "seq", None, "tp")
    line, mix = P(None, "tp"), P(None, None, "tp")
    columns, depths = P(None, None, "tp"), P(None, "tp", None)
    entry = P(None, None, None, "tp")
    state = P(None, None, "seq", "tp")
    tokens = P(None, "seq", "section", "tp")
    return jax.shard_map(
        partial(per_device, mesh.axis_names),
        mesh=mesh,
        in_specs=(
            rows, rows, state, state, state, state,
            line, line, mix, line, line, entry, depths,
            line, line, mix, columns, depths, columns,
        ),
        out_specs=(
            tokens, tokens, state, state, state, state,
            line, line, mix, line, line, entry, depths,
            line, line, mix, columns, depths, columns,
        ),
        check_vma=False,
    )
```

```python
from functools import partial

import jax
import jax.numpy as jnp
from jax import lax
from jax.experimental import pallas as pl
from jax.experimental.pallas import tpu as pltpu
from jax.sharding import PartitionSpec as P

BLOCK = 128


epsilon = 1e-05


def product(left_side, right_side):
    return jnp.dot(left_side, right_side, preferred_element_type=jnp.float32)


def inner_rows(left_side, right_side):
    return lax.dot_general(
        left_side, right_side, (((0,), (0,)), ((), ())), preferred_element_type=jnp.float32
    )


def against(left_side, right_side):
    return lax.dot_general(
        left_side, right_side, (((1,), (1,)), ((), ())), preferred_element_type=jnp.float32
    )


def weighted_value_blocks(
    block_length,
    incoming_lookups,
    incoming_contents,
    fading_entries,
    reward_entries,
    dividend_entries,
    divisor_entries,
    peak_line,
):
    decay_rate = jnp.exp(fading_entries)
    total_rows, channels = incoming_lookups.shape
    places = jnp.arange(block_length, dtype=jnp.float32)
    earlier = places[:, None] > places[None, :]
    spacing = places[:, None] - 1.0 - places[None, :]
    remain = block_length - 1.0 - places

    def advance(state_in, block_in):
        numer_in, denom_in, topmost = state_in
        lookup_piece_tile, value_block = block_in
        spread_exp = lookup_piece_tile[None, :, :] - spacing[:, :, None] * decay_rate
        spread_exp = jnp.where(earlier[:, :, None], spread_exp, -1e30)
        leading_power = reward_entries + lookup_piece_tile
        start_exp = topmost[None, :] - places[:, None] * decay_rate
        peak_exp = jnp.maximum(jnp.maximum(jnp.max(spread_exp, axis=1), leading_power), start_exp)
        weights = jnp.exp(spread_exp - peak_exp[:, None, :])
        from_state = jnp.exp(start_exp - peak_exp)
        own_term = jnp.exp(leading_power - peak_exp)
        numer_out = (
            from_state * numer_in
            + jnp.sum(weights * value_block[None, :, :], axis=1)
            + own_term * value_block
        )
        denom_out = from_state * denom_in + jnp.sum(weights, axis=1) + own_term
        ending = lookup_piece_tile - remain[:, None] * decay_rate
        stopping = topmost - block_length * decay_rate
        new_top = jnp.maximum(jnp.max(ending, axis=0), stopping)
        scaled = jnp.exp(ending - new_top[None, :])
        carried = jnp.exp(stopping - new_top)
        new_numer = carried * numer_in + jnp.sum(scaled * value_block, axis=0)
        new_denom = carried * denom_in + jnp.sum(scaled, axis=0)
        return ((new_numer, new_denom, new_top), numer_out / denom_out)

    blocks = total_rows // block_length
    unused, results = lax.scan(
        jax.checkpoint(advance),
        (dividend_entries, divisor_entries, peak_line),
        (
            incoming_lookups.reshape(blocks, block_length, channels),
            incoming_contents.reshape(blocks, block_length, channels),
        ),
    )
    return results.reshape(total_rows, channels)


def spread_plain(rows_in):
    features = rows_in.shape[1] * lax.axis_size("tp")
    mean_row = lax.psum(jnp.sum(rows_in, axis=1), "tp") / features
    center = rows_in - mean_row[:, None]
    inv_std = lax.rsqrt(lax.psum(jnp.sum(center * center, axis=1), "tp") / features + epsilon)
    normal_share = center * inv_std[:, None]
    normal_full = lax.all_gather(normal_share.astype(jnp.bfloat16), "tp", axis=1, tiled=True)
    return normal_share, inv_std, normal_full


def mix_plain(normal_full, small_full, mix_count):
    normed = normal_full.astype(jnp.float32) * small_full[0] + small_full[1]
    shifted = jnp.concatenate([small_full[2:3], normed[:-1]], axis=0)
    gap = normed - shifted
    mixed = [(shifted + gap * small_full[3 + i]).astype(jnp.bfloat16) for i in range(mix_count)]
    return mixed, gap


def scatter_plain(branch):
    return lax.psum_scatter(
        branch.astype(jnp.bfloat16), "tp", scatter_dimension=1, tiled=True
    ).astype(jnp.float32)


def time_forward_plain(rows_in, small_full, small_own, wkv_rows, entry_matrix, exit_matrix):
    normal_share, inv_std, normal_full = spread_plain(rows_in)
    mixed, gap = mix_plain(normal_full, small_full, 3)
    lookups, contents, recept = [product(mixed[i], entry_matrix[i]) for i in range(3)]
    averaged, pullback = jax.vjp(
        partial(weighted_value_blocks, BLOCK), lookups, contents, *[wkv_rows[i] for i in range(5)]
    )
    gate = jax.nn.sigmoid(recept)
    output = (gate * averaged).astype(jnp.bfloat16)
    rows_out = rows_in + scatter_plain(product(output, exit_matrix))
    kept = (normal_share, inv_std, normal_full, mixed, gap, averaged, pullback, gate, output)
    return rows_out, kept


def channel_forward_plain(rows_in, small_full, small_own, w_key, w_value, w_gate):
    normal_share, inv_std, normal_full = spread_plain(rows_in)
    mixed, gap = mix_plain(normal_full, small_full, 2)
    hidden_pre = product(mixed[0], w_key)
    soft = jax.nn.softplus(hidden_pre)
    hidden = jnp.square(soft).astype(jnp.bfloat16)
    gate = jax.nn.sigmoid(product(mixed[1], w_gate))
    kv_share = scatter_plain(product(hidden, w_value))
    kept = (normal_share, inv_std, normal_full, mixed, gap, hidden_pre, soft, hidden, gate, kv_share)
    return rows_in + gate * kv_share, kept


def norm_back_plain(rows_grad, mix_grads, gap, normal_full, normal_share, inv_std, small_full, small_own):
    share = normal_share.shape[1]
    features = small_full.shape[1]
    to_normed = sum(grad * small_full[3 + i] for i, grad in enumerate(mix_grads))
    to_shifted = sum(grad * (1.0 - small_full[3 + i]) for i, grad in enumerate(mix_grads))
    ratio_grads = [jnp.sum(grad * gap, axis=0) for grad in mix_grads]
    ratio_grads += [jnp.zeros_like(ratio_grads[0])] * (3 - len(mix_grads))
    to_normed = to_normed + jnp.concatenate([to_shifted[1:], jnp.zeros_like(to_shifted[:1])], axis=0)
    normed_grad = scatter_plain(to_normed)
    edge = lax.psum_scatter(
        jnp.stack([to_shifted[0]] + ratio_grads), "tp", scatter_dimension=1, tiled=True
    )
    scaled = normed_grad * small_own[0]
    first, second = lax.psum((jnp.sum(scaled, axis=1), jnp.sum(scaled * normal_share, axis=1)), "tp")
    rows_back = rows_grad + inv_std[:, None] * (
        scaled - first[:, None] / features - normal_share * (second[:, None] / features)
    )
    gain_grad = jnp.sum(normed_grad * normal_share, axis=0)
    bias_grad = jnp.sum(normed_grad, axis=0)
    zero = jnp.zeros((2, share), jnp.float32)
    return rows_back, jnp.concatenate([gain_grad[None], bias_grad[None], edge, zero], axis=0)


def time_backward_plain(rows_grad, kept, small_full, small_own, wkv_rows, entry_matrix, exit_matrix):
    normal_share, inv_std, normal_full, mixed, gap, averaged, pullback, gate, output = kept
    branch_grad = lax.all_gather(rows_grad.astype(jnp.bfloat16), "tp", axis=1, tiled=True)
    exit_grad = inner_rows(output, branch_grad)
    output_grad = against(branch_grad, exit_matrix)
    state_grads = pullback(output_grad * gate)
    pre_grads = [
        state_grads[0].astype(jnp.bfloat16),
        state_grads[1].astype(jnp.bfloat16),
        (output_grad * averaged * gate * (1.0 - gate)).astype(jnp.bfloat16),
    ]
    entry_grad = jnp.stack([inner_rows(mixed[i], pre_grads[i]) for i in range(3)])
    mix_grads = [against(pre_grads[i], entry_matrix[i]) for i in range(3)]
    rows_back, small_grad = norm_back_plain(
        rows_grad, mix_grads, gap, normal_full, normal_share, inv_std, small_full, small_own
    )
    wkv_grad = jnp.concatenate([jnp.stack(state_grads[2:]), jnp.zeros((3, gate.shape[1]))], axis=0)
    return rows_back, small_grad, wkv_grad, (entry_grad.astype(jnp.bfloat16), exit_grad.astype(jnp.bfloat16))


def channel_backward_plain(rows_grad, kept, small_full, small_own, w_key, w_value, w_gate):
    normal_share, inv_std, normal_full, mixed, gap, hidden_pre, soft, hidden, gate, kv_share = kept
    branch_grad = lax.all_gather((rows_grad * gate).astype(jnp.bfloat16), "tp", axis=1, tiled=True)
    value_grad = inner_rows(hidden, branch_grad)
    hidden_grad = (
        against(branch_grad, w_value) * 2.0 * soft * jax.nn.sigmoid(hidden_pre)
    ).astype(jnp.bfloat16)
    gate_grad = (rows_grad * kv_share * gate * (1.0 - gate)).astype(jnp.bfloat16)
    key_grad = inner_rows(mixed[0], hidden_grad)
    recept_grad = inner_rows(mixed[1], gate_grad)
    mix_grads = [against(hidden_grad, w_key), against(gate_grad, w_gate)]
    rows_back, small_grad = norm_back_plain(
        rows_grad, mix_grads, gap, normal_full, normal_share, inv_std, small_full, small_own
    )
    grads = tuple(grad.astype(jnp.bfloat16) for grad in (key_grad, value_grad, recept_grad))
    return rows_back, small_grad, grads


CHUNK = 128
LANES = 128
SUB = 8
PAIR = 2
MESH = pl.DeviceIdType.MESH
NO_POWER = -1e30


def to_row_tile(*columns):
    lane = lax.broadcasted_iota(jnp.int32, (CHUNK, LANES), 1)
    wide = jnp.zeros((CHUNK, LANES), jnp.float32)
    for place, column in enumerate(columns):
        wide = jnp.where(lane == place, column, wide)
    return jnp.transpose(wide)[:PAIR]


def to_columns(tiles):
    count = len(tiles)
    filler = [jnp.zeros((LANES - PAIR * count, CHUNK), jnp.float32)]
    return jnp.transpose(jnp.concatenate(list(tiles) + filler, axis=0))


STEP = CHUNK // SUB


def shift_rows(value, first_row):
    ends = pltpu.roll(value[CHUNK - SUB :], 1, 0)
    at = lax.broadcasted_iota(jnp.int32, ends.shape, 0)
    return jnp.concatenate([jnp.where(at == 0, first_row, ends), value[: CHUNK - SUB]], axis=0)


def unshift_rows(value, last_row):
    starts = pltpu.roll(value[:SUB], SUB - 1, 0)
    at = lax.broadcasted_iota(jnp.int32, starts.shape, 0)
    return jnp.concatenate([value[SUB:], jnp.where(at == SUB - 1, last_row, starts)], axis=0)


def to_stretches(tokens_ref, rows_ref):
    def step(c, unused):
        base = pl.multiple_of(c * CHUNK, CHUNK)
        for s in range(STEP):
            for g in range(tokens_ref.shape[0]):
                rows_ref[pl.ds(base + s * SUB, SUB), g * LANES : (g + 1) * LANES] = tokens_ref[
                    g, pl.ds(base + s, SUB, stride=STEP), :
                ]
        return unused

    lax.fori_loop(0, rows_ref.shape[0] // CHUNK, step, 0)


def to_tokens(rows_ref, tokens_ref, c):
    base = pl.multiple_of(c * CHUNK, CHUNK)
    for s in range(STEP):
        for g in range(tokens_ref.shape[0]):
            tokens_ref[g, pl.ds(base + s, SUB, stride=STEP), :] = rows_ref[
                pl.ds(base + s * SUB, SUB), g * LANES : (g + 1) * LANES
            ]


def halves(value, most):
    if isinstance(value, int):
        return value // 2
    return sum(jnp.where(value >= 2 * k, 1, 0) for k in range(1, most // 2 + 1))


def odd(value, most):
    return value - 2 * halves(value, most)


class Here:
    def __init__(self, names):
        self.names, self.at = names, {name: lax.axis_index(name) for name in names}

    def device(self, **other):
        return tuple(other.get(name, self.at[name]) for name in self.names)


class Peers:
    def __init__(self, here, count, width, passes):
        self.here, self.count, self.width, self.passes = here, count, width, passes
        self.me = here.at["tp"]
        self.others = [lax.rem(self.me + k, count) for k in range(count)]
        self.sources = [lax.rem(self.me + count - k, count) for k in range(count)]
        self.beside = jnp.minimum(self.me + 1, count - 1), jnp.maximum(self.me - 1, 0)

    def to(self, k):
        return self.others[k]

    def source(self, k):
        return self.sources[k]

    def slot(self, which):
        return odd(which, self.passes)

    def columns(self, owner):
        if isinstance(owner, int):
            return slice(owner * self.width, (owner + 1) * self.width)
        return pl.ds(pl.multiple_of(owner * self.width, LANES), self.width)

    def greet(self, others):
        barrier = pltpu.get_barrier_semaphore()
        places = [self.here.device(tp=self.to(k)) for k in range(1, self.count)] + others
        for place in places:
            pl.semaphore_signal(barrier, inc=1, device_id=place, device_id_type=MESH)
        pl.semaphore_wait(barrier, len(places))

    def copy(self, device, source_ref, target_ref, send, receive):
        return pltpu.make_async_remote_copy(
            src_ref=source_ref, dst_ref=target_ref, send_sem=send, recv_sem=receive,
            device_id=self.here.device(tp=device), device_id_type=MESH,
        )


def rows_of(c):
    return pl.ds(pl.multiple_of(c * CHUNK, CHUNK), CHUNK)


class Tiles:
    def __init__(self, peers, stat, sems):
        self.peers, self.stat, self.sems = peers, stat, sems

    def copy(self, k, c, owner):
        tile = self.stat.at[owner, c]
        return self.peers.copy(
            self.peers.to(k), tile, tile, self.sems[0].at[k - 1, c], self.sems[1].at[k - 1, c]
        )

    def start(self, c):
        for k in range(1, self.peers.count):
            self.copy(k, c, self.peers.me).start()

    def arrived(self, c):
        for k in range(1, self.peers.count):
            self.copy(k, c, self.peers.source(k)).wait_recv()

    def sent(self, c):
        for k in range(1, self.peers.count):
            self.copy(k, c, self.peers.me).wait_send()


class Gather:
    def __init__(self, peers, pay, sems):
        self.peers, self.pay, self.sems = peers, pay, sems

    def copy(self, way, hop, c, owner, which):
        slot = self.peers.slot(which)
        block = self.pay.at[slot, rows_of(c), self.peers.columns(owner)]
        device = self.peers.beside[way]
        return self.peers.copy(
            device, block, block, self.sems[0].at[slot, way, hop - 1, c], self.sems[1].at[slot, way, hop - 1, c]
        )

    def onward(self, way):
        return self.peers.me < self.peers.count - 1 if way == 0 else self.peers.me > 0

    def owner(self, way, hop):
        return self.peers.me - hop if way == 0 else self.peers.me + hop

    def comes(self, way, hop):
        owner = self.owner(way, hop)
        return owner >= 0 if way == 0 else owner < self.peers.count

    def start(self, c, which):
        for way in (0, 1):
            @pl.when(self.onward(way))
            def _():
                self.copy(way, 1, c, self.peers.me, which).start()

    def relay(self, hop, c, which):
        for way in (0, 1):
            @pl.when(self.comes(way, hop))
            def _():
                self.copy(way, hop, c, self.owner(way, hop), which).wait_recv()
                if hop < self.peers.count - 1:
                    @pl.when(self.onward(way))
                    def _():
                        self.copy(way, hop + 1, c, self.owner(way, hop), which).start()

    def sent(self, c, which):
        for way in (0, 1):
            for hop in range(1, self.peers.count):
                @pl.when(self.comes(way, hop - 1) & self.onward(way))
                def _():
                    self.copy(way, hop, c, self.owner(way, hop - 1), which).wait_send()


class Scatter:
    def __init__(self, peers, part, stage, land, sems):
        self.peers, self.part, self.stage, self.land, self.sems = peers, part, stage, land, sems

    def landing(self, way, target, owner):
        if way == 0:
            return self.peers.columns(target)
        return self.peers.columns(jnp.where(target == owner, self.peers.count, target))

    def copy(self, way, c, target, which):
        slot, device = self.peers.slot(which), self.peers.beside[way]
        return self.peers.copy(
            device, self.stage.at[rows_of(c), self.peers.columns(target)],
            self.land.at[slot, rows_of(c), self.landing(way, target, device)],
            self.sems[0].at[slot, way, target, c], self.sems[1].at[slot, way, target, c],
        )

    def come(self, way, c, target, which):
        slot, columns = self.peers.slot(which), self.landing(way, target, self.peers.me)
        block = self.land.at[slot, rows_of(c), columns]
        self.peers.copy(
            self.peers.me, block, block, self.sems[0].at[slot, way, target, c], self.sems[1].at[slot, way, target, c]
        ).wait_recv()
        return self.land[slot, rows_of(c), columns].astype(jnp.float32)

    def inward(self, way):
        return self.peers.me > 0 if way == 0 else self.peers.me < self.peers.count - 1

    def passes(self, way, target):
        return self.peers.me < target if way == 0 else self.peers.me > target

    def lag(self, way):
        return self.peers.me if way == 0 else self.peers.count - 1 - self.peers.me

    def push(self, way, c, which):
        rows = rows_of(c)
        targets = range(self.peers.count - 1, 0, -1) if way == 0 else range(self.peers.count - 1)
        for target in targets:
            columns = self.peers.columns(target)

            @pl.when(self.passes(way, target))
            def _():
                @pl.when(which > 0)
                def _():
                    self.copy(way, c, target, which - 1).wait_send()

                @pl.when(self.inward(way))
                def _():
                    self.stage[rows, columns] = (
                        self.part[rows, columns] + self.come(way, c, target, which)
                    ).astype(jnp.bfloat16)

                @pl.when(jnp.logical_not(self.inward(way)))
                def _():
                    self.stage[rows, columns] = self.part[rows, columns].astype(jnp.bfloat16)

                self.copy(way, c, target, which).start()

    def total(self, c, which):
        rows, mine = rows_of(c), self.peers.columns(self.peers.me)
        for way in (0, 1):
            @pl.when(self.inward(way))
            def _():
                self.part[rows, mine] += self.come(way, c, self.peers.me, which)
        return self.part[rows, mine]

    def sent(self, c, which):
        for target in range(self.peers.count):
            for way in (0, 1):
                @pl.when(self.passes(way, target))
                def _():
                    self.copy(way, c, target, which).wait_send()


def ticks_of(peers, chunks, passes, before, backward, begin, gather, compute, scatter):
    count = peers.count
    period = max(2 * count - 2, chunks + 1)

    def split(w, i, behind):
        early = i >= behind
        which, at = jnp.where(early, w, w - 1), jnp.where(early, i - behind, i - behind + period)
        chunk = chunks - 1 - at if backward else at
        return which, jnp.clip(chunk, 0, chunks - 1), (which >= 0) & (which < passes) & (at < chunks)

    def tick(w, i):
        which, c, there = split(w, i, 0)
        last = (w == passes) & (i < chunks)

        @pl.when(there | last)
        def _():
            begin(which, c)

        def relay(hop):
            moved, c_hop, there = split(w, i, hop)

            @pl.when(there)
            def _():
                gather.relay(hop, c_hop, moved + before)

        def push(middle):
            for way in (0, 1):
                lag = scatter.lag(way)
                moved, c_way, there = split(w, i, count - 1 + lag)

                @pl.when(there & ((lag == 1) == middle))
                def _():
                    scatter.push(way, c_way, moved + before)

        relay(count - 1)
        which, c, there = split(w, i, count - 1)

        @pl.when(there)
        def _():
            compute(which, c)

        push(False)
        for hop in range(1, count - 1):
            relay(hop)
        push(True)
    return tick


def mix_chunk(peers, c, pay, tiles, full_ref, mixed_ref, normal_ref, edge_ref, std_ref, last_ref):
    count, width = peers.count, peers.width
    tiles.arrived(c)
    columns = to_columns([tiles.stat[source, c] for source in range(count)])
    middles = [columns[:, PAIR * source : PAIR * source + 1] for source in range(count)]
    center = sum(middles) / count
    square = sum(columns[:, PAIR * source + 1 : PAIR * source + 2] for source in range(count))
    square = square + width * sum((middle - center) * (middle - center) for middle in middles)
    inv_std = lax.rsqrt(square / (count * width) + epsilon)
    std_ref[rows_of(c), :] = jnp.broadcast_to(inv_std, (CHUNK, LANES))
    for source in range(count):
        part = slice(source * width, (source + 1) * width)
        normal = (
            pay[rows_of(c), part].astype(jnp.float32) + (middles[source] - center)
        ) * inv_std
        normal_ref[rows_of(c), part] = normal.astype(jnp.bfloat16)
        normed = normal * full_ref[0:1, part] + full_ref[1:2, part]
        before = last_ref[0:1, part]
        edge_ref[pl.ds(c, 1), part] = before
        shifted = shift_rows(normed, before)
        last_ref[0:1, part] = normed[CHUNK - 1 : CHUNK]
        gap = normed - shifted
        for i in range(mixed_ref.shape[0]):
            mixed_ref[i, :, part] = (shifted + gap * full_ref[3 + i : 4 + i, part]).astype(
                jnp.bfloat16
            )


def wkv_join(left, right, fall):
    fallen = left[2] - fall
    peak = jnp.maximum(fallen, right[2])
    old, new = jnp.exp(fallen - peak), jnp.exp(right[2] - peak)
    return old * left[0] + new * right[0], old * left[1] + new * right[1], peak


def choose(mask, first, second):
    return tuple(jnp.where(mask, a, b) for a, b in zip(first, second))


def wkv_forward(base, key_ref, value_ref, decay, bonus, carry_ref, out_ref, state_ref):
    steps = STEP

    def at(s):
        return pl.ds(base + s * SUB, SUB)

    state = (value_ref[at(0), :], jnp.ones_like(decay), key_ref[at(0), :])
    for s in range(1, steps):
        key = key_ref[at(s), :]
        state = wkv_join(state, (value_ref[at(s), :], 1.0, key), decay)
    place = lax.broadcasted_iota(jnp.int32, decay.shape, 0)
    carry = tuple(carry_ref[i] for i in range(3))
    state = choose(place == 0, wkv_join(carry, state, steps * decay), state)
    for reach in (1, 2, 4):
        left = tuple(pltpu.roll(part, reach, 0) for part in state)
        state = choose(place >= reach, wkv_join(left, state, reach * steps * decay), state)
    after = tuple(pltpu.roll(part, 1, 0) for part in state)
    for i in range(3):
        carry_ref[i] = after[i]
    numer, denom, power = choose(place == 0, carry, after)
    for s in range(steps):
        key, value = key_ref[at(s), :], value_ref[at(s), :]
        lead = bonus + key
        peak = jnp.maximum(power, lead)
        old, new = jnp.exp(power - peak), jnp.exp(lead - peak)
        out_ref[at(s), :] = (old * numer + new * value) / (old * denom + new)
        state_ref[0, at(s), :] = numer
        state_ref[1, at(s), :] = denom
        state_ref[2, at(s), :] = power
        numer, denom, power = wkv_join((numer, denom, power), (value, 1.0, key), decay)


def wkv_backward(
    base, key_ref, value_ref, decay, bonus, out_ref, state_ref, up_ref, carry_ref, sum_ref, work_ref, grad_ref
):
    steps = STEP

    def at(s):
        return pl.ds(base + s * SUB, SUB)

    state = None
    for s in reversed(range(steps)):
        lead = bonus + key_ref[at(s), :]
        power = state_ref[2, at(s), :]
        peak = jnp.maximum(power, lead)
        new = jnp.exp(lead - peak)
        share = up_ref[s * SUB : (s + 1) * SUB, :] / (
            jnp.exp(power - peak) * state_ref[1, at(s), :] + new
        )
        work_ref[0, s], work_ref[1, s], work_ref[2, s] = share, peak, new * share
        here = (share, -share * out_ref[at(s), :], -peak)
        state = here if state is None else wkv_join(state, here, decay)
    place = lax.broadcasted_iota(jnp.int32, decay.shape, 0)
    carry = tuple(carry_ref[i] for i in range(3))
    state = choose(place == SUB - 1, wkv_join(carry, state, steps * decay), state)
    for reach in (1, 2, 4):
        later = tuple(pltpu.roll(part, SUB - reach, 0) for part in state)
        state = choose(place < SUB - reach, wkv_join(later, state, reach * steps * decay), state)
    after = tuple(pltpu.roll(part, SUB - 1, 0) for part in state)
    for i in range(3):
        carry_ref[i] = after[i]
    numer, denom, power = choose(place == SUB - 1, carry, after)
    for s in reversed(range(steps)):
        key, value, out = key_ref[at(s), :], value_ref[at(s), :], out_ref[at(s), :]
        share, peak, own = work_ref[0, s], work_ref[1, s], work_ref[2, s]
        reach = jnp.exp(key + power)
        direct = own * (value - out)
        grad_ref[0, s * SUB : (s + 1) * SUB, :] = direct + reach * (value * numer + denom)
        grad_ref[1, s * SUB : (s + 1) * SUB, :] = own + reach * numer
        sum_ref[1] += direct
        sum_ref[0] += jnp.exp(state_ref[2, at(s), :] + power - decay) * (
            state_ref[0, at(s), :] * numer + state_ref[1, at(s), :] * denom
        )
        numer, denom, power = wkv_join(
            (numer, denom, power), (share, -share * out, -peak), decay
        )


def load(pairs, sems, start):
    copies = [
        pltpu.make_async_copy(source, target, sems.at[start + i]) for i, (source, target) in enumerate(pairs)
    ]
    for copy in copies:
        copy.start()
    return copies


def soft_plus(value):
    small = jnp.exp(-jnp.abs(value))
    share = 1.0 / (1.0 + small)
    rest = jnp.where(small < 1e-3, small - 0.5 * small * small, jnp.log(1.0 + small))
    return jnp.maximum(value, 0.0) + rest, jnp.where(value >= 0.0, share, small * share)


def from_tokens(tokens_hbm, micro, tokens_ref, sems):
    return [
        pltpu.make_async_copy(tokens_hbm.at[micro, 0, :, pl.ds(g * LANES, LANES)], tokens_ref.at[g], sems.at[g])
        for g in range(tokens_ref.shape[0])
    ]


def to_sections(here, sections, rows_ref, tokens_ref, out_hbm, sems):
    send, receive = sems
    micro = here.at["section"]
    groups = range(tokens_ref.shape[0])

    def ends(c, source, g):
        return tokens_ref.at[g, rows_of(c)], out_hbm.at[source, 0, :, pl.ds(g * LANES, LANES)]

    def copy(c, source, g):
        held, target = ends(c, source, g)
        return pltpu.make_async_remote_copy(
            src_ref=held, dst_ref=target, send_sem=send.at[c, g], recv_sem=receive.at[source, g],
            device_id=here.device(section=c), device_id_type=MESH,
        )

    def own(g):
        return pltpu.make_async_copy(*ends(micro, micro, g), send.at[micro, g])

    def start(c):
        to_tokens(rows_ref, tokens_ref, c)

        @pl.when(c == micro)
        def _():
            for g in groups:
                own(g).start()

        @pl.when(c != micro)
        def _():
            for g in groups:
                copy(c, micro, g).start()

    def wait():
        for g in groups:
            for k in range(1, sections):
                other = lax.rem(micro + k, sections)
                copy(other, micro, g).wait_send()
                copy(other, other, g).wait_recv()
            own(g).wait()

    return start, wait


def mix_chunk_back(
    peers, c, ratios, full_ref, normal_ref, edge_ref, mixed_ref, mix_grad, later_ref, edges_ref, part_ref, tiles
):
    count = peers.count
    rows = rows_of(c)
    first = second = 0.0
    for source in range(count):
        part = peers.columns(source)
        normal = normal_ref[rows, part].astype(jnp.float32)
        gain = full_ref[0:1, part]
        normed = normal * gain + full_ref[1:2, part]
        before = shift_rows(normed, edge_ref[pl.ds(c, 1), part])
        gap = normed - before
        direct = shifted = 0.0
        for i in range(ratios):
            grad = mix_grad(i, part)
            ratio = full_ref[3 + i : 4 + i, part]
            mixed_ref[i, rows, part] = (before + gap * ratio).astype(jnp.bfloat16)
            taken = grad * ratio
            direct = direct + taken
            shifted = shifted + (grad - taken)
            edges_ref[3 + i : 4 + i, part] += jnp.sum(grad * gap, axis=0, keepdims=True)
        value = direct + unshift_rows(shifted, later_ref[0:1, part])
        later_ref[0:1, part] = shifted[0:1]
        part_ref[rows, part] = value
        scaled = value * gain
        first = first + jnp.sum(scaled, axis=1, keepdims=True)
        second = second + jnp.sum(scaled * normal, axis=1, keepdims=True)
    tiles.stat[peers.me, c] = to_row_tile(first, second)
    tiles.start(c)


STEPS = 7
COPIES = 15
EVERY = slice(None)


class Summed:
    def __init__(self, around, grad, core_land, cross_land, own_land, result, sems):
        self.grad, self.core_land, self.cross_land, self.own_land = grad, core_land, cross_land, own_land
        self.result, self.sems = result, sems
        self.lead = (EVERY,) * (len(grad.shape) - 6)
        (self.q, self.y, self.x), (self.sibling, self.over_x, self.over_y) = around

    def at(self, ref, *place):
        return ref.at[(*self.lead, *place)]

    def send(self, which, source, target, place):
        return pltpu.make_async_remote_copy(
            src_ref=source, dst_ref=target, send_sem=self.sems[0].at[which], recv_sem=self.sems[1].at[which],
            device_id=place, device_id_type=MESH,
        )

    def share(self, which, held, device, *place):
        return self.send(which, self.at(held, *place), self.at(self.result, *place), device)

    def arrive(self, which, ref, *place):
        view = self.at(ref, *place)
        self.send(which, view, view, self.sibling).wait_recv()

    def add(self, place, land, land_place):
        mine, come = self.at(self.grad, *place), self.at(land, *land_place)
        rows = mine.shape[-2]
        block = min(rows, 32)
        for k in range(3 if self.lead else 1):
            for start in range(0, rows, block):
                view = (*((k,) if self.lead else ()), slice(start, start + block), EVERY)
                mine[view] = (mine[view].astype(jnp.float32) + come[view].astype(jnp.float32)).astype(jnp.bfloat16)

    def add_half(self):
        def step(i, unused):
            y, rest = halves(halves(i, 7), 3), i - 4 * halves(halves(i, 7), 3)
            place = y, halves(rest, 3), odd(rest, 3)
            self.add((self.q, *place), self.core_land, place)
            return unused

        lax.fori_loop(0, 8, step, 0)

    def to_core(self):
        return [self.send(0, self.at(self.grad, 1 - self.q), self.core_land, self.sibling)]

    def cross(self):
        first, second = (EVERY, 1 - self.x, 0), (1 - self.y, EVERY, 1)
        return [
            self.send(1, self.at(self.grad, self.q, *first), self.at(self.cross_land, *first), self.over_x),
            self.send(2, self.at(self.grad, self.q, *second), self.at(self.cross_land, *second), self.over_y),
        ]

    def own(self):
        q, y, x = self.q, self.y, self.x
        return [
            self.send(3, self.at(self.grad, q, 1 - y, x, 0), self.at(self.own_land, 0), self.over_y),
            self.send(4, self.at(self.grad, q, y, 1 - x, 1), self.at(self.own_land, 1), self.over_x),
        ]

    def back_own(self):
        q, y, x = self.q, self.y, self.x
        return [
            self.share(5, self.grad, self.over_y, q, y, x, 0), self.share(6, self.grad, self.over_x, q, y, x, 1),
            self.share(7, self.grad, self.sibling, q, y, x),
        ]

    def back_cross(self):
        q, y, x = self.q, self.y, self.x
        return [
            self.share(8, self.result, self.over_x, q, EVERY, x, 0), self.share(9, self.result, self.over_y, q, y, EVERY, 1),
            self.share(10, self.result, self.sibling, q, 1 - y, x, 0),
            self.share(11, self.result, self.sibling, q, y, 1 - x, 1),
        ]

    def back_core(self):
        q, y, x = self.q, self.y, self.x
        return [
            self.share(12, self.result, self.sibling, q, EVERY, 1 - x, 0),
            self.share(13, self.result, self.sibling, q, 1 - y, EVERY, 1),
        ]

    def keep(self):
        place = self.q, self.y, self.x
        return pltpu.make_async_copy(self.at(self.grad, *place), self.at(self.result, *place), self.sems[0].at[14])

    def step(self, number):
        q, y, x = self.q, self.y, self.x
        started = []
        if number == 0:
            started = self.to_core()
        elif number == 1:
            self.arrive(0, self.core_land)
            self.add_half()
            started = self.cross()
        elif number == 2:
            self.arrive(1, self.cross_land, EVERY, x, 0)
            self.arrive(2, self.cross_land, y, EVERY, 1)
            for k in (0, 1):
                self.add((q, k, x, 0), self.cross_land, (k, x, 0))
                self.add((q, y, k, 1), self.cross_land, (y, k, 1))
            started = self.own()
        elif number == 3:
            for part in (0, 1):
                self.arrive(3 + part, self.own_land, part)
                self.add((q, y, x, part), self.own_land, (part,))
            started = self.back_own() + [self.keep()]
        elif number == 4:
            self.arrive(5, self.result, q, 1 - y, x, 0)
            self.arrive(6, self.result, q, y, 1 - x, 1)
            self.keep().wait()
            started = self.back_cross()
        elif number == 5:
            self.arrive(7, self.result, 1 - q, y, x)
            self.arrive(8, self.result, q, EVERY, 1 - x, 0)
            self.arrive(9, self.result, q, 1 - y, EVERY, 1)
            started = self.back_core()
        else:
            self.arrive(10, self.result, 1 - q, 1 - y, x, 0)
            self.arrive(11, self.result, 1 - q, y, 1 - x, 1)
            self.arrive(12, self.result, 1 - q, EVERY, 1 - x, 0)
            self.arrive(13, self.result, 1 - q, 1 - y, EVERY, 1)
        for copy in started:
            copy.start()

    def sent_grad(self):
        for copy in self.to_core() + self.cross() + self.own() + self.back_own():
            copy.wait_send()

    def sent_rest(self):
        for copy in self.back_cross() + self.back_core():
            copy.wait_send()


GROUPS = (
    (0, (1,), (1, 3, 5, 7, 9, 12)),
    (0, (0, 2), (0, 2, 4, 6, 8, 11)),
    (1, (3, 4), (1, 2, 4, 5, 7, 12)),
)


def both_kernel(
    names, count, sections, cores, depth,
    rows_hbm, up_hbm, lead_ref, numer_ref, denom_ref, power_ref, attend_gain, attend_bias, attend_mix, fading_ref, bonus_ref,
    feed_gain, feed_bias, feed_mix, entry_hbm, exit_hbm, key_hbm, content_hbm, gate_hbm,
    out_hbm, back_hbm, table_ref, entry_sum, exit_sum, key_sum, content_sum, gate_sum,
    normal_ref, std_ref, key_ref, value_ref, averaged_ref, state_ref, open_ref, hidden_ref, slope_ref, gate_ref, kv_ref,
    full_ref, edge_ref, rows_ref, tokens_ref, grad_ref, back_ref,
    entry_ref, exit_ref, w_key, w_content, w_gate,
    entry_grad, exit_grad, key_grad, content_grad, gate_grad,
    entry_core, exit_core, key_core, content_core, gate_core,
    entry_cross, exit_cross, key_cross, content_cross, gate_cross,
    entry_own, exit_own, key_own, content_own, gate_own,
    pay, stat, part, stage, land, mixed_ref, pre_grads, up_ref, work_ref, pair_ref, carry_ref, sum_ref,
    output_ref, hidden_grad, last_ref, later_ref, edges_ref, edge_land, small_ref,
    load_sems, token_sems, back_sems, fs, fr, os, orr, bs, br, gs, gr, ts, tr, ss, sr, es, er, ws, wr,
    table_send, table_recv,
):
    length, width = rows_ref.shape
    hidden_width = hidden_ref.shape[2]
    chunks = length // CHUNK
    passes = 2 * depth
    period = max(2 * count - 2, chunks + 1)
    here = Here(names)
    peers = Peers(here, count, width, 2 * passes)
    mine = peers.columns(peers.me)
    micro, core = here.at["section"], here.at["seq"]
    y, x = lax.div(micro, 2), lax.rem(micro, 2)
    neighbours = (
        here.device(seq=1 - core), here.device(section=micro + 1 - 2 * x), here.device(section=micro + 2 - 4 * y)
    )
    around = (core, y, x), neighbours
    first = from_tokens(rows_hbm, micro, tokens_ref, token_sems)
    second = from_tokens(up_hbm, micro, back_ref, back_sems)
    for copy in first + second:
        copy.start()
    weights = load(
        (
            (entry_hbm, entry_ref), (exit_hbm, exit_ref), (key_hbm, w_key), (content_hbm, w_content),
            (gate_hbm, w_gate),
        ),
        load_sems,
        0,
    )
    full_ref[...] = jnp.zeros_like(full_ref)
    for j in range(2 * depth):
        level = j // 2
        gain, bias, mix = (attend_gain, attend_bias, attend_mix) if j % 2 == 0 else (feed_gain, feed_bias, feed_mix)
        full_ref[j, 0:1, mine] = gain[level : level + 1, :]
        full_ref[j, 1:2, mine] = bias[level : level + 1, :]
        full_ref[j, 2:3, mine] = lead_ref[j, micro]
        for i in range(mix.shape[0] if j % 2 == 0 else mix.shape[1]):
            full_ref[j, 3 + i : 4 + i, mine] = mix[i, level : level + 1] if j % 2 == 0 else mix[level, i : i + 1]
    gather = Gather(peers, pay, (gs, gr))
    tiles = Tiles(peers, stat, (ts, tr))
    scatter = Scatter(peers, part, stage, land, (ss, sr))
    start_out, wait_out = to_sections(here, sections, rows_ref, tokens_ref, out_hbm, (os, orr))
    start_back, wait_back = to_sections(here, sections, grad_ref, back_ref, back_hbm, (bs, br))

    def full_copy(k, owner):
        block = full_ref.at[:, :, peers.columns(owner)]
        return peers.copy(peers.to(k), block, block, fs.at[k - 1], fr.at[k - 1])

    def sums(group, level):
        parts = (
            (key_grad, key_core, key_cross, key_own, key_sum),
            (content_grad, content_core, content_cross, content_own, content_sum),
            (gate_grad, gate_core, gate_cross, gate_own, gate_sum),
        )
        entry = (entry_grad, entry_core, entry_cross, entry_own, entry_sum)
        parts += (entry, (exit_grad, exit_core, exit_cross, exit_own, exit_sum))
        out = []
        for place in GROUPS[group][1]:
            grad, core_land, cross_land, own_land, result = parts[place]
            out.append(
                Summed(
                    around, grad, core_land, cross_land, own_land, result.at[level],
                    (ws.at[level, place], wr.at[level, place]),
                )
            )
        return out

    def sum_step(group, level, number):
        for matrix in sums(group, level):
            matrix.step(number)

    def table_place(k):
        return lax.rem(micro * cores + core + k, sections * cores)

    def table_copy(k, owner):
        other = table_place(k)
        return pltpu.make_async_remote_copy(
            src_ref=small_ref, dst_ref=table_ref.at[owner], send_sem=table_send.at[k - 1], recv_sem=table_recv.at[k - 1],
            device_id=here.device(section=lax.div(other, cores), seq=lax.rem(other, cores)), device_id_type=MESH,
        )

    others = [table_place(k) for k in range(1, sections * cores)]
    peers.greet([here.device(section=lax.div(other, cores), seq=lax.rem(other, cores)) for other in others])
    for k in range(1, count):
        full_copy(k, peers.me).start()
    for copy in first:
        copy.wait()
    to_stretches(tokens_ref, rows_ref)

    def begin_forward(j, c):
        rows = rows_of(c)

        @pl.when(j > 0)
        def _():
            value = scatter.total(c, j - 1)
            tiles.sent(c)

            @pl.when(odd(j, passes) == 1)
            def _():
                rows_ref[rows, :] += value

            @pl.when(odd(j, passes) == 0)
            def _():
                level = halves(j, passes) - 1
                kv_ref[level, rows, :] = value
                rows_ref[rows, :] += gate_ref[level, rows, :] * value

        @pl.when(j < 2 * depth)
        def _():
            lines = rows_ref[rows, :]
            middle = jnp.mean(lines, axis=1, keepdims=True)
            center = lines - middle
            square = jnp.sum(center * center, axis=1, keepdims=True)
            pay[odd(j, passes), rows, mine] = center.astype(jnp.bfloat16)
            tiles.stat[peers.me, c] = to_row_tile(middle, square)
            tiles.start(c)
            gather.start(c, j)

        @pl.when(j == 2 * depth)
        def _():
            start_out(c)

    def attend_forward(level, c):
        rows = rows_of(c)

        @pl.when(c == 0)
        def _():
            for i, start_ref in enumerate((numer_ref, denom_ref, power_ref)):
                carry_ref[i] = jnp.broadcast_to(start_ref[level, micro], (SUB, width))

        decay = jnp.broadcast_to(jnp.exp(fading_ref[pl.ds(level, 1), :]), (SUB, width))
        bonus = jnp.broadcast_to(bonus_ref[pl.ds(level, 1), :], (SUB, width))
        key_ref[level, rows, :] = product(mixed_ref[0, 0:CHUNK], entry_ref[level, 0])
        value_ref[level, rows, :] = product(mixed_ref[1, 0:CHUNK], entry_ref[level, 1])
        gate = jax.nn.sigmoid(product(mixed_ref[2, 0:CHUNK], entry_ref[level, 2]))
        open_ref[level, rows, :] = gate
        wkv_forward(
            pl.multiple_of(c * CHUNK, CHUNK), key_ref.at[level], value_ref.at[level], decay, bonus, carry_ref,
            averaged_ref.at[level], state_ref.at[level],
        )
        output = (gate * averaged_ref[level, rows, :]).astype(jnp.bfloat16)
        for target in range(count):
            block = peers.columns(target)
            part[rows, block] = product(output, exit_ref[level, :, block])

    def feed_forward(level, c):
        rows = rows_of(c)
        for start in range(0, hidden_ref.shape[2], width):
            block = slice(start, start + width)
            soft, slope = soft_plus(product(mixed_ref[0, 0:CHUNK], w_key[level, :, block]))
            hidden_ref[level, rows, block] = (soft * soft).astype(jnp.bfloat16)
            slope_ref[level, rows, block] = (2.0 * soft * slope).astype(jnp.bfloat16)
        for target in range(count):
            block = peers.columns(target)
            part[rows, block] = product(hidden_ref[level, rows, :], w_content[level, :, block])
        gate_ref[level, rows, :] = jax.nn.sigmoid(product(mixed_ref[1, 0:CHUNK], w_gate[level]))

    def forward(j, c):
        @pl.when((j == 0) & (c == 0))
        def _():
            for k in range(1, count):
                full_copy(k, peers.source(k)).wait_recv()
            for copy in weights:
                copy.wait()

        @pl.when(c == 0)
        def _():
            last_ref[0:1, :] = full_ref[j, 2:3, :]

        def mix(count_mixed):
            mix_chunk(
                peers, c, pay.at[odd(j, passes)], tiles, full_ref.at[j], mixed_ref.at[pl.ds(0, count_mixed), pl.ds(0, CHUNK)],
                normal_ref.at[j], edge_ref.at[j], std_ref.at[j], last_ref,
            )

        level = halves(j, passes)

        @pl.when(odd(j, passes) == 0)
        def _():
            mix(3)
            attend_forward(level, c)

        @pl.when(odd(j, passes) == 1)
        def _():
            mix(2)
            feed_forward(level, c)

        gather.sent(c, j)

    def edge_copies(j, source_of):
        return [
            peers.copy(
                peers.to(k), edges_ref.at[j, :, peers.columns(peers.to(k))], edge_land.at[j, source_of(k)],
                es.at[j, k - 1], er.at[j, k - 1],
            )
            for k in range(1, count)
        ]

    def end_pass(j, c):
        rows = rows_of(c)
        normed_grad = scatter.total(c, 2 * passes - 1 - j)
        tiles.arrived(c)
        totals = tiles.stat[0, c]
        for source in range(1, count):
            totals = totals + tiles.stat[source, c]
        columns = to_columns([totals])
        normal = normal_ref[j, rows, mine].astype(jnp.float32)
        scale = 1.0 / (count * width)
        grad_ref[rows, :] += std_ref[j, rows, 0:1] * (
            normed_grad * full_ref[j, 0:1, mine] - columns[:, 0:1] * scale - normal * (columns[:, 1:2] * scale)
        )
        small_ref[j, 0:1, :] += jnp.sum(normed_grad * normal, axis=0, keepdims=True)
        small_ref[j, 1:2, :] += jnp.sum(normed_grad, axis=0, keepdims=True)

        @pl.when(c == 0)
        def _():
            for copy in edge_copies(j, peers.source):
                copy.wait_recv()
            edges = edges_ref[j, :, mine]
            for k in range(1, count):
                edges = edges + edge_land[j, peers.source(k)]
            small_ref[j, 2:6, :] = edges[2:6]

    def begin_backward(which, c):
        rows = rows_of(c)
        j = passes - 1 - which

        @pl.when(which > 0)
        def _():
            end_pass(j + 1, c)
            gather.sent(c, passes + which - 1)
            tiles.sent(c)

        @pl.when((which < passes) & (odd(which, passes) == 0))
        def _():
            pay[odd(which, passes), rows, mine] = (grad_ref[rows, :] * gate_ref[halves(j, passes), rows, :]).astype(jnp.bfloat16)

        @pl.when((which < passes) & (odd(which, passes) == 1))
        def _():
            pay[odd(which, passes), rows, mine] = grad_ref[rows, :].astype(jnp.bfloat16)

        @pl.when(which < passes)
        def _():
            gather.start(c, passes + which)

        @pl.when(which == passes)
        def _():
            start_back(c)

    def attend_backward(j, c):
        level = halves(j, passes)
        rows = rows_of(c)
        decay = jnp.broadcast_to(jnp.exp(fading_ref[pl.ds(level, 1), :]), (SUB, width))
        bonus = jnp.broadcast_to(bonus_ref[pl.ds(level, 1), :], (SUB, width))

        @pl.when(c == chunks - 1)
        def _():
            sum_ref[...] = jnp.zeros_like(sum_ref)
            carry_ref[0] = jnp.zeros((SUB, width), jnp.float32)
            carry_ref[1] = jnp.zeros((SUB, width), jnp.float32)
            carry_ref[2] = jnp.full((SUB, width), NO_POWER, jnp.float32)

        output_grad = against(pay[1, rows, :], exit_ref[level])
        gate = open_ref[level, rows, :]
        up = output_grad * gate
        up_ref[...] = up
        averaged = averaged_ref[level, rows, :]
        pre_grads[2, rows, :] = (up * averaged * (1.0 - gate)).astype(jnp.bfloat16)
        output_ref[rows, :] = (gate * averaged).astype(jnp.bfloat16)
        wkv_backward(
            pl.multiple_of(c * CHUNK, CHUNK), key_ref.at[level], value_ref.at[level], decay, bonus,
            averaged_ref.at[level], state_ref.at[level],
            up_ref, carry_ref, sum_ref, work_ref, pair_ref,
        )
        pre_grads[0, rows, :] = pair_ref[0].astype(jnp.bfloat16)
        pre_grads[1, rows, :] = pair_ref[1].astype(jnp.bfloat16)
        mix_chunk_back(
            peers, c, 3, full_ref.at[j], normal_ref.at[j], edge_ref.at[j], mixed_ref,
            lambda i, columns: against(pre_grads[i, rows, :], entry_ref[level, i, columns, :]),
            later_ref, edges_ref.at[j], part, tiles,
        )

        @pl.when(c == 0)
        def _():
            numer, denom = carry_ref[0, SUB - 1 :, :], carry_ref[1, SUB - 1 :, :]
            lift = jnp.exp(power_ref[level, micro] + carry_ref[2, SUB - 1 :, :])
            out = passes + level
            small_ref[out, 0:1, :] = -decay[0:1] * jnp.sum(sum_ref[0], axis=0, keepdims=True)
            small_ref[out, 1:2, :] = jnp.sum(sum_ref[1], axis=0, keepdims=True)
            small_ref[out, 2:3, :] = lift * numer
            small_ref[out, 3:4, :] = lift * denom
            small_ref[out, 4:5, :] = lift * (numer_ref[level, micro] * numer + denom_ref[level, micro] * denom)

    def feed_backward(j, c):
        rows = rows_of(c)
        level = halves(j, passes)
        gate = gate_ref[level, rows, :]
        pre_grads[0, rows, :] = (grad_ref[rows, :] * gate * kv_ref[level, rows, :] * (1.0 - gate)).astype(jnp.bfloat16)
        for start in range(0, hidden_width, width):
            block = slice(start, start + width)
            into = against(pay[0, rows, :], w_content[level, block, :])
            hidden_grad[rows, block] = (into * slope_ref[level, rows, block].astype(jnp.float32)).astype(jnp.bfloat16)

        def mix_grad(i, columns):
            if i == 0:
                return against(hidden_grad[rows, :], w_key[level, columns, :])
            return against(pre_grads[0, rows, :], w_gate[level, columns, :])

        mix_chunk_back(
            peers, c, 2, full_ref.at[j], normal_ref.at[j], edge_ref.at[j], mixed_ref, mix_grad,
            later_ref, edges_ref.at[j], part, tiles,
        )

    def backward(which, c):
        j = passes - 1 - which

        @pl.when(c == chunks - 1)
        def _():
            later_ref[...] = jnp.zeros_like(later_ref)

        @pl.when(odd(which, passes) == 0)
        def _():
            feed_backward(j, c)

        @pl.when(odd(which, passes) == 1)
        def _():
            attend_backward(j, c)

        @pl.when(c == 0)
        def _():
            edges_ref[j, 2:3, :] = later_ref[0:1, :]
            for copy in edge_copies(j, lambda k: peers.me):
                copy.start()

    def weigh(place, level):
        if place == 4:
            for source in range(count):
                block = peers.columns(source)
                grad = inner_rows(output_ref[...], pay[1, :, block]).astype(jnp.bfloat16)
                exit_grad[..., block] = grad.reshape(*exit_grad.shape[:-1], width)
            return
        for i in range(4):
            at = i // 2, i % 2
            if place == 1:
                rows = hidden_width // 4
                grad = inner_rows(hidden_ref[level, :, i * rows : (i + 1) * rows], pay[0]).astype(jnp.bfloat16)
                content_grad[at] = grad.reshape(content_grad.shape[2:])
                continue
            rows = slice(i * (pay.shape[2] // 4), (i + 1) * (pay.shape[2] // 4))
            if place == 0:
                grad = inner_rows(mixed_ref[0, :, rows], hidden_grad[...]).astype(jnp.bfloat16)
                key_grad[at] = grad.reshape(key_grad.shape[2:])
            elif place == 2:
                grad = inner_rows(mixed_ref[1, :, rows], pre_grads[0]).astype(jnp.bfloat16)
                gate_grad[at] = grad.reshape(gate_grad.shape[2:])
            else:
                for k in range(3):
                    grad = inner_rows(mixed_ref[k, :, rows], pre_grads[k]).astype(jnp.bfloat16)
                    entry_grad[(k, *at)] = grad.reshape(entry_grad.shape[3:])

    base, final = chunks + count - 1, passes * period + chunks - 1

    def when_taken(group, number, t):
        kind, places, later = GROUPS[group]
        taken, chosen = False, 0
        for level in range(depth):
            now = t == base + period * kind + later[number] + 2 * period * (depth - 1 - level)
            taken, chosen = taken | now, chosen + jnp.where(now, level, 0)
        return taken, chosen

    def extra(t):
        for group in range(len(GROUPS)):
            for number in reversed(range(STEPS - 1)):
                taken, level = when_taken(group, number, t)

                @pl.when(taken)
                def _():
                    if number == 0:
                        @pl.when(level < depth - 1)
                        def _():
                            for matrix in sums(group, jnp.minimum(level + 1, depth - 1)):
                                matrix.sent_grad()

                        for place in GROUPS[group][1]:
                            weigh(place, jnp.clip(level, 0, depth - 1))
                    sum_step(group, jnp.clip(level, 0, depth - 1), number)

    forward_tick = ticks_of(peers, chunks, passes, 0, False, begin_forward, gather, forward, scatter)
    backward_tick = ticks_of(peers, chunks, passes, passes, True, begin_backward, gather, backward, scatter)
    turn = (passes - 1) * period + chunks + count - 1

    def onward(w, i):
        ends = i == period - 1
        return jnp.where(ends, w + 1, w), jnp.where(ends, 0, i + 1)

    def tick(t, places):
        ahead, behind = places

        @pl.when(t < passes * period + chunks)
        def _():
            forward_tick(*ahead)

        @pl.when(t == turn - 1)
        def _():
            for copy in second:
                copy.wait()
            to_stretches(back_ref, grad_ref)
            small_ref[...] = jnp.zeros_like(small_ref)
            edges_ref[...] = jnp.zeros_like(edges_ref)

        @pl.when(t >= turn)
        def _():
            backward_tick(*behind)
            extra(t - turn)

        moved = onward(*behind)
        return onward(*ahead), tuple(jnp.where(t >= turn, a, b) for a, b in zip(moved, behind))

    start = (jnp.int32(0), jnp.int32(0))
    lax.fori_loop(0, turn + final + 1, tick, (start, start))

    for k in range(1, sections * cores):
        table_copy(k, micro * cores + core).start()
    table_ref[micro * cores + core] = small_ref[...]
    left = []
    for group, (kind, places, later) in enumerate(GROUPS):
        for level in reversed(range(depth)):
            start = base + period * (kind + 2 * (depth - 1 - level))
            for number in range(STEPS):
                at = start + (later[number] if number < STEPS - 1 else later[-1] + 5)
                if at > final or number == STEPS - 1:
                    left.append((at, group, level, number))
    for at, group, level, number in sorted(left):
        sum_step(group, level, number)
    for c in range(chunks):
        scatter.sent(c, 2 * passes - 1)
    for j in range(passes):
        for copy in edge_copies(j, lambda k: peers.me):
            copy.wait_send()
    for group in range(len(GROUPS)):
        for level in range(depth):
            for matrix in sums(group, level):
                matrix.sent_rest()
                if level == 0:
                    matrix.sent_grad()
    for k in range(1, sections * cores):
        table_copy(k, micro * cores + core).wait_send()
        other = lax.rem(micro * cores + core + sections * cores - k, sections * cores)
        table_copy(k, other).wait_recv()
    for k in range(1, count):
        full_copy(k, peers.me).wait_send()
    wait_out()
    wait_back()


BF16, F32 = jnp.bfloat16, jnp.float32


def struct(*shape, dtype=F32):
    return jax.ShapeDtypeStruct(shape, dtype)


def run_kernel(body, collective, outs, scratch, operands, flops):
    def spec(inside):
        return pl.BlockSpec(memory_space=pltpu.VMEM if inside else pl.ANY)

    return pl.pallas_call(
        body,
        out_shape=[out for out, inside in outs],
        in_specs=[spec(inside) for operand, inside in operands],
        out_specs=[spec(inside) for out, inside in outs],
        scratch_shapes=scratch,
        compiler_params=pltpu.CompilerParams(
            collective_id=collective, has_side_effects=True, vmem_limit_bytes=63 * 1024 * 1024
        ),
        cost_estimate=pl.CostEstimate(flops=flops, bytes_accessed=2**25, transcendentals=2**23),
    )(*[operand for operand, inside in operands])


def pair_of(shape):
    return [pltpu.SemaphoreType.DMA(shape)] * 2


def run_fast(
    names, residual_entering, upstream_sensitivity, piece_lead_lines, dividend_start, divisor_start, power_offset_start,
    attend_standard_scale, attend_standard_offset, attend_lag_fractions, fading_log_rate, reward_first_word,
    attend_entry_matrix, attend_exit_matrix, feed_standard_scale, feed_standard_offset, feed_lag_fractions,
    feed_lookup_matrix, feed_content_matrix, feed_gate_matrix,
):
    count, sections, cores = (lax.axis_size(axis) for axis in ("tp", "section", "seq"))
    length, width = residual_entering.shape[2:]
    depth, features, hidden = feed_lookup_matrix.shape[0], count * width, feed_lookup_matrix.shape[2]
    chunks, subs = length // CHUNK, 2 * depth
    flops = 2 * depth * length * features * (4 * width + 2 * hidden + width)
    groups = width // LANES
    starts = (dividend_start, divisor_start, power_offset_start)
    weights = (attend_entry_matrix, attend_exit_matrix, feed_lookup_matrix, feed_content_matrix, feed_gate_matrix)
    shares = struct(sections, 1, CHUNK, width)
    lines = (depth, length, width)
    shapes = [weight.shape[1:] for weight in weights]

    def held(*shape, dtype=F32):
        return pltpu.VMEM(shape, dtype)

    def cut(*parts):
        return [(*shape[:-2], *parts, shape[-2] // 16, shape[-1]) for shape in shapes]

    outs = [(shares, False), (shares, False), (struct(sections * cores, subs + depth, SUB, width), True)]
    outs += [(struct(depth, *shape, dtype=BF16), False) for shape in cut(2, 2, 2, 2)]
    scratch = [held(subs, length, features, dtype=BF16), held(subs, length, LANES), held(*lines), held(*lines)]
    scratch += [held(*lines), held(depth, 3, *lines[1:]), held(*lines)]
    scratch += [held(depth, length, hidden, dtype=BF16)] * 2 + [held(*lines)] * 2
    scratch += [held(subs, SUB, features)] * 2 + [held(length, width), held(groups, length, LANES)] * 2
    scratch += [held(*weight.shape, dtype=BF16) for weight in weights]
    scratch += [
        held(*shape, dtype=BF16)
        for shape in cut(2, 2, 2, 2) + cut(2, 2, 2) + cut(2, 2, 2) + cut(2)
    ]
    scratch += [
        held(2, length, features, dtype=BF16), held(count, chunks, PAIR, LANES), held(length, features),
        held(length, features, dtype=BF16), held(2, length, features + width, dtype=BF16),
    ]
    scratch += [
        held(3, length, features, dtype=BF16), held(3, length, width, dtype=BF16), held(CHUNK, width),
        held(3, STEP, SUB, width), held(2, CHUNK, width), held(3, SUB, width), held(2, SUB, width),
        held(length, width, dtype=BF16), held(length, hidden, dtype=BF16), held(SUB, features), held(SUB, features),
        held(subs, SUB, features), held(subs, count, SUB, width), held(subs + depth, SUB, width),
    ]
    scratch += [pltpu.SemaphoreType.DMA((n,)) for n in (len(weights), groups, groups)] + pair_of((count - 1,))
    scratch += pair_of((sections, groups)) + pair_of((sections, groups))
    scratch += pair_of((2, 2, count - 1, chunks)) + pair_of((count - 1, chunks)) + pair_of((2, 2, count, chunks))
    scratch += pair_of((subs, count - 1)) + pair_of((depth, len(weights), COPIES))
    scratch += pair_of((sections * cores - 1,))
    operands = [(residual_entering, False), (upstream_sensitivity, False)]
    operands += [
        (value, True)
        for value in (
            piece_lead_lines, *starts, attend_standard_scale, attend_standard_offset,
            jnp.swapaxes(attend_lag_fractions, 0, 1),
            fading_log_rate, reward_first_word, feed_standard_scale, feed_standard_offset, feed_lag_fractions,
        )
    ]
    operands += [(value, False) for value in weights]
    out_share, back_share, table, *sums = run_kernel(
        partial(both_kernel, names, count, sections, cores, depth), 0, outs, scratch, operands, 3 * flops
    )
    return finish(cores, depth, out_share, back_share, table, sums, [weight.shape for weight in weights])


def finish_kernel(cores, depth, table_ref, *refs):
    wide, narrow = refs[:7], refs[7:14]
    prev, numer, denom, power = refs[14:18]
    attend_gain, attend_bias, attend_mix, decay, bonus, feed_gain, feed_bias, feed_mix = refs[18:]
    for source, target in zip(wide, narrow):
        target[...] = source[...].astype(jnp.float32)

    @pl.when(pl.program_id(0) == 0)
    def _():
        core = lax.axis_index("seq")
        places, subs = table_ref.shape[0], 2 * depth
        for m in range(places // cores):
            for j in range(subs):
                prev[j, m] = table_ref[m * cores + core, j, 2:3, :]
            for level in range(depth):
                for i, state in enumerate((numer, denom, power)):
                    state[level, m] = table_ref[m * cores + core, subs + level, 2 + i : 3 + i, :]
        for level in range(depth):
            for j, gain, bias, mix in (
                (2 * level, attend_gain, attend_bias, attend_mix), (2 * level + 1, feed_gain, feed_bias, feed_mix),
            ):
                total = sum(table_ref[place, j] for place in range(places))
                gain[level : level + 1, :] = total[0:1]
                bias[level : level + 1, :] = total[1:2]
                for i in range(mix.shape[0] if mix is attend_mix else mix.shape[1]):
                    place = (i, slice(level, level + 1)) if mix is attend_mix else (level, slice(i, i + 1))
                    mix[place] = total[3 + i : 4 + i]
            total = sum(table_ref[place, subs + level] for place in range(places))
            decay[level : level + 1, :] = total[0:1]
            bonus[level : level + 1, :] = total[1:2]


def finish(cores, depth, out_share, back_share, table, sums, shapes):
    steps = 4
    wide = [value.reshape(-1, value.shape[-1]) for value in (out_share, back_share, *sums)]
    blocks = [
        pl.BlockSpec((value.shape[0] // steps, value.shape[1]), lambda i: (i, 0)) for value in wide
    ]
    width = table.shape[-1]
    micros = table.shape[0] // cores
    small = [(2 * depth, micros, 1, width)] + [(depth, micros, 1, width)] * 3
    small += [(depth, width), (depth, width), (3, depth, width), (depth, width), (depth, width)]
    small += [(depth, width), (depth, width), (depth, 2, width)]

    def whole(shape):
        return pl.BlockSpec(shape, lambda i: (0,) * len(shape))

    got = pl.pallas_call(
        partial(finish_kernel, cores, depth),
        grid=(steps,),
        out_shape=[struct(*value.shape) for value in wide] + [struct(*shape) for shape in small],
        in_specs=[whole(table.shape)] + blocks,
        out_specs=blocks + [whole(shape) for shape in small],
        compiler_params=pltpu.CompilerParams(vmem_limit_bytes=60 * 1024 * 1024),
    )(table, *wide)
    shares = [value.reshape(whole.shape) for value, whole in zip(got, (out_share, back_share))]
    entry, leave, key, content, gate = [
        value.reshape(shape) for value, shape in zip(got[2:7], shapes)
    ]
    small = list(got[7:])
    small[6] = jnp.swapaxes(small[6], 0, 1)
    return (*shares, *small[:9], entry, leave, *small[9:], key, content, gate)


def run_plain(
    residual_entering,
    upstream_sensitivity,
    piece_lead_lines,
    dividend_start,
    divisor_start,
    power_offset_start,
    attend_standard_scale,
    attend_standard_offset,
    attend_lag_fractions,
    fading_log_rate,
    reward_first_word,
    attend_entry_matrix,
    attend_exit_matrix,
    feed_standard_scale,
    feed_standard_offset,
    feed_lag_fractions,
    feed_lookup_matrix,
    feed_content_matrix,
    feed_gate_matrix,
):
    sections = lax.axis_size("section")
    micro = lax.axis_index("section")
    length, share = residual_entering.shape[2:]
    depth = attend_entry_matrix.shape[0]

    def own(array):
        return lax.dynamic_index_in_dim(array, micro, 0, keepdims=False)

    blank = jnp.zeros((1, share), jnp.float32)
    lead = lax.dynamic_index_in_dim(piece_lead_lines[:, :, 0], micro, 1, keepdims=False)
    starts = [
        lax.dynamic_index_in_dim(start[:, :, 0], micro, 1, keepdims=False)
        for start in (dividend_start, divisor_start, power_offset_start)
    ]
    small_rows, wkv_rows = [], []
    for level in range(depth):
        for gain, bias, mix, j in (
            (attend_standard_scale, attend_standard_offset, attend_lag_fractions, 2 * level),
            (feed_standard_scale, feed_standard_offset, feed_lag_fractions, 2 * level + 1),
        ):
            rows = [gain[level][None], bias[level][None], lead[j][None], mix[level]]
            rows += [blank] * (5 - mix.shape[1])
            small_rows.append(jnp.concatenate(rows, axis=0))
        wkv_rows.append(
            jnp.stack(
                [fading_log_rate[level], reward_first_word[level]]
                + [start[level] for start in starts]
                + [blank[0]] * 3
            )
        )
    small_own = jnp.stack(small_rows)
    small_full = lax.all_gather(small_own, "tp", axis=2, tiled=True)

    rows = own(residual_entering)[0]
    kept = []
    for level in range(depth):
        for j in (2 * level, 2 * level + 1):
            if j % 2 == 0:
                rows, saved = time_forward_plain(
                    rows, small_full[j], small_own[j], wkv_rows[level],
                    attend_entry_matrix[level], attend_exit_matrix[level],
                )
            else:
                rows, saved = channel_forward_plain(
                    rows, small_full[j], small_own[j],
                    feed_lookup_matrix[level], feed_content_matrix[level], feed_gate_matrix[level],
                )
            kept.append(saved)

    def to_tokens(value):
        pieces = value.reshape(sections, length // sections, share)
        return lax.all_to_all(pieces, "section", 0, 0)[:, None]

    out_share = to_tokens(rows)
    grad = own(upstream_sensitivity)[0]
    small_grads, wkv_grads = [None] * (2 * depth), [None] * depth
    weight_grads = [None] * (2 * depth)
    summed = None
    for level in reversed(range(depth)):
        for j in (2 * level + 1, 2 * level):
            if j % 2 == 0:
                grad, small_grads[j], wkv_grads[level], weights = time_backward_plain(
                    grad, kept[j], small_full[j], small_own[j], wkv_rows[level],
                    attend_entry_matrix[level], attend_exit_matrix[level],
                )
            else:
                grad, small_grads[j], weights = channel_backward_plain(
                    grad, kept[j], small_full[j], small_own[j],
                    feed_lookup_matrix[level], feed_content_matrix[level], feed_gate_matrix[level],
                )
            weight_grads[j] = weights
        both = weight_grads[2 * level + 1], weight_grads[2 * level]
        if summed is not None:
            both, summed = lax.optimization_barrier((both, summed))
            weight_grads[2 * level + 3], weight_grads[2 * level + 2] = summed
        summed = lax.psum(both, ("section", "seq"))
    weight_grads[1], weight_grads[0] = summed
    back_share = to_tokens(grad)

    table = jnp.stack(small_grads + wkv_grads)
    tables = lax.all_gather(table, ("section", "seq"), axis=0)
    sums = [
        jnp.stack([weight_grads[2 * level + kind][place] for level in range(depth)])
        for kind, place in ((0, 0), (0, 1), (1, 0), (1, 1), (1, 2))
    ]
    return out_share, back_share, tables, sums


def per_device(names, *arrays):
    residual_entering, lookup = arrays[0], arrays[16]
    sections, cores = lax.axis_size("section"), lax.axis_size("seq")
    micros, unused, length, share = residual_entering.shape
    depth, features, hidden = lookup.shape
    fits = sections == 4 and cores == 2 and micros == sections and length == sections * CHUNK
    fits = fits and share % 256 == 0 and features % 256 == 0 and hidden % 256 == 0 and hidden % share == 0
    fits = fits and 2 < lax.axis_size("tp") <= LANES // SUB
    if fits:
        return run_fast(names, *arrays)
    out_share, back_share, table, sums = run_plain(*arrays)
    tables = table.reshape(sections, cores, *table.shape[1:])
    mine = lax.dynamic_index_in_dim(tables, lax.axis_index("seq"), 1, keepdims=False)
    total = jnp.sum(tables, axis=(0, 1))
    prev_grad = jnp.moveaxis(mine[:, : 2 * depth, 2], 0, 1)[:, :, None]
    state_grads = [jnp.moveaxis(mine[:, 2 * depth :, 2 + i], 0, 1)[:, :, None] for i in range(3)]

    weights = [grad.astype(jnp.float32) for grad in sums]
    return (
        out_share,
        back_share,
        prev_grad,
        *state_grads,
        total[0 : 2 * depth : 2, 0],
        total[0 : 2 * depth : 2, 1],
        total[0 : 2 * depth : 2, 3:6],
        total[2 * depth :, 0],
        total[2 * depth :, 1],
        weights[0],
        weights[1],
        total[1 : 2 * depth : 2, 0],
        total[1 : 2 * depth : 2, 1],
        total[1 : 2 * depth : 2, 3:5],
        weights[2],
        weights[3],
        weights[4],
    )


def solution(mesh):
    rows = P(None, "seq", None, "tp")
    line, mix = P(None, "tp"), P(None, None, "tp")
    columns, depths = P(None, None, "tp"), P(None, "tp", None)
    entry = P(None, None, None, "tp")
    state = P(None, None, "seq", "tp")
    tokens = P(None, "seq", "section", "tp")
    return jax.shard_map(
        partial(per_device, mesh.axis_names),
        mesh=mesh,
        in_specs=(
            rows, rows, state, state, state, state,
            line, line, mix, line, line, entry, depths,
            line, line, mix, columns, depths, columns,
        ),
        out_specs=(
            tokens, tokens, state, state, state, state,
            line, line, mix, line, line, entry, depths,
            line, line, mix, columns, depths, columns,
        ),
        check_vma=False,
    )
```

```python
from functools import partial

import jax
import jax.numpy as jnp
from jax import lax
from jax.experimental import pallas as pl
from jax.experimental.pallas import tpu as pltpu
from jax.sharding import PartitionSpec as P

BLOCK = 128


epsilon = 1e-05


def product(left_side, right_side):
    return jnp.dot(left_side, right_side, preferred_element_type=jnp.float32)


def inner_rows(left_side, right_side):
    return lax.dot_general(
        left_side, right_side, (((0,), (0,)), ((), ())), preferred_element_type=jnp.float32
    )


def against(left_side, right_side):
    return lax.dot_general(
        left_side, right_side, (((1,), (1,)), ((), ())), preferred_element_type=jnp.float32
    )


def weighted_value_blocks(
    block_length,
    incoming_lookups,
    incoming_contents,
    fading_entries,
    reward_entries,
    dividend_entries,
    divisor_entries,
    peak_line,
):
    decay_rate = jnp.exp(fading_entries)
    total_rows, channels = incoming_lookups.shape
    places = jnp.arange(block_length, dtype=jnp.float32)
    earlier = places[:, None] > places[None, :]
    spacing = places[:, None] - 1.0 - places[None, :]
    remain = block_length - 1.0 - places

    def advance(state_in, block_in):
        numer_in, denom_in, topmost = state_in
        lookup_piece_tile, value_block = block_in
        spread_exp = lookup_piece_tile[None, :, :] - spacing[:, :, None] * decay_rate
        spread_exp = jnp.where(earlier[:, :, None], spread_exp, -1e30)
        leading_power = reward_entries + lookup_piece_tile
        start_exp = topmost[None, :] - places[:, None] * decay_rate
        peak_exp = jnp.maximum(jnp.maximum(jnp.max(spread_exp, axis=1), leading_power), start_exp)
        weights = jnp.exp(spread_exp - peak_exp[:, None, :])
        from_state = jnp.exp(start_exp - peak_exp)
        own_term = jnp.exp(leading_power - peak_exp)
        numer_out = (
            from_state * numer_in
            + jnp.sum(weights * value_block[None, :, :], axis=1)
            + own_term * value_block
        )
        denom_out = from_state * denom_in + jnp.sum(weights, axis=1) + own_term
        ending = lookup_piece_tile - remain[:, None] * decay_rate
        stopping = topmost - block_length * decay_rate
        new_top = jnp.maximum(jnp.max(ending, axis=0), stopping)
        scaled = jnp.exp(ending - new_top[None, :])
        carried = jnp.exp(stopping - new_top)
        new_numer = carried * numer_in + jnp.sum(scaled * value_block, axis=0)
        new_denom = carried * denom_in + jnp.sum(scaled, axis=0)
        return ((new_numer, new_denom, new_top), numer_out / denom_out)

    blocks = total_rows // block_length
    unused, results = lax.scan(
        jax.checkpoint(advance),
        (dividend_entries, divisor_entries, peak_line),
        (
            incoming_lookups.reshape(blocks, block_length, channels),
            incoming_contents.reshape(blocks, block_length, channels),
        ),
    )
    return results.reshape(total_rows, channels)


def spread_plain(rows_in):
    features = rows_in.shape[1] * lax.axis_size("tp")
    mean_row = lax.psum(jnp.sum(rows_in, axis=1), "tp") / features
    center = rows_in - mean_row[:, None]
    inv_std = lax.rsqrt(lax.psum(jnp.sum(center * center, axis=1), "tp") / features + epsilon)
    normal_share = center * inv_std[:, None]
    normal_full = lax.all_gather(normal_share.astype(jnp.bfloat16), "tp", axis=1, tiled=True)
    return normal_share, inv_std, normal_full


def mix_plain(normal_full, small_full, mix_count):
    normed = normal_full.astype(jnp.float32) * small_full[0] + small_full[1]
    shifted = jnp.concatenate([small_full[2:3], normed[:-1]], axis=0)
    gap = normed - shifted
    mixed = [(shifted + gap * small_full[3 + i]).astype(jnp.bfloat16) for i in range(mix_count)]
    return mixed, gap


def scatter_plain(branch):
    return lax.psum_scatter(
        branch.astype(jnp.bfloat16), "tp", scatter_dimension=1, tiled=True
    ).astype(jnp.float32)


def time_forward_plain(rows_in, small_full, small_own, wkv_rows, entry_matrix, exit_matrix):
    normal_share, inv_std, normal_full = spread_plain(rows_in)
    mixed, gap = mix_plain(normal_full, small_full, 3)
    lookups, contents, recept = [product(mixed[i], entry_matrix[i]) for i in range(3)]
    averaged, pullback = jax.vjp(
        partial(weighted_value_blocks, BLOCK), lookups, contents, *[wkv_rows[i] for i in range(5)]
    )
    gate = jax.nn.sigmoid(recept)
    output = (gate * averaged).astype(jnp.bfloat16)
    rows_out = rows_in + scatter_plain(product(output, exit_matrix))
    kept = (normal_share, inv_std, normal_full, mixed, gap, averaged, pullback, gate, output)
    return rows_out, kept


def channel_forward_plain(rows_in, small_full, small_own, w_key, w_value, w_gate):
    normal_share, inv_std, normal_full = spread_plain(rows_in)
    mixed, gap = mix_plain(normal_full, small_full, 2)
    hidden_pre = product(mixed[0], w_key)
    soft = jax.nn.softplus(hidden_pre)
    hidden = jnp.square(soft).astype(jnp.bfloat16)
    gate = jax.nn.sigmoid(product(mixed[1], w_gate))
    kv_share = scatter_plain(product(hidden, w_value))
    kept = (normal_share, inv_std, normal_full, mixed, gap, hidden_pre, soft, hidden, gate, kv_share)
    return rows_in + gate * kv_share, kept


def norm_back_plain(rows_grad, mix_grads, gap, normal_full, normal_share, inv_std, small_full, small_own):
    share = normal_share.shape[1]
    features = small_full.shape[1]
    to_normed = sum(grad * small_full[3 + i] for i, grad in enumerate(mix_grads))
    to_shifted = sum(grad * (1.0 - small_full[3 + i]) for i, grad in enumerate(mix_grads))
    ratio_grads = [jnp.sum(grad * gap, axis=0) for grad in mix_grads]
    ratio_grads += [jnp.zeros_like(ratio_grads[0])] * (3 - len(mix_grads))
    to_normed = to_normed + jnp.concatenate([to_shifted[1:], jnp.zeros_like(to_shifted[:1])], axis=0)
    normed_grad = scatter_plain(to_normed)
    edge = lax.psum_scatter(
        jnp.stack([to_shifted[0]] + ratio_grads), "tp", scatter_dimension=1, tiled=True
    )
    scaled = normed_grad * small_own[0]
    first, second = lax.psum((jnp.sum(scaled, axis=1), jnp.sum(scaled * normal_share, axis=1)), "tp")
    rows_back = rows_grad + inv_std[:, None] * (
        scaled - first[:, None] / features - normal_share * (second[:, None] / features)
    )
    gain_grad = jnp.sum(normed_grad * normal_share, axis=0)
    bias_grad = jnp.sum(normed_grad, axis=0)
    zero = jnp.zeros((2, share), jnp.float32)
    return rows_back, jnp.concatenate([gain_grad[None], bias_grad[None], edge, zero], axis=0)


def time_backward_plain(rows_grad, kept, small_full, small_own, wkv_rows, entry_matrix, exit_matrix):
    normal_share, inv_std, normal_full, mixed, gap, averaged, pullback, gate, output = kept
    branch_grad = lax.all_gather(rows_grad.astype(jnp.bfloat16), "tp", axis=1, tiled=True)
    exit_grad = inner_rows(output, branch_grad)
    output_grad = against(branch_grad, exit_matrix)
    state_grads = pullback(output_grad * gate)
    pre_grads = [
        state_grads[0].astype(jnp.bfloat16),
        state_grads[1].astype(jnp.bfloat16),
        (output_grad * averaged * gate * (1.0 - gate)).astype(jnp.bfloat16),
    ]
    entry_grad = jnp.stack([inner_rows(mixed[i], pre_grads[i]) for i in range(3)])
    mix_grads = [against(pre_grads[i], entry_matrix[i]) for i in range(3)]
    rows_back, small_grad = norm_back_plain(
        rows_grad, mix_grads, gap, normal_full, normal_share, inv_std, small_full, small_own
    )
    wkv_grad = jnp.concatenate([jnp.stack(state_grads[2:]), jnp.zeros((3, gate.shape[1]))], axis=0)
    return rows_back, small_grad, wkv_grad, (entry_grad.astype(jnp.bfloat16), exit_grad.astype(jnp.bfloat16))


def channel_backward_plain(rows_grad, kept, small_full, small_own, w_key, w_value, w_gate):
    normal_share, inv_std, normal_full, mixed, gap, hidden_pre, soft, hidden, gate, kv_share = kept
    branch_grad = lax.all_gather((rows_grad * gate).astype(jnp.bfloat16), "tp", axis=1, tiled=True)
    value_grad = inner_rows(hidden, branch_grad)
    hidden_grad = (
        against(branch_grad, w_value) * 2.0 * soft * jax.nn.sigmoid(hidden_pre)
    ).astype(jnp.bfloat16)
    gate_grad = (rows_grad * kv_share * gate * (1.0 - gate)).astype(jnp.bfloat16)
    key_grad = inner_rows(mixed[0], hidden_grad)
    recept_grad = inner_rows(mixed[1], gate_grad)
    mix_grads = [against(hidden_grad, w_key), against(gate_grad, w_gate)]
    rows_back, small_grad = norm_back_plain(
        rows_grad, mix_grads, gap, normal_full, normal_share, inv_std, small_full, small_own
    )
    grads = tuple(grad.astype(jnp.bfloat16) for grad in (key_grad, value_grad, recept_grad))
    return rows_back, small_grad, grads


CHUNK = 128
LANES = 128
SUB = 8
PAIR = 2
MESH = pl.DeviceIdType.MESH
NO_POWER = -1e30


def to_row_tile(*columns):
    lane = lax.broadcasted_iota(jnp.int32, (CHUNK, LANES), 1)
    wide = jnp.zeros((CHUNK, LANES), jnp.float32)
    for place, column in enumerate(columns):
        wide = jnp.where(lane == place, column, wide)
    return jnp.transpose(wide)[:PAIR]


def to_columns(tiles):
    count = len(tiles)
    filler = [jnp.zeros((LANES - PAIR * count, CHUNK), jnp.float32)]
    return jnp.transpose(jnp.concatenate(list(tiles) + filler, axis=0))


STEP = CHUNK // SUB


def shift_rows(value, first_row):
    ends = pltpu.roll(value[CHUNK - SUB :], 1, 0)
    at = lax.broadcasted_iota(jnp.int32, ends.shape, 0)
    return jnp.concatenate([jnp.where(at == 0, first_row, ends), value[: CHUNK - SUB]], axis=0)


def unshift_rows(value, last_row):
    starts = pltpu.roll(value[:SUB], SUB - 1, 0)
    at = lax.broadcasted_iota(jnp.int32, starts.shape, 0)
    return jnp.concatenate([value[SUB:], jnp.where(at == SUB - 1, last_row, starts)], axis=0)


def to_stretches(tokens_ref, rows_ref):
    def step(c, unused):
        base = pl.multiple_of(c * CHUNK, CHUNK)
        for s in range(STEP):
            for g in range(tokens_ref.shape[0]):
                rows_ref[pl.ds(base + s * SUB, SUB), g * LANES : (g + 1) * LANES] = tokens_ref[
                    g, pl.ds(base + s, SUB, stride=STEP), :
                ]
        return unused

    lax.fori_loop(0, rows_ref.shape[0] // CHUNK, step, 0)


def to_tokens(rows_ref, tokens_ref, c):
    base = pl.multiple_of(c * CHUNK, CHUNK)
    for s in range(STEP):
        for g in range(tokens_ref.shape[0]):
            tokens_ref[g, pl.ds(base + s, SUB, stride=STEP), :] = rows_ref[
                pl.ds(base + s * SUB, SUB), g * LANES : (g + 1) * LANES
            ]


def halves(value, most):
    if isinstance(value, int):
        return value // 2
    return sum(jnp.where(value >= 2 * k, 1, 0) for k in range(1, most // 2 + 1))


def odd(value, most):
    return value - 2 * halves(value, most)


class Here:
    def __init__(self, names):
        self.names, self.at = names, {name: lax.axis_index(name) for name in names}

    def device(self, **other):
        return tuple(other.get(name, self.at[name]) for name in self.names)


class Peers:
    def __init__(self, here, count, width, passes):
        self.here, self.count, self.width, self.passes = here, count, width, passes
        self.me = here.at["tp"]
        self.others = [lax.rem(self.me + k, count) for k in range(count)]
        self.sources = [lax.rem(self.me + count - k, count) for k in range(count)]
        self.beside = jnp.minimum(self.me + 1, count - 1), jnp.maximum(self.me - 1, 0)

    def to(self, k):
        return self.others[k]

    def source(self, k):
        return self.sources[k]

    def slot(self, which):
        return odd(which, self.passes)

    def columns(self, owner):
        if isinstance(owner, int):
            return slice(owner * self.width, (owner + 1) * self.width)
        return pl.ds(pl.multiple_of(owner * self.width, LANES), self.width)

    def greet(self, others):
        barrier = pltpu.get_barrier_semaphore()
        places = [self.here.device(tp=self.to(k)) for k in range(1, self.count)] + others
        for place in places:
            pl.semaphore_signal(barrier, inc=1, device_id=place, device_id_type=MESH)
        pl.semaphore_wait(barrier, len(places))

    def copy(self, device, source_ref, target_ref, send, receive):
        return pltpu.make_async_remote_copy(
            src_ref=source_ref, dst_ref=target_ref, send_sem=send, recv_sem=receive,
            device_id=self.here.device(tp=device), device_id_type=MESH,
        )


def rows_of(c):
    return pl.ds(pl.multiple_of(c * CHUNK, CHUNK), CHUNK)


class Tiles:
    def __init__(self, peers, stat, sems):
        self.peers, self.stat, self.sems = peers, stat, sems

    def copy(self, k, c, owner):
        tile = self.stat.at[owner, c]
        return self.peers.copy(
            self.peers.to(k), tile, tile, self.sems[0].at[k - 1, c], self.sems[1].at[k - 1, c]
        )

    def start(self, c):
        for k in range(1, self.peers.count):
            self.copy(k, c, self.peers.me).start()

    def arrived(self, c):
        for k in range(1, self.peers.count):
            self.copy(k, c, self.peers.source(k)).wait_recv()

    def sent(self, c):
        for k in range(1, self.peers.count):
            self.copy(k, c, self.peers.me).wait_send()


class Gather:
    def __init__(self, peers, pay, sems):
        self.peers, self.pay, self.sems = peers, pay, sems

    def copy(self, way, hop, c, owner, which):
        slot = self.peers.slot(which)
        block = self.pay.at[slot, rows_of(c), self.peers.columns(owner)]
        device = self.peers.beside[way]
        return self.peers.copy(
            device, block, block, self.sems[0].at[slot, way, hop - 1, c], self.sems[1].at[slot, way, hop - 1, c]
        )

    def onward(self, way):
        return self.peers.me < self.peers.count - 1 if way == 0 else self.peers.me > 0

    def owner(self, way, hop):
        return self.peers.me - hop if way == 0 else self.peers.me + hop

    def comes(self, way, hop):
        owner = self.owner(way, hop)
        return owner >= 0 if way == 0 else owner < self.peers.count

    def start(self, c, which):
        for way in (0, 1):
            @pl.when(self.onward(way))
            def _():
                self.copy(way, 1, c, self.peers.me, which).start()

    def relay(self, hop, c, which):
        for way in (0, 1):
            @pl.when(self.comes(way, hop))
            def _():
                self.copy(way, hop, c, self.owner(way, hop), which).wait_recv()
                if hop < self.peers.count - 1:
                    @pl.when(self.onward(way))
                    def _():
                        self.copy(way, hop + 1, c, self.owner(way, hop), which).start()

    def sent(self, c, which):
        for way in (0, 1):
            for hop in range(1, self.peers.count):
                @pl.when(self.comes(way, hop - 1) & self.onward(way))
                def _():
                    self.copy(way, hop, c, self.owner(way, hop - 1), which).wait_send()


class Scatter:
    def __init__(self, peers, part, stage, land, sems):
        self.peers, self.part, self.stage, self.land, self.sems = peers, part, stage, land, sems

    def landing(self, way, target, owner):
        if way == 0:
            return self.peers.columns(target)
        return self.peers.columns(jnp.where(target == owner, self.peers.count, target))

    def copy(self, way, c, target, which):
        slot, device = self.peers.slot(which), self.peers.beside[way]
        return self.peers.copy(
            device, self.stage.at[rows_of(c), self.peers.columns(target)],
            self.land.at[slot, rows_of(c), self.landing(way, target, device)],
            self.sems[0].at[slot, way, target, c], self.sems[1].at[slot, way, target, c],
        )

    def come(self, way, c, target, which):
        slot, columns = self.peers.slot(which), self.landing(way, target, self.peers.me)
        block = self.land.at[slot, rows_of(c), columns]
        self.peers.copy(
            self.peers.me, block, block, self.sems[0].at[slot, way, target, c], self.sems[1].at[slot, way, target, c]
        ).wait_recv()
        return self.land[slot, rows_of(c), columns].astype(jnp.float32)

    def inward(self, way):
        return self.peers.me > 0 if way == 0 else self.peers.me < self.peers.count - 1

    def passes(self, way, target):
        return self.peers.me < target if way == 0 else self.peers.me > target

    def lag(self, way):
        return self.peers.me if way == 0 else self.peers.count - 1 - self.peers.me

    def push(self, way, c, which):
        rows = rows_of(c)
        targets = range(self.peers.count - 1, 0, -1) if way == 0 else range(self.peers.count - 1)
        for target in targets:
            columns = self.peers.columns(target)

            @pl.when(self.passes(way, target))
            def _():
                @pl.when(which > 0)
                def _():
                    self.copy(way, c, target, which - 1).wait_send()

                @pl.when(self.inward(way))
                def _():
                    self.stage[rows, columns] = (
                        self.part[rows, columns] + self.come(way, c, target, which)
                    ).astype(jnp.bfloat16)

                @pl.when(jnp.logical_not(self.inward(way)))
                def _():
                    self.stage[rows, columns] = self.part[rows, columns].astype(jnp.bfloat16)

                self.copy(way, c, target, which).start()

    def total(self, c, which):
        rows, mine = rows_of(c), self.peers.columns(self.peers.me)
        for way in (0, 1):
            @pl.when(self.inward(way))
            def _():
                self.part[rows, mine] += self.come(way, c, self.peers.me, which)
        return self.part[rows, mine]

    def sent(self, c, which):
        for target in range(self.peers.count):
            for way in (0, 1):
                @pl.when(self.passes(way, target))
                def _():
                    self.copy(way, c, target, which).wait_send()


def ticks_of(peers, chunks, passes, before, backward, begin, gather, compute, scatter):
    count = peers.count
    period = max(2 * count - 2, chunks + 1)

    def split(w, i, behind):
        early = i >= behind
        which, at = jnp.where(early, w, w - 1), jnp.where(early, i - behind, i - behind + period)
        chunk = chunks - 1 - at if backward else at
        return which, jnp.clip(chunk, 0, chunks - 1), (which >= 0) & (which < passes) & (at < chunks)

    def tick(w, i):
        which, c, there = split(w, i, 0)
        last = (w == passes) & (i < chunks)

        @pl.when(there | last)
        def _():
            begin(which, c)

        def relay(hop):
            moved, c_hop, there = split(w, i, hop)

            @pl.when(there)
            def _():
                gather.relay(hop, c_hop, moved + before)

        def push(middle):
            for way in (0, 1):
                lag = scatter.lag(way)
                moved, c_way, there = split(w, i, count - 1 + lag)

                @pl.when(there & ((lag == 1) == middle))
                def _():
                    scatter.push(way, c_way, moved + before)

        relay(count - 1)
        which, c, there = split(w, i, count - 1)

        @pl.when(there)
        def _():
            compute(which, c)

        push(False)
        for hop in range(1, count - 1):
            relay(hop)
        push(True)
    return tick


def mix_chunk(peers, c, pay, tiles, full_ref, mixed_ref, normal_ref, edge_ref, std_ref, last_ref):
    count, width = peers.count, peers.width
    tiles.arrived(c)
    columns = to_columns([tiles.stat[source, c] for source in range(count)])
    middles = [columns[:, PAIR * source : PAIR * source + 1] for source in range(count)]
    center = sum(middles) / count
    square = sum(columns[:, PAIR * source + 1 : PAIR * source + 2] for source in range(count))
    square = square + width * sum((middle - center) * (middle - center) for middle in middles)
    inv_std = lax.rsqrt(square / (count * width) + epsilon)
    std_ref[rows_of(c), :] = jnp.broadcast_to(inv_std, (CHUNK, LANES))
    for source in range(count):
        part = slice(source * width, (source + 1) * width)
        normal = (
            pay[rows_of(c), part].astype(jnp.float32) + (middles[source] - center)
        ) * inv_std
        normal_ref[rows_of(c), part] = normal.astype(jnp.bfloat16)
        normed = normal * full_ref[0:1, part] + full_ref[1:2, part]
        before = last_ref[0:1, part]
        edge_ref[pl.ds(c, 1), part] = before
        shifted = shift_rows(normed, before)
        last_ref[0:1, part] = normed[CHUNK - 1 : CHUNK]
        gap = normed - shifted
        for i in range(mixed_ref.shape[0]):
            mixed_ref[i, :, part] = (shifted + gap * full_ref[3 + i : 4 + i, part]).astype(
                jnp.bfloat16
            )


def wkv_join(left, right, fall):
    fallen = left[2] - fall
    peak = jnp.maximum(fallen, right[2])
    old, new = jnp.exp(fallen - peak), jnp.exp(right[2] - peak)
    return old * left[0] + new * right[0], old * left[1] + new * right[1], peak


def choose(mask, first, second):
    return tuple(jnp.where(mask, a, b) for a, b in zip(first, second))


def wkv_forward(base, key_ref, value_ref, decay, bonus, carry_ref, out_ref, state_ref):
    steps = STEP

    def at(s):
        return pl.ds(base + s * SUB, SUB)

    state = (value_ref[at(0), :], jnp.ones_like(decay), key_ref[at(0), :])
    for s in range(1, steps):
        key = key_ref[at(s), :]
        state = wkv_join(state, (value_ref[at(s), :], 1.0, key), decay)
    place = lax.broadcasted_iota(jnp.int32, decay.shape, 0)
    carry = tuple(carry_ref[i] for i in range(3))
    state = choose(place == 0, wkv_join(carry, state, steps * decay), state)
    for reach in (1, 2, 4):
        left = tuple(pltpu.roll(part, reach, 0) for part in state)
        state = choose(place >= reach, wkv_join(left, state, reach * steps * decay), state)
    after = tuple(pltpu.roll(part, 1, 0) for part in state)
    for i in range(3):
        carry_ref[i] = after[i]
    numer, denom, power = choose(place == 0, carry, after)
    for s in range(steps):
        key, value = key_ref[at(s), :], value_ref[at(s), :]
        lead = bonus + key
        peak = jnp.maximum(power, lead)
        old, new = jnp.exp(power - peak), jnp.exp(lead - peak)
        out_ref[at(s), :] = (old * numer + new * value) / (old * denom + new)
        state_ref[0, at(s), :] = numer
        state_ref[1, at(s), :] = denom
        state_ref[2, at(s), :] = power
        numer, denom, power = wkv_join((numer, denom, power), (value, 1.0, key), decay)


def wkv_backward(
    base, key_ref, value_ref, decay, bonus, out_ref, state_ref, up_ref, carry_ref, sum_ref, work_ref, grad_ref
):
    steps = STEP

    def at(s):
        return pl.ds(base + s * SUB, SUB)

    state = None
    for s in reversed(range(steps)):
        lead = bonus + key_ref[at(s), :]
        power = state_ref[2, at(s), :]
        peak = jnp.maximum(power, lead)
        new = jnp.exp(lead - peak)
        share = up_ref[s * SUB : (s + 1) * SUB, :] / (
            jnp.exp(power - peak) * state_ref[1, at(s), :] + new
        )
        work_ref[0, s], work_ref[1, s], work_ref[2, s] = share, peak, new * share
        here = (share, -share * out_ref[at(s), :], -peak)
        state = here if state is None else wkv_join(state, here, decay)
    place = lax.broadcasted_iota(jnp.int32, decay.shape, 0)
    carry = tuple(carry_ref[i] for i in range(3))
    state = choose(place == SUB - 1, wkv_join(carry, state, steps * decay), state)
    for reach in (1, 2, 4):
        later = tuple(pltpu.roll(part, SUB - reach, 0) for part in state)
        state = choose(place < SUB - reach, wkv_join(later, state, reach * steps * decay), state)
    after = tuple(pltpu.roll(part, SUB - 1, 0) for part in state)
    for i in range(3):
        carry_ref[i] = after[i]
    numer, denom, power = choose(place == SUB - 1, carry, after)
    for s in reversed(range(steps)):
        key, value, out = key_ref[at(s), :], value_ref[at(s), :], out_ref[at(s), :]
        share, peak, own = work_ref[0, s], work_ref[1, s], work_ref[2, s]
        reach = jnp.exp(key + power)
        direct = own * (value - out)
        grad_ref[0, s * SUB : (s + 1) * SUB, :] = direct + reach * (value * numer + denom)
        grad_ref[1, s * SUB : (s + 1) * SUB, :] = own + reach * numer
        sum_ref[1] += direct
        sum_ref[0] += jnp.exp(state_ref[2, at(s), :] + power - decay) * (
            state_ref[0, at(s), :] * numer + state_ref[1, at(s), :] * denom
        )
        numer, denom, power = wkv_join(
            (numer, denom, power), (share, -share * out, -peak), decay
        )


def load(pairs, sems, start):
    copies = [
        pltpu.make_async_copy(source, target, sems.at[start + i]) for i, (source, target) in enumerate(pairs)
    ]
    for copy in copies:
        copy.start()
    return copies


def soft_plus(value):
    small = jnp.exp(-jnp.abs(value))
    share = 1.0 / (1.0 + small)
    rest = jnp.where(small < 1e-3, small - 0.5 * small * small, jnp.log(1.0 + small))
    return jnp.maximum(value, 0.0) + rest, jnp.where(value >= 0.0, share, small * share)


def from_tokens(tokens_hbm, micro, tokens_ref, sems):
    return [
        pltpu.make_async_copy(tokens_hbm.at[micro, 0, :, pl.ds(g * LANES, LANES)], tokens_ref.at[g], sems.at[g])
        for g in range(tokens_ref.shape[0])
    ]


def to_sections(here, sections, rows_ref, tokens_ref, out_hbm, sems):
    send, receive = sems
    micro = here.at["section"]
    groups = range(tokens_ref.shape[0])

    def ends(c, source, g):
        return tokens_ref.at[g, rows_of(c)], out_hbm.at[source, 0, :, pl.ds(g * LANES, LANES)]

    def copy(c, source, g):
        held, target = ends(c, source, g)
        return pltpu.make_async_remote_copy(
            src_ref=held, dst_ref=target, send_sem=send.at[c, g], recv_sem=receive.at[source, g],
            device_id=here.device(section=c), device_id_type=MESH,
        )

    def own(g):
        return pltpu.make_async_copy(*ends(micro, micro, g), send.at[micro, g])

    def start(c):
        to_tokens(rows_ref, tokens_ref, c)

        @pl.when(c == micro)
        def _():
            for g in groups:
                own(g).start()

        @pl.when(c != micro)
        def _():
            for g in groups:
                copy(c, micro, g).start()

    def wait():
        for g in groups:
            for k in range(1, sections):
                other = lax.rem(micro + k, sections)
                copy(other, micro, g).wait_send()
                copy(other, other, g).wait_recv()
            own(g).wait()

    return start, wait


def mix_chunk_back(
    peers, c, ratios, full_ref, normal_ref, edge_ref, mixed_ref, mix_grad, later_ref, edges_ref, part_ref, tiles
):
    count = peers.count
    rows = rows_of(c)
    first = second = 0.0
    for source in range(count):
        part = peers.columns(source)
        normal = normal_ref[rows, part].astype(jnp.float32)
        gain = full_ref[0:1, part]
        normed = normal * gain + full_ref[1:2, part]
        before = shift_rows(normed, edge_ref[pl.ds(c, 1), part])
        gap = normed - before
        direct = shifted = 0.0
        for i in range(ratios):
            grad = mix_grad(i, part)
            ratio = full_ref[3 + i : 4 + i, part]
            mixed_ref[i, rows, part] = (before + gap * ratio).astype(jnp.bfloat16)
            taken = grad * ratio
            direct = direct + taken
            shifted = shifted + (grad - taken)
            edges_ref[3 + i : 4 + i, part] += jnp.sum(grad * gap, axis=0, keepdims=True)
        value = direct + unshift_rows(shifted, later_ref[0:1, part])
        later_ref[0:1, part] = shifted[0:1]
        part_ref[rows, part] = value
        scaled = value * gain
        first = first + jnp.sum(scaled, axis=1, keepdims=True)
        second = second + jnp.sum(scaled * normal, axis=1, keepdims=True)
    tiles.stat[peers.me, c] = to_row_tile(first, second)
    tiles.start(c)


STEPS = 7
COPIES = 15
EVERY = slice(None)


class Summed:
    def __init__(self, around, grad, core_land, cross_land, own_land, result, sems):
        self.grad, self.core_land, self.cross_land, self.own_land = grad, core_land, cross_land, own_land
        self.result, self.sems = result, sems
        self.lead = (EVERY,) * (len(grad.shape) - 6)
        (self.q, self.y, self.x), (self.sibling, self.over_x, self.over_y) = around

    def at(self, ref, *place):
        return ref.at[(*self.lead, *place)]

    def send(self, which, source, target, place):
        return pltpu.make_async_remote_copy(
            src_ref=source, dst_ref=target, send_sem=self.sems[0].at[which], recv_sem=self.sems[1].at[which],
            device_id=place, device_id_type=MESH,
        )

    def share(self, which, held, device, *place):
        return self.send(which, self.at(held, *place), self.at(self.result, *place), device)

    def arrive(self, which, ref, *place):
        view = self.at(ref, *place)
        self.send(which, view, view, self.sibling).wait_recv()

    def add(self, place, land, land_place):
        mine, come = self.at(self.grad, *place), self.at(land, *land_place)
        rows = mine.shape[-2]
        block = min(rows, 32)
        for k in range(3 if self.lead else 1):
            for start in range(0, rows, block):
                view = (*((k,) if self.lead else ()), slice(start, start + block), EVERY)
                mine[view] = (mine[view].astype(jnp.float32) + come[view].astype(jnp.float32)).astype(jnp.bfloat16)

    def add_half(self):
        def step(i, unused):
            y, rest = halves(halves(i, 7), 3), i - 4 * halves(halves(i, 7), 3)
            place = y, halves(rest, 3), odd(rest, 3)
            self.add((self.q, *place), self.core_land, place)
            return unused

        lax.fori_loop(0, 8, step, 0)

    def to_core(self):
        return [self.send(0, self.at(self.grad, 1 - self.q), self.core_land, self.sibling)]

    def cross(self):
        first, second = (EVERY, 1 - self.x, 0), (1 - self.y, EVERY, 1)
        return [
            self.send(1, self.at(self.grad, self.q, *first), self.at(self.cross_land, *first), self.over_x),
            self.send(2, self.at(self.grad, self.q, *second), self.at(self.cross_land, *second), self.over_y),
        ]

    def own(self):
        q, y, x = self.q, self.y, self.x
        return [
            self.send(3, self.at(self.grad, q, 1 - y, x, 0), self.at(self.own_land, 0), self.over_y),
            self.send(4, self.at(self.grad, q, y, 1 - x, 1), self.at(self.own_land, 1), self.over_x),
        ]

    def back_own(self):
        q, y, x = self.q, self.y, self.x
        return [
            self.share(5, self.grad, self.over_y, q, y, x, 0), self.share(6, self.grad, self.over_x, q, y, x, 1),
            self.share(7, self.grad, self.sibling, q, y, x),
        ]

    def back_cross(self):
        q, y, x = self.q, self.y, self.x
        return [
            self.share(8, self.result, self.over_x, q, EVERY, x, 0), self.share(9, self.result, self.over_y, q, y, EVERY, 1),
            self.share(10, self.result, self.sibling, q, 1 - y, x, 0),
            self.share(11, self.result, self.sibling, q, y, 1 - x, 1),
        ]

    def back_core(self):
        q, y, x = self.q, self.y, self.x
        return [
            self.share(12, self.result, self.sibling, q, EVERY, 1 - x, 0),
            self.share(13, self.result, self.sibling, q, 1 - y, EVERY, 1),
        ]

    def keep(self):
        place = self.q, self.y, self.x
        return pltpu.make_async_copy(self.at(self.grad, *place), self.at(self.result, *place), self.sems[0].at[14])

    def step(self, number):
        q, y, x = self.q, self.y, self.x
        started = []
        if number == 0:
            started = self.to_core()
        elif number == 1:
            self.arrive(0, self.core_land)
            self.add_half()
            started = self.cross()
        elif number == 2:
            self.arrive(1, self.cross_land, EVERY, x, 0)
            self.arrive(2, self.cross_land, y, EVERY, 1)
            for k in (0, 1):
                self.add((q, k, x, 0), self.cross_land, (k, x, 0))
                self.add((q, y, k, 1), self.cross_land, (y, k, 1))
            started = self.own()
        elif number == 3:
            for part in (0, 1):
                self.arrive(3 + part, self.own_land, part)
                self.add((q, y, x, part), self.own_land, (part,))
            started = self.back_own() + [self.keep()]
        elif number == 4:
            self.arrive(5, self.result, q, 1 - y, x, 0)
            self.arrive(6, self.result, q, y, 1 - x, 1)
            self.keep().wait()
            started = self.back_cross()
        elif number == 5:
            self.arrive(7, self.result, 1 - q, y, x)
            self.arrive(8, self.result, q, EVERY, 1 - x, 0)
            self.arrive(9, self.result, q, 1 - y, EVERY, 1)
            started = self.back_core()
        else:
            self.arrive(10, self.result, 1 - q, 1 - y, x, 0)
            self.arrive(11, self.result, 1 - q, y, 1 - x, 1)
            self.arrive(12, self.result, 1 - q, EVERY, 1 - x, 0)
            self.arrive(13, self.result, 1 - q, 1 - y, EVERY, 1)
        for copy in started:
            copy.start()

    def sent_grad(self):
        for copy in self.to_core() + self.cross() + self.own() + self.back_own():
            copy.wait_send()

    def sent_rest(self):
        for copy in self.back_cross() + self.back_core():
            copy.wait_send()


GROUPS = (
    (0, (1,), (1, 2, 4, 5, 6, 11)),
    (0, (0, 2), (0, 1, 3, 4, 5, 11)),
    (1, (3, 4), (1, 2, 4, 5, 6, 12)),
)


def both_kernel(
    names, count, sections, cores, depth,
    rows_hbm, up_hbm, lead_ref, numer_ref, denom_ref, power_ref, attend_gain, attend_bias, attend_mix, fading_ref, bonus_ref,
    feed_gain, feed_bias, feed_mix, entry_hbm, exit_hbm, key_hbm, content_hbm, gate_hbm,
    out_hbm, back_hbm, table_ref, entry_sum, exit_sum, key_sum, content_sum, gate_sum,
    normal_ref, std_ref, key_ref, value_ref, averaged_ref, state_ref, open_ref, hidden_ref, slope_ref, gate_ref, kv_ref,
    full_ref, edge_ref, rows_ref, tokens_ref, grad_ref, back_ref,
    entry_ref, exit_ref, w_key, w_content, w_gate,
    entry_grad, exit_grad, key_grad, content_grad, gate_grad,
    entry_core, exit_core, key_core, content_core, gate_core,
    entry_cross, exit_cross, key_cross, content_cross, gate_cross,
    entry_own, exit_own, key_own, content_own, gate_own,
    pay, stat, part, stage, land, mixed_ref, pre_grads, up_ref, work_ref, pair_ref, carry_ref, sum_ref,
    output_ref, hidden_grad, last_ref, later_ref, edges_ref, edge_land, small_ref,
    load_sems, token_sems, back_sems, fs, fr, os, orr, bs, br, gs, gr, ts, tr, ss, sr, es, er, ws, wr,
    table_send, table_recv,
):
    length, width = rows_ref.shape
    hidden_width = hidden_ref.shape[2]
    chunks = length // CHUNK
    passes = 2 * depth
    period = max(2 * count - 2, chunks + 1)
    here = Here(names)
    peers = Peers(here, count, width, 2 * passes)
    mine = peers.columns(peers.me)
    micro, core = here.at["section"], here.at["seq"]
    y, x = lax.div(micro, 2), lax.rem(micro, 2)
    neighbours = (
        here.device(seq=1 - core), here.device(section=micro + 1 - 2 * x), here.device(section=micro + 2 - 4 * y)
    )
    around = (core, y, x), neighbours
    first = from_tokens(rows_hbm, micro, tokens_ref, token_sems)
    second = from_tokens(up_hbm, micro, back_ref, back_sems)
    for copy in first:
        copy.start()
    full_ref[...] = jnp.zeros_like(full_ref)
    gather = Gather(peers, pay, (gs, gr))
    tiles = Tiles(peers, stat, (ts, tr))
    scatter = Scatter(peers, part, stage, land, (ss, sr))
    start_out, wait_out = to_sections(here, sections, rows_ref, tokens_ref, out_hbm, (os, orr))
    start_back, wait_back = to_sections(here, sections, grad_ref, back_ref, back_hbm, (bs, br))

    def full_copy(k, owner):
        block = full_ref.at[:, :, peers.columns(owner)]
        return peers.copy(peers.to(k), block, block, fs.at[k - 1], fr.at[k - 1])

    def sums(group, level):
        parts = (
            (key_grad, key_core, key_cross, key_own, key_sum),
            (content_grad, content_core, content_cross, content_own, content_sum),
            (gate_grad, gate_core, gate_cross, gate_own, gate_sum),
        )
        entry = (entry_grad, entry_core, entry_cross, entry_own, entry_sum)
        parts += (entry, (exit_grad, exit_core, exit_cross, exit_own, exit_sum))
        out = []
        for place in GROUPS[group][1]:
            grad, core_land, cross_land, own_land, result = parts[place]
            out.append(
                Summed(
                    around, grad, core_land, cross_land, own_land, result.at[level],
                    (ws.at[level, place], wr.at[level, place]),
                )
            )
        return out

    def sum_step(group, level, number):
        for matrix in sums(group, level):
            matrix.step(number)

    def table_place(k):
        return lax.rem(micro * cores + core + k, sections * cores)

    def table_copy(k, owner):
        other = table_place(k)
        return pltpu.make_async_remote_copy(
            src_ref=small_ref, dst_ref=table_ref.at[owner], send_sem=table_send.at[k - 1], recv_sem=table_recv.at[k - 1],
            device_id=here.device(section=lax.div(other, cores), seq=lax.rem(other, cores)), device_id_type=MESH,
        )

    others = [table_place(k) for k in range(1, sections * cores)]
    peers.greet([here.device(section=lax.div(other, cores), seq=lax.rem(other, cores)) for other in others])
    for j in range(2 * depth):
        level = j // 2
        gain, bias, mix = (attend_gain, attend_bias, attend_mix) if j % 2 == 0 else (feed_gain, feed_bias, feed_mix)
        full_ref[j, 0:1, mine] = gain[level : level + 1, :]
        full_ref[j, 1:2, mine] = bias[level : level + 1, :]
        full_ref[j, 2:3, mine] = lead_ref[j, micro]
        for i in range(mix.shape[0] if j % 2 == 0 else mix.shape[1]):
            full_ref[j, 3 + i : 4 + i, mine] = mix[i, level : level + 1] if j % 2 == 0 else mix[level, i : i + 1]
    for k in range(1, count):
        full_copy(k, peers.me).start()
    for copy in first:
        copy.wait()
    weights = load(
        (
            (entry_hbm, entry_ref), (exit_hbm, exit_ref), (key_hbm, w_key), (content_hbm, w_content),
            (gate_hbm, w_gate),
        ),
        load_sems,
        0,
    )
    for copy in second:
        copy.start()
    to_stretches(tokens_ref, rows_ref)

    def begin_forward(j, c):
        rows = rows_of(c)

        @pl.when(j > 0)
        def _():
            value = scatter.total(c, j - 1)
            tiles.sent(c)

            @pl.when(odd(j, passes) == 1)
            def _():
                rows_ref[rows, :] += value

            @pl.when(odd(j, passes) == 0)
            def _():
                level = halves(j, passes) - 1
                kv_ref[level, rows, :] = value
                rows_ref[rows, :] += gate_ref[level, rows, :] * value

        @pl.when(j < 2 * depth)
        def _():
            lines = rows_ref[rows, :]
            middle = jnp.mean(lines, axis=1, keepdims=True)
            center = lines - middle
            square = jnp.sum(center * center, axis=1, keepdims=True)
            pay[odd(j, passes), rows, mine] = center.astype(jnp.bfloat16)
            tiles.stat[peers.me, c] = to_row_tile(middle, square)
            tiles.start(c)
            gather.start(c, j)

        @pl.when(j == 2 * depth)
        def _():
            start_out(c)

    def attend_forward(level, c):
        rows = rows_of(c)

        @pl.when(c == 0)
        def _():
            for i, start_ref in enumerate((numer_ref, denom_ref, power_ref)):
                carry_ref[i] = jnp.broadcast_to(start_ref[level, micro], (SUB, width))

        decay = jnp.broadcast_to(jnp.exp(fading_ref[pl.ds(level, 1), :]), (SUB, width))
        bonus = jnp.broadcast_to(bonus_ref[pl.ds(level, 1), :], (SUB, width))
        key_ref[level, rows, :] = product(mixed_ref[0, 0:CHUNK], entry_ref[level, 0])
        value_ref[level, rows, :] = product(mixed_ref[1, 0:CHUNK], entry_ref[level, 1])
        gate = jax.nn.sigmoid(product(mixed_ref[2, 0:CHUNK], entry_ref[level, 2]))
        open_ref[level, rows, :] = gate
        wkv_forward(
            pl.multiple_of(c * CHUNK, CHUNK), key_ref.at[level], value_ref.at[level], decay, bonus, carry_ref,
            averaged_ref.at[level], state_ref.at[level],
        )
        output = (gate * averaged_ref[level, rows, :]).astype(jnp.bfloat16)
        for target in range(count):
            block = peers.columns(target)
            part[rows, block] = product(output, exit_ref[level, :, block])

    def feed_forward(level, c):
        rows = rows_of(c)
        for start in range(0, hidden_ref.shape[2], width):
            block = slice(start, start + width)
            soft, slope = soft_plus(product(mixed_ref[0, 0:CHUNK], w_key[level, :, block]))
            hidden_ref[level, rows, block] = (soft * soft).astype(jnp.bfloat16)
            slope_ref[level, rows, block] = (2.0 * soft * slope).astype(jnp.bfloat16)
        for target in range(count):
            block = peers.columns(target)
            part[rows, block] = product(hidden_ref[level, rows, :], w_content[level, :, block])
        gate_ref[level, rows, :] = jax.nn.sigmoid(product(mixed_ref[1, 0:CHUNK], w_gate[level]))

    def forward(j, c):
        @pl.when((j == 0) & (c == 0))
        def _():
            for k in range(1, count):
                full_copy(k, peers.source(k)).wait_recv()
            for copy in weights:
                copy.wait()

        @pl.when(c == 0)
        def _():
            last_ref[0:1, :] = full_ref[j, 2:3, :]

        def mix(count_mixed):
            mix_chunk(
                peers, c, pay.at[odd(j, passes)], tiles, full_ref.at[j], mixed_ref.at[pl.ds(0, count_mixed), pl.ds(0, CHUNK)],
                normal_ref.at[j], edge_ref.at[j], std_ref.at[j], last_ref,
            )

        level = halves(j, passes)

        @pl.when(odd(j, passes) == 0)
        def _():
            mix(3)
            attend_forward(level, c)

        @pl.when(odd(j, passes) == 1)
        def _():
            mix(2)
            feed_forward(level, c)

        gather.sent(c, j)

    def edge_copies(j, source_of):
        return [
            peers.copy(
                peers.to(k), edges_ref.at[j, :, peers.columns(peers.to(k))], edge_land.at[j, source_of(k)],
                es.at[j, k - 1], er.at[j, k - 1],
            )
            for k in range(1, count)
        ]

    def end_pass(j, c):
        rows = rows_of(c)
        normed_grad = scatter.total(c, 2 * passes - 1 - j)
        tiles.arrived(c)
        totals = tiles.stat[0, c]
        for source in range(1, count):
            totals = totals + tiles.stat[source, c]
        columns = to_columns([totals])
        normal = normal_ref[j, rows, mine].astype(jnp.float32)
        scale = 1.0 / (count * width)
        grad_ref[rows, :] += std_ref[j, rows, 0:1] * (
            normed_grad * full_ref[j, 0:1, mine] - columns[:, 0:1] * scale - normal * (columns[:, 1:2] * scale)
        )
        small_ref[j, 0:1, :] += jnp.sum(normed_grad * normal, axis=0, keepdims=True)
        small_ref[j, 1:2, :] += jnp.sum(normed_grad, axis=0, keepdims=True)

        @pl.when(c == 0)
        def _():
            for copy in edge_copies(j, peers.source):
                copy.wait_recv()
            edges = edges_ref[j, :, mine]
            for k in range(1, count):
                edges = edges + edge_land[j, peers.source(k)]
            small_ref[j, 2:6, :] = edges[2:6]

    def begin_backward(which, c):
        rows = rows_of(c)
        j = passes - 1 - which

        @pl.when(which > 0)
        def _():
            end_pass(j + 1, c)
            gather.sent(c, passes + which - 1)
            tiles.sent(c)

        @pl.when((which < passes) & (odd(which, passes) == 0))
        def _():
            pay[odd(which, passes), rows, mine] = (grad_ref[rows, :] * gate_ref[halves(j, passes), rows, :]).astype(jnp.bfloat16)

        @pl.when((which < passes) & (odd(which, passes) == 1))
        def _():
            pay[odd(which, passes), rows, mine] = grad_ref[rows, :].astype(jnp.bfloat16)

        @pl.when(which < passes)
        def _():
            gather.start(c, passes + which)

        @pl.when(which == passes)
        def _():
            start_back(c)

    def attend_backward(j, c):
        level = halves(j, passes)
        rows = rows_of(c)
        decay = jnp.broadcast_to(jnp.exp(fading_ref[pl.ds(level, 1), :]), (SUB, width))
        bonus = jnp.broadcast_to(bonus_ref[pl.ds(level, 1), :], (SUB, width))

        @pl.when(c == chunks - 1)
        def _():
            sum_ref[...] = jnp.zeros_like(sum_ref)
            carry_ref[0] = jnp.zeros((SUB, width), jnp.float32)
            carry_ref[1] = jnp.zeros((SUB, width), jnp.float32)
            carry_ref[2] = jnp.full((SUB, width), NO_POWER, jnp.float32)

        output_grad = against(pay[1, rows, :], exit_ref[level])
        gate = open_ref[level, rows, :]
        up = output_grad * gate
        up_ref[...] = up
        averaged = averaged_ref[level, rows, :]
        pre_grads[2, rows, :] = (up * averaged * (1.0 - gate)).astype(jnp.bfloat16)
        output_ref[rows, :] = (gate * averaged).astype(jnp.bfloat16)
        wkv_backward(
            pl.multiple_of(c * CHUNK, CHUNK), key_ref.at[level], value_ref.at[level], decay, bonus,
            averaged_ref.at[level], state_ref.at[level],
            up_ref, carry_ref, sum_ref, work_ref, pair_ref,
        )
        pre_grads[0, rows, :] = pair_ref[0].astype(jnp.bfloat16)
        pre_grads[1, rows, :] = pair_ref[1].astype(jnp.bfloat16)
        mix_chunk_back(
            peers, c, 3, full_ref.at[j], normal_ref.at[j], edge_ref.at[j], mixed_ref,
            lambda i, columns: against(pre_grads[i, rows, :], entry_ref[level, i, columns, :]),
            later_ref, edges_ref.at[j], part, tiles,
        )

        @pl.when(c == 0)
        def _():
            numer, denom = carry_ref[0, SUB - 1 :, :], carry_ref[1, SUB - 1 :, :]
            lift = jnp.exp(power_ref[level, micro] + carry_ref[2, SUB - 1 :, :])
            out = passes + level
            small_ref[out, 0:1, :] = -decay[0:1] * jnp.sum(sum_ref[0], axis=0, keepdims=True)
            small_ref[out, 1:2, :] = jnp.sum(sum_ref[1], axis=0, keepdims=True)
            small_ref[out, 2:3, :] = lift * numer
            small_ref[out, 3:4, :] = lift * denom
            small_ref[out, 4:5, :] = lift * (numer_ref[level, micro] * numer + denom_ref[level, micro] * denom)

    def feed_backward(j, c):
        rows = rows_of(c)
        level = halves(j, passes)
        gate = gate_ref[level, rows, :]
        pre_grads[0, rows, :] = (grad_ref[rows, :] * gate * kv_ref[level, rows, :] * (1.0 - gate)).astype(jnp.bfloat16)
        for start in range(0, hidden_width, width):
            block = slice(start, start + width)
            into = against(pay[0, rows, :], w_content[level, block, :])
            hidden_grad[rows, block] = (into * slope_ref[level, rows, block].astype(jnp.float32)).astype(jnp.bfloat16)

        def mix_grad(i, columns):
            if i == 0:
                return against(hidden_grad[rows, :], w_key[level, columns, :])
            return against(pre_grads[0, rows, :], w_gate[level, columns, :])

        mix_chunk_back(
            peers, c, 2, full_ref.at[j], normal_ref.at[j], edge_ref.at[j], mixed_ref, mix_grad,
            later_ref, edges_ref.at[j], part, tiles,
        )

    def backward(which, c):
        j = passes - 1 - which

        @pl.when(c == chunks - 1)
        def _():
            later_ref[...] = jnp.zeros_like(later_ref)

        @pl.when(odd(which, passes) == 0)
        def _():
            feed_backward(j, c)

        @pl.when(odd(which, passes) == 1)
        def _():
            attend_backward(j, c)

        @pl.when(c == 0)
        def _():
            edges_ref[j, 2:3, :] = later_ref[0:1, :]
            for copy in edge_copies(j, lambda k: peers.me):
                copy.start()

    def weigh(place, level):
        if place == 4:
            for source in range(count):
                block = peers.columns(source)
                grad = inner_rows(output_ref[...], pay[1, :, block]).astype(jnp.bfloat16)
                exit_grad[..., block] = grad.reshape(*exit_grad.shape[:-1], width)
            return
        for i in range(4):
            at = i // 2, i % 2
            if place == 1:
                rows = hidden_width // 4
                grad = inner_rows(hidden_ref[level, :, i * rows : (i + 1) * rows], pay[0]).astype(jnp.bfloat16)
                content_grad[at] = grad.reshape(content_grad.shape[2:])
                continue
            rows = slice(i * (pay.shape[2] // 4), (i + 1) * (pay.shape[2] // 4))
            if place == 0:
                grad = inner_rows(mixed_ref[0, :, rows], hidden_grad[...]).astype(jnp.bfloat16)
                key_grad[at] = grad.reshape(key_grad.shape[2:])
            elif place == 2:
                grad = inner_rows(mixed_ref[1, :, rows], pre_grads[0]).astype(jnp.bfloat16)
                gate_grad[at] = grad.reshape(gate_grad.shape[2:])
            else:
                for k in range(3):
                    grad = inner_rows(mixed_ref[k, :, rows], pre_grads[k]).astype(jnp.bfloat16)
                    entry_grad[(k, *at)] = grad.reshape(entry_grad.shape[3:])

    base, final = chunks + count - 1, passes * period + chunks - 1

    def when_taken(group, number, t):
        kind, places, later = GROUPS[group]
        taken, chosen = False, 0
        for level in range(depth):
            now = t == base + period * kind + later[number] + 2 * period * (depth - 1 - level)
            taken, chosen = taken | now, chosen + jnp.where(now, level, 0)
        return taken, chosen

    def extra(t):
        for group in range(len(GROUPS)):
            for number in reversed(range(STEPS - 1)):
                taken, level = when_taken(group, number, t)

                @pl.when(taken)
                def _():
                    if number == 0:
                        @pl.when(level < depth - 1)
                        def _():
                            for matrix in sums(group, jnp.minimum(level + 1, depth - 1)):
                                matrix.sent_grad()

                        for place in GROUPS[group][1]:
                            weigh(place, jnp.clip(level, 0, depth - 1))
                    sum_step(group, jnp.clip(level, 0, depth - 1), number)

    forward_tick = ticks_of(peers, chunks, passes, 0, False, begin_forward, gather, forward, scatter)
    backward_tick = ticks_of(peers, chunks, passes, passes, True, begin_backward, gather, backward, scatter)
    turn = (passes - 1) * period + chunks + count - 2

    def onward(w, i):
        ends = i == period - 1
        return jnp.where(ends, w + 1, w), jnp.where(ends, 0, i + 1)

    def tick(t, places):
        ahead, behind = places

        @pl.when(t < passes * period + chunks)
        def _():
            forward_tick(*ahead)

        @pl.when(t == turn - 1)
        def _():
            for copy in second:
                copy.wait()
            to_stretches(back_ref, grad_ref)
            small_ref[...] = jnp.zeros_like(small_ref)
            edges_ref[...] = jnp.zeros_like(edges_ref)

        @pl.when(t >= turn)
        def _():
            backward_tick(*behind)
            extra(t - turn)

        moved = onward(*behind)
        return onward(*ahead), tuple(jnp.where(t >= turn, a, b) for a, b in zip(moved, behind))

    start = (jnp.int32(0), jnp.int32(0))
    lax.fori_loop(0, turn + final + 1, tick, (start, start))

    for k in range(1, sections * cores):
        table_copy(k, micro * cores + core).start()
    table_ref[micro * cores + core] = small_ref[...]
    left = []
    for group, (kind, places, later) in enumerate(GROUPS):
        for level in reversed(range(depth)):
            start = base + period * (kind + 2 * (depth - 1 - level))
            for number in range(STEPS):
                at = start + (later[number] if number < STEPS - 1 else later[-1] + 5)
                if at > final or number == STEPS - 1:
                    left.append((at, group, level, number))
    for at, group, level, number in sorted(left):
        sum_step(group, level, number)
    for c in range(chunks):
        scatter.sent(c, 2 * passes - 1)
    for j in range(passes):
        for copy in edge_copies(j, lambda k: peers.me):
            copy.wait_send()
    for group in range(len(GROUPS)):
        for level in range(depth):
            for matrix in sums(group, level):
                matrix.sent_rest()
                if level == 0:
                    matrix.sent_grad()
    for k in range(1, sections * cores):
        table_copy(k, micro * cores + core).wait_send()
        other = lax.rem(micro * cores + core + sections * cores - k, sections * cores)
        table_copy(k, other).wait_recv()
    for k in range(1, count):
        full_copy(k, peers.me).wait_send()
    wait_out()
    wait_back()


BF16, F32 = jnp.bfloat16, jnp.float32


def struct(*shape, dtype=F32):
    return jax.ShapeDtypeStruct(shape, dtype)


def run_kernel(body, collective, outs, scratch, operands, flops):
    def spec(inside):
        return pl.BlockSpec(memory_space=pltpu.VMEM if inside else pl.ANY)

    return pl.pallas_call(
        body,
        out_shape=[out for out, inside in outs],
        in_specs=[spec(inside) for operand, inside in operands],
        out_specs=[spec(inside) for out, inside in outs],
        scratch_shapes=scratch,
        compiler_params=pltpu.CompilerParams(
            collective_id=collective, has_side_effects=True, vmem_limit_bytes=63 * 1024 * 1024
        ),
        cost_estimate=pl.CostEstimate(flops=flops, bytes_accessed=2**25, transcendentals=2**23),
    )(*[operand for operand, inside in operands])


def pair_of(shape):
    return [pltpu.SemaphoreType.DMA(shape)] * 2


def run_fast(
    names, residual_entering, upstream_sensitivity, piece_lead_lines, dividend_start, divisor_start, power_offset_start,
    attend_standard_scale, attend_standard_offset, attend_lag_fractions, fading_log_rate, reward_first_word,
    attend_entry_matrix, attend_exit_matrix, feed_standard_scale, feed_standard_offset, feed_lag_fractions,
    feed_lookup_matrix, feed_content_matrix, feed_gate_matrix,
):
    count, sections, cores = (lax.axis_size(axis) for axis in ("tp", "section", "seq"))
    length, width = residual_entering.shape[2:]
    depth, features, hidden = feed_lookup_matrix.shape[0], count * width, feed_lookup_matrix.shape[2]
    chunks, subs = length // CHUNK, 2 * depth
    flops = 2 * depth * length * features * (4 * width + 2 * hidden + width)
    groups = width // LANES
    starts = (dividend_start, divisor_start, power_offset_start)
    weights = (attend_entry_matrix, attend_exit_matrix, feed_lookup_matrix, feed_content_matrix, feed_gate_matrix)
    shares = struct(sections, 1, CHUNK, width)
    lines = (depth, length, width)
    shapes = [weight.shape[1:] for weight in weights]

    def held(*shape, dtype=F32):
        return pltpu.VMEM(shape, dtype)

    def cut(*parts):
        return [(*shape[:-2], *parts, shape[-2] // 16, shape[-1]) for shape in shapes]

    outs = [(shares, False), (shares, False), (struct(sections * cores, subs + depth, SUB, width), True)]
    outs += [(struct(depth, *shape, dtype=BF16), False) for shape in cut(2, 2, 2, 2)]
    scratch = [held(subs, length, features, dtype=BF16), held(subs, length, LANES), held(*lines), held(*lines)]
    scratch += [held(*lines), held(depth, 3, *lines[1:]), held(*lines)]
    scratch += [held(depth, length, hidden, dtype=BF16)] * 2 + [held(*lines)] * 2
    scratch += [held(subs, SUB, features)] * 2 + [held(length, width), held(groups, length, LANES)] * 2
    scratch += [held(*weight.shape, dtype=BF16) for weight in weights]
    scratch += [
        held(*shape, dtype=BF16)
        for shape in cut(2, 2, 2, 2) + cut(2, 2, 2) + cut(2, 2, 2) + cut(2)
    ]
    scratch += [
        held(2, length, features, dtype=BF16), held(count, chunks, PAIR, LANES), held(length, features),
        held(length, features, dtype=BF16), held(2, length, features + width, dtype=BF16),
    ]
    scratch += [
        held(3, length, features, dtype=BF16), held(3, length, width, dtype=BF16), held(CHUNK, width),
        held(3, STEP, SUB, width), held(2, CHUNK, width), held(3, SUB, width), held(2, SUB, width),
        held(length, width, dtype=BF16), held(length, hidden, dtype=BF16), held(SUB, features), held(SUB, features),
        held(subs, SUB, features), held(subs, count, SUB, width), held(subs + depth, SUB, width),
    ]
    scratch += [pltpu.SemaphoreType.DMA((n,)) for n in (len(weights), groups, groups)] + pair_of((count - 1,))
    scratch += pair_of((sections, groups)) + pair_of((sections, groups))
    scratch += pair_of((2, 2, count - 1, chunks)) + pair_of((count - 1, chunks)) + pair_of((2, 2, count, chunks))
    scratch += pair_of((subs, count - 1)) + pair_of((depth, len(weights), COPIES))
    scratch += pair_of((sections * cores - 1,))
    operands = [(residual_entering, False), (upstream_sensitivity, False)]
    operands += [
        (value, True)
        for value in (
            piece_lead_lines, *starts, attend_standard_scale, attend_standard_offset,
            jnp.swapaxes(attend_lag_fractions, 0, 1),
            fading_log_rate, reward_first_word, feed_standard_scale, feed_standard_offset, feed_lag_fractions,
        )
    ]
    operands += [(value, False) for value in weights]
    out_share, back_share, table, *sums = run_kernel(
        partial(both_kernel, names, count, sections, cores, depth), 0, outs, scratch, operands, 3 * flops
    )
    return finish(cores, depth, out_share, back_share, table, sums, [weight.shape for weight in weights])


def finish_kernel(cores, depth, table_ref, *refs):
    wide, narrow = refs[:7], refs[7:14]
    prev, numer, denom, power = refs[14:18]
    attend_gain, attend_bias, attend_mix, decay, bonus, feed_gain, feed_bias, feed_mix = refs[18:]
    for source, target in zip(wide, narrow):
        target[...] = source[...].astype(jnp.float32)

    @pl.when(pl.program_id(0) == 0)
    def _():
        core = lax.axis_index("seq")
        places, subs = table_ref.shape[0], 2 * depth
        for m in range(places // cores):
            for j in range(subs):
                prev[j, m] = table_ref[m * cores + core, j, 2:3, :]
            for level in range(depth):
                for i, state in enumerate((numer, denom, power)):
                    state[level, m] = table_ref[m * cores + core, subs + level, 2 + i : 3 + i, :]
        for level in range(depth):
            for j, gain, bias, mix in (
                (2 * level, attend_gain, attend_bias, attend_mix), (2 * level + 1, feed_gain, feed_bias, feed_mix),
            ):
                total = sum(table_ref[place, j] for place in range(places))
                gain[level : level + 1, :] = total[0:1]
                bias[level : level + 1, :] = total[1:2]
                for i in range(mix.shape[0] if mix is attend_mix else mix.shape[1]):
                    place = (i, slice(level, level + 1)) if mix is attend_mix else (level, slice(i, i + 1))
                    mix[place] = total[3 + i : 4 + i]
            total = sum(table_ref[place, subs + level] for place in range(places))
            decay[level : level + 1, :] = total[0:1]
            bonus[level : level + 1, :] = total[1:2]


def finish(cores, depth, out_share, back_share, table, sums, shapes):
    steps = 4
    wide = [value.reshape(-1, value.shape[-1]) for value in (out_share, back_share, *sums)]
    blocks = [
        pl.BlockSpec((value.shape[0] // steps, value.shape[1]), lambda i: (i, 0)) for value in wide
    ]
    width = table.shape[-1]
    micros = table.shape[0] // cores
    small = [(2 * depth, micros, 1, width)] + [(depth, micros, 1, width)] * 3
    small += [(depth, width), (depth, width), (3, depth, width), (depth, width), (depth, width)]
    small += [(depth, width), (depth, width), (depth, 2, width)]

    def whole(shape):
        return pl.BlockSpec(shape, lambda i: (0,) * len(shape))

    got = pl.pallas_call(
        partial(finish_kernel, cores, depth),
        grid=(steps,),
        out_shape=[struct(*value.shape) for value in wide] + [struct(*shape) for shape in small],
        in_specs=[whole(table.shape)] + blocks,
        out_specs=blocks + [whole(shape) for shape in small],
        compiler_params=pltpu.CompilerParams(vmem_limit_bytes=60 * 1024 * 1024),
    )(table, *wide)
    shares = [value.reshape(whole.shape) for value, whole in zip(got, (out_share, back_share))]
    entry, leave, key, content, gate = [
        value.reshape(shape) for value, shape in zip(got[2:7], shapes)
    ]
    small = list(got[7:])
    small[6] = jnp.swapaxes(small[6], 0, 1)
    return (*shares, *small[:9], entry, leave, *small[9:], key, content, gate)


def run_plain(
    residual_entering,
    upstream_sensitivity,
    piece_lead_lines,
    dividend_start,
    divisor_start,
    power_offset_start,
    attend_standard_scale,
    attend_standard_offset,
    attend_lag_fractions,
    fading_log_rate,
    reward_first_word,
    attend_entry_matrix,
    attend_exit_matrix,
    feed_standard_scale,
    feed_standard_offset,
    feed_lag_fractions,
    feed_lookup_matrix,
    feed_content_matrix,
    feed_gate_matrix,
):
    sections = lax.axis_size("section")
    micro = lax.axis_index("section")
    length, share = residual_entering.shape[2:]
    depth = attend_entry_matrix.shape[0]

    def own(array):
        return lax.dynamic_index_in_dim(array, micro, 0, keepdims=False)

    blank = jnp.zeros((1, share), jnp.float32)
    lead = lax.dynamic_index_in_dim(piece_lead_lines[:, :, 0], micro, 1, keepdims=False)
    starts = [
        lax.dynamic_index_in_dim(start[:, :, 0], micro, 1, keepdims=False)
        for start in (dividend_start, divisor_start, power_offset_start)
    ]
    small_rows, wkv_rows = [], []
    for level in range(depth):
        for gain, bias, mix, j in (
            (attend_standard_scale, attend_standard_offset, attend_lag_fractions, 2 * level),
            (feed_standard_scale, feed_standard_offset, feed_lag_fractions, 2 * level + 1),
        ):
            rows = [gain[level][None], bias[level][None], lead[j][None], mix[level]]
            rows += [blank] * (5 - mix.shape[1])
            small_rows.append(jnp.concatenate(rows, axis=0))
        wkv_rows.append(
            jnp.stack(
                [fading_log_rate[level], reward_first_word[level]]
                + [start[level] for start in starts]
                + [blank[0]] * 3
            )
        )
    small_own = jnp.stack(small_rows)
    small_full = lax.all_gather(small_own, "tp", axis=2, tiled=True)

    rows = own(residual_entering)[0]
    kept = []
    for level in range(depth):
        for j in (2 * level, 2 * level + 1):
            if j % 2 == 0:
                rows, saved = time_forward_plain(
                    rows, small_full[j], small_own[j], wkv_rows[level],
                    attend_entry_matrix[level], attend_exit_matrix[level],
                )
            else:
                rows, saved = channel_forward_plain(
                    rows, small_full[j], small_own[j],
                    feed_lookup_matrix[level], feed_content_matrix[level], feed_gate_matrix[level],
                )
            kept.append(saved)

    def to_tokens(value):
        pieces = value.reshape(sections, length // sections, share)
        return lax.all_to_all(pieces, "section", 0, 0)[:, None]

    out_share = to_tokens(rows)
    grad = own(upstream_sensitivity)[0]
    small_grads, wkv_grads = [None] * (2 * depth), [None] * depth
    weight_grads = [None] * (2 * depth)
    summed = None
    for level in reversed(range(depth)):
        for j in (2 * level + 1, 2 * level):
            if j % 2 == 0:
                grad, small_grads[j], wkv_grads[level], weights = time_backward_plain(
                    grad, kept[j], small_full[j], small_own[j], wkv_rows[level],
                    attend_entry_matrix[level], attend_exit_matrix[level],
                )
            else:
                grad, small_grads[j], weights = channel_backward_plain(
                    grad, kept[j], small_full[j], small_own[j],
                    feed_lookup_matrix[level], feed_content_matrix[level], feed_gate_matrix[level],
                )
            weight_grads[j] = weights
        both = weight_grads[2 * level + 1], weight_grads[2 * level]
        if summed is not None:
            both, summed = lax.optimization_barrier((both, summed))
            weight_grads[2 * level + 3], weight_grads[2 * level + 2] = summed
        summed = lax.psum(both, ("section", "seq"))
    weight_grads[1], weight_grads[0] = summed
    back_share = to_tokens(grad)

    table = jnp.stack(small_grads + wkv_grads)
    tables = lax.all_gather(table, ("section", "seq"), axis=0)
    sums = [
        jnp.stack([weight_grads[2 * level + kind][place] for level in range(depth)])
        for kind, place in ((0, 0), (0, 1), (1, 0), (1, 1), (1, 2))
    ]
    return out_share, back_share, tables, sums


def per_device(names, *arrays):
    residual_entering, lookup = arrays[0], arrays[16]
    sections, cores = lax.axis_size("section"), lax.axis_size("seq")
    micros, unused, length, share = residual_entering.shape
    depth, features, hidden = lookup.shape
    fits = sections == 4 and cores == 2 and micros == sections and length == sections * CHUNK
    fits = fits and share % 256 == 0 and features % 256 == 0 and hidden % 256 == 0 and hidden % share == 0
    fits = fits and 2 < lax.axis_size("tp") <= LANES // SUB
    if fits:
        return run_fast(names, *arrays)
    out_share, back_share, table, sums = run_plain(*arrays)
    tables = table.reshape(sections, cores, *table.shape[1:])
    mine = lax.dynamic_index_in_dim(tables, lax.axis_index("seq"), 1, keepdims=False)
    total = jnp.sum(tables, axis=(0, 1))
    prev_grad = jnp.moveaxis(mine[:, : 2 * depth, 2], 0, 1)[:, :, None]
    state_grads = [jnp.moveaxis(mine[:, 2 * depth :, 2 + i], 0, 1)[:, :, None] for i in range(3)]

    weights = [grad.astype(jnp.float32) for grad in sums]
    return (
        out_share,
        back_share,
        prev_grad,
        *state_grads,
        total[0 : 2 * depth : 2, 0],
        total[0 : 2 * depth : 2, 1],
        total[0 : 2 * depth : 2, 3:6],
        total[2 * depth :, 0],
        total[2 * depth :, 1],
        weights[0],
        weights[1],
        total[1 : 2 * depth : 2, 0],
        total[1 : 2 * depth : 2, 1],
        total[1 : 2 * depth : 2, 3:5],
        weights[2],
        weights[3],
        weights[4],
    )


def solution(mesh):
    rows = P(None, "seq", None, "tp")
    line, mix = P(None, "tp"), P(None, None, "tp")
    columns, depths = P(None, None, "tp"), P(None, "tp", None)
    entry = P(None, None, None, "tp")
    state = P(None, None, "seq", "tp")
    tokens = P(None, "seq", "section", "tp")
    return jax.shard_map(
        partial(per_device, mesh.axis_names),
        mesh=mesh,
        in_specs=(
            rows, rows, state, state, state, state,
            line, line, mix, line, line, entry, depths,
            line, line, mix, columns, depths, columns,
        ),
        out_specs=(
            tokens, tokens, state, state, state, state,
            line, line, mix, line, line, entry, depths,
            line, line, mix, columns, depths, columns,
        ),
        check_vma=False,
    )
```

```python
from functools import partial

import jax
import jax.numpy as jnp
from jax import lax
from jax.experimental import pallas as pl
from jax.experimental.pallas import tpu as pltpu
from jax.sharding import PartitionSpec as P

BLOCK = 128


epsilon = 1e-05


def product(left_side, right_side):
    return jnp.dot(left_side, right_side, preferred_element_type=jnp.float32)


def inner_rows(left_side, right_side):
    return lax.dot_general(
        left_side, right_side, (((0,), (0,)), ((), ())), preferred_element_type=jnp.float32
    )


def against(left_side, right_side):
    return lax.dot_general(
        left_side, right_side, (((1,), (1,)), ((), ())), preferred_element_type=jnp.float32
    )


def weighted_value_blocks(
    block_length,
    incoming_lookups,
    incoming_contents,
    fading_entries,
    reward_entries,
    dividend_entries,
    divisor_entries,
    peak_line,
):
    decay_rate = jnp.exp(fading_entries)
    total_rows, channels = incoming_lookups.shape
    places = jnp.arange(block_length, dtype=jnp.float32)
    earlier = places[:, None] > places[None, :]
    spacing = places[:, None] - 1.0 - places[None, :]
    remain = block_length - 1.0 - places

    def advance(state_in, block_in):
        numer_in, denom_in, topmost = state_in
        lookup_piece_tile, value_block = block_in
        spread_exp = lookup_piece_tile[None, :, :] - spacing[:, :, None] * decay_rate
        spread_exp = jnp.where(earlier[:, :, None], spread_exp, -1e30)
        leading_power = reward_entries + lookup_piece_tile
        start_exp = topmost[None, :] - places[:, None] * decay_rate
        peak_exp = jnp.maximum(jnp.maximum(jnp.max(spread_exp, axis=1), leading_power), start_exp)
        weights = jnp.exp(spread_exp - peak_exp[:, None, :])
        from_state = jnp.exp(start_exp - peak_exp)
        own_term = jnp.exp(leading_power - peak_exp)
        numer_out = (
            from_state * numer_in
            + jnp.sum(weights * value_block[None, :, :], axis=1)
            + own_term * value_block
        )
        denom_out = from_state * denom_in + jnp.sum(weights, axis=1) + own_term
        ending = lookup_piece_tile - remain[:, None] * decay_rate
        stopping = topmost - block_length * decay_rate
        new_top = jnp.maximum(jnp.max(ending, axis=0), stopping)
        scaled = jnp.exp(ending - new_top[None, :])
        carried = jnp.exp(stopping - new_top)
        new_numer = carried * numer_in + jnp.sum(scaled * value_block, axis=0)
        new_denom = carried * denom_in + jnp.sum(scaled, axis=0)
        return ((new_numer, new_denom, new_top), numer_out / denom_out)

    blocks = total_rows // block_length
    unused, results = lax.scan(
        jax.checkpoint(advance),
        (dividend_entries, divisor_entries, peak_line),
        (
            incoming_lookups.reshape(blocks, block_length, channels),
            incoming_contents.reshape(blocks, block_length, channels),
        ),
    )
    return results.reshape(total_rows, channels)


def spread_plain(rows_in):
    features = rows_in.shape[1] * lax.axis_size("tp")
    mean_row = lax.psum(jnp.sum(rows_in, axis=1), "tp") / features
    center = rows_in - mean_row[:, None]
    inv_std = lax.rsqrt(lax.psum(jnp.sum(center * center, axis=1), "tp") / features + epsilon)
    normal_share = center * inv_std[:, None]
    normal_full = lax.all_gather(normal_share.astype(jnp.bfloat16), "tp", axis=1, tiled=True)
    return normal_share, inv_std, normal_full


def mix_plain(normal_full, small_full, mix_count):
    normed = normal_full.astype(jnp.float32) * small_full[0] + small_full[1]
    shifted = jnp.concatenate([small_full[2:3], normed[:-1]], axis=0)
    gap = normed - shifted
    mixed = [(shifted + gap * small_full[3 + i]).astype(jnp.bfloat16) for i in range(mix_count)]
    return mixed, gap


def scatter_plain(branch):
    return lax.psum_scatter(
        branch.astype(jnp.bfloat16), "tp", scatter_dimension=1, tiled=True
    ).astype(jnp.float32)


def time_forward_plain(rows_in, small_full, small_own, wkv_rows, entry_matrix, exit_matrix):
    normal_share, inv_std, normal_full = spread_plain(rows_in)
    mixed, gap = mix_plain(normal_full, small_full, 3)
    lookups, contents, recept = [product(mixed[i], entry_matrix[i]) for i in range(3)]
    averaged, pullback = jax.vjp(
        partial(weighted_value_blocks, BLOCK), lookups, contents, *[wkv_rows[i] for i in range(5)]
    )
    gate = jax.nn.sigmoid(recept)
    output = (gate * averaged).astype(jnp.bfloat16)
    rows_out = rows_in + scatter_plain(product(output, exit_matrix))
    kept = (normal_share, inv_std, normal_full, mixed, gap, averaged, pullback, gate, output)
    return rows_out, kept


def channel_forward_plain(rows_in, small_full, small_own, w_key, w_value, w_gate):
    normal_share, inv_std, normal_full = spread_plain(rows_in)
    mixed, gap = mix_plain(normal_full, small_full, 2)
    hidden_pre = product(mixed[0], w_key)
    soft = jax.nn.softplus(hidden_pre)
    hidden = jnp.square(soft).astype(jnp.bfloat16)
    gate = jax.nn.sigmoid(product(mixed[1], w_gate))
    kv_share = scatter_plain(product(hidden, w_value))
    kept = (normal_share, inv_std, normal_full, mixed, gap, hidden_pre, soft, hidden, gate, kv_share)
    return rows_in + gate * kv_share, kept


def norm_back_plain(rows_grad, mix_grads, gap, normal_full, normal_share, inv_std, small_full, small_own):
    share = normal_share.shape[1]
    features = small_full.shape[1]
    to_normed = sum(grad * small_full[3 + i] for i, grad in enumerate(mix_grads))
    to_shifted = sum(grad * (1.0 - small_full[3 + i]) for i, grad in enumerate(mix_grads))
    ratio_grads = [jnp.sum(grad * gap, axis=0) for grad in mix_grads]
    ratio_grads += [jnp.zeros_like(ratio_grads[0])] * (3 - len(mix_grads))
    to_normed = to_normed + jnp.concatenate([to_shifted[1:], jnp.zeros_like(to_shifted[:1])], axis=0)
    normed_grad = scatter_plain(to_normed)
    edge = lax.psum_scatter(
        jnp.stack([to_shifted[0]] + ratio_grads), "tp", scatter_dimension=1, tiled=True
    )
    scaled = normed_grad * small_own[0]
    first, second = lax.psum((jnp.sum(scaled, axis=1), jnp.sum(scaled * normal_share, axis=1)), "tp")
    rows_back = rows_grad + inv_std[:, None] * (
        scaled - first[:, None] / features - normal_share * (second[:, None] / features)
    )
    gain_grad = jnp.sum(normed_grad * normal_share, axis=0)
    bias_grad = jnp.sum(normed_grad, axis=0)
    zero = jnp.zeros((2, share), jnp.float32)
    return rows_back, jnp.concatenate([gain_grad[None], bias_grad[None], edge, zero], axis=0)


def time_backward_plain(rows_grad, kept, small_full, small_own, wkv_rows, entry_matrix, exit_matrix):
    normal_share, inv_std, normal_full, mixed, gap, averaged, pullback, gate, output = kept
    branch_grad = lax.all_gather(rows_grad.astype(jnp.bfloat16), "tp", axis=1, tiled=True)
    exit_grad = inner_rows(output, branch_grad)
    output_grad = against(branch_grad, exit_matrix)
    state_grads = pullback(output_grad * gate)
    pre_grads = [
        state_grads[0].astype(jnp.bfloat16),
        state_grads[1].astype(jnp.bfloat16),
        (output_grad * averaged * gate * (1.0 - gate)).astype(jnp.bfloat16),
    ]
    entry_grad = jnp.stack([inner_rows(mixed[i], pre_grads[i]) for i in range(3)])
    mix_grads = [against(pre_grads[i], entry_matrix[i]) for i in range(3)]
    rows_back, small_grad = norm_back_plain(
        rows_grad, mix_grads, gap, normal_full, normal_share, inv_std, small_full, small_own
    )
    wkv_grad = jnp.concatenate([jnp.stack(state_grads[2:]), jnp.zeros((3, gate.shape[1]))], axis=0)
    return rows_back, small_grad, wkv_grad, (entry_grad.astype(jnp.bfloat16), exit_grad.astype(jnp.bfloat16))


def channel_backward_plain(rows_grad, kept, small_full, small_own, w_key, w_value, w_gate):
    normal_share, inv_std, normal_full, mixed, gap, hidden_pre, soft, hidden, gate, kv_share = kept
    branch_grad = lax.all_gather((rows_grad * gate).astype(jnp.bfloat16), "tp", axis=1, tiled=True)
    value_grad = inner_rows(hidden, branch_grad)
    hidden_grad = (
        against(branch_grad, w_value) * 2.0 * soft * jax.nn.sigmoid(hidden_pre)
    ).astype(jnp.bfloat16)
    gate_grad = (rows_grad * kv_share * gate * (1.0 - gate)).astype(jnp.bfloat16)
    key_grad = inner_rows(mixed[0], hidden_grad)
    recept_grad = inner_rows(mixed[1], gate_grad)
    mix_grads = [against(hidden_grad, w_key), against(gate_grad, w_gate)]
    rows_back, small_grad = norm_back_plain(
        rows_grad, mix_grads, gap, normal_full, normal_share, inv_std, small_full, small_own
    )
    grads = tuple(grad.astype(jnp.bfloat16) for grad in (key_grad, value_grad, recept_grad))
    return rows_back, small_grad, grads


CHUNK = 128
LANES = 128
SUB = 8
PAIR = 2
MESH = pl.DeviceIdType.MESH
NO_POWER = -1e30


def to_row_tile(*columns):
    lane = lax.broadcasted_iota(jnp.int32, (CHUNK, LANES), 1)
    wide = jnp.zeros((CHUNK, LANES), jnp.float32)
    for place, column in enumerate(columns):
        wide = jnp.where(lane == place, column, wide)
    return jnp.transpose(wide)[:PAIR]


def to_columns(tiles):
    count = len(tiles)
    filler = [jnp.zeros((LANES - PAIR * count, CHUNK), jnp.float32)]
    return jnp.transpose(jnp.concatenate(list(tiles) + filler, axis=0))


STEP = CHUNK // SUB


def shift_rows(value, first_row):
    ends = pltpu.roll(value[CHUNK - SUB :], 1, 0)
    at = lax.broadcasted_iota(jnp.int32, ends.shape, 0)
    return jnp.concatenate([jnp.where(at == 0, first_row, ends), value[: CHUNK - SUB]], axis=0)


def unshift_rows(value, last_row):
    starts = pltpu.roll(value[:SUB], SUB - 1, 0)
    at = lax.broadcasted_iota(jnp.int32, starts.shape, 0)
    return jnp.concatenate([value[SUB:], jnp.where(at == SUB - 1, last_row, starts)], axis=0)


def to_stretches(tokens_ref, rows_ref):
    def step(c, unused):
        base = pl.multiple_of(c * CHUNK, CHUNK)
        for s in range(STEP):
            for g in range(tokens_ref.shape[0]):
                rows_ref[pl.ds(base + s * SUB, SUB), g * LANES : (g + 1) * LANES] = tokens_ref[
                    g, pl.ds(base + s, SUB, stride=STEP), :
                ]
        return unused

    lax.fori_loop(0, rows_ref.shape[0] // CHUNK, step, 0)


def to_tokens(rows_ref, tokens_ref, c):
    base = pl.multiple_of(c * CHUNK, CHUNK)
    for s in range(STEP):
        for g in range(tokens_ref.shape[0]):
            tokens_ref[g, pl.ds(base + s, SUB, stride=STEP), :] = rows_ref[
                pl.ds(base + s * SUB, SUB), g * LANES : (g + 1) * LANES
            ]


def halves(value, most):
    if isinstance(value, int):
        return value // 2
    return sum(jnp.where(value >= 2 * k, 1, 0) for k in range(1, most // 2 + 1))


def odd(value, most):
    return value - 2 * halves(value, most)


class Here:
    def __init__(self, names):
        self.names, self.at = names, {name: lax.axis_index(name) for name in names}

    def device(self, **other):
        return tuple(other.get(name, self.at[name]) for name in self.names)


class Peers:
    def __init__(self, here, count, width, passes):
        self.here, self.count, self.width, self.passes = here, count, width, passes
        self.me = here.at["tp"]
        self.others = [lax.rem(self.me + k, count) for k in range(count)]
        self.sources = [lax.rem(self.me + count - k, count) for k in range(count)]
        self.beside = jnp.minimum(self.me + 1, count - 1), jnp.maximum(self.me - 1, 0)

    def to(self, k):
        return self.others[k]

    def source(self, k):
        return self.sources[k]

    def slot(self, which):
        return odd(which, self.passes)

    def columns(self, owner):
        if isinstance(owner, int):
            return slice(owner * self.width, (owner + 1) * self.width)
        return pl.ds(pl.multiple_of(owner * self.width, LANES), self.width)

    def greet(self, others):
        barrier = pltpu.get_barrier_semaphore()
        places = [self.here.device(tp=self.to(k)) for k in range(1, self.count)] + others
        for place in places:
            pl.semaphore_signal(barrier, inc=1, device_id=place, device_id_type=MESH)
        pl.semaphore_wait(barrier, len(places))

    def copy(self, device, source_ref, target_ref, send, receive):
        return pltpu.make_async_remote_copy(
            src_ref=source_ref, dst_ref=target_ref, send_sem=send, recv_sem=receive,
            device_id=self.here.device(tp=device), device_id_type=MESH,
        )


def rows_of(c):
    return pl.ds(pl.multiple_of(c * CHUNK, CHUNK), CHUNK)


class Tiles:
    def __init__(self, peers, stat, sems):
        self.peers, self.stat, self.sems = peers, stat, sems

    def copy(self, k, c, owner):
        tile = self.stat.at[owner, c]
        return self.peers.copy(
            self.peers.to(k), tile, tile, self.sems[0].at[k - 1, c], self.sems[1].at[k - 1, c]
        )

    def start(self, c):
        for k in range(1, self.peers.count):
            self.copy(k, c, self.peers.me).start()

    def arrived(self, c):
        for k in range(1, self.peers.count):
            self.copy(k, c, self.peers.source(k)).wait_recv()

    def sent(self, c):
        for k in range(1, self.peers.count):
            self.copy(k, c, self.peers.me).wait_send()


class Gather:
    def __init__(self, peers, pay, sems):
        self.peers, self.pay, self.sems = peers, pay, sems

    def copy(self, way, hop, c, owner, which):
        slot = self.peers.slot(which)
        block = self.pay.at[slot, rows_of(c), self.peers.columns(owner)]
        device = self.peers.beside[way]
        return self.peers.copy(
            device, block, block, self.sems[0].at[slot, way, hop - 1, c], self.sems[1].at[slot, way, hop - 1, c]
        )

    def onward(self, way):
        return self.peers.me < self.peers.count - 1 if way == 0 else self.peers.me > 0

    def owner(self, way, hop):
        return self.peers.me - hop if way == 0 else self.peers.me + hop

    def comes(self, way, hop):
        owner = self.owner(way, hop)
        return owner >= 0 if way == 0 else owner < self.peers.count

    def start(self, c, which):
        for way in (0, 1):
            @pl.when(self.onward(way))
            def _():
                self.copy(way, 1, c, self.peers.me, which).start()

    def relay(self, hop, c, which):
        for way in (0, 1):
            @pl.when(self.comes(way, hop))
            def _():
                self.copy(way, hop, c, self.owner(way, hop), which).wait_recv()
                if hop < self.peers.count - 1:
                    @pl.when(self.onward(way))
                    def _():
                        self.copy(way, hop + 1, c, self.owner(way, hop), which).start()

    def sent(self, c, which):
        for way in (0, 1):
            for hop in range(1, self.peers.count):
                @pl.when(self.comes(way, hop - 1) & self.onward(way))
                def _():
                    self.copy(way, hop, c, self.owner(way, hop - 1), which).wait_send()


class Scatter:
    def __init__(self, peers, part, stage, land, sems):
        self.peers, self.part, self.stage, self.land, self.sems = peers, part, stage, land, sems

    def landing(self, way, target, owner):
        if way == 0:
            return self.peers.columns(target)
        return self.peers.columns(jnp.where(target == owner, self.peers.count, target))

    def copy(self, way, c, target, which):
        slot, device = self.peers.slot(which), self.peers.beside[way]
        return self.peers.copy(
            device, self.stage.at[rows_of(c), self.peers.columns(target)],
            self.land.at[slot, rows_of(c), self.landing(way, target, device)],
            self.sems[0].at[slot, way, target, c], self.sems[1].at[slot, way, target, c],
        )

    def come(self, way, c, target, which):
        slot, columns = self.peers.slot(which), self.landing(way, target, self.peers.me)
        block = self.land.at[slot, rows_of(c), columns]
        self.peers.copy(
            self.peers.me, block, block, self.sems[0].at[slot, way, target, c], self.sems[1].at[slot, way, target, c]
        ).wait_recv()
        return self.land[slot, rows_of(c), columns].astype(jnp.float32)

    def inward(self, way):
        return self.peers.me > 0 if way == 0 else self.peers.me < self.peers.count - 1

    def passes(self, way, target):
        return self.peers.me < target if way == 0 else self.peers.me > target

    def lag(self, way):
        return self.peers.me if way == 0 else self.peers.count - 1 - self.peers.me

    def push(self, way, c, which):
        rows = rows_of(c)
        targets = range(self.peers.count - 1, 0, -1) if way == 0 else range(self.peers.count - 1)
        for target in targets:
            columns = self.peers.columns(target)

            @pl.when(self.passes(way, target))
            def _():
                @pl.when(which > 0)
                def _():
                    self.copy(way, c, target, which - 1).wait_send()

                @pl.when(self.inward(way))
                def _():
                    self.stage[rows, columns] = (
                        self.part[rows, columns] + self.come(way, c, target, which)
                    ).astype(jnp.bfloat16)

                @pl.when(jnp.logical_not(self.inward(way)))
                def _():
                    self.stage[rows, columns] = self.part[rows, columns].astype(jnp.bfloat16)

                self.copy(way, c, target, which).start()

    def total(self, c, which):
        rows, mine = rows_of(c), self.peers.columns(self.peers.me)
        for way in (0, 1):
            @pl.when(self.inward(way))
            def _():
                self.part[rows, mine] += self.come(way, c, self.peers.me, which)
        return self.part[rows, mine]

    def sent(self, c, which):
        for target in range(self.peers.count):
            for way in (0, 1):
                @pl.when(self.passes(way, target))
                def _():
                    self.copy(way, c, target, which).wait_send()


def ticks_of(peers, chunks, passes, before, backward, begin, gather, compute, scatter):
    count = peers.count
    period = max(2 * count - 2, chunks + 1)

    def split(w, i, behind):
        early = i >= behind
        which, at = jnp.where(early, w, w - 1), jnp.where(early, i - behind, i - behind + period)
        chunk = chunks - 1 - at if backward else at
        return which, jnp.clip(chunk, 0, chunks - 1), (which >= 0) & (which < passes) & (at < chunks)

    def tick(w, i):
        which, c, there = split(w, i, 0)
        last = (w == passes) & (i < chunks)

        @pl.when(there | last)
        def _():
            begin(which, c)

        def relay(hop):
            moved, c_hop, there = split(w, i, hop)

            @pl.when(there)
            def _():
                gather.relay(hop, c_hop, moved + before)

        def push(middle):
            for way in (0, 1):
                lag = scatter.lag(way)
                moved, c_way, there = split(w, i, count - 1 + lag)

                @pl.when(there & ((lag == 1) == middle))
                def _():
                    scatter.push(way, c_way, moved + before)

        relay(count - 1)
        which, c, there = split(w, i, count - 1)

        @pl.when(there)
        def _():
            compute(which, c)

        push(False)
        for hop in range(1, count - 1):
            relay(hop)
        push(True)
    return tick


def mix_chunk(peers, c, pay, tiles, full_ref, mixed_ref, normal_ref, edge_ref, std_ref, last_ref):
    count, width = peers.count, peers.width
    tiles.arrived(c)
    columns = to_columns([tiles.stat[source, c] for source in range(count)])
    middles = [columns[:, PAIR * source : PAIR * source + 1] for source in range(count)]
    center = sum(middles) / count
    square = sum(columns[:, PAIR * source + 1 : PAIR * source + 2] for source in range(count))
    square = square + width * sum((middle - center) * (middle - center) for middle in middles)
    inv_std = lax.rsqrt(square / (count * width) + epsilon)
    std_ref[rows_of(c), :] = jnp.broadcast_to(inv_std, (CHUNK, LANES))
    for source in range(count):
        part = slice(source * width, (source + 1) * width)
        normal = (
            pay[rows_of(c), part].astype(jnp.float32) + (middles[source] - center)
        ) * inv_std
        normal_ref[rows_of(c), part] = normal.astype(jnp.bfloat16)
        normed = normal * full_ref[0:1, part] + full_ref[1:2, part]
        before = last_ref[0:1, part]
        edge_ref[pl.ds(c, 1), part] = before
        shifted = shift_rows(normed, before)
        last_ref[0:1, part] = normed[CHUNK - 1 : CHUNK]
        gap = normed - shifted
        for i in range(mixed_ref.shape[0]):
            mixed_ref[i, :, part] = (shifted + gap * full_ref[3 + i : 4 + i, part]).astype(
                jnp.bfloat16
            )


def wkv_join(left, right, fall):
    fallen = left[2] - fall
    peak = jnp.maximum(fallen, right[2])
    old, new = jnp.exp(fallen - peak), jnp.exp(right[2] - peak)
    return old * left[0] + new * right[0], old * left[1] + new * right[1], peak


def choose(mask, first, second):
    return tuple(jnp.where(mask, a, b) for a, b in zip(first, second))


def wkv_forward(base, key_ref, value_ref, decay, bonus, carry_ref, out_ref, state_ref):
    steps = STEP

    def at(s):
        return pl.ds(base + s * SUB, SUB)

    state = (value_ref[at(0), :], jnp.ones_like(decay), key_ref[at(0), :])
    for s in range(1, steps):
        key = key_ref[at(s), :]
        state = wkv_join(state, (value_ref[at(s), :], 1.0, key), decay)
    place = lax.broadcasted_iota(jnp.int32, decay.shape, 0)
    carry = tuple(carry_ref[i] for i in range(3))
    state = choose(place == 0, wkv_join(carry, state, steps * decay), state)
    for reach in (1, 2, 4):
        left = tuple(pltpu.roll(part, reach, 0) for part in state)
        state = choose(place >= reach, wkv_join(left, state, reach * steps * decay), state)
    after = tuple(pltpu.roll(part, 1, 0) for part in state)
    for i in range(3):
        carry_ref[i] = after[i]
    numer, denom, power = choose(place == 0, carry, after)
    for s in range(steps):
        key, value = key_ref[at(s), :], value_ref[at(s), :]
        lead = bonus + key
        peak = jnp.maximum(power, lead)
        old, new = jnp.exp(power - peak), jnp.exp(lead - peak)
        out_ref[at(s), :] = (old * numer + new * value) / (old * denom + new)
        state_ref[0, at(s), :] = numer
        state_ref[1, at(s), :] = denom
        state_ref[2, at(s), :] = power
        numer, denom, power = wkv_join((numer, denom, power), (value, 1.0, key), decay)


def wkv_backward(
    base, key_ref, value_ref, decay, bonus, out_ref, state_ref, up_ref, carry_ref, sum_ref, work_ref, grad_ref
):
    steps = STEP

    def at(s):
        return pl.ds(base + s * SUB, SUB)

    state = None
    for s in reversed(range(steps)):
        lead = bonus + key_ref[at(s), :]
        power = state_ref[2, at(s), :]
        peak = jnp.maximum(power, lead)
        new = jnp.exp(lead - peak)
        share = up_ref[s * SUB : (s + 1) * SUB, :] / (
            jnp.exp(power - peak) * state_ref[1, at(s), :] + new
        )
        work_ref[0, s], work_ref[1, s], work_ref[2, s] = share, peak, new * share
        here = (share, -share * out_ref[at(s), :], -peak)
        state = here if state is None else wkv_join(state, here, decay)
    place = lax.broadcasted_iota(jnp.int32, decay.shape, 0)
    carry = tuple(carry_ref[i] for i in range(3))
    state = choose(place == SUB - 1, wkv_join(carry, state, steps * decay), state)
    for reach in (1, 2, 4):
        later = tuple(pltpu.roll(part, SUB - reach, 0) for part in state)
        state = choose(place < SUB - reach, wkv_join(later, state, reach * steps * decay), state)
    after = tuple(pltpu.roll(part, SUB - 1, 0) for part in state)
    for i in range(3):
        carry_ref[i] = after[i]
    numer, denom, power = choose(place == SUB - 1, carry, after)
    for s in reversed(range(steps)):
        key, value, out = key_ref[at(s), :], value_ref[at(s), :], out_ref[at(s), :]
        share, peak, own = work_ref[0, s], work_ref[1, s], work_ref[2, s]
        reach = jnp.exp(key + power)
        direct = own * (value - out)
        grad_ref[0, s * SUB : (s + 1) * SUB, :] = direct + reach * (value * numer + denom)
        grad_ref[1, s * SUB : (s + 1) * SUB, :] = own + reach * numer
        sum_ref[1] += direct
        sum_ref[0] += jnp.exp(state_ref[2, at(s), :] + power - decay) * (
            state_ref[0, at(s), :] * numer + state_ref[1, at(s), :] * denom
        )
        numer, denom, power = wkv_join(
            (numer, denom, power), (share, -share * out, -peak), decay
        )


def load(pairs, sems, start):
    copies = [
        pltpu.make_async_copy(source, target, sems.at[start + i]) for i, (source, target) in enumerate(pairs)
    ]
    for copy in copies:
        copy.start()
    return copies


def soft_plus(value):
    small = jnp.exp(-jnp.abs(value))
    share = 1.0 / (1.0 + small)
    rest = jnp.where(small < 1e-3, small - 0.5 * small * small, jnp.log(1.0 + small))
    return jnp.maximum(value, 0.0) + rest, jnp.where(value >= 0.0, share, small * share)


def from_tokens(tokens_hbm, micro, tokens_ref, sems):
    return [
        pltpu.make_async_copy(tokens_hbm.at[micro, 0, :, pl.ds(g * LANES, LANES)], tokens_ref.at[g], sems.at[g])
        for g in range(tokens_ref.shape[0])
    ]


def to_sections(here, sections, rows_ref, tokens_ref, out_hbm, sems):
    send, receive = sems
    micro = here.at["section"]
    groups = range(tokens_ref.shape[0])

    def ends(c, source, g):
        return tokens_ref.at[g, rows_of(c)], out_hbm.at[source, 0, :, pl.ds(g * LANES, LANES)]

    def copy(c, source, g):
        held, target = ends(c, source, g)
        return pltpu.make_async_remote_copy(
            src_ref=held, dst_ref=target, send_sem=send.at[c, g], recv_sem=receive.at[source, g],
            device_id=here.device(section=c), device_id_type=MESH,
        )

    def own(g):
        return pltpu.make_async_copy(*ends(micro, micro, g), send.at[micro, g])

    def start(c):
        to_tokens(rows_ref, tokens_ref, c)

        @pl.when(c == micro)
        def _():
            for g in groups:
                own(g).start()

        @pl.when(c != micro)
        def _():
            for g in groups:
                copy(c, micro, g).start()

    def wait():
        for g in groups:
            for k in range(1, sections):
                other = lax.rem(micro + k, sections)
                copy(other, micro, g).wait_send()
                copy(other, other, g).wait_recv()
            own(g).wait()

    return start, wait


def mix_chunk_back(
    peers, c, ratios, full_ref, normal_ref, edge_ref, mixed_ref, mix_grad, later_ref, edges_ref, part_ref, tiles
):
    count = peers.count
    rows = rows_of(c)
    first = second = 0.0
    for source in range(count):
        part = peers.columns(source)
        normal = normal_ref[rows, part].astype(jnp.float32)
        gain = full_ref[0:1, part]
        normed = normal * gain + full_ref[1:2, part]
        before = shift_rows(normed, edge_ref[pl.ds(c, 1), part])
        gap = normed - before
        direct = shifted = 0.0
        for i in range(ratios):
            grad = mix_grad(i, part)
            ratio = full_ref[3 + i : 4 + i, part]
            mixed_ref[i, rows, part] = (before + gap * ratio).astype(jnp.bfloat16)
            taken = grad * ratio
            direct = direct + taken
            shifted = shifted + (grad - taken)
            edges_ref[3 + i : 4 + i, part] += jnp.sum(grad * gap, axis=0, keepdims=True)
        value = direct + unshift_rows(shifted, later_ref[0:1, part])
        later_ref[0:1, part] = shifted[0:1]
        part_ref[rows, part] = value
        scaled = value * gain
        first = first + jnp.sum(scaled, axis=1, keepdims=True)
        second = second + jnp.sum(scaled * normal, axis=1, keepdims=True)
    tiles.stat[peers.me, c] = to_row_tile(first, second)
    tiles.start(c)


STEPS = 7
COPIES = 15
EVERY = slice(None)


class Summed:
    def __init__(self, around, grad, core_land, cross_land, own_land, result, sems):
        self.grad, self.core_land, self.cross_land, self.own_land = grad, core_land, cross_land, own_land
        self.result, self.sems = result, sems
        self.lead = (EVERY,) * (len(grad.shape) - 6)
        (self.q, self.y, self.x), (self.sibling, self.over_x, self.over_y) = around

    def at(self, ref, *place):
        return ref.at[(*self.lead, *place)]

    def send(self, which, source, target, place):
        return pltpu.make_async_remote_copy(
            src_ref=source, dst_ref=target, send_sem=self.sems[0].at[which], recv_sem=self.sems[1].at[which],
            device_id=place, device_id_type=MESH,
        )

    def share(self, which, held, device, *place):
        return self.send(which, self.at(held, *place), self.at(self.result, *place), device)

    def arrive(self, which, ref, *place):
        view = self.at(ref, *place)
        self.send(which, view, view, self.sibling).wait_recv()

    def add(self, place, land, land_place):
        mine, come = self.at(self.grad, *place), self.at(land, *land_place)
        rows = mine.shape[-2]
        block = min(rows, 32)
        for k in range(3 if self.lead else 1):
            for start in range(0, rows, block):
                view = (*((k,) if self.lead else ()), slice(start, start + block), EVERY)
                mine[view] = (mine[view].astype(jnp.float32) + come[view].astype(jnp.float32)).astype(jnp.bfloat16)

    def add_half(self):
        def step(i, unused):
            y, rest = halves(halves(i, 7), 3), i - 4 * halves(halves(i, 7), 3)
            place = y, halves(rest, 3), odd(rest, 3)
            self.add((self.q, *place), self.core_land, place)
            return unused

        lax.fori_loop(0, 8, step, 0)

    def to_core(self):
        return [self.send(0, self.at(self.grad, 1 - self.q), self.core_land, self.sibling)]

    def cross(self):
        first, second = (EVERY, 1 - self.x, 0), (1 - self.y, EVERY, 1)
        return [
            self.send(1, self.at(self.grad, self.q, *first), self.at(self.cross_land, *first), self.over_x),
            self.send(2, self.at(self.grad, self.q, *second), self.at(self.cross_land, *second), self.over_y),
        ]

    def own(self):
        q, y, x = self.q, self.y, self.x
        return [
            self.send(3, self.at(self.grad, q, 1 - y, x, 0), self.at(self.own_land, 0), self.over_y),
            self.send(4, self.at(self.grad, q, y, 1 - x, 1), self.at(self.own_land, 1), self.over_x),
        ]

    def back_own(self):
        q, y, x = self.q, self.y, self.x
        return [
            self.share(5, self.grad, self.over_y, q, y, x, 0), self.share(6, self.grad, self.over_x, q, y, x, 1),
            self.share(7, self.grad, self.sibling, q, y, x),
        ]

    def back_cross(self):
        q, y, x = self.q, self.y, self.x
        return [
            self.share(8, self.result, self.over_x, q, EVERY, x, 0), self.share(9, self.result, self.over_y, q, y, EVERY, 1),
            self.share(10, self.result, self.sibling, q, 1 - y, x, 0),
            self.share(11, self.result, self.sibling, q, y, 1 - x, 1),
        ]

    def back_core(self):
        q, y, x = self.q, self.y, self.x
        return [
            self.share(12, self.result, self.sibling, q, EVERY, 1 - x, 0),
            self.share(13, self.result, self.sibling, q, 1 - y, EVERY, 1),
        ]

    def keep(self):
        place = self.q, self.y, self.x
        return pltpu.make_async_copy(self.at(self.grad, *place), self.at(self.result, *place), self.sems[0].at[14])

    def step(self, number):
        q, y, x = self.q, self.y, self.x
        started = []
        if number == 0:
            started = self.to_core()
        elif number == 1:
            self.arrive(0, self.core_land)
            self.add_half()
            started = self.cross()
        elif number == 2:
            self.arrive(1, self.cross_land, EVERY, x, 0)
            self.arrive(2, self.cross_land, y, EVERY, 1)
            for k in (0, 1):
                self.add((q, k, x, 0), self.cross_land, (k, x, 0))
                self.add((q, y, k, 1), self.cross_land, (y, k, 1))
            started = self.own()
        elif number == 3:
            for part in (0, 1):
                self.arrive(3 + part, self.own_land, part)
                self.add((q, y, x, part), self.own_land, (part,))
            started = self.back_own() + [self.keep()]
        elif number == 4:
            self.arrive(5, self.result, q, 1 - y, x, 0)
            self.arrive(6, self.result, q, y, 1 - x, 1)
            self.keep().wait()
            started = self.back_cross()
        elif number == 5:
            self.arrive(7, self.result, 1 - q, y, x)
            self.arrive(8, self.result, q, EVERY, 1 - x, 0)
            self.arrive(9, self.result, q, 1 - y, EVERY, 1)
            started = self.back_core()
        else:
            self.arrive(10, self.result, 1 - q, 1 - y, x, 0)
            self.arrive(11, self.result, 1 - q, y, 1 - x, 1)
            self.arrive(12, self.result, 1 - q, EVERY, 1 - x, 0)
            self.arrive(13, self.result, 1 - q, 1 - y, EVERY, 1)
        for copy in started:
            copy.start()

    def sent_grad(self):
        for copy in self.to_core() + self.cross() + self.own() + self.back_own():
            copy.wait_send()

    def sent_rest(self):
        for copy in self.back_cross() + self.back_core():
            copy.wait_send()


GROUPS = (
    (0, (1, 2), (1, 2, 4, 5, 6, 11)),
    (0, (0,), (0, 1, 3, 4, 5, 11)),
    (1, (3, 4), (1, 2, 4, 5, 6, 12)),
)


def both_kernel(
    names, count, sections, cores, depth,
    rows_hbm, up_hbm, lead_ref, numer_ref, denom_ref, power_ref, attend_gain, attend_bias, attend_mix, fading_ref, bonus_ref,
    feed_gain, feed_bias, feed_mix, entry_hbm, exit_hbm, key_hbm, content_hbm, gate_hbm,
    out_hbm, back_hbm, table_ref, entry_sum, exit_sum, key_sum, content_sum, gate_sum,
    normal_ref, std_ref, key_ref, value_ref, averaged_ref, state_ref, open_ref, hidden_ref, slope_ref, gate_ref, kv_ref,
    full_ref, edge_ref, rows_ref, tokens_ref, grad_ref, back_ref,
    entry_ref, exit_ref, w_key, w_content, w_gate,
    entry_grad, exit_grad, key_grad, content_grad, gate_grad,
    entry_core, exit_core, key_core, content_core, gate_core,
    entry_cross, exit_cross, key_cross, content_cross, gate_cross,
    entry_own, exit_own, key_own, content_own, gate_own,
    pay, stat, part, stage, land, mixed_ref, pre_grads, up_ref, work_ref, pair_ref, carry_ref, sum_ref,
    output_ref, hidden_grad, last_ref, later_ref, edges_ref, edge_land, small_ref,
    load_sems, token_sems, back_sems, fs, fr, os, orr, bs, br, gs, gr, ts, tr, ss, sr, es, er, ws, wr,
    table_send, table_recv,
):
    length, width = rows_ref.shape
    hidden_width = hidden_ref.shape[2]
    chunks = length // CHUNK
    passes = 2 * depth
    period = max(2 * count - 2, chunks + 1)
    here = Here(names)
    peers = Peers(here, count, width, 2 * passes)
    mine = peers.columns(peers.me)
    micro, core = here.at["section"], here.at["seq"]
    y, x = lax.div(micro, 2), lax.rem(micro, 2)
    neighbours = (
        here.device(seq=1 - core), here.device(section=micro + 1 - 2 * x), here.device(section=micro + 2 - 4 * y)
    )
    around = (core, y, x), neighbours
    first = from_tokens(rows_hbm, micro, tokens_ref, token_sems)
    second = from_tokens(up_hbm, micro, back_ref, back_sems)
    for copy in first:
        copy.start()
    full_ref[...] = jnp.zeros_like(full_ref)
    gather = Gather(peers, pay, (gs, gr))
    tiles = Tiles(peers, stat, (ts, tr))
    scatter = Scatter(peers, part, stage, land, (ss, sr))
    start_out, wait_out = to_sections(here, sections, rows_ref, tokens_ref, out_hbm, (os, orr))
    start_back, wait_back = to_sections(here, sections, grad_ref, back_ref, back_hbm, (bs, br))

    def full_copy(k, owner):
        block = full_ref.at[:, :, peers.columns(owner)]
        return peers.copy(peers.to(k), block, block, fs.at[k - 1], fr.at[k - 1])

    def sums(group, level):
        parts = (
            (key_grad, key_core, key_cross, key_own, key_sum),
            (content_grad, content_core, content_cross, content_own, content_sum),
            (gate_grad, gate_core, gate_cross, gate_own, gate_sum),
        )
        entry = (entry_grad, entry_core, entry_cross, entry_own, entry_sum)
        parts += (entry, (exit_grad, exit_core, exit_cross, exit_own, exit_sum))
        out = []
        for place in GROUPS[group][1]:
            grad, core_land, cross_land, own_land, result = parts[place]
            out.append(
                Summed(
                    around, grad, core_land, cross_land, own_land, result.at[level],
                    (ws.at[level, place], wr.at[level, place]),
                )
            )
        return out

    def sum_step(group, level, number):
        for matrix in sums(group, level):
            matrix.step(number)

    def table_place(k):
        return lax.rem(micro * cores + core + k, sections * cores)

    def table_copy(k, owner):
        other = table_place(k)
        return pltpu.make_async_remote_copy(
            src_ref=small_ref, dst_ref=table_ref.at[owner], send_sem=table_send.at[k - 1], recv_sem=table_recv.at[k - 1],
            device_id=here.device(section=lax.div(other, cores), seq=lax.rem(other, cores)), device_id_type=MESH,
        )

    others = [table_place(k) for k in range(1, sections * cores)]
    peers.greet([here.device(section=lax.div(other, cores), seq=lax.rem(other, cores)) for other in others])
    for j in range(2 * depth):
        level = j // 2
        gain, bias, mix = (attend_gain, attend_bias, attend_mix) if j % 2 == 0 else (feed_gain, feed_bias, feed_mix)
        full_ref[j, 0:1, mine] = gain[level : level + 1, :]
        full_ref[j, 1:2, mine] = bias[level : level + 1, :]
        full_ref[j, 2:3, mine] = lead_ref[j, micro]
        for i in range(mix.shape[0] if j % 2 == 0 else mix.shape[1]):
            full_ref[j, 3 + i : 4 + i, mine] = mix[i, level : level + 1] if j % 2 == 0 else mix[level, i : i + 1]
    for k in range(1, count):
        full_copy(k, peers.me).start()
    for copy in first:
        copy.wait()
    weights = load(
        (
            (entry_hbm, entry_ref), (exit_hbm, exit_ref), (key_hbm, w_key), (content_hbm, w_content),
            (gate_hbm, w_gate),
        ),
        load_sems,
        0,
    )
    for copy in second:
        copy.start()
    to_stretches(tokens_ref, rows_ref)

    def begin_forward(j, c):
        rows = rows_of(c)

        @pl.when(j > 0)
        def _():
            value = scatter.total(c, j - 1)
            tiles.sent(c)

            @pl.when(odd(j, passes) == 1)
            def _():
                rows_ref[rows, :] += value

            @pl.when(odd(j, passes) == 0)
            def _():
                level = halves(j, passes) - 1
                kv_ref[level, rows, :] = value
                rows_ref[rows, :] += gate_ref[level, rows, :] * value

        @pl.when(j < 2 * depth)
        def _():
            lines = rows_ref[rows, :]
            middle = jnp.mean(lines, axis=1, keepdims=True)
            center = lines - middle
            square = jnp.sum(center * center, axis=1, keepdims=True)
            pay[odd(j, passes), rows, mine] = center.astype(jnp.bfloat16)
            tiles.stat[peers.me, c] = to_row_tile(middle, square)
            tiles.start(c)
            gather.start(c, j)

        @pl.when(j == 2 * depth)
        def _():
            start_out(c)

    def attend_forward(level, c):
        rows = rows_of(c)

        @pl.when(c == 0)
        def _():
            for i, start_ref in enumerate((numer_ref, denom_ref, power_ref)):
                carry_ref[i] = jnp.broadcast_to(start_ref[level, micro], (SUB, width))

        decay = jnp.broadcast_to(jnp.exp(fading_ref[pl.ds(level, 1), :]), (SUB, width))
        bonus = jnp.broadcast_to(bonus_ref[pl.ds(level, 1), :], (SUB, width))
        key_ref[level, rows, :] = product(mixed_ref[0, 0:CHUNK], entry_ref[level, 0])
        value_ref[level, rows, :] = product(mixed_ref[1, 0:CHUNK], entry_ref[level, 1])
        gate = jax.nn.sigmoid(product(mixed_ref[2, 0:CHUNK], entry_ref[level, 2]))
        open_ref[level, rows, :] = gate
        wkv_forward(
            pl.multiple_of(c * CHUNK, CHUNK), key_ref.at[level], value_ref.at[level], decay, bonus, carry_ref,
            averaged_ref.at[level], state_ref.at[level],
        )
        output = (gate * averaged_ref[level, rows, :]).astype(jnp.bfloat16)
        for target in range(count):
            block = peers.columns(target)
            part[rows, block] = product(output, exit_ref[level, :, block])

    def feed_forward(level, c):
        rows = rows_of(c)
        for start in range(0, hidden_ref.shape[2], width):
            block = slice(start, start + width)
            soft, slope = soft_plus(product(mixed_ref[0, 0:CHUNK], w_key[level, :, block]))
            hidden_ref[level, rows, block] = (soft * soft).astype(jnp.bfloat16)
            slope_ref[level, rows, block] = (2.0 * soft * slope).astype(jnp.bfloat16)
        for target in range(count):
            block = peers.columns(target)
            part[rows, block] = product(hidden_ref[level, rows, :], w_content[level, :, block])
        gate_ref[level, rows, :] = jax.nn.sigmoid(product(mixed_ref[1, 0:CHUNK], w_gate[level]))

    def forward(j, c):
        @pl.when((j == 0) & (c == 0))
        def _():
            for k in range(1, count):
                full_copy(k, peers.source(k)).wait_recv()
            for copy in weights:
                copy.wait()

        @pl.when(c == 0)
        def _():
            last_ref[0:1, :] = full_ref[j, 2:3, :]

        def mix(count_mixed):
            mix_chunk(
                peers, c, pay.at[odd(j, passes)], tiles, full_ref.at[j], mixed_ref.at[pl.ds(0, count_mixed), pl.ds(0, CHUNK)],
                normal_ref.at[j], edge_ref.at[j], std_ref.at[j], last_ref,
            )

        level = halves(j, passes)

        @pl.when(odd(j, passes) == 0)
        def _():
            mix(3)
            attend_forward(level, c)

        @pl.when(odd(j, passes) == 1)
        def _():
            mix(2)
            feed_forward(level, c)

        gather.sent(c, j)

    def edge_copies(j, source_of):
        return [
            peers.copy(
                peers.to(k), edges_ref.at[j, :, peers.columns(peers.to(k))], edge_land.at[j, source_of(k)],
                es.at[j, k - 1], er.at[j, k - 1],
            )
            for k in range(1, count)
        ]

    def end_pass(j, c):
        rows = rows_of(c)
        normed_grad = scatter.total(c, 2 * passes - 1 - j)
        tiles.arrived(c)
        totals = tiles.stat[0, c]
        for source in range(1, count):
            totals = totals + tiles.stat[source, c]
        columns = to_columns([totals])
        normal = normal_ref[j, rows, mine].astype(jnp.float32)
        scale = 1.0 / (count * width)
        grad_ref[rows, :] += std_ref[j, rows, 0:1] * (
            normed_grad * full_ref[j, 0:1, mine] - columns[:, 0:1] * scale - normal * (columns[:, 1:2] * scale)
        )
        small_ref[j, 0:1, :] += jnp.sum(normed_grad * normal, axis=0, keepdims=True)
        small_ref[j, 1:2, :] += jnp.sum(normed_grad, axis=0, keepdims=True)

        @pl.when(c == 0)
        def _():
            for copy in edge_copies(j, peers.source):
                copy.wait_recv()
            edges = edges_ref[j, :, mine]
            for k in range(1, count):
                edges = edges + edge_land[j, peers.source(k)]
            small_ref[j, 2:6, :] = edges[2:6]

    def begin_backward(which, c):
        rows = rows_of(c)
        j = passes - 1 - which

        @pl.when(which > 0)
        def _():
            end_pass(j + 1, c)
            gather.sent(c, passes + which - 1)
            tiles.sent(c)

        @pl.when((which < passes) & (odd(which, passes) == 0))
        def _():
            pay[odd(which, passes), rows, mine] = (grad_ref[rows, :] * gate_ref[halves(j, passes), rows, :]).astype(jnp.bfloat16)

        @pl.when((which < passes) & (odd(which, passes) == 1))
        def _():
            pay[odd(which, passes), rows, mine] = grad_ref[rows, :].astype(jnp.bfloat16)

        @pl.when(which < passes)
        def _():
            gather.start(c, passes + which)

        @pl.when(which == passes)
        def _():
            start_back(c)

    def attend_backward(j, c):
        level = halves(j, passes)
        rows = rows_of(c)
        decay = jnp.broadcast_to(jnp.exp(fading_ref[pl.ds(level, 1), :]), (SUB, width))
        bonus = jnp.broadcast_to(bonus_ref[pl.ds(level, 1), :], (SUB, width))

        @pl.when(c == chunks - 1)
        def _():
            sum_ref[...] = jnp.zeros_like(sum_ref)
            carry_ref[0] = jnp.zeros((SUB, width), jnp.float32)
            carry_ref[1] = jnp.zeros((SUB, width), jnp.float32)
            carry_ref[2] = jnp.full((SUB, width), NO_POWER, jnp.float32)

        output_grad = against(pay[1, rows, :], exit_ref[level])
        gate = open_ref[level, rows, :]
        up = output_grad * gate
        up_ref[...] = up
        averaged = averaged_ref[level, rows, :]
        pre_grads[2, rows, :] = (up * averaged * (1.0 - gate)).astype(jnp.bfloat16)
        output_ref[rows, :] = (gate * averaged).astype(jnp.bfloat16)
        wkv_backward(
            pl.multiple_of(c * CHUNK, CHUNK), key_ref.at[level], value_ref.at[level], decay, bonus,
            averaged_ref.at[level], state_ref.at[level],
            up_ref, carry_ref, sum_ref, work_ref, pair_ref,
        )
        pre_grads[0, rows, :] = pair_ref[0].astype(jnp.bfloat16)
        pre_grads[1, rows, :] = pair_ref[1].astype(jnp.bfloat16)
        mix_chunk_back(
            peers, c, 3, full_ref.at[j], normal_ref.at[j], edge_ref.at[j], mixed_ref,
            lambda i, columns: against(pre_grads[i, rows, :], entry_ref[level, i, columns, :]),
            later_ref, edges_ref.at[j], part, tiles,
        )

        @pl.when(c == 0)
        def _():
            numer, denom = carry_ref[0, SUB - 1 :, :], carry_ref[1, SUB - 1 :, :]
            lift = jnp.exp(power_ref[level, micro] + carry_ref[2, SUB - 1 :, :])
            out = passes + level
            small_ref[out, 0:1, :] = -decay[0:1] * jnp.sum(sum_ref[0], axis=0, keepdims=True)
            small_ref[out, 1:2, :] = jnp.sum(sum_ref[1], axis=0, keepdims=True)
            small_ref[out, 2:3, :] = lift * numer
            small_ref[out, 3:4, :] = lift * denom
            small_ref[out, 4:5, :] = lift * (numer_ref[level, micro] * numer + denom_ref[level, micro] * denom)

    def feed_backward(j, c):
        rows = rows_of(c)
        level = halves(j, passes)
        gate = gate_ref[level, rows, :]
        pre_grads[0, rows, :] = (grad_ref[rows, :] * gate * kv_ref[level, rows, :] * (1.0 - gate)).astype(jnp.bfloat16)
        for start in range(0, hidden_width, width):
            block = slice(start, start + width)
            into = against(pay[0, rows, :], w_content[level, block, :])
            hidden_grad[rows, block] = (into * slope_ref[level, rows, block].astype(jnp.float32)).astype(jnp.bfloat16)

        def mix_grad(i, columns):
            if i == 0:
                return against(hidden_grad[rows, :], w_key[level, columns, :])
            return against(pre_grads[0, rows, :], w_gate[level, columns, :])

        mix_chunk_back(
            peers, c, 2, full_ref.at[j], normal_ref.at[j], edge_ref.at[j], mixed_ref, mix_grad,
            later_ref, edges_ref.at[j], part, tiles,
        )

    def backward(which, c):
        j = passes - 1 - which

        @pl.when(c == chunks - 1)
        def _():
            later_ref[...] = jnp.zeros_like(later_ref)

        @pl.when(odd(which, passes) == 0)
        def _():
            feed_backward(j, c)

        @pl.when(odd(which, passes) == 1)
        def _():
            attend_backward(j, c)

        @pl.when(c == 0)
        def _():
            edges_ref[j, 2:3, :] = later_ref[0:1, :]
            for copy in edge_copies(j, lambda k: peers.me):
                copy.start()

    def weigh(place, level):
        if place == 4:
            for source in range(count):
                block = peers.columns(source)
                grad = inner_rows(output_ref[...], pay[1, :, block]).astype(jnp.bfloat16)
                exit_grad[..., block] = grad.reshape(*exit_grad.shape[:-1], width)
            return
        for i in range(4):
            at = i // 2, i % 2
            if place == 1:
                rows = hidden_width // 4
                grad = inner_rows(hidden_ref[level, :, i * rows : (i + 1) * rows], pay[0]).astype(jnp.bfloat16)
                content_grad[at] = grad.reshape(content_grad.shape[2:])
                continue
            rows = slice(i * (pay.shape[2] // 4), (i + 1) * (pay.shape[2] // 4))
            if place == 0:
                grad = inner_rows(mixed_ref[0, :, rows], hidden_grad[...]).astype(jnp.bfloat16)
                key_grad[at] = grad.reshape(key_grad.shape[2:])
            elif place == 2:
                grad = inner_rows(mixed_ref[1, :, rows], pre_grads[0]).astype(jnp.bfloat16)
                gate_grad[at] = grad.reshape(gate_grad.shape[2:])
            else:
                for k in range(3):
                    grad = inner_rows(mixed_ref[k, :, rows], pre_grads[k]).astype(jnp.bfloat16)
                    entry_grad[(k, *at)] = grad.reshape(entry_grad.shape[3:])

    base, final = chunks + count - 1, passes * period + chunks - 1

    def when_taken(group, number, t):
        kind, places, later = GROUPS[group]
        taken, chosen = False, 0
        for level in range(depth):
            now = t == base + period * kind + later[number] + 2 * period * (depth - 1 - level)
            taken, chosen = taken | now, chosen + jnp.where(now, level, 0)
        return taken, chosen

    def extra(t):
        for group in range(len(GROUPS)):
            for number in reversed(range(STEPS - 1)):
                taken, level = when_taken(group, number, t)

                @pl.when(taken)
                def _():
                    if number == 0:
                        @pl.when(level < depth - 1)
                        def _():
                            for matrix in sums(group, jnp.minimum(level + 1, depth - 1)):
                                matrix.sent_grad()

                        for place in GROUPS[group][1]:
                            weigh(place, jnp.clip(level, 0, depth - 1))
                    sum_step(group, jnp.clip(level, 0, depth - 1), number)

    forward_tick = ticks_of(peers, chunks, passes, 0, False, begin_forward, gather, forward, scatter)
    backward_tick = ticks_of(peers, chunks, passes, passes, True, begin_backward, gather, backward, scatter)
    turn = (passes - 1) * period + chunks + count - 2

    def onward(w, i):
        ends = i == period - 1
        return jnp.where(ends, w + 1, w), jnp.where(ends, 0, i + 1)

    def tick(t, places):
        ahead, behind = places

        @pl.when(t < passes * period + chunks)
        def _():
            forward_tick(*ahead)

        @pl.when(t == turn - 1)
        def _():
            for copy in second:
                copy.wait()
            to_stretches(back_ref, grad_ref)
            small_ref[...] = jnp.zeros_like(small_ref)
            edges_ref[...] = jnp.zeros_like(edges_ref)

        @pl.when(t >= turn)
        def _():
            backward_tick(*behind)
            extra(t - turn)

        moved = onward(*behind)
        return onward(*ahead), tuple(jnp.where(t >= turn, a, b) for a, b in zip(moved, behind))

    start = (jnp.int32(0), jnp.int32(0))
    lax.fori_loop(0, turn + final + 1, tick, (start, start))

    for k in range(1, sections * cores):
        table_copy(k, micro * cores + core).start()
    table_ref[micro * cores + core] = small_ref[...]
    left = []
    for group, (kind, places, later) in enumerate(GROUPS):
        for level in reversed(range(depth)):
            start = base + period * (kind + 2 * (depth - 1 - level))
            for number in range(STEPS):
                at = start + (later[number] if number < STEPS - 1 else later[-1] + 5)
                if at > final or number == STEPS - 1:
                    left.append((at, group, level, number))
    for at, group, level, number in sorted(left):
        sum_step(group, level, number)
    for c in range(chunks):
        scatter.sent(c, 2 * passes - 1)
    for j in range(passes):
        for copy in edge_copies(j, lambda k: peers.me):
            copy.wait_send()
    for group in range(len(GROUPS)):
        for level in range(depth):
            for matrix in sums(group, level):
                matrix.sent_rest()
                if level == 0:
                    matrix.sent_grad()
    for k in range(1, sections * cores):
        table_copy(k, micro * cores + core).wait_send()
        other = lax.rem(micro * cores + core + sections * cores - k, sections * cores)
        table_copy(k, other).wait_recv()
    for k in range(1, count):
        full_copy(k, peers.me).wait_send()
    wait_out()
    wait_back()


BF16, F32 = jnp.bfloat16, jnp.float32


def struct(*shape, dtype=F32):
    return jax.ShapeDtypeStruct(shape, dtype)


def run_kernel(body, collective, outs, scratch, operands, flops):
    def spec(inside):
        return pl.BlockSpec(memory_space=pltpu.VMEM if inside else pl.ANY)

    return pl.pallas_call(
        body,
        out_shape=[out for out, inside in outs],
        in_specs=[spec(inside) for operand, inside in operands],
        out_specs=[spec(inside) for out, inside in outs],
        scratch_shapes=scratch,
        compiler_params=pltpu.CompilerParams(
            collective_id=collective, has_side_effects=True, vmem_limit_bytes=63 * 1024 * 1024
        ),
        cost_estimate=pl.CostEstimate(flops=flops, bytes_accessed=2**25, transcendentals=2**23),
    )(*[operand for operand, inside in operands])


def pair_of(shape):
    return [pltpu.SemaphoreType.DMA(shape)] * 2


def run_fast(
    names, residual_entering, upstream_sensitivity, piece_lead_lines, dividend_start, divisor_start, power_offset_start,
    attend_standard_scale, attend_standard_offset, attend_lag_fractions, fading_log_rate, reward_first_word,
    attend_entry_matrix, attend_exit_matrix, feed_standard_scale, feed_standard_offset, feed_lag_fractions,
    feed_lookup_matrix, feed_content_matrix, feed_gate_matrix,
):
    count, sections, cores = (lax.axis_size(axis) for axis in ("tp", "section", "seq"))
    length, width = residual_entering.shape[2:]
    depth, features, hidden = feed_lookup_matrix.shape[0], count * width, feed_lookup_matrix.shape[2]
    chunks, subs = length // CHUNK, 2 * depth
    flops = 2 * depth * length * features * (4 * width + 2 * hidden + width)
    groups = width // LANES
    starts = (dividend_start, divisor_start, power_offset_start)
    weights = (attend_entry_matrix, attend_exit_matrix, feed_lookup_matrix, feed_content_matrix, feed_gate_matrix)
    shares = struct(sections, 1, CHUNK, width)
    lines = (depth, length, width)
    shapes = [weight.shape[1:] for weight in weights]

    def held(*shape, dtype=F32):
        return pltpu.VMEM(shape, dtype)

    def cut(*parts):
        return [(*shape[:-2], *parts, shape[-2] // 16, shape[-1]) for shape in shapes]

    outs = [(shares, False), (shares, False), (struct(sections * cores, subs + depth, SUB, width), True)]
    outs += [(struct(depth, *shape, dtype=BF16), False) for shape in cut(2, 2, 2, 2)]
    scratch = [held(subs, length, features, dtype=BF16), held(subs, length, LANES), held(*lines), held(*lines)]
    scratch += [held(*lines), held(depth, 3, *lines[1:]), held(*lines)]
    scratch += [held(depth, length, hidden, dtype=BF16)] * 2 + [held(*lines)] * 2
    scratch += [held(subs, SUB, features)] * 2 + [held(length, width), held(groups, length, LANES)] * 2
    scratch += [held(*weight.shape, dtype=BF16) for weight in weights]
    scratch += [
        held(*shape, dtype=BF16)
        for shape in cut(2, 2, 2, 2) + cut(2, 2, 2) + cut(2, 2, 2) + cut(2)
    ]
    scratch += [
        held(2, length, features, dtype=BF16), held(count, chunks, PAIR, LANES), held(length, features),
        held(length, features, dtype=BF16), held(2, length, features + width, dtype=BF16),
    ]
    scratch += [
        held(3, length, features, dtype=BF16), held(3, length, width, dtype=BF16), held(CHUNK, width),
        held(3, STEP, SUB, width), held(2, CHUNK, width), held(3, SUB, width), held(2, SUB, width),
        held(length, width, dtype=BF16), held(length, hidden, dtype=BF16), held(SUB, features), held(SUB, features),
        held(subs, SUB, features), held(subs, count, SUB, width), held(subs + depth, SUB, width),
    ]
    scratch += [pltpu.SemaphoreType.DMA((n,)) for n in (len(weights), groups, groups)] + pair_of((count - 1,))
    scratch += pair_of((sections, groups)) + pair_of((sections, groups))
    scratch += pair_of((2, 2, count - 1, chunks)) + pair_of((count - 1, chunks)) + pair_of((2, 2, count, chunks))
    scratch += pair_of((subs, count - 1)) + pair_of((depth, len(weights), COPIES))
    scratch += pair_of((sections * cores - 1,))
    operands = [(residual_entering, False), (upstream_sensitivity, False)]
    operands += [
        (value, True)
        for value in (
            piece_lead_lines, *starts, attend_standard_scale, attend_standard_offset,
            jnp.swapaxes(attend_lag_fractions, 0, 1),
            fading_log_rate, reward_first_word, feed_standard_scale, feed_standard_offset, feed_lag_fractions,
        )
    ]
    operands += [(value, False) for value in weights]
    out_share, back_share, table, *sums = run_kernel(
        partial(both_kernel, names, count, sections, cores, depth), 0, outs, scratch, operands, 3 * flops
    )
    return finish(cores, depth, out_share, back_share, table, sums, [weight.shape for weight in weights])


def finish_kernel(cores, depth, table_ref, *refs):
    wide, narrow = refs[:7], refs[7:14]
    prev, numer, denom, power = refs[14:18]
    attend_gain, attend_bias, attend_mix, decay, bonus, feed_gain, feed_bias, feed_mix = refs[18:]
    for source, target in zip(wide, narrow):
        target[...] = source[...].astype(jnp.float32)

    @pl.when(pl.program_id(0) == 0)
    def _():
        core = lax.axis_index("seq")
        places, subs = table_ref.shape[0], 2 * depth
        for m in range(places // cores):
            for j in range(subs):
                prev[j, m] = table_ref[m * cores + core, j, 2:3, :]
            for level in range(depth):
                for i, state in enumerate((numer, denom, power)):
                    state[level, m] = table_ref[m * cores + core, subs + level, 2 + i : 3 + i, :]
        for level in range(depth):
            for j, gain, bias, mix in (
                (2 * level, attend_gain, attend_bias, attend_mix), (2 * level + 1, feed_gain, feed_bias, feed_mix),
            ):
                total = sum(table_ref[place, j] for place in range(places))
                gain[level : level + 1, :] = total[0:1]
                bias[level : level + 1, :] = total[1:2]
                for i in range(mix.shape[0] if mix is attend_mix else mix.shape[1]):
                    place = (i, slice(level, level + 1)) if mix is attend_mix else (level, slice(i, i + 1))
                    mix[place] = total[3 + i : 4 + i]
            total = sum(table_ref[place, subs + level] for place in range(places))
            decay[level : level + 1, :] = total[0:1]
            bonus[level : level + 1, :] = total[1:2]


def finish(cores, depth, out_share, back_share, table, sums, shapes):
    steps = 4
    wide = [value.reshape(-1, value.shape[-1]) for value in (out_share, back_share, *sums)]
    blocks = [
        pl.BlockSpec((value.shape[0] // steps, value.shape[1]), lambda i: (i, 0)) for value in wide
    ]
    width = table.shape[-1]
    micros = table.shape[0] // cores
    small = [(2 * depth, micros, 1, width)] + [(depth, micros, 1, width)] * 3
    small += [(depth, width), (depth, width), (3, depth, width), (depth, width), (depth, width)]
    small += [(depth, width), (depth, width), (depth, 2, width)]

    def whole(shape):
        return pl.BlockSpec(shape, lambda i: (0,) * len(shape))

    got = pl.pallas_call(
        partial(finish_kernel, cores, depth),
        grid=(steps,),
        out_shape=[struct(*value.shape) for value in wide] + [struct(*shape) for shape in small],
        in_specs=[whole(table.shape)] + blocks,
        out_specs=blocks + [whole(shape) for shape in small],
        compiler_params=pltpu.CompilerParams(vmem_limit_bytes=60 * 1024 * 1024),
    )(table, *wide)
    shares = [value.reshape(whole.shape) for value, whole in zip(got, (out_share, back_share))]
    entry, leave, key, content, gate = [
        value.reshape(shape) for value, shape in zip(got[2:7], shapes)
    ]
    small = list(got[7:])
    small[6] = jnp.swapaxes(small[6], 0, 1)
    return (*shares, *small[:9], entry, leave, *small[9:], key, content, gate)


def run_plain(
    residual_entering,
    upstream_sensitivity,
    piece_lead_lines,
    dividend_start,
    divisor_start,
    power_offset_start,
    attend_standard_scale,
    attend_standard_offset,
    attend_lag_fractions,
    fading_log_rate,
    reward_first_word,
    attend_entry_matrix,
    attend_exit_matrix,
    feed_standard_scale,
    feed_standard_offset,
    feed_lag_fractions,
    feed_lookup_matrix,
    feed_content_matrix,
    feed_gate_matrix,
):
    sections = lax.axis_size("section")
    micro = lax.axis_index("section")
    length, share = residual_entering.shape[2:]
    depth = attend_entry_matrix.shape[0]

    def own(array):
        return lax.dynamic_index_in_dim(array, micro, 0, keepdims=False)

    blank = jnp.zeros((1, share), jnp.float32)
    lead = lax.dynamic_index_in_dim(piece_lead_lines[:, :, 0], micro, 1, keepdims=False)
    starts = [
        lax.dynamic_index_in_dim(start[:, :, 0], micro, 1, keepdims=False)
        for start in (dividend_start, divisor_start, power_offset_start)
    ]
    small_rows, wkv_rows = [], []
    for level in range(depth):
        for gain, bias, mix, j in (
            (attend_standard_scale, attend_standard_offset, attend_lag_fractions, 2 * level),
            (feed_standard_scale, feed_standard_offset, feed_lag_fractions, 2 * level + 1),
        ):
            rows = [gain[level][None], bias[level][None], lead[j][None], mix[level]]
            rows += [blank] * (5 - mix.shape[1])
            small_rows.append(jnp.concatenate(rows, axis=0))
        wkv_rows.append(
            jnp.stack(
                [fading_log_rate[level], reward_first_word[level]]
                + [start[level] for start in starts]
                + [blank[0]] * 3
            )
        )
    small_own = jnp.stack(small_rows)
    small_full = lax.all_gather(small_own, "tp", axis=2, tiled=True)

    rows = own(residual_entering)[0]
    kept = []
    for level in range(depth):
        for j in (2 * level, 2 * level + 1):
            if j % 2 == 0:
                rows, saved = time_forward_plain(
                    rows, small_full[j], small_own[j], wkv_rows[level],
                    attend_entry_matrix[level], attend_exit_matrix[level],
                )
            else:
                rows, saved = channel_forward_plain(
                    rows, small_full[j], small_own[j],
                    feed_lookup_matrix[level], feed_content_matrix[level], feed_gate_matrix[level],
                )
            kept.append(saved)

    def to_tokens(value):
        pieces = value.reshape(sections, length // sections, share)
        return lax.all_to_all(pieces, "section", 0, 0)[:, None]

    out_share = to_tokens(rows)
    grad = own(upstream_sensitivity)[0]
    small_grads, wkv_grads = [None] * (2 * depth), [None] * depth
    weight_grads = [None] * (2 * depth)
    summed = None
    for level in reversed(range(depth)):
        for j in (2 * level + 1, 2 * level):
            if j % 2 == 0:
                grad, small_grads[j], wkv_grads[level], weights = time_backward_plain(
                    grad, kept[j], small_full[j], small_own[j], wkv_rows[level],
                    attend_entry_matrix[level], attend_exit_matrix[level],
                )
            else:
                grad, small_grads[j], weights = channel_backward_plain(
                    grad, kept[j], small_full[j], small_own[j],
                    feed_lookup_matrix[level], feed_content_matrix[level], feed_gate_matrix[level],
                )
            weight_grads[j] = weights
        both = weight_grads[2 * level + 1], weight_grads[2 * level]
        if summed is not None:
            both, summed = lax.optimization_barrier((both, summed))
            weight_grads[2 * level + 3], weight_grads[2 * level + 2] = summed
        summed = lax.psum(both, ("section", "seq"))
    weight_grads[1], weight_grads[0] = summed
    back_share = to_tokens(grad)

    table = jnp.stack(small_grads + wkv_grads)
    tables = lax.all_gather(table, ("section", "seq"), axis=0)
    sums = [
        jnp.stack([weight_grads[2 * level + kind][place] for level in range(depth)])
        for kind, place in ((0, 0), (0, 1), (1, 0), (1, 1), (1, 2))
    ]
    return out_share, back_share, tables, sums


def per_device(names, *arrays):
    residual_entering, lookup = arrays[0], arrays[16]
    sections, cores = lax.axis_size("section"), lax.axis_size("seq")
    micros, unused, length, share = residual_entering.shape
    depth, features, hidden = lookup.shape
    fits = sections == 4 and cores == 2 and micros == sections and length == sections * CHUNK
    fits = fits and share % 256 == 0 and features % 256 == 0 and hidden % 256 == 0 and hidden % share == 0
    fits = fits and 2 < lax.axis_size("tp") <= LANES // SUB
    if fits:
        return run_fast(names, *arrays)
    out_share, back_share, table, sums = run_plain(*arrays)
    tables = table.reshape(sections, cores, *table.shape[1:])
    mine = lax.dynamic_index_in_dim(tables, lax.axis_index("seq"), 1, keepdims=False)
    total = jnp.sum(tables, axis=(0, 1))
    prev_grad = jnp.moveaxis(mine[:, : 2 * depth, 2], 0, 1)[:, :, None]
    state_grads = [jnp.moveaxis(mine[:, 2 * depth :, 2 + i], 0, 1)[:, :, None] for i in range(3)]

    weights = [grad.astype(jnp.float32) for grad in sums]
    return (
        out_share,
        back_share,
        prev_grad,
        *state_grads,
        total[0 : 2 * depth : 2, 0],
        total[0 : 2 * depth : 2, 1],
        total[0 : 2 * depth : 2, 3:6],
        total[2 * depth :, 0],
        total[2 * depth :, 1],
        weights[0],
        weights[1],
        total[1 : 2 * depth : 2, 0],
        total[1 : 2 * depth : 2, 1],
        total[1 : 2 * depth : 2, 3:5],
        weights[2],
        weights[3],
        weights[4],
    )


def solution(mesh):
    rows = P(None, "seq", None, "tp")
    line, mix = P(None, "tp"), P(None, None, "tp")
    columns, depths = P(None, None, "tp"), P(None, "tp", None)
    entry = P(None, None, None, "tp")
    state = P(None, None, "seq", "tp")
    tokens = P(None, "seq", "section", "tp")
    return jax.shard_map(
        partial(per_device, mesh.axis_names),
        mesh=mesh,
        in_specs=(
            rows, rows, state, state, state, state,
            line, line, mix, line, line, entry, depths,
            line, line, mix, columns, depths, columns,
        ),
        out_specs=(
            tokens, tokens, state, state, state, state,
            line, line, mix, line, line, entry, depths,
            line, line, mix, columns, depths, columns,
        ),
        check_vma=False,
    )
```
